32 devices in a mesh: dp: 2 (over x), context: 4 (over z), tensor: 4 (over y, core).
Axes of the slice: x: 2, y: 2, z: 4, core: 2. Of those that a mesh axis runs over, the one named last changes fastest.
Arguments:
- tokens: bfloat16 [8192, 2560], P(('dp', 'context')), may hold values from -60 to 60
- gain_attn: bfloat16 [2560], P(('dp', 'context')), may hold values from 0.5 to 1.5
- w_query: bfloat16 [2560, 2560], P(('dp', 'context'), 'tensor'), may hold values from -0.15625 to 0.15625
- key_weight: bfloat16 [2560, 640], P(('dp', 'context'), 'tensor'), may hold values from -0.15625 to 0.15625
- value_weight: bfloat16 [2560, 640], P(('dp', 'context'), 'tensor'), may hold values from -0.125 to 0.125
- w_out: bfloat16 [2560, 2560], P('tensor', ('dp', 'context')), may hold values from -1 to 1
- gain_mlp: bfloat16 [2560], P(('dp', 'context')), may hold values from 0.5 to 1.5
- w_gate: bfloat16 [2560, 7168], P(('dp', 'context'), 'tensor'), may hold values from -0.125 to 0.125
- w_up: bfloat16 [2560, 7168], P(('dp', 'context'), 'tensor'), may hold values from -0.125 to 0.125
- w_down: bfloat16 [7168, 2560], P('tensor', ('dp', 'context')), may hold values from -0.0625 to 0.0625
- cotangent: bfloat16 [8192, 2560], P(('dp', 'context')), may hold values from -6 to 6
- lengths: int32 [4, 3], replicated, may hold values from 256 to 1024, as said below
- order_perm: int32 [8192], replicated, may hold values from 0 to 8191, as said below
- block_order: int32 [8], replicated, may hold values from 0 to 7, as said below
Outputs:
- output: bfloat16 [8192, 2560], P(('dp', 'context'))
- input_grad: bfloat16 [8192, 2560], P(('dp', 'context'))
- grad_gain_attn: float32 [2560], P(('dp', 'context'))
- grad_query: float32 [2560, 2560], P(('dp', 'context'), 'tensor')
- grad_key: float32 [2560, 640], P(('dp', 'context'), 'tensor')
- grad_value: float32 [2560, 640], P(('dp', 'context'), 'tensor')
- grad_out: float32 [2560, 2560], P('tensor', ('dp', 'context'))
- grad_gain_mlp: float32 [2560], P(('dp', 'context'))
- grad_gate: float32 [2560, 7168], P(('dp', 'context'), 'tensor')
- grad_up: float32 [2560, 7168], P(('dp', 'context'), 'tensor')
- grad_down: float32 [7168, 2560], P('tensor', ('dp', 'context'))
The draws below stay inside these ranges and needn't reach their ends.
Inputs may be any that keep to these rules, and one draw needn't show every extreme that they name: A permutation of the 8192 data rows: place q of the sequence order takes data row order_perm[q]. Each run of 1024 places, starting at a multiple of 1024, takes exactly 128 rows from each such run of data rows. `block_order`: A permutation in which entries 2 c and 2 c + 1 sum to 7. `lengths`: each row sums to 2048; its first entry is 1024.
All inputs are finite; a program needn't handle non-finite values.
Results may differ from the reference program's by a relative error of at most 0.025.
Values may be sent and summed in bfloat16 or wider, within the bound.
A program may use at most 320 MiB of HBM per device.

```python
import math
import jax
import jax.numpy as jnp
from jax import lax

MODEL_WIDTH = 2560
QUERY_HEADS = 32
KEY_VALUE_HEADS = 8
HEAD_SIZE = 80
FF = 7168
MB = 2
PACK_TOKENS = 2048
BLOCK = 512
HALFBLOCK = 256
NBLOCKS = 8
ROWS = 1024
PACKS = 4
TOKENS = 8192
N_DP = 2
N_CONTEXT = 4


def draw_tokens(key, part):
    key = jax.random.fold_in(key, 11)
    key_base, key_row, key_col = jax.random.split(key, 3)
    row_scale = jnp.exp(jax.random.uniform(key_row, (TOKENS, 1), jnp.float32, 0.0, math.log(10.0)))
    col_scale = jnp.exp(jax.random.uniform(key_col, (1, MODEL_WIDTH), jnp.float32, 0.0, math.log(10.0)))
    base = jnp.clip(jax.random.normal(key_base, (TOKENS, MODEL_WIDTH), jnp.float32), -6.0, 6.0)
    return (base * row_scale * col_scale / 10.0).astype(jnp.bfloat16)


def draw_lengths(key, part):
    key = jax.random.fold_in(key, 5)
    middle = jax.random.randint(key, (PACKS, 1), PACK_TOKENS // 8, 3 * PACK_TOKENS // 8 + 1).astype(jnp.int32)
    first = jnp.full((PACKS, 1), PACK_TOKENS // 2, jnp.int32)
    return jnp.concatenate([first, middle, PACK_TOKENS // 2 - middle], axis=1).astype(jnp.int32)


def draw_block_order(key, part):
    key = jax.random.fold_in(key, 7)
    key_pairs, key_flip = jax.random.split(key)
    pairs = jax.random.permutation(key_pairs, NBLOCKS // 2).astype(jnp.int32)
    flip = jax.random.randint(key_flip, (NBLOCKS // 2,), 0, 2)
    upper = NBLOCKS - 1 - pairs
    first = jnp.where(flip == 1, upper, pairs)
    second = jnp.where(flip == 1, pairs, upper)
    return jnp.stack([first, second], axis=1).reshape(NBLOCKS).astype(jnp.int32)


def shuffle_rows(key):
    return jax.random.permutation(key, ROWS).astype(jnp.int32)


def draw_order_perm(key, part):
    key = jax.random.fold_in(key, 3)
    key_source, key_dest = jax.random.split(key)
    groups = TOKENS // ROWS
    share = ROWS // groups
    source_perm = jax.vmap(shuffle_rows)(jax.random.split(key_source, groups))
    dest_perm = jax.vmap(shuffle_rows)(jax.random.split(key_dest, groups))
    dest_idx = jnp.arange(groups, dtype=jnp.int32)[:, None, None]
    source_idx = jnp.arange(groups, dtype=jnp.int32)[None, :, None]
    slot_idx = jnp.arange(share, dtype=jnp.int32)[None, None, :]
    data_row = source_idx * ROWS + source_perm[source_idx, dest_idx * share + slot_idx]
    place = dest_idx * ROWS + dest_perm[dest_idx, source_idx * share + slot_idx]
    return jnp.zeros((TOKENS,), jnp.int32).at[place.reshape(-1)].set(data_row.reshape(-1))


def with_spikes(values, key, source, target, blocks, factor):
    owner, partner = [(jnp.arange(values.shape[dim]) // (values.shape[dim] // blocks)).reshape([-1 if axis == dim else 1 for axis in range(values.ndim)]) for dim in (source, target)]
    chosen = jax.random.permutation(key, blocks)[partner]
    strong = (owner == chosen) | (owner == (partner + blocks // 2) % blocks)
    return jnp.where(strong, factor * values, values)


def shard_levels(rng, shape, shards, low, largest):
    def one(dim, blocks):
        draws = jax.random.uniform(jax.random.fold_in(jax.random.fold_in(rng, 6), dim), (blocks,), jnp.float32, low / len(shards), largest / len(shards))
        return jnp.repeat(jnp.exp(draws), shape[dim] // blocks).reshape((-1,) + (1,) * (len(shape) - dim - 1))

    level = one(*shards[0])
    for cut in shards[1:]:
        level = level * one(*cut)
    return level


def scatter_about(key, extent, deviation, most, cuts=(), kind=jnp.bfloat16):
    values = jax.random.normal(key, extent, jnp.float32) * deviation
    if len(cuts) > 0:
        values = shard_levels(key, extent, cuts, -0.22, 0.18) * values
    return jnp.clip(values, min=-most, max=most).astype(kind)


def gaussian_with(rng, dims, deviation, most, cuts, heavy, kind=jnp.bfloat16):
    values = deviation * jax.random.normal(rng, dims, jnp.float32)
    if cuts:
        values = values * shard_levels(rng, dims, cuts, -0.22, 0.18)
    return jnp.clip(with_spikes(values, jax.random.fold_in(rng, 3), *heavy), -most, most).astype(kind)


def setup_inputs(seed: int = 0) -> dict:
    key_of = jax.random.split(jax.random.key(seed), 15)
    return {
        "tokens": draw_tokens(jax.random.fold_in(key_of[14], 71), 0),
        "gain_attn": jnp.clip(1.0 + 0.1 * jax.random.normal(key_of[1], (MODEL_WIDTH,), jnp.float32), 0.5, 1.5).astype(jnp.bfloat16),
        "w_query": scatter_about(key_of[2], (MODEL_WIDTH, QUERY_HEADS * HEAD_SIZE), (MODEL_WIDTH // 2) ** -0.5, 0.15625, ((0, 8), (1, 4))),
        "key_weight": scatter_about(key_of[3], (MODEL_WIDTH, KEY_VALUE_HEADS * HEAD_SIZE), (MODEL_WIDTH // 2) ** -0.5, 0.15625, ((0, 8), (1, 4))),
        "value_weight": scatter_about(key_of[4], (MODEL_WIDTH, KEY_VALUE_HEADS * HEAD_SIZE), MODEL_WIDTH ** -0.5, 0.125, ((0, 8), (1, 4))),
        "w_out": scatter_about(key_of[5], (QUERY_HEADS * HEAD_SIZE, MODEL_WIDTH), (max(QUERY_HEADS * HEAD_SIZE // 64, 1)) ** -0.5, 1.0, ((0, 4), (1, 8))),
        "gain_mlp": jnp.clip(1.0 + 0.1 * jax.random.normal(key_of[6], (MODEL_WIDTH,), jnp.float32), 0.5, 1.5).astype(jnp.bfloat16),
        "w_gate": scatter_about(key_of[7], (MODEL_WIDTH, FF), MODEL_WIDTH ** -0.5, 0.125, ((0, 8), (1, 4))),
        "w_up": scatter_about(key_of[8], (MODEL_WIDTH, FF), MODEL_WIDTH ** -0.5, 0.125, ((0, 8), (1, 4))),
        "w_down": scatter_about(key_of[9], (FF, MODEL_WIDTH), FF ** -0.5, 0.0625, ((0, 4), (1, 8))),
        "cotangent": gaussian_with(key_of[10], (TOKENS, MODEL_WIDTH), 1.0, 6.0, ((0, 8),), (0, 1, 8, 2.0)),
        "lengths": draw_lengths(jax.random.fold_in(key_of[14], 71), 0),
        "order_perm": draw_order_perm(jax.random.fold_in(key_of[14], 71), 0),
        "block_order": draw_block_order(jax.random.fold_in(key_of[14], 71), 0),
    }


EPS = 1e-05
THETA = 1000000.0
MASKED = -1e+30
HIGH = lax.Precision.HIGHEST

@jax.custom_vjp
def lower_precision(v):
    return lax.optimization_barrier(v.astype(jnp.bfloat16)).astype(jnp.float32)

@jax.custom_vjp
def lower_precision_back(v):
    return v

def low_keep(v):
    return (lower_precision(v), None)

def low_pass(kept, grad):
    return (grad,)

def back_keep(v):
    return (v, None)

def back_low(kept, grad):
    return (lower_precision(grad),)
lower_precision.defvjp(low_keep, low_pass)
lower_precision_back.defvjp(back_keep, back_low)

def matrix_multiply(left, right):
    return jnp.dot(left, right, precision=HIGH, preferred_element_type=jnp.float32)

def rotate(field, positions):
    half_width = field.shape[-1] // 2
    freq = THETA ** (-2.0 * jnp.arange(half_width, dtype=jnp.float32) / field.shape[-1])
    angle = positions.astype(jnp.float32)[:, None] * freq[None, :]
    cosine = jnp.cos(angle)[:, None, :]
    sine = jnp.sin(angle)[:, None, :]
    first = field[..., :half_width]
    second = field[..., half_width:]
    return jnp.concatenate([first * cosine - second * sine, second * cosine + first * sine], axis=-1)

def rms_norm(value_tensor, gain):
    return value_tensor * lax.rsqrt(lax.optimization_barrier(jnp.mean(value_tensor * value_tensor, axis=-1, keepdims=True)) + EPS) * gain

def attention(queries, key_tensor, value_tensor, segment, position):
    step_spacing = 512 if PACK_TOKENS % 512 == 0 else PACK_TOKENS
    count = PACK_TOKENS // step_spacing
    repeat_heads = QUERY_HEADS // KEY_VALUE_HEADS

    def one_block(item):
        query_block, s_block, p_block = item
        grouped_heads = query_block.reshape(step_spacing, KEY_VALUE_HEADS, repeat_heads, HEAD_SIZE)
        scores = lower_precision_back(jnp.einsum('qgrd,kgd->grqk', grouped_heads, key_tensor, precision=HIGH) * HEAD_SIZE ** (-0.5))
        allowed = (s_block[:, None] == segment[None, :]) & (position[None, :] <= p_block[:, None])
        scores = jnp.where(allowed, scores, MASKED)
        expo = jnp.exp(scores - lax.optimization_barrier(jnp.max(scores, axis=-1, keepdims=True)))
        probs = lower_precision(expo / lax.optimization_barrier(jnp.sum(expo, axis=-1, keepdims=True)))
        mixed = jnp.einsum('grqk,kgd->qgrd', probs, value_tensor, precision=HIGH)
        return mixed.reshape(step_spacing, QUERY_HEADS * HEAD_SIZE)
    blocks = lax.map(jax.checkpoint(one_block), (queries.reshape(count, step_spacing, QUERY_HEADS, HEAD_SIZE), segment.reshape(count, step_spacing), position.reshape(count, step_spacing)))
    return blocks.reshape(PACK_TOKENS, QUERY_HEADS * HEAD_SIZE)

def pack_layer(weights, inputs, segment, position):
    gain_attn, w_query, key_weight, value_weight, w_out, gain_mlp, w_gate, w_up, w_down = weights
    normalized_input = lower_precision(rms_norm(inputs, gain_attn))
    queries = lower_precision_back(matrix_multiply(normalized_input, w_query)).reshape(PACK_TOKENS, QUERY_HEADS, HEAD_SIZE)
    key_tensor = lower_precision_back(matrix_multiply(normalized_input, key_weight)).reshape(PACK_TOKENS, KEY_VALUE_HEADS, HEAD_SIZE)
    value_tensor = lower_precision(lower_precision_back(matrix_multiply(normalized_input, value_weight))).reshape(PACK_TOKENS, KEY_VALUE_HEADS, HEAD_SIZE)
    queries = lower_precision(rotate(queries, position))
    key_tensor = lower_precision(rotate(key_tensor, position))
    mixed = lower_precision(lower_precision_back(attention(queries, key_tensor, value_tensor, segment, position)))
    middle = inputs + lower_precision_back(matrix_multiply(mixed, w_out))
    normed_two = lower_precision(rms_norm(middle, gain_mlp))
    gate = lower_precision_back(matrix_multiply(normed_two, w_gate))
    up_proj = lower_precision_back(matrix_multiply(normed_two, w_up))
    inner = lower_precision(jax.nn.silu(gate) * up_proj)
    return middle + matrix_multiply(inner, w_down)

def pack_rows(order_perm, block_order):
    slots = jnp.arange(NBLOCKS, dtype=jnp.int32)
    where_block = lax.optimization_barrier(jnp.sum(slots[None, :] * (block_order[None, :] == slots[:, None]).astype(jnp.int32), axis=1))
    place = jnp.arange(PACK_TOKENS, dtype=jnp.int32)
    slot = where_block[place // HALFBLOCK]
    device = slot // 2
    local = slot % 2 * HALFBLOCK + place % HALFBLOCK
    group = jnp.arange(N_DP, dtype=jnp.int32)[:, None, None]
    micro = jnp.arange(MB, dtype=jnp.int32)[None, :, None]
    index = (group * N_CONTEXT + device[None, None, :]) * ROWS + micro * BLOCK + local[None, None, :]
    return order_perm[index.reshape(PACKS, PACK_TOKENS)]

def segments_of(lengths_row):
    place = jnp.arange(PACK_TOKENS, dtype=jnp.int32)
    first = lengths_row[0]
    second = lengths_row[0] + lengths_row[1]
    segment = (place >= first).astype(jnp.int32) + (place >= second).astype(jnp.int32)
    start = jnp.where(segment == 0, 0, jnp.where(segment == 1, first, second))
    return (segment, place - start)

def reference(tokens, gain_attn, w_query, key_weight, value_weight, w_out, gain_mlp, w_gate, w_up, w_down, cotangent, lengths, order_perm, block_order):
    rows_index = pack_rows(order_perm, block_order)
    flat = rows_index.reshape(-1)
    inverse = jnp.zeros((TOKENS,), jnp.int32).at[flat].set(jnp.arange(TOKENS, dtype=jnp.int32))
    segment, position = jax.vmap(segments_of)(lengths)
    layer = jax.checkpoint(pack_layer)

    def forward(inputs, weights):
        packed = inputs[rows_index]

        def step(carry, item):
            return (carry, layer(weights, item[0], item[1], item[2]))
        unused, result = lax.scan(step, jnp.zeros((), jnp.float32), (packed, segment, position))
        return result.reshape(TOKENS, MODEL_WIDTH)[inverse]
    weights = (gain_attn.astype(jnp.float32), w_query.astype(jnp.float32), key_weight.astype(jnp.float32), value_weight.astype(jnp.float32), w_out.astype(jnp.float32), gain_mlp.astype(jnp.float32), w_gate.astype(jnp.float32), w_up.astype(jnp.float32), w_down.astype(jnp.float32))
    output, pull = jax.vjp(forward, tokens.astype(jnp.float32), weights)
    input_grad, grads = pull(cotangent.astype(jnp.float32))
    return (output.astype(jnp.bfloat16), input_grad.astype(jnp.bfloat16), grads[0], grads[1], grads[2], grads[3], grads[4], grads[5], grads[6], grads[7], grads[8])
```

```python
import functools

import jax
import jax.numpy as jnp
import numpy as np
from jax import lax
from jax.experimental import pallas as pl
from jax.experimental.pallas import tpu as pltpu
from jax.sharding import PartitionSpec as P

HEAD_SIZE = 80
MB = 2


EPS = 1e-05
THETA = 1000000.0
MASKED = -1e30


def rotate(field, positions, sign):
    half_width = field.shape[-1] // 2
    freq = THETA ** (-2.0 * jnp.arange(half_width, dtype=jnp.float32) / field.shape[-1])
    angle = positions.astype(jnp.float32)[:, None] * freq[None, :]
    cosine = jnp.cos(angle)[:, None, :]
    sine = sign * jnp.sin(angle)[:, None, :]
    first = field[..., :half_width]
    second = field[..., half_width:]
    return jnp.concatenate(
        [first * cosine - second * sine, second * cosine + first * sine], axis=-1
    )


def times_t(left, right):
    return lax.dot_general(
        left, right, (((1,), (1,)), ((), ())), preferred_element_type=jnp.float32
    )


def t_times(left, right):
    return lax.dot_general(
        left, right, (((0,), (0,)), ((), ())), preferred_element_type=jnp.float32
    )


def invert(index):
    count = index.shape[0]
    iota = jnp.arange(count, dtype=jnp.int32)
    return jnp.sum(iota[None, :] * (index[None, :] == iota[:, None]).astype(jnp.int32), axis=1)


def route_plan(order_perm, groups, rows, my_index):
    share = rows // groups
    places = order_perm.reshape(groups, rows)
    source = places // rows
    mine = (source == my_index).astype(jnp.int32)
    rank = jnp.cumsum(mine, axis=1) - 1
    slots = jnp.arange(share, dtype=jnp.int32)
    pick = mine[:, :, None] * (rank[:, :, None] == slots[None, None, :]).astype(jnp.int32)
    send_index = jnp.sum(pick * (places % rows)[:, :, None], axis=1).reshape(rows)
    own = lax.dynamic_index_in_dim(places, my_index, 0, keepdims=False)
    own_source = own // rows
    onehot = (own_source[:, None] == jnp.arange(groups, dtype=jnp.int32)[None, :]).astype(jnp.int32)
    own_rank = jnp.sum((jnp.cumsum(onehot, axis=0) - 1) * onehot, axis=1)
    return (send_index, own_source * share + own_rank)


def pack_places(count, block_rows, half_rows, block_order):
    index = jnp.arange(count, dtype=jnp.int32)
    slot = 2 * (index // block_rows) + index % block_rows // half_rows
    table = (slot[:, None] == jnp.arange(block_order.shape[0], dtype=jnp.int32)[None, :]).astype(
        jnp.int32
    )
    which = jnp.sum(table * block_order[None, :], axis=1)
    return which * half_rows + index % half_rows


def segment_info(places, seq_lengths):
    first = seq_lengths[0]
    second = seq_lengths[0] + seq_lengths[1]
    segment = (places >= first).astype(jnp.int32) + (places >= second).astype(jnp.int32)
    start = jnp.where(segment == 0, 0, jnp.where(segment == 1, first, second))
    return (segment, places - start)


def norm_forward(value_tensor, gain):
    root = lax.rsqrt(jnp.mean(value_tensor * value_tensor, axis=-1, keepdims=True) + EPS)
    return (root, (value_tensor * root * gain).astype(jnp.bfloat16))


def norm_backward(value_tensor, root, gain, grad):
    weighted = grad * gain
    cubed = root * root * root
    d_values = root * weighted - value_tensor * cubed * jnp.mean(
        weighted * value_tensor, axis=-1, keepdims=True
    )
    return (d_values, jnp.sum(grad * value_tensor * root, axis=0))


def key_split(count):
    step = 512
    return (count // step, step)


def block_scores(q_group, key_block, pos_block, seg_block, q_pos, q_seg, scale):
    scores = (
        jnp.einsum("qgrd,kgd->grqk", q_group, key_block, preferred_element_type=jnp.float32) * scale
    )
    allowed = (q_seg[:, None] == seg_block[None, :]) & (pos_block[None, :] <= q_pos[:, None])
    return (jnp.where(allowed, scores, MASKED), allowed)


def key_items(key_tensor, value_tensor, k_pos, k_seg, heads_kv):
    count, step = key_split(key_tensor.shape[0])
    return (
        key_tensor.reshape(count, step, heads_kv, HEAD_SIZE),
        value_tensor.reshape(count, step, heads_kv, HEAD_SIZE),
        k_pos.reshape(count, step),
        k_seg.reshape(count, step),
    )


def attention_forward(q_group, key_tensor, value_tensor, q_pos, q_seg, k_pos, k_seg, scale):
    heads_kv = q_group.shape[1]
    items = key_items(key_tensor, value_tensor, k_pos, k_seg, heads_kv)
    stat_shape = (heads_kv, q_group.shape[2], q_group.shape[0])

    def measure(carry, item):
        top, total = carry
        scores, allowed = block_scores(q_group, item[0], item[2], item[3], q_pos, q_seg, scale)
        new_top = jnp.maximum(top, jnp.max(scores, axis=-1))
        kept = jnp.where(allowed, jnp.exp(scores - new_top[..., None]), 0.0)
        return ((new_top, total * jnp.exp(top - new_top) + jnp.sum(kept, axis=-1)), None)

    start = (jnp.full(stat_shape, MASKED, jnp.float32), jnp.zeros(stat_shape, jnp.float32))
    (top, total), unused = lax.scan(measure, start, items)

    def mix(acc, item):
        scores, allowed = block_scores(q_group, item[0], item[2], item[3], q_pos, q_seg, scale)
        probs = jnp.where(allowed, jnp.exp(scores - top[..., None]) / total[..., None], 0.0).astype(
            jnp.bfloat16
        )
        return (
            acc + jnp.einsum("grqk,kgd->qgrd", probs, item[1], preferred_element_type=jnp.float32),
            None,
        )

    attended, unused = lax.scan(mix, jnp.zeros(q_group.shape, jnp.float32), items)
    return (attended, top, total)


def attention_backward(
    q_group, key_tensor, value_tensor, q_pos, q_seg, k_pos, k_seg, top, total, d_out, delta, scale
):
    heads_kv = q_group.shape[1]
    items = key_items(key_tensor, value_tensor, k_pos, k_seg, heads_kv)
    step = items[2].shape[1]

    def visit(d_query, item):
        scores, allowed = block_scores(q_group, item[0], item[2], item[3], q_pos, q_seg, scale)
        weight = jnp.where(allowed, jnp.exp(scores - top[..., None]) / total[..., None], 0.0)
        d_prob = jnp.einsum("qgrd,kgd->grqk", d_out, item[1], preferred_element_type=jnp.float32)
        d_score = (weight * (d_prob - delta[..., None])).astype(jnp.bfloat16)
        d_query = d_query + jnp.einsum(
            "grqk,kgd->qgrd", d_score, item[0], preferred_element_type=jnp.float32
        )
        d_key = (
            jnp.einsum("grqk,qgrd->kgd", d_score, q_group, preferred_element_type=jnp.float32)
            * scale
        )
        d_value = jnp.einsum(
            "grqk,qgrd->kgd", weight.astype(jnp.bfloat16), d_out, preferred_element_type=jnp.float32
        )
        return (d_query, (d_key.reshape(step, -1), d_value.reshape(step, -1)))

    d_query, (d_keys, d_values) = lax.scan(visit, jnp.zeros(q_group.shape, jnp.float32), items)
    return (
        d_query * scale,
        d_keys.reshape(key_tensor.shape[0], -1),
        d_values.reshape(key_tensor.shape[0], -1),
    )


def fetch_attention(gain_attn, w_query, key_weight, value_weight, w_out):
    return (
        lax.all_gather(gain_attn, ("dp", "context"), axis=0, tiled=True),
        lax.all_gather(w_query, ("dp", "context"), axis=0, tiled=True),
        lax.all_gather(key_weight, ("dp", "context"), axis=0, tiled=True),
        lax.all_gather(value_weight, ("dp", "context"), axis=0, tiled=True),
        lax.all_gather(w_out, ("dp", "context"), axis=1, tiled=True),
    )


def fetch_mlp(gain_mlp, w_gate, w_up, w_down):
    return (
        lax.all_gather(gain_mlp, ("dp", "context"), axis=0, tiled=True),
        lax.all_gather(w_gate, ("dp", "context"), axis=0, tiled=True),
        lax.all_gather(w_up, ("dp", "context"), axis=0, tiled=True),
        lax.all_gather(w_down, ("dp", "context"), axis=1, tiled=True),
    )


def head_sum(partial_sum):
    return lax.psum(partial_sum.astype(jnp.bfloat16), "tensor").astype(jnp.float32)


def on_device(
    tokens,
    gain_attn,
    w_query,
    key_weight,
    value_weight,
    w_out,
    gain_mlp,
    w_gate,
    w_up,
    w_down,
    cotangent,
    lengths,
    order_perm,
    block_order,
):
    devices_ctx = lax.axis_size("context")
    groups = lax.axis_size("dp") * devices_ctx
    group_id = lax.axis_index("dp")
    place = lax.axis_index("context")
    my_index = group_id * devices_ctx + place
    rows = tokens.shape[0]
    width = tokens.shape[1]
    block_rows = rows // MB
    half_rows = block_rows // 2
    share = rows // groups
    scale = HEAD_SIZE ** (-0.5)
    send_index, recv_index = route_plan(order_perm, groups, rows, my_index)
    arrived = (
        lax.all_to_all(
            tokens[send_index].reshape(groups, share, width),
            ("dp", "context"),
            split_axis=0,
            concat_axis=0,
            tiled=True,
        ),
        lax.all_to_all(
            cotangent[send_index].reshape(groups, share, width),
            ("dp", "context"),
            split_axis=0,
            concat_axis=0,
            tiled=True,
        ),
    )
    seq_tokens = arrived[0].reshape(rows, width)[recv_index]
    seq_cot = arrived[1].reshape(rows, width)[recv_index]
    whole_place = pack_places(block_rows * devices_ctx, block_rows, half_rows, block_order)
    acc_gain_a = jnp.zeros((width,), jnp.float32)
    acc_query = jnp.zeros((width, w_query.shape[1]), jnp.float32)
    acc_key = jnp.zeros((width, key_weight.shape[1]), jnp.float32)
    acc_value = jnp.zeros((width, value_weight.shape[1]), jnp.float32)
    acc_out = jnp.zeros((w_out.shape[0], width), jnp.float32)
    acc_gain_m = jnp.zeros((width,), jnp.float32)
    acc_gate = jnp.zeros((width, w_gate.shape[1]), jnp.float32)
    acc_up = jnp.zeros((width, w_up.shape[1]), jnp.float32)
    acc_down = jnp.zeros((w_down.shape[0], width), jnp.float32)
    outputs = []
    input_grads = []
    for micro in range(MB):
        seq_lengths = lax.dynamic_index_in_dim(lengths, group_id * MB + micro, 0, keepdims=False)
        key_seg, key_pos = segment_info(whole_place, seq_lengths)
        q_seg = lax.dynamic_slice_in_dim(key_seg, place * block_rows, block_rows)
        q_pos = lax.dynamic_slice_in_dim(key_pos, place * block_rows, block_rows)
        inputs_f = seq_tokens[micro * block_rows : (micro + 1) * block_rows].astype(jnp.float32)
        d_y = seq_cot[micro * block_rows : (micro + 1) * block_rows]
        attn_now = fetch_attention(gain_attn, w_query, key_weight, value_weight, w_out)
        gain_a, w_q, w_k, w_v, w_o = attn_now
        root_a, normed_one = norm_forward(inputs_f, gain_a.astype(jnp.float32))
        q_lin = jnp.dot(normed_one, w_q, preferred_element_type=jnp.float32)
        k_lin = jnp.dot(normed_one, w_k, preferred_element_type=jnp.float32)
        v_lin = jnp.dot(normed_one, w_v, preferred_element_type=jnp.float32)
        heads_kv = k_lin.shape[1] // HEAD_SIZE
        q_group = rotate(q_lin.reshape(block_rows, -1, HEAD_SIZE), q_pos, 1.0).astype(jnp.bfloat16)
        q_group = q_group.reshape(block_rows, heads_kv, -1, HEAD_SIZE)
        k_in = (
            rotate(k_lin.reshape(block_rows, heads_kv, HEAD_SIZE), q_pos, 1.0)
            .astype(jnp.bfloat16)
            .reshape(block_rows, -1)
        )
        v_in = v_lin.astype(jnp.bfloat16)
        key_tensor, value_tensor = (
            lax.all_gather(k_in, "context", axis=0, tiled=True),
            lax.all_gather(v_in, "context", axis=0, tiled=True),
        )
        attended, top, total = attention_forward(
            q_group, key_tensor, value_tensor, q_pos, q_seg, key_pos, key_seg, scale
        )
        o_in = attended.reshape(block_rows, -1).astype(jnp.bfloat16)
        mid_state = inputs_f + head_sum(jnp.dot(o_in, w_o, preferred_element_type=jnp.float32))
        mlp_now = fetch_mlp(gain_mlp, w_gate, w_up, w_down)
        gain_m, w_g, w_u, w_d = mlp_now
        root_m, normed_two = norm_forward(mid_state, gain_m.astype(jnp.float32))
        gate = jnp.dot(normed_two, w_g, preferred_element_type=jnp.float32)
        up_proj = jnp.dot(normed_two, w_u, preferred_element_type=jnp.float32)
        sigma = jax.nn.sigmoid(gate)
        silu_gate = gate * sigma
        inner = (silu_gate * up_proj).astype(jnp.bfloat16)
        result = mid_state + head_sum(jnp.dot(inner, w_d, preferred_element_type=jnp.float32))
        outputs.append(result.astype(jnp.bfloat16))
        mlp_back = fetch_mlp(gain_mlp, w_gate, w_up, w_down)
        gain_m, w_g, w_u, w_d = mlp_back
        d_inner = times_t(d_y, w_d)
        acc_down = acc_down + t_times(inner, d_y)
        d_gate = (d_inner * up_proj * sigma * (1.0 + gate * (1.0 - sigma))).astype(jnp.bfloat16)
        d_up = (d_inner * silu_gate).astype(jnp.bfloat16)
        d_two = head_sum(times_t(d_gate, w_g) + times_t(d_up, w_u))
        acc_gate = acc_gate + t_times(normed_two, d_gate)
        acc_up = acc_up + t_times(normed_two, d_up)
        d_mid, gain_grad_m = norm_backward(mid_state, root_m, gain_m.astype(jnp.float32), d_two)
        acc_gain_m = acc_gain_m + gain_grad_m
        d_mid = d_y.astype(jnp.float32) + d_mid
        d_mid_low = d_mid.astype(jnp.bfloat16)
        attn_back = fetch_attention(gain_attn, w_query, key_weight, value_weight, w_out)
        gain_a, w_q, w_k, w_v, w_o = attn_back
        acc_out = acc_out + t_times(o_in, d_mid_low)
        d_out = times_t(d_mid_low, w_o).astype(jnp.bfloat16).reshape(q_group.shape)
        delta = jnp.sum(d_out.astype(jnp.float32) * attended, axis=-1).transpose(1, 2, 0)
        d_query, d_keys, d_values = attention_backward(
            q_group,
            key_tensor,
            value_tensor,
            q_pos,
            q_seg,
            key_pos,
            key_seg,
            top,
            total,
            d_out,
            delta,
            scale,
        )
        own_keys, own_values = (
            lax.psum_scatter(
                d_keys.astype(jnp.bfloat16), "context", scatter_dimension=0, tiled=True
            ).astype(jnp.float32),
            lax.psum_scatter(
                d_values.astype(jnp.bfloat16), "context", scatter_dimension=0, tiled=True
            ).astype(jnp.float32),
        )
        d_q_low = (
            rotate(d_query.reshape(block_rows, -1, HEAD_SIZE), q_pos, -1.0)
            .astype(jnp.bfloat16)
            .reshape(block_rows, -1)
        )
        d_k_low = (
            rotate(own_keys.reshape(block_rows, -1, HEAD_SIZE), q_pos, -1.0)
            .astype(jnp.bfloat16)
            .reshape(block_rows, -1)
        )
        d_v_low = own_values.astype(jnp.bfloat16)
        d_one = head_sum(times_t(d_q_low, w_q) + times_t(d_k_low, w_k) + times_t(d_v_low, w_v))
        acc_query = acc_query + t_times(normed_one, d_q_low)
        acc_key = acc_key + t_times(normed_one, d_k_low)
        acc_value = acc_value + t_times(normed_one, d_v_low)
        d_inputs, gain_grad_a = norm_backward(inputs_f, root_a, gain_a.astype(jnp.float32), d_one)
        acc_gain_a = acc_gain_a + gain_grad_a
        input_grads.append((d_mid + d_inputs).astype(jnp.bfloat16))
    grads_attn = (
        lax.psum_scatter(
            acc_gain_a.astype(jnp.bfloat16), ("dp", "context"), scatter_dimension=0, tiled=True
        ).astype(jnp.float32),
        lax.psum_scatter(
            acc_query.astype(jnp.bfloat16), ("dp", "context"), scatter_dimension=0, tiled=True
        ).astype(jnp.float32),
        lax.psum_scatter(
            acc_key.astype(jnp.bfloat16), ("dp", "context"), scatter_dimension=0, tiled=True
        ).astype(jnp.float32),
        lax.psum_scatter(
            acc_value.astype(jnp.bfloat16), ("dp", "context"), scatter_dimension=0, tiled=True
        ).astype(jnp.float32),
        lax.psum_scatter(
            acc_out.astype(jnp.bfloat16), ("dp", "context"), scatter_dimension=1, tiled=True
        ).astype(jnp.float32),
    )
    grads_mlp = (
        lax.psum_scatter(
            acc_gain_m.astype(jnp.bfloat16), ("dp", "context"), scatter_dimension=0, tiled=True
        ).astype(jnp.float32),
        lax.psum_scatter(
            acc_gate.astype(jnp.bfloat16), ("dp", "context"), scatter_dimension=0, tiled=True
        ).astype(jnp.float32),
        lax.psum_scatter(
            acc_up.astype(jnp.bfloat16), ("dp", "context"), scatter_dimension=0, tiled=True
        ).astype(jnp.float32),
        lax.psum_scatter(
            acc_down.astype(jnp.bfloat16), ("dp", "context"), scatter_dimension=1, tiled=True
        ).astype(jnp.float32),
    )
    seq_out = jnp.concatenate(outputs, axis=0)
    seq_grad = jnp.concatenate(input_grads, axis=0)
    back_index = invert(recv_index)
    returned = (
        lax.all_to_all(
            seq_out[back_index].reshape(groups, share, width),
            ("dp", "context"),
            split_axis=0,
            concat_axis=0,
            tiled=True,
        ),
        lax.all_to_all(
            seq_grad[back_index].reshape(groups, share, width),
            ("dp", "context"),
            split_axis=0,
            concat_axis=0,
            tiled=True,
        ),
    )
    data_index = invert(send_index)
    output = returned[0].reshape(rows, width)[data_index]
    input_grad = returned[1].reshape(rows, width)[data_index]
    return (
        output,
        input_grad,
        grads_attn[0],
        grads_attn[1],
        grads_attn[2],
        grads_attn[3],
        grads_attn[4],
        grads_mlp[0],
        grads_mlp[1],
        grads_mlp[2],
        grads_mlp[3],
    )


BF = jnp.bfloat16
F32 = jnp.float32
TILE = 256
LANES = 128
GROUP = 4


def mm(left, right):
    return jnp.dot(left, right, preferred_element_type=F32)


def one_hot(rows, columns):
    return jnp.where(rows == columns, 1.0, 0.0).astype(BF)


def turn(u, cosine, sine):
    return u * cosine + pltpu.roll(u, LANES // 2, 1) * sine


def place_rows(index_col_ref, count):
    column = index_col_ref[0]
    lanes = lax.broadcasted_iota(jnp.int32, (column.shape[0], count), 1)
    return one_hot(lanes, column)


def arrival_rows(index_row_ref, count):
    row = index_row_ref[0]
    rows = lax.broadcasted_iota(jnp.int32, (count, row.shape[1]), 0)
    return one_hot(rows, row)


def sort_kernel(mine, other, cosine, sine, index_col, q_out, kv_out, picks):
    group = pl.program_id(1)

    @pl.when(group == 0)
    def _():
        picks[...] = place_rows(index_col, picks.shape[1])

    u = jnp.concatenate([mine[...], other[...]], axis=0)
    cos_t, sin_t = cosine[0], sine[0]
    first = turn(u[:, :LANES], cos_t, sin_t)

    @pl.when(group < 2)
    def _():
        second = turn(u[:, LANES:], cos_t, sin_t)
        both = jnp.concatenate([first, second], axis=1).astype(BF)
        q_out[...] = mm(picks[...], both).astype(BF)

    @pl.when(group == 2)
    def _():
        both = jnp.concatenate([first, u[:, LANES:]], axis=1).astype(BF)
        kv_out[...] = mm(picks[...], both).astype(BF)


def scores_of(meta, block, q_head, kv, count, scale):
    limit = meta[block, 1]
    rows = lax.broadcasted_iota(jnp.int32, (TILE, TILE), 0)
    lanes = lax.broadcasted_iota(jnp.int32, (TILE, TILE), 1)
    places = (count - 1) * TILE + rows
    found = []
    for item in range(count):
        start = pl.multiple_of(meta[block, 2 + item], TILE)
        keys = kv[pl.ds(start, TILE), :LANES]
        scores = times_t(q_head, keys) * scale
        allowed = (item * TILE + lanes >= limit) | (places < limit)
        if item == count - 1:
            allowed = allowed & (lanes <= rows)
        found.append(jnp.where(allowed, scores, MASKED))
    return found


def probabilities(found):
    top = functools.reduce(jnp.maximum, [jnp.max(s, axis=1, keepdims=True) for s in found])
    raised = [jnp.exp(s - top) for s in found]
    total = functools.reduce(jnp.add, [jnp.sum(e, axis=1, keepdims=True) for e in raised])
    inverse = 1.0 / total
    return [e * inverse for e in raised]


def forward_kernel(
    meta, q, kv, index_row, unpad, mine, other, total, picks, *, scale, blocks, per_run
):
    block, head = pl.program_id(0), pl.program_id(1)
    columns = pl.ds(pl.multiple_of(head * LANES, LANES), LANES)
    part = lax.rem(block, per_run)

    @pl.when(head == 0)
    def _():
        picks[...] = arrival_rows(index_row, picks.shape[0])

    @pl.when((head == 0) & (part == 0))
    def _():
        total[...] = jnp.zeros_like(total)

    def attend(count):
        found = scores_of(meta, block, q[...], kv, count, scale)
        probs = probabilities(found)
        mixed = jnp.zeros((TILE, LANES), F32)
        for item in range(count):
            start = pl.multiple_of(meta[block, 2 + item], TILE)
            mixed = mixed + mm(probs[item].astype(BF), kv[pl.ds(start, TILE), LANES:])
        total[:, columns] += mm(picks[...], mixed.astype(BF))

    for count in range(1, blocks + 1):
        pl.when(meta[block, 0] == count - 1)(functools.partial(attend, count))

    @pl.when((head == GROUP - 1) & (part == per_run - 1))
    def _():
        packed = mm(total[...].astype(BF), unpad[...]).astype(BF)
        half = packed.shape[0] // 2
        rows = pl.ds(pl.multiple_of(block // per_run * half, TILE), half)
        mine[rows, :] = packed[:half]
        other[rows, :] = packed[half:]


def backward_kernel(
    meta,
    q,
    kv,
    d_mine,
    d_other,
    index_col,
    index_row,
    cosine,
    sine,
    q_mine,
    q_other,
    own,
    sent,
    total,
    picks,
    places,
    keys_grad,
    *,
    scale,
    blocks,
    per_run,
):
    block, head = pl.program_id(0), pl.program_id(1)
    columns = pl.ds(pl.multiple_of(head * LANES, LANES), LANES)
    part = lax.rem(block, per_run)
    half = picks.shape[0] // 2

    @pl.when((block == 0) & (head == 0))
    def _():
        keys_grad[...] = jnp.zeros_like(keys_grad)

    @pl.when(head == 0)
    def _():
        picks[...] = arrival_rows(index_row, picks.shape[0])
        places[...] = place_rows(index_col, places.shape[1])

    @pl.when((head == 0) & (part == 0))
    def _():
        total[...] = jnp.zeros_like(total)

    def attend(count):
        found = scores_of(meta, block, q[...], kv, count, scale)
        probs = probabilities(found)
        d_out = mm(places[:, :half], d_mine[...]) + mm(places[:, half:], d_other[...])
        d_out = d_out.astype(BF)
        starts = [pl.multiple_of(meta[block, 2 + item], TILE) for item in range(count)]
        d_probs = [times_t(d_out, kv[pl.ds(start, TILE), LANES:]) for start in starts]
        delta = functools.reduce(
            jnp.add,
            [jnp.sum(p * d, axis=1, keepdims=True) for p, d in zip(probs, d_probs, strict=True)],
        )
        d_query = jnp.zeros((TILE, LANES), F32)
        for item, start in enumerate(starts):
            rows = pl.ds(start, TILE)
            d_score = (probs[item] * (d_probs[item] - delta)).astype(BF)
            d_query = d_query + mm(d_score, kv[rows, :LANES])
            keys_grad[rows, :LANES] += t_times(d_score, q[...])
            keys_grad[rows, LANES:] += t_times(probs[item].astype(BF), d_out)
        turned = turn(d_query * scale, cosine[...], -sine[...])
        total[:, columns] += mm(picks[...], turned.astype(BF))

    for count in range(1, blocks + 1):
        pl.when(meta[block, 0] == count - 1)(functools.partial(attend, count))

    @pl.when((head == GROUP - 1) & (part == per_run - 1))
    def _():
        rows = pl.ds(pl.multiple_of(block // per_run * half, TILE), half)
        q_mine[rows, :] = total[:half].astype(BF)
        q_other[rows, :] = total[half:].astype(BF)

    @pl.when((head == GROUP - 1) & (block == pl.num_programs(0) - 1))
    def _():
        count = own.shape[0]
        own[...] = keys_grad[:count]
        sent[...] = keys_grad[count:].astype(BF)


def unsort_kernel(
    own, got, cosine, sine, index_row, q_mine, q_other, unpad, mine, other, *, scale
):
    both = own[...] + got[...].astype(F32)
    d_keys = turn(both[:, :LANES] * scale, cosine[0], -sine[0])
    low = jnp.concatenate([d_keys, both[:, LANES:]], axis=1).astype(BF)
    moved = mm(arrival_rows(index_row, low.shape[0]), low).astype(BF)
    half = moved.shape[0] // 2
    split = q_mine.shape[1]
    for rows, d_query, out in (
        (moved[:half], q_mine, mine),
        (moved[half:], q_other, other),
    ):
        packed = mm(d_query[...], unpad[:split]) + mm(rows, unpad[split:])
        out[...] = packed.astype(BF)


def resident(shape):
    return pl.BlockSpec(shape, lambda *unused: (0,) * len(shape))


def call_sort(lin_mine, lin_other, cosine, sine, index_col):
    half, runs = lin_mine.shape[0] // 2, 2
    run_rows = 2 * half
    wide = 2 * LANES
    return pl.pallas_call(
        sort_kernel,
        grid=(runs, 3),
        in_specs=[
            pl.BlockSpec((half, wide), lambda d, g: (d, g)),
            pl.BlockSpec((half, wide), lambda d, g: (d, g)),
            pl.BlockSpec((1, run_rows, LANES), lambda d, g: (d, 0, 0)),
            pl.BlockSpec((1, run_rows, LANES), lambda d, g: (d, 0, 0)),
            pl.BlockSpec((1, run_rows, 1), lambda d, g: (d, 0, 0)),
        ],
        out_specs=[
            pl.BlockSpec((run_rows, wide), lambda d, g: (d, jnp.minimum(g, 1))),
            pl.BlockSpec((run_rows, wide), lambda d, g: (d, 0)),
        ],
        out_shape=[
            jax.ShapeDtypeStruct((runs * run_rows, GROUP * LANES), BF),
            jax.ShapeDtypeStruct((runs * run_rows, wide), BF),
        ],
        scratch_shapes=[pltpu.VMEM((run_rows, run_rows), BF)],
        compiler_params=pltpu.CompilerParams(vmem_limit_bytes=40 * 2**20),
        cost_estimate=pl.CostEstimate(
            flops=12 * run_rows * run_rows * wide, bytes_accessed=20 * 2**20, transcendentals=0
        ),
        name="sort_tokens",
    )(lin_mine, lin_other, cosine, sine, index_col)


def call_forward(meta, q, kv, index_row, unpad, scale):
    tokens = q.shape[0]
    run_rows = tokens // 2
    per_run = run_rows // TILE
    blocks = meta.shape[1] - 2
    body = functools.partial(forward_kernel, scale=scale, blocks=blocks, per_run=per_run)
    out = jax.ShapeDtypeStruct((run_rows, unpad.shape[1]), BF)
    return pl.pallas_call(
        body,
        grid=(2 * per_run, GROUP),
        in_specs=[
            pl.BlockSpec(memory_space=pltpu.SMEM),
            pl.BlockSpec((TILE, LANES), lambda b, h: (b, h)),
            resident(kv.shape),
            pl.BlockSpec((1, 1, TILE), lambda b, h: (b // per_run, 0, b % per_run)),
            resident(unpad.shape),
        ],
        out_specs=[resident(out.shape), resident(out.shape)],
        out_shape=[out, out],
        scratch_shapes=[
            pltpu.VMEM((run_rows, GROUP * LANES), F32),
            pltpu.VMEM((run_rows, TILE), BF),
        ],
        compiler_params=pltpu.CompilerParams(vmem_limit_bytes=40 * 2**20),
        cost_estimate=pl.CostEstimate(
            flops=2 * 10**10, bytes_accessed=8 * 2**20, transcendentals=6 * 10**6
        ),
        name="attention_forward",
    )(meta, q, kv, index_row, unpad)


def call_backward(meta, q, kv, d_mine, d_other, index_col, index_row, cosine, sine, scale):
    tokens = q.shape[0]
    run_rows = tokens // 2
    per_run = run_rows // TILE
    blocks = meta.shape[1] - 2
    body = functools.partial(backward_kernel, scale=scale, blocks=blocks, per_run=per_run)
    run_half = run_rows // 2
    d_query = jax.ShapeDtypeStruct((run_rows, GROUP * LANES), BF)
    shape = (tokens, 2 * LANES)
    table = pl.BlockSpec((TILE, LANES), lambda b, h: (b, 0))
    return pl.pallas_call(
        body,
        grid=(2 * per_run, GROUP),
        in_specs=[
            pl.BlockSpec(memory_space=pltpu.SMEM),
            pl.BlockSpec((TILE, LANES), lambda b, h: (b, h)),
            resident(kv.shape),
            pl.BlockSpec((run_half, LANES), lambda b, h: (b // per_run, h)),
            pl.BlockSpec((run_half, LANES), lambda b, h: (b // per_run, h)),
            pl.BlockSpec((1, TILE, 1), lambda b, h: (b // per_run, b % per_run, 0)),
            pl.BlockSpec((1, 1, TILE), lambda b, h: (b // per_run, 0, b % per_run)),
            table,
            table,
        ],
        out_specs=[
            resident(d_query.shape),
            resident(d_query.shape),
            resident(shape),
            resident(shape),
        ],
        out_shape=[
            d_query,
            d_query,
            jax.ShapeDtypeStruct(shape, F32),
            jax.ShapeDtypeStruct(shape, BF),
        ],
        scratch_shapes=[
            pltpu.VMEM((run_rows, GROUP * LANES), F32),
            pltpu.VMEM((run_rows, TILE), BF),
            pltpu.VMEM((TILE, run_rows), BF),
            pltpu.VMEM((kv.shape[0], 2 * LANES), F32),
        ],
        compiler_params=pltpu.CompilerParams(vmem_limit_bytes=48 * 2**20),
        cost_estimate=pl.CostEstimate(
            flops=5 * 10**10, bytes_accessed=16 * 2**20, transcendentals=6 * 10**6
        ),
        name="attention_backward",
    )(meta, q, kv, d_mine, d_other, index_col, index_row, cosine, sine)


def call_unsort(own, got, cosine, sine, index_row, q_mine, q_other, unpad, scale):
    run_rows = own.shape[0] // 2
    half = run_rows // 2
    wide = own.shape[1]
    out = jax.ShapeDtypeStruct((run_rows, unpad.shape[1]), BF)
    block = pl.BlockSpec((half, unpad.shape[1]), lambda d: (d, 0))
    d_query = pl.BlockSpec((half, q_mine.shape[1]), lambda d: (d, 0))
    return pl.pallas_call(
        functools.partial(unsort_kernel, scale=scale),
        grid=(2,),
        in_specs=[
            pl.BlockSpec((run_rows, wide), lambda d: (d, 0)),
            pl.BlockSpec((run_rows, wide), lambda d: (d, 0)),
            pl.BlockSpec((1, run_rows, LANES), lambda d: (d, 0, 0)),
            pl.BlockSpec((1, run_rows, LANES), lambda d: (d, 0, 0)),
            pl.BlockSpec((1, 1, run_rows), lambda d: (d, 0, 0)),
            d_query,
            d_query,
            resident(unpad.shape),
        ],
        out_specs=[block, block],
        out_shape=[out, out],
        compiler_params=pltpu.CompilerParams(vmem_limit_bytes=40 * 2**20),
        cost_estimate=pl.CostEstimate(
            flops=4 * 10**9, bytes_accessed=10 * 2**20, transcendentals=0
        ),
        name="unsort_tokens",
    )(own, got, cosine, sine, index_row, q_mine, q_other, unpad)


def head_columns(part, base):
    half = part // 2
    entry = np.arange(part)
    return base + np.where(entry < half, entry, LANES // 2 + entry - half)


def after(value, *events):
    return lax.optimization_barrier((value, *events))[0]


def on_device_paired(
    tokens,
    gain_attn,
    w_query,
    key_weight,
    value_weight,
    w_out,
    gain_mlp,
    w_gate,
    w_up,
    w_down,
    cotangent,
    lengths,
    order_perm,
    block_order,
):
    names = ("dp", "context", "tensor")
    n_dp, n_ctx, n_ten = (lax.axis_size(name) for name in names)
    devices = n_dp * n_ctx * n_ten
    on_core, on_y, on_lo, on_hi, on_dp = 1, 2, n_ten, 2 * n_ten, n_ctx * n_ten
    group = lax.axis_index("dp")
    place = lax.axis_index("context")
    shard = lax.axis_index("tensor")
    high, low = place // 2, place % 2
    row, core = shard // 2, shard % 2
    groups = n_dp * n_ctx
    my_index = group * n_ctx + place
    rows, width = tokens.shape
    share = rows // groups
    part = share // n_ten
    local = rows // n_ten
    block_rows = rows // MB
    half_rows = block_rows // 2
    pack = block_rows * n_ctx
    n_blocks = block_order.shape[0]
    blocks = n_blocks // 2
    scale = HEAD_SIZE ** (-0.5)
    quarter = width // (2 * n_dp)
    eighth = quarter // 2

    def swap(value, bit):
        return lax.ppermute(value, names, [(i, i ^ bit) for i in range(devices)])

    def pick(flag, yes, no):
        return jnp.where(flag == 1, yes, no)

    def relative(value):
        chunks = [value[..., i * quarter : (i + 1) * quarter] for i in range(4)]
        chunks = [pick(high, chunks[i ^ 1], chunks[i]) for i in range(4)]
        chunks = [pick(group, chunks[i ^ 2], chunks[i]) for i in range(4)]
        return jnp.concatenate(chunks, axis=-1)

    def by_low(mine, partner, axis):
        return jnp.concatenate(
            [pick(low, partner, mine), pick(low, mine, partner)], axis=axis
        )

    def gather_weight(value, axis, event=None):
        if event is not None:
            value = after(value, event)
        from_high = swap(value, on_hi)
        from_dp = swap(value, on_dp)
        from_both = swap(from_high, on_dp)
        return jnp.concatenate([value, from_high, from_dp, from_both], axis=axis), from_high

    def scatter_grad(sent, kept):
        kept = kept + swap(sent, on_dp).astype(F32)
        return kept

    def scatter_rows(sent, kept):
        kept = kept + swap(sent, on_dp).astype(F32)
        kept = kept[:quarter] + swap(kept[quarter:].astype(BF), on_hi).astype(F32)
        keep = pick(low, kept[eighth:], kept[:eighth])
        got = swap(pick(low, kept[:eighth], kept[eighth:]).astype(BF), on_lo).astype(F32)
        return keep, got

    def scatter_columns(sent, kept):
        kept = kept + swap(sent, on_dp).astype(F32)
        kept = kept[:, :quarter] + swap(kept[:, quarter:].astype(BF), on_hi).astype(F32)
        keep = pick(low, kept[:, eighth:], kept[:, :eighth])
        got = swap(pick(low, kept[:, :eighth], kept[:, eighth:]).astype(BF), on_lo).astype(F32)
        return keep, got

    def gather_tokens(value):
        half = value.shape[0] // 2
        from_y = swap(value, on_y)
        from_lo = swap(value, on_lo)
        corner = [swap(from_y[:half], on_lo), swap(from_lo[half:], on_y)]
        mine = jnp.concatenate([value, from_y, from_lo, *corner], axis=0)
        other = jnp.concatenate(
            [
                swap(value, on_core),
                swap(from_y, on_core),
                swap(from_lo, on_core),
                swap(jnp.concatenate(corner, axis=0), on_core),
            ],
            axis=0,
        )
        return mine, other

    def scatter_tokens(mine, other):
        summed = mine + swap(other, on_core).astype(F32)
        summed = summed.reshape(2, 2, -1, width)
        cut = width // 2
        first, second = summed[..., :cut], summed[..., cut:]
        first = first[:, 0] + swap(first[:, 1].astype(BF), on_y).astype(F32)
        second = second[0] + swap(second[1].astype(BF), on_lo).astype(F32)
        first = first[0] + swap(first[1].astype(BF), on_lo).astype(F32)
        second = second[0] + swap(second[1].astype(BF), on_y).astype(F32)
        return jnp.concatenate([first, second], axis=-1)

    places = order_perm.reshape(groups, rows)
    source = places // rows
    is_mine = (source == my_index).astype(jnp.int32)
    rank = jnp.cumsum(is_mine, axis=1) - 1
    slots = jnp.arange(share, dtype=jnp.int32)
    chosen = is_mine[:, :, None] * (rank[:, :, None] == slots).astype(jnp.int32)
    send_all = jnp.sum(chosen * (places % rows)[:, :, None], axis=1)
    send_index = lax.dynamic_slice_in_dim(send_all, shard * part, part, 1).reshape(local)

    def arrivals(run):
        own = lax.dynamic_index_in_dim(places, run, 0, keepdims=False) // rows
        onehot = (own[:, None] == jnp.arange(groups, dtype=jnp.int32)[None, :]).astype(jnp.int32)
        own_rank = jnp.sum((jnp.cumsum(onehot, axis=0) - 1) * onehot, axis=1)
        holder = own_rank // part
        device = ((holder % 2) ^ core) * 2 + ((holder // 2) ^ row)
        return (device * groups + own) * part + own_rank % part

    runs = [group * n_ctx + 2 * high + (low ^ d) for d in range(2)]
    index = jnp.stack([arrivals(run) for run in runs])
    index_col, index_row = index[:, :, None], index[:, None, :]

    block_at = block_order.astype(jnp.int32)
    slot_of = invert(block_at)
    meta_rows, position_rows = [], []
    for d in range(2):
        slot_base = 2 * (2 * high + (low ^ d))
        for micro in range(MB):
            seq = lax.dynamic_index_in_dim(lengths, group * MB + micro, 0, keepdims=False)
            for h in range(2):
                which = lax.dynamic_index_in_dim(block_at, slot_base + h, 0, keepdims=False)
                part_half = which // blocks
                limit = jnp.where(part_half == 0, pack // 2, seq[0] + seq[1] - pack // 2)
                entry = [which % blocks, limit]
                for item in range(blocks):
                    slot = lax.dynamic_index_in_dim(
                        slot_of, part_half * blocks + item, 0, keepdims=False
                    )
                    where = ((slot // 4) ^ high) * 2 + (((slot // 2) % 2) ^ low)
                    entry.append(((where * MB + micro) * 2 + slot % 2) * half_rows)
                meta_rows.append(jnp.stack(entry))
                at = which * half_rows + jnp.arange(half_rows, dtype=jnp.int32)
                position_rows.append(segment_info(at, seq)[1])
    meta = jnp.stack(meta_rows).astype(jnp.int32)
    position = jnp.concatenate(position_rows).reshape(2, rows)
    hit = index[:, :, None] == jnp.arange(rows, dtype=jnp.int32)[None, None, :]
    position_arrived = jnp.sum(jnp.where(hit, position[:, :, None], 0), axis=1)

    lane = np.arange(LANES)
    entry_of = lane % (LANES // 2)
    used = entry_of < HEAD_SIZE // 2
    freq = np.where(used, THETA ** (-2.0 * entry_of / HEAD_SIZE), 0.0).astype(np.float32)
    sign = np.where(used, np.where(lane < LANES // 2, -1.0, 1.0), 0.0).astype(np.float32)

    def tables(pos):
        angle = pos.astype(F32)[..., None] * freq
        return jnp.cos(angle), jnp.sin(angle) * sign

    cos_arrived, sin_arrived = tables(position_arrived)
    cos_place, sin_place = tables(position)

    q_width, kv_width = GROUP * HEAD_SIZE, HEAD_SIZE
    all_width = q_width + 2 * kv_width
    target = np.concatenate(
        [head_columns(HEAD_SIZE, h * LANES) for h in range(GROUP + 1)]
        + [(GROUP + 1) * LANES + np.arange(HEAD_SIZE)]
    )
    spread_np = np.zeros((all_width, (GROUP + 2) * LANES), np.float32)
    spread_np[np.arange(all_width), target] = 1.0
    spread = jnp.asarray(spread_np, BF)
    out_target = np.concatenate([h * LANES + np.arange(HEAD_SIZE) for h in range(GROUP)])
    out_np = np.zeros((q_width, GROUP * LANES), np.float32)
    out_np[np.arange(q_width), out_target] = 1.0
    out_spread = jnp.asarray(out_np, BF)

    def route_in(value):
        moved = lax.all_to_all(
            value[send_index].reshape(groups, part, width),
            ("dp", "context"),
            split_axis=0,
            concat_axis=0,
            tiled=True,
        )
        return relative(moved.reshape(local, width))

    def halves(value, axis):
        size = value.shape[axis] // 2
        first = lax.slice_in_dim(value, 0, size, axis=axis)
        second = lax.slice_in_dim(value, size, 2 * size, axis=axis)
        return pick(low, second, first), pick(low, first, second)

    def exchange(values, cut_axis, join_axis, pack_axis):
        kept, given = zip(*(halves(v, cut_axis) for v in values), strict=True)
        kept = jnp.concatenate(kept, axis=pack_axis) if len(kept) > 1 else kept[0]
        given = jnp.concatenate(given, axis=pack_axis) if len(given) > 1 else given[0]
        return by_low(kept, swap(given, on_lo), join_axis)

    gains = jnp.stack([gain_attn, gain_mlp])
    gains = by_low(gains, swap(gains, on_lo), 1)
    gains, unused = gather_weight(gains, 1)
    gains = gains.astype(F32)
    gain_a, gain_m = gains[0], gains[1]

    x_low = route_in(tokens)
    part_qkv = exchange([w_query, key_weight, value_weight], 1, 0, 1)
    part_out = exchange([w_out], 0, 1, 0)
    part_gate = exchange([w_gate], 1, 0, 1)
    part_up = exchange([w_up], 1, 0, 1)
    part_down = exchange([w_down], 0, 1, 0)
    w_qkv, event = gather_weight(part_qkv, 0)
    w_o, event = gather_weight(part_out, 1, event)
    w_g, event = gather_weight(part_gate, 0, event)
    w_u, event = gather_weight(part_up, 0, event)
    w_d, event = gather_weight(part_down, 1, event)

    x_local = x_low.astype(F32)
    root_a, one_local = norm_forward(x_local, gain_a)
    one_mine, one_other = gather_tokens(one_local)
    cot_low = route_in(after(cotangent, x_low))

    w_qkv_wide = mm(w_qkv, spread).astype(BF)
    w_o_wide = mm(out_spread.T, w_o).astype(BF)
    q_sorted, kv_own = call_sort(
        mm(one_mine, w_qkv_wide), mm(one_other, w_qkv_wide), cos_arrived, sin_arrived, index_col
    )
    kv_all = jnp.concatenate([kv_own, swap(kv_own, on_hi)], axis=0)
    o_mine, o_other = call_forward(meta, q_sorted, kv_all, index_row, out_spread.T, scale)
    mid_sum = scatter_tokens(mm(o_mine, w_o), mm(o_other, w_o).astype(BF))
    mid = x_local + mid_sum

    dy_mine, dy_other = gather_tokens(after(cot_low, kv_own))
    root_m, two_local = norm_forward(mid, gain_m)
    two_mine, two_other = gather_tokens(two_local)

    def mlp(two, dy):
        gate, up = mm(two, w_g), mm(two, w_u)
        sigma = jax.nn.sigmoid(gate)
        silu_gate = gate * sigma
        inner = (silu_gate * up).astype(BF)
        d_inner = times_t(dy, w_d)
        d_gate = (d_inner * up * sigma * (1.0 + gate * (1.0 - sigma))).astype(BF)
        d_up = (d_inner * silu_gate).astype(BF)
        return inner, d_gate, d_up, times_t(d_gate, w_g) + times_t(d_up, w_u)

    inner_other, d_gate_other, d_up_other, d_two_other = mlp(two_other, dy_other)
    inner_mine, d_gate_mine, d_up_mine, d_two_mine = mlp(two_mine, dy_mine)
    d_two = scatter_tokens(d_two_mine, d_two_other.astype(BF))

    def both(mine, other):
        return jnp.concatenate([mine, other], axis=0)

    two_all, dy_all = both(two_mine, two_other), both(dy_mine, dy_other)
    inner_all = both(inner_mine, inner_other)
    d_gate_all, d_up_all = both(d_gate_mine, d_gate_other), both(d_up_mine, d_up_other)
    cut = width // 2

    def rows_grad(left, right):
        return scatter_rows(
            t_times(left[:, cut:], right).astype(BF), t_times(left[:, :cut], right)
        )

    def columns_grad(left, right):
        return scatter_columns(
            t_times(left, right[:, cut:]).astype(BF), t_times(left, right[:, :cut])
        )

    grad_gate = by_low(*rows_grad(two_all, d_gate_all), 1)
    grad_up = by_low(*rows_grad(two_all, d_up_all), 1)
    grad_down = by_low(*columns_grad(inner_all, dy_all), 0)

    d_mid, gain_grad_m = norm_backward(mid, root_m, gain_m, d_two)
    d_mid = cot_low.astype(F32) + d_mid
    d_mid_low = d_mid.astype(BF)
    dh_mine, dh_other = gather_tokens(d_mid_low)
    dq_mine, dq_other, dkv_own, dkv_sent = call_backward(
        meta,
        q_sorted,
        kv_all,
        times_t(dh_mine, w_o_wide).astype(BF),
        times_t(dh_other, w_o_wide).astype(BF),
        index_col,
        index_row,
        cos_place.reshape(2 * rows, LANES),
        sin_place.reshape(2 * rows, LANES),
        scale,
    )
    d_mine, d_other = call_unsort(
        dkv_own,
        swap(dkv_sent, on_hi),
        cos_place,
        sin_place,
        index_row,
        dq_mine,
        dq_other,
        spread.T,
        scale,
    )
    d_one = scatter_tokens(times_t(d_mine, w_qkv), times_t(d_other, w_qkv).astype(BF))

    inner_mine, inner_other = lax.optimization_barrier((inner_mine, inner_other, dh_mine))[:2]
    y_local = mid + scatter_tokens(mm(inner_mine, w_d), mm(inner_other, w_d).astype(BF))

    grad_out = by_low(*columns_grad(both(o_mine, o_other), both(dh_mine, dh_other)), 0)
    keep, got = rows_grad(both(one_mine, one_other), both(d_mine, d_other))
    qkv_parts = []
    for first, last in ((0, q_width), (q_width, q_width + kv_width), (q_width + kv_width, all_width)):
        qkv_parts.append(by_low(keep[:, first:last], got[:, first:last], 1))
    grad_query, grad_key, grad_value = qkv_parts

    d_inputs, gain_grad_a = norm_backward(x_local, root_a, gain_a, d_one)
    x_grad_local = d_mid + d_inputs

    def spread_gain(total):
        for bit in (on_core, on_y, on_lo):
            total = total + swap(total, bit)
        total = total[:, :cut] + swap(total[:, cut:], on_dp)
        total = total[:, :quarter] + swap(total[:, quarter:], on_hi)
        return pick(low, total[0, eighth:], total[0, :eighth])

    grad_gain_m = spread_gain(gain_grad_m[None])
    grad_gain_a = spread_gain(gain_grad_a[None])

    held = [row * 2 + core, (row ^ 1) * 2 + core, row * 2 + (core ^ 1), (row ^ 1) * 2 + (core ^ 1)]
    from_slot = jnp.concatenate(
        [
            lax.dynamic_slice_in_dim(send_all, device * part, part, 1).reshape(local)
            for device in held
        ]
    )
    data_rows = one_hot(jnp.arange(rows, dtype=jnp.int32)[:, None], from_slot[None, :])

    def route_out(value):
        moved = lax.all_to_all(
            relative(value.astype(BF)).reshape(groups, part, width),
            ("dp", "context"),
            split_axis=0,
            concat_axis=0,
            tiled=True,
        ).reshape(local, width)
        pair = jnp.concatenate([moved, swap(moved, on_y)], axis=0)
        return mm(data_rows, jnp.concatenate([pair, swap(pair, on_core)], axis=0)).astype(BF)

    output = route_out(y_local)
    input_grad = route_out(x_grad_local)
    return (
        output,
        input_grad,
        grad_gain_a,
        grad_query,
        grad_key,
        grad_value,
        grad_out,
        grad_gain_m,
        grad_gate,
        grad_up,
        grad_down,
    )


def solution(mesh):
    placed = (
        P(("dp", "context"), None),
        P(("dp", "context")),
        P(("dp", "context"), "tensor"),
        P(("dp", "context"), "tensor"),
        P(("dp", "context"), "tensor"),
        P("tensor", ("dp", "context")),
        P(("dp", "context")),
        P(("dp", "context"), "tensor"),
        P(("dp", "context"), "tensor"),
        P("tensor", ("dp", "context")),
        P(("dp", "context"), None),
        P(),
        P(),
        P(),
    )
    paired = tuple(mesh.shape[name] for name in ("dp", "context", "tensor")) == (2, 4, 4)
    return jax.shard_map(
        on_device_paired if paired else on_device,
        mesh=mesh,
        in_specs=placed,
        out_specs=(
            P(("dp", "context"), None),
            P(("dp", "context"), None),
            P(("dp", "context")),
            P(("dp", "context"), "tensor"),
            P(("dp", "context"), "tensor"),
            P(("dp", "context"), "tensor"),
            P("tensor", ("dp", "context")),
            P(("dp", "context")),
            P(("dp", "context"), "tensor"),
            P(("dp", "context"), "tensor"),
            P("tensor", ("dp", "context")),
        ),
        check_vma=False,
    )
```

```python
import functools

import jax
import jax.numpy as jnp
import numpy as np
from jax import lax
from jax.experimental import pallas as pl
from jax.experimental.pallas import tpu as pltpu
from jax.sharding import PartitionSpec as P

HEAD_SIZE = 80
MB = 2


EPS = 1e-05
THETA = 1000000.0
MASKED = -1e30
DP, CONTEXT, TENSOR = "dp", "context", "tensor"
TOKEN_AXES, MESH_AXES = (DP, CONTEXT), (DP, CONTEXT, TENSOR)


def rotate(field, positions, sign):
    half_width = field.shape[-1] // 2
    freq = THETA ** (-2.0 * jnp.arange(half_width, dtype=jnp.float32) / field.shape[-1])
    angle = positions.astype(jnp.float32)[:, None] * freq[None, :]
    cosine = jnp.cos(angle)[:, None, :]
    sine = sign * jnp.sin(angle)[:, None, :]
    first = field[..., :half_width]
    second = field[..., half_width:]
    return jnp.concatenate(
        [first * cosine - second * sine, second * cosine + first * sine], axis=-1
    )


def times_t(left, right):
    return lax.dot_general(
        left, right, (((1,), (1,)), ((), ())), preferred_element_type=jnp.float32
    )


def t_times(left, right):
    return lax.dot_general(
        left, right, (((0,), (0,)), ((), ())), preferred_element_type=jnp.float32
    )


def invert(index):
    count = index.shape[0]
    iota = jnp.arange(count, dtype=jnp.int32)
    return jnp.sum(iota[None, :] * (index[None, :] == iota[:, None]).astype(jnp.int32), axis=1)


def route_plan(order_perm, groups, rows, my_index):
    share = rows // groups
    places = order_perm.reshape(groups, rows)
    source = places // rows
    mine = (source == my_index).astype(jnp.int32)
    rank = jnp.cumsum(mine, axis=1) - 1
    slots = jnp.arange(share, dtype=jnp.int32)
    pick = mine[:, :, None] * (rank[:, :, None] == slots[None, None, :]).astype(jnp.int32)
    send_index = jnp.sum(pick * (places % rows)[:, :, None], axis=1).reshape(rows)
    own = lax.dynamic_index_in_dim(places, my_index, 0, keepdims=False)
    own_source = own // rows
    onehot = (own_source[:, None] == jnp.arange(groups, dtype=jnp.int32)[None, :]).astype(jnp.int32)
    own_rank = jnp.sum((jnp.cumsum(onehot, axis=0) - 1) * onehot, axis=1)
    return (send_index, own_source * share + own_rank)


def pack_places(count, block_rows, half_rows, block_order):
    index = jnp.arange(count, dtype=jnp.int32)
    slot = 2 * (index // block_rows) + index % block_rows // half_rows
    table = (slot[:, None] == jnp.arange(block_order.shape[0], dtype=jnp.int32)[None, :]).astype(
        jnp.int32
    )
    which = jnp.sum(table * block_order[None, :], axis=1)
    return which * half_rows + index % half_rows


def segment_info(places, seq_lengths):
    first = seq_lengths[0]
    second = seq_lengths[0] + seq_lengths[1]
    segment = (places >= first).astype(jnp.int32) + (places >= second).astype(jnp.int32)
    start = jnp.where(segment == 0, 0, jnp.where(segment == 1, first, second))
    return (segment, places - start)


def norm_forward(value_tensor, gain):
    root = lax.rsqrt(jnp.mean(value_tensor * value_tensor, axis=-1, keepdims=True) + EPS)
    return (root, (value_tensor * root * gain).astype(jnp.bfloat16))


def norm_backward(value_tensor, root, gain, grad):
    weighted = grad * gain
    cubed = root * root * root
    d_values = root * weighted - value_tensor * cubed * jnp.mean(
        weighted * value_tensor, axis=-1, keepdims=True
    )
    return (d_values, jnp.sum(grad * value_tensor * root, axis=0))


def key_split(count):
    step = 512
    return (count // step, step)


def block_scores(q_group, key_block, pos_block, seg_block, q_pos, q_seg, scale):
    scores = (
        jnp.einsum("qgrd,kgd->grqk", q_group, key_block, preferred_element_type=jnp.float32) * scale
    )
    allowed = (q_seg[:, None] == seg_block[None, :]) & (pos_block[None, :] <= q_pos[:, None])
    return (jnp.where(allowed, scores, MASKED), allowed)


def key_items(key_tensor, value_tensor, k_pos, k_seg, heads_kv):
    count, step = key_split(key_tensor.shape[0])
    return (
        key_tensor.reshape(count, step, heads_kv, HEAD_SIZE),
        value_tensor.reshape(count, step, heads_kv, HEAD_SIZE),
        k_pos.reshape(count, step),
        k_seg.reshape(count, step),
    )


def attention_forward(q_group, key_tensor, value_tensor, q_pos, q_seg, k_pos, k_seg, scale):
    heads_kv = q_group.shape[1]
    items = key_items(key_tensor, value_tensor, k_pos, k_seg, heads_kv)
    stat_shape = (heads_kv, q_group.shape[2], q_group.shape[0])

    def measure(carry, item):
        top, total = carry
        scores, allowed = block_scores(q_group, item[0], item[2], item[3], q_pos, q_seg, scale)
        new_top = jnp.maximum(top, jnp.max(scores, axis=-1))
        kept = jnp.where(allowed, jnp.exp(scores - new_top[..., None]), 0.0)
        return ((new_top, total * jnp.exp(top - new_top) + jnp.sum(kept, axis=-1)), None)

    start = (jnp.full(stat_shape, MASKED, jnp.float32), jnp.zeros(stat_shape, jnp.float32))
    (top, total), unused = lax.scan(measure, start, items)

    def mix(acc, item):
        scores, allowed = block_scores(q_group, item[0], item[2], item[3], q_pos, q_seg, scale)
        probs = jnp.where(allowed, jnp.exp(scores - top[..., None]) / total[..., None], 0.0).astype(
            jnp.bfloat16
        )
        return (
            acc + jnp.einsum("grqk,kgd->qgrd", probs, item[1], preferred_element_type=jnp.float32),
            None,
        )

    attended, unused = lax.scan(mix, jnp.zeros(q_group.shape, jnp.float32), items)
    return (attended, top, total)


def attention_backward(
    q_group, key_tensor, value_tensor, q_pos, q_seg, k_pos, k_seg, top, total, d_out, delta, scale
):
    heads_kv = q_group.shape[1]
    items = key_items(key_tensor, value_tensor, k_pos, k_seg, heads_kv)
    step = items[2].shape[1]

    def visit(d_query, item):
        scores, allowed = block_scores(q_group, item[0], item[2], item[3], q_pos, q_seg, scale)
        weight = jnp.where(allowed, jnp.exp(scores - top[..., None]) / total[..., None], 0.0)
        d_prob = jnp.einsum("qgrd,kgd->grqk", d_out, item[1], preferred_element_type=jnp.float32)
        d_score = (weight * (d_prob - delta[..., None])).astype(jnp.bfloat16)
        d_query = d_query + jnp.einsum(
            "grqk,kgd->qgrd", d_score, item[0], preferred_element_type=jnp.float32
        )
        d_key = (
            jnp.einsum("grqk,qgrd->kgd", d_score, q_group, preferred_element_type=jnp.float32)
            * scale
        )
        d_value = jnp.einsum(
            "grqk,qgrd->kgd", weight.astype(jnp.bfloat16), d_out, preferred_element_type=jnp.float32
        )
        return (d_query, (d_key.reshape(step, -1), d_value.reshape(step, -1)))

    d_query, (d_keys, d_values) = lax.scan(visit, jnp.zeros(q_group.shape, jnp.float32), items)
    return (
        d_query * scale,
        d_keys.reshape(key_tensor.shape[0], -1),
        d_values.reshape(key_tensor.shape[0], -1),
    )


def fetch_attention(gain_attn, w_query, key_weight, value_weight, w_out):
    return (
        lax.all_gather(gain_attn, TOKEN_AXES, axis=0, tiled=True),
        lax.all_gather(w_query, TOKEN_AXES, axis=0, tiled=True),
        lax.all_gather(key_weight, TOKEN_AXES, axis=0, tiled=True),
        lax.all_gather(value_weight, TOKEN_AXES, axis=0, tiled=True),
        lax.all_gather(w_out, TOKEN_AXES, axis=1, tiled=True),
    )


def fetch_mlp(gain_mlp, w_gate, w_up, w_down):
    return (
        lax.all_gather(gain_mlp, TOKEN_AXES, axis=0, tiled=True),
        lax.all_gather(w_gate, TOKEN_AXES, axis=0, tiled=True),
        lax.all_gather(w_up, TOKEN_AXES, axis=0, tiled=True),
        lax.all_gather(w_down, TOKEN_AXES, axis=1, tiled=True),
    )


def head_sum(partial_sum):
    return lax.psum(partial_sum.astype(jnp.bfloat16), TENSOR).astype(jnp.float32)


def on_device(
    tokens,
    gain_attn,
    w_query,
    key_weight,
    value_weight,
    w_out,
    gain_mlp,
    w_gate,
    w_up,
    w_down,
    cotangent,
    lengths,
    order_perm,
    block_order,
):
    devices_ctx = lax.axis_size(CONTEXT)
    groups = lax.axis_size(DP) * devices_ctx
    group_id = lax.axis_index(DP)
    place = lax.axis_index(CONTEXT)
    my_index = group_id * devices_ctx + place
    rows = tokens.shape[0]
    width = tokens.shape[1]
    block_rows = rows // MB
    half_rows = block_rows // 2
    share = rows // groups
    scale = HEAD_SIZE ** (-0.5)
    send_index, recv_index = route_plan(order_perm, groups, rows, my_index)
    arrived = (
        lax.all_to_all(
            tokens[send_index].reshape(groups, share, width),
            TOKEN_AXES,
            split_axis=0,
            concat_axis=0,
            tiled=True,
        ),
        lax.all_to_all(
            cotangent[send_index].reshape(groups, share, width),
            TOKEN_AXES,
            split_axis=0,
            concat_axis=0,
            tiled=True,
        ),
    )
    seq_tokens = arrived[0].reshape(rows, width)[recv_index]
    seq_cot = arrived[1].reshape(rows, width)[recv_index]
    whole_place = pack_places(block_rows * devices_ctx, block_rows, half_rows, block_order)
    acc_gain_a = jnp.zeros((width,), jnp.float32)
    acc_query = jnp.zeros((width, w_query.shape[1]), jnp.float32)
    acc_key = jnp.zeros((width, key_weight.shape[1]), jnp.float32)
    acc_value = jnp.zeros((width, value_weight.shape[1]), jnp.float32)
    acc_out = jnp.zeros((w_out.shape[0], width), jnp.float32)
    acc_gain_m = jnp.zeros((width,), jnp.float32)
    acc_gate = jnp.zeros((width, w_gate.shape[1]), jnp.float32)
    acc_up = jnp.zeros((width, w_up.shape[1]), jnp.float32)
    acc_down = jnp.zeros((w_down.shape[0], width), jnp.float32)
    outputs = []
    input_grads = []
    for micro in range(MB):
        seq_lengths = lax.dynamic_index_in_dim(lengths, group_id * MB + micro, 0, keepdims=False)
        key_seg, key_pos = segment_info(whole_place, seq_lengths)
        q_seg = lax.dynamic_slice_in_dim(key_seg, place * block_rows, block_rows)
        q_pos = lax.dynamic_slice_in_dim(key_pos, place * block_rows, block_rows)
        inputs_f = seq_tokens[micro * block_rows : (micro + 1) * block_rows].astype(jnp.float32)
        d_y = seq_cot[micro * block_rows : (micro + 1) * block_rows]
        attn_now = fetch_attention(gain_attn, w_query, key_weight, value_weight, w_out)
        gain_a, w_q, w_k, w_v, w_o = attn_now
        root_a, normed_one = norm_forward(inputs_f, gain_a.astype(jnp.float32))
        q_lin = jnp.dot(normed_one, w_q, preferred_element_type=jnp.float32)
        k_lin = jnp.dot(normed_one, w_k, preferred_element_type=jnp.float32)
        v_lin = jnp.dot(normed_one, w_v, preferred_element_type=jnp.float32)
        heads_kv = k_lin.shape[1] // HEAD_SIZE
        q_group = rotate(q_lin.reshape(block_rows, -1, HEAD_SIZE), q_pos, 1.0).astype(jnp.bfloat16)
        q_group = q_group.reshape(block_rows, heads_kv, -1, HEAD_SIZE)
        k_in = (
            rotate(k_lin.reshape(block_rows, heads_kv, HEAD_SIZE), q_pos, 1.0)
            .astype(jnp.bfloat16)
            .reshape(block_rows, -1)
        )
        v_in = v_lin.astype(jnp.bfloat16)
        key_tensor, value_tensor = (
            lax.all_gather(k_in, CONTEXT, axis=0, tiled=True),
            lax.all_gather(v_in, CONTEXT, axis=0, tiled=True),
        )
        attended, top, total = attention_forward(
            q_group, key_tensor, value_tensor, q_pos, q_seg, key_pos, key_seg, scale
        )
        o_in = attended.reshape(block_rows, -1).astype(jnp.bfloat16)
        mid_state = inputs_f + head_sum(jnp.dot(o_in, w_o, preferred_element_type=jnp.float32))
        mlp_now = fetch_mlp(gain_mlp, w_gate, w_up, w_down)
        gain_m, w_g, w_u, w_d = mlp_now
        root_m, normed_two = norm_forward(mid_state, gain_m.astype(jnp.float32))
        gate = jnp.dot(normed_two, w_g, preferred_element_type=jnp.float32)
        up_proj = jnp.dot(normed_two, w_u, preferred_element_type=jnp.float32)
        sigma = jax.nn.sigmoid(gate)
        silu_gate = gate * sigma
        inner = (silu_gate * up_proj).astype(jnp.bfloat16)
        result = mid_state + head_sum(jnp.dot(inner, w_d, preferred_element_type=jnp.float32))
        outputs.append(result.astype(jnp.bfloat16))
        mlp_back = fetch_mlp(gain_mlp, w_gate, w_up, w_down)
        gain_m, w_g, w_u, w_d = mlp_back
        d_inner = times_t(d_y, w_d)
        acc_down = acc_down + t_times(inner, d_y)
        d_gate = (d_inner * up_proj * sigma * (1.0 + gate * (1.0 - sigma))).astype(jnp.bfloat16)
        d_up = (d_inner * silu_gate).astype(jnp.bfloat16)
        d_two = head_sum(times_t(d_gate, w_g) + times_t(d_up, w_u))
        acc_gate = acc_gate + t_times(normed_two, d_gate)
        acc_up = acc_up + t_times(normed_two, d_up)
        d_mid, gain_grad_m = norm_backward(mid_state, root_m, gain_m.astype(jnp.float32), d_two)
        acc_gain_m = acc_gain_m + gain_grad_m
        d_mid = d_y.astype(jnp.float32) + d_mid
        d_mid_low = d_mid.astype(jnp.bfloat16)
        attn_back = fetch_attention(gain_attn, w_query, key_weight, value_weight, w_out)
        gain_a, w_q, w_k, w_v, w_o = attn_back
        acc_out = acc_out + t_times(o_in, d_mid_low)
        d_out = times_t(d_mid_low, w_o).astype(jnp.bfloat16).reshape(q_group.shape)
        delta = jnp.sum(d_out.astype(jnp.float32) * attended, axis=-1).transpose(1, 2, 0)
        d_query, d_keys, d_values = attention_backward(
            q_group,
            key_tensor,
            value_tensor,
            q_pos,
            q_seg,
            key_pos,
            key_seg,
            top,
            total,
            d_out,
            delta,
            scale,
        )
        own_keys, own_values = (
            lax.psum_scatter(
                d_keys.astype(jnp.bfloat16), CONTEXT, scatter_dimension=0, tiled=True
            ).astype(jnp.float32),
            lax.psum_scatter(
                d_values.astype(jnp.bfloat16), CONTEXT, scatter_dimension=0, tiled=True
            ).astype(jnp.float32),
        )
        d_q_low = (
            rotate(d_query.reshape(block_rows, -1, HEAD_SIZE), q_pos, -1.0)
            .astype(jnp.bfloat16)
            .reshape(block_rows, -1)
        )
        d_k_low = (
            rotate(own_keys.reshape(block_rows, -1, HEAD_SIZE), q_pos, -1.0)
            .astype(jnp.bfloat16)
            .reshape(block_rows, -1)
        )
        d_v_low = own_values.astype(jnp.bfloat16)
        d_one = head_sum(times_t(d_q_low, w_q) + times_t(d_k_low, w_k) + times_t(d_v_low, w_v))
        acc_query = acc_query + t_times(normed_one, d_q_low)
        acc_key = acc_key + t_times(normed_one, d_k_low)
        acc_value = acc_value + t_times(normed_one, d_v_low)
        d_inputs, gain_grad_a = norm_backward(inputs_f, root_a, gain_a.astype(jnp.float32), d_one)
        acc_gain_a = acc_gain_a + gain_grad_a
        input_grads.append((d_mid + d_inputs).astype(jnp.bfloat16))
    grads_attn = (
        lax.psum_scatter(
            acc_gain_a.astype(jnp.bfloat16), TOKEN_AXES, scatter_dimension=0, tiled=True
        ).astype(jnp.float32),
        lax.psum_scatter(
            acc_query.astype(jnp.bfloat16), TOKEN_AXES, scatter_dimension=0, tiled=True
        ).astype(jnp.float32),
        lax.psum_scatter(
            acc_key.astype(jnp.bfloat16), TOKEN_AXES, scatter_dimension=0, tiled=True
        ).astype(jnp.float32),
        lax.psum_scatter(
            acc_value.astype(jnp.bfloat16), TOKEN_AXES, scatter_dimension=0, tiled=True
        ).astype(jnp.float32),
        lax.psum_scatter(
            acc_out.astype(jnp.bfloat16), TOKEN_AXES, scatter_dimension=1, tiled=True
        ).astype(jnp.float32),
    )
    grads_mlp = (
        lax.psum_scatter(
            acc_gain_m.astype(jnp.bfloat16), TOKEN_AXES, scatter_dimension=0, tiled=True
        ).astype(jnp.float32),
        lax.psum_scatter(
            acc_gate.astype(jnp.bfloat16), TOKEN_AXES, scatter_dimension=0, tiled=True
        ).astype(jnp.float32),
        lax.psum_scatter(
            acc_up.astype(jnp.bfloat16), TOKEN_AXES, scatter_dimension=0, tiled=True
        ).astype(jnp.float32),
        lax.psum_scatter(
            acc_down.astype(jnp.bfloat16), TOKEN_AXES, scatter_dimension=1, tiled=True
        ).astype(jnp.float32),
    )
    seq_out = jnp.concatenate(outputs, axis=0)
    seq_grad = jnp.concatenate(input_grads, axis=0)
    back_index = invert(recv_index)
    returned = (
        lax.all_to_all(
            seq_out[back_index].reshape(groups, share, width),
            TOKEN_AXES,
            split_axis=0,
            concat_axis=0,
            tiled=True,
        ),
        lax.all_to_all(
            seq_grad[back_index].reshape(groups, share, width),
            TOKEN_AXES,
            split_axis=0,
            concat_axis=0,
            tiled=True,
        ),
    )
    data_index = invert(send_index)
    output = returned[0].reshape(rows, width)[data_index]
    input_grad = returned[1].reshape(rows, width)[data_index]
    return (
        output,
        input_grad,
        grads_attn[0],
        grads_attn[1],
        grads_attn[2],
        grads_attn[3],
        grads_attn[4],
        grads_mlp[0],
        grads_mlp[1],
        grads_mlp[2],
        grads_mlp[3],
    )


BF = jnp.bfloat16
F32 = jnp.float32
TILE = 256
LANES = 128
GROUP = 4
QUICK = pl.CostEstimate(flops=10**6, bytes_accessed=10**5, transcendentals=0)


def mm(left, right):
    return jnp.dot(left, right, preferred_element_type=F32)


def one_hot(rows, columns):
    return jnp.where(rows == columns, 1.0, 0.0).astype(BF)


def turn(u, cosine, sine):
    return u * cosine + pltpu.roll(u, LANES // 2, 1) * sine


def place_rows(index_col_ref, count):
    column = index_col_ref[0]
    lanes = lax.broadcasted_iota(jnp.int32, (column.shape[0], count), 1)
    return one_hot(lanes, column)


def arrival_rows(index_row_ref, count):
    row = index_row_ref[0]
    rows = lax.broadcasted_iota(jnp.int32, (count, row.shape[1]), 0)
    return one_hot(rows, row)


def sort_kernel(mine, other, cosine, sine, index_col, out, picks, *, turned):
    @pl.when(pl.program_id(1) == 0)
    def _():
        picks[...] = place_rows(index_col, picks.shape[1])

    u = jnp.concatenate([mine[...], other[...]], axis=0)
    cos_t, sin_t = cosine[0], sine[0]
    parts = [turn(u[:, :LANES], cos_t, sin_t), u[:, LANES:]]
    if turned == 2:
        parts[1] = turn(parts[1], cos_t, sin_t)
    out[...] = mm(picks[...], jnp.concatenate(parts, axis=1).astype(BF)).astype(BF)


def scores_of(meta, block, q_head, kv, count, scale):
    limit = meta[block, 1]
    rows = lax.broadcasted_iota(jnp.int32, (TILE, TILE), 0)
    lanes = lax.broadcasted_iota(jnp.int32, (TILE, TILE), 1)
    places = (count - 1) * TILE + rows
    found = []
    for item in range(count):
        start = pl.multiple_of(meta[block, 2 + item], TILE)
        keys = kv[pl.ds(start, TILE), :LANES]
        scores = times_t(q_head, keys) * scale
        allowed = (item * TILE + lanes >= limit) | (places < limit)
        if item == count - 1:
            allowed = allowed & (lanes <= rows)
        found.append(jnp.where(allowed, scores, MASKED))
    return found


def probabilities(found):
    top = functools.reduce(jnp.maximum, [jnp.max(s, axis=1, keepdims=True) for s in found])
    raised = [jnp.exp(s - top) for s in found]
    total = functools.reduce(jnp.add, [jnp.sum(e, axis=1, keepdims=True) for e in raised])
    inverse = 1.0 / total
    return [e * inverse for e in raised]


def forward_kernel(
    meta, q, kv, index_row, unpad, out, total, picks, *, scale, blocks, per_run
):
    block, head = pl.program_id(0), pl.program_id(1)
    columns = pl.ds(pl.multiple_of(head * LANES, LANES), LANES)
    part = lax.rem(block, per_run)

    @pl.when(head == 0)
    def _():
        picks[...] = arrival_rows(index_row, picks.shape[0])

    @pl.when((head == 0) & (part == 0))
    def _():
        total[...] = jnp.zeros_like(total)

    def attend(count):
        found = scores_of(meta, block, q[...], kv, count, scale)
        probs = probabilities(found)
        mixed = jnp.zeros((TILE, LANES), F32)
        for item in range(count):
            start = pl.multiple_of(meta[block, 2 + item], TILE)
            mixed = mixed + mm(probs[item].astype(BF), kv[pl.ds(start, TILE), LANES:])
        total[:, columns] += mm(picks[...], mixed.astype(BF))

    for count in range(1, blocks + 1):
        pl.when(meta[block, 0] == count - 1)(functools.partial(attend, count))

    @pl.when((head == GROUP - 1) & (part == per_run - 1))
    def _():
        packed = mm(total[...].astype(BF), unpad[...]).astype(BF)
        half = packed.shape[0] // 2
        first = pl.multiple_of(block // per_run * half, TILE)
        out[pl.ds(first, half), :] = packed[:half]
        out[pl.ds(2 * half + first, half), :] = packed[half:]


def backward_kernel(
    meta,
    q,
    kv,
    d_mine,
    d_other,
    index_col,
    index_row,
    cosine,
    sine,
    q_grad,
    own,
    sent,
    total,
    picks,
    places,
    keys_grad,
    *,
    scale,
    blocks,
    per_run,
):
    block, head = pl.program_id(0), pl.program_id(1)
    columns = pl.ds(pl.multiple_of(head * LANES, LANES), LANES)
    part = lax.rem(block, per_run)
    half = picks.shape[0] // 2

    @pl.when((block == 0) & (head == 0))
    def _():
        keys_grad[...] = jnp.zeros_like(keys_grad)

    @pl.when(head == 0)
    def _():
        picks[...] = arrival_rows(index_row, picks.shape[0])
        places[...] = place_rows(index_col, places.shape[1])

    @pl.when((head == 0) & (part == 0))
    def _():
        total[...] = jnp.zeros_like(total)

    def attend(count):
        found = scores_of(meta, block, q[...], kv, count, scale)
        probs = probabilities(found)
        d_out = mm(places[:, :half], d_mine[...]) + mm(places[:, half:], d_other[...])
        d_out = d_out.astype(BF)
        starts = [pl.multiple_of(meta[block, 2 + item], TILE) for item in range(count)]
        d_probs = [times_t(d_out, kv[pl.ds(start, TILE), LANES:]) for start in starts]
        delta = functools.reduce(
            jnp.add,
            [jnp.sum(p * d, axis=1, keepdims=True) for p, d in zip(probs, d_probs, strict=True)],
        )
        d_query = jnp.zeros((TILE, LANES), F32)
        for item, start in enumerate(starts):
            rows = pl.ds(start, TILE)
            d_score = (probs[item] * (d_probs[item] - delta)).astype(BF)
            d_query = d_query + mm(d_score, kv[rows, :LANES])
            keys_grad[rows, :LANES] += t_times(d_score, q[...])
            keys_grad[rows, LANES:] += t_times(probs[item].astype(BF), d_out)
        turned = turn(d_query * scale, cosine[...], -sine[...])
        total[:, columns] += mm(picks[...], turned.astype(BF))

    for count in range(1, blocks + 1):
        pl.when(meta[block, 0] == count - 1)(functools.partial(attend, count))

    @pl.when((head == GROUP - 1) & (part == per_run - 1))
    def _():
        first = pl.multiple_of(block // per_run * half, TILE)
        q_grad[pl.ds(first, half), :] = total[:half].astype(BF)
        q_grad[pl.ds(2 * half + first, half), :] = total[half:].astype(BF)

    @pl.when((head == GROUP - 1) & (block == pl.num_programs(0) - 1))
    def _():
        count = own.shape[0]
        own[...] = keys_grad[:count]
        sent[...] = keys_grad[count:].astype(BF)


def unsort_kernel(own, got, cosine, sine, index_row, q_mine, q_other, unpad, out, *, scale):
    both = own[...] + got[...].astype(F32)
    d_keys = turn(both[:, :LANES] * scale, cosine[0], -sine[0])
    low = jnp.concatenate([d_keys, both[:, LANES:]], axis=1).astype(BF)
    moved = mm(arrival_rows(index_row, low.shape[0]), low).astype(BF)
    half = moved.shape[0] // 2
    split = q_mine.shape[1]
    first = pl.multiple_of(pl.program_id(0) * half, TILE)
    for rows, d_query, at in (
        (moved[:half], q_mine, first),
        (moved[half:], q_other, 2 * half + first),
    ):
        packed = mm(d_query[...], unpad[:split]) + mm(rows, unpad[split:])
        out[pl.ds(at, half), :] = packed.astype(BF)


def resident(shape):
    return pl.BlockSpec(shape, lambda *unused: (0,) * len(shape))


def call_sort(lin, cosine, sine, index_col, turned):
    run_rows = lin.shape[0] // 2
    half = run_rows // 2
    wide = 2 * LANES
    steps = lin.shape[1] // wide
    table = pl.BlockSpec((1, run_rows, LANES), lambda d, g: (d, 0, 0))
    return pl.pallas_call(
        functools.partial(sort_kernel, turned=turned),
        grid=(2, steps),
        in_specs=[
            pl.BlockSpec((half, wide), lambda d, g: (d, g)),
            pl.BlockSpec((half, wide), lambda d, g: (2 + d, g)),
            table,
            table,
            pl.BlockSpec((1, run_rows, 1), lambda d, g: (d, 0, 0)),
        ],
        out_specs=pl.BlockSpec((run_rows, wide), lambda d, g: (d, g)),
        out_shape=jax.ShapeDtypeStruct(lin.shape, BF),
        scratch_shapes=[pltpu.VMEM((run_rows, run_rows), BF)],
        compiler_params=pltpu.CompilerParams(vmem_limit_bytes=40 * 2**20),
        cost_estimate=QUICK,
        name="sort_tokens",
    )(lin, lin, cosine, sine, index_col)


def call_forward(meta, q, kv, index_row, unpad, scale):
    tokens = q.shape[0]
    run_rows = tokens // 2
    per_run = run_rows // TILE
    blocks = meta.shape[1] - 2
    body = functools.partial(forward_kernel, scale=scale, blocks=blocks, per_run=per_run)
    out = jax.ShapeDtypeStruct((tokens, unpad.shape[1]), BF)
    return pl.pallas_call(
        body,
        grid=(2 * per_run, GROUP),
        in_specs=[
            pl.BlockSpec(memory_space=pltpu.SMEM),
            pl.BlockSpec((TILE, LANES), lambda b, h: (b, h)),
            resident(kv.shape),
            pl.BlockSpec((1, 1, TILE), lambda b, h: (b // per_run, 0, b % per_run)),
            resident(unpad.shape),
        ],
        out_specs=resident(out.shape),
        out_shape=out,
        scratch_shapes=[
            pltpu.VMEM((run_rows, GROUP * LANES), F32),
            pltpu.VMEM((run_rows, TILE), BF),
        ],
        compiler_params=pltpu.CompilerParams(vmem_limit_bytes=40 * 2**20),
        cost_estimate=QUICK,
        name="attention_forward",
    )(meta, q, kv, index_row, unpad)


def call_backward(meta, q, kv, d_out, index_col, index_row, cosine, sine, scale):
    tokens = q.shape[0]
    run_rows = tokens // 2
    per_run = run_rows // TILE
    blocks = meta.shape[1] - 2
    body = functools.partial(backward_kernel, scale=scale, blocks=blocks, per_run=per_run)
    run_half = run_rows // 2
    shape = (tokens, 2 * LANES)
    table = pl.BlockSpec((TILE, LANES), lambda b, h: (b, 0))
    return pl.pallas_call(
        body,
        grid=(2 * per_run, GROUP),
        in_specs=[
            pl.BlockSpec(memory_space=pltpu.SMEM),
            pl.BlockSpec((TILE, LANES), lambda b, h: (b, h)),
            resident(kv.shape),
            pl.BlockSpec((run_half, LANES), lambda b, h: (b // per_run, h)),
            pl.BlockSpec((run_half, LANES), lambda b, h: (2 + b // per_run, h)),
            pl.BlockSpec((1, TILE, 1), lambda b, h: (b // per_run, b % per_run, 0)),
            pl.BlockSpec((1, 1, TILE), lambda b, h: (b // per_run, 0, b % per_run)),
            table,
            table,
        ],
        out_specs=[resident(q.shape), resident(shape), resident(shape)],
        out_shape=[
            jax.ShapeDtypeStruct(q.shape, BF),
            jax.ShapeDtypeStruct(shape, F32),
            jax.ShapeDtypeStruct(shape, BF),
        ],
        scratch_shapes=[
            pltpu.VMEM((run_rows, GROUP * LANES), F32),
            pltpu.VMEM((run_rows, TILE), BF),
            pltpu.VMEM((TILE, run_rows), BF),
            pltpu.VMEM((kv.shape[0], 2 * LANES), F32),
        ],
        compiler_params=pltpu.CompilerParams(vmem_limit_bytes=48 * 2**20),
        cost_estimate=QUICK,
        name="attention_backward",
    )(meta, q, kv, d_out, d_out, index_col, index_row, cosine, sine)


def call_unsort(own, got, cosine, sine, index_row, q_grad, unpad, scale):
    tokens, wide = own.shape
    run_rows = tokens // 2
    half = run_rows // 2
    table = pl.BlockSpec((1, run_rows, LANES), lambda d: (d, 0, 0))
    out = jax.ShapeDtypeStruct((tokens, unpad.shape[1]), BF)
    return pl.pallas_call(
        functools.partial(unsort_kernel, scale=scale),
        grid=(2,),
        in_specs=[
            pl.BlockSpec((run_rows, wide), lambda d: (d, 0)),
            pl.BlockSpec((run_rows, wide), lambda d: (d, 0)),
            table,
            table,
            pl.BlockSpec((1, 1, run_rows), lambda d: (d, 0, 0)),
            pl.BlockSpec((half, q_grad.shape[1]), lambda d: (d, 0)),
            pl.BlockSpec((half, q_grad.shape[1]), lambda d: (2 + d, 0)),
            resident(unpad.shape),
        ],
        out_specs=resident(out.shape),
        out_shape=out,
        compiler_params=pltpu.CompilerParams(vmem_limit_bytes=40 * 2**20),
        cost_estimate=QUICK,
        name="unsort_tokens",
    )(own, got, cosine, sine, index_row, q_grad, q_grad, unpad)


ROUNDS = 4
FIRST, MIDDLE, BACK, LAST, PLAIN, SUM = range(6)
KINDS = 13
CORE, RY, RL, SL, SY, GY, GL, GC, FL, FY, CY, CL, CC = range(KINDS)
MESH_IDS = pl.DeviceIdType.MESH


def partners():
    group, place, shard = (lax.axis_index(name) for name in MESH_AXES)
    return (
        (group, place, shard + 2 - 4 * (shard // 2)),
        (group, place + 1 - 2 * (place % 2), shard),
        (group, place, shard + 1 - 2 * (shard % 2)),
    )


def route_partner(q, e):
    group, place, shard = (lax.axis_index(name) for name in MESH_AXES)
    high, low = place // 2, place % 2
    group = 1 - group if q // 2 else group
    high = 1 - high if q % 2 else high
    low = 1 - low if e else low
    return (group, 2 * high + low, shard), 4 * group + 2 * high + low


ROUTES = [(q, e) for q in range(4) for e in range(2)]


class Router:
    def __init__(self, src, dst, send_sem, recv_sem, local_sem, spread=False):
        self.src, self.dst, self.copies, self.spread = src, dst, {}, spread
        self.send_sem, self.recv_sem, self.local_sem = send_sem, recv_sem, local_sem
        self.size = src.shape[0]
        self.share = self.size // len(ROUTES)

    def rows(self, index, slot=0):
        return pl.ds(pl.multiple_of(slot * self.size + index * self.share, 16), self.share)

    def start(self, what, q, e, src, dst, device):
        at = what * len(ROUTES) + 2 * q + e
        copy = pltpu.make_async_remote_copy(
            src_ref=src,
            dst_ref=dst,
            send_sem=self.send_sem.at[at],
            recv_sem=self.recv_sem.at[at],
            device_id=device,
            device_id_type=MESH_IDS,
        )
        copy.start()
        self.copies[what, q, e] = copy

    def send(self, q, e):
        device, index = route_partner(q, e)
        own = route_partner(0, 0)[1]
        if (q, e) == (0, 0):
            copy = pltpu.make_async_copy(
                self.src.at[self.rows(own), :], self.dst.at[self.rows(own), :], self.local_sem
            )
            copy.start()
            self.copies[0, 0, 0] = copy
        else:
            self.start(
                0, q, e, self.src.at[self.rows(index), :], self.dst.at[self.rows(own), :], device
            )

    def arrived(self, what, q, e):
        copy = self.copies[what, q, e]
        if (what, q, e) == (0, 0, 0):
            copy.wait()
        else:
            copy.wait_recv()

    def pass_on(self, q, e):
        on_y, unused, on_core = partners()
        index = route_partner(q, e)[1]
        self.arrived(0, q, e)
        here = self.dst.at[self.rows(index), :]
        self.start(1, q, e, here, self.dst.at[self.rows(index, 1), :], on_y)
        self.start(2, q, e, here, self.dst.at[self.rows(index, 2), :], on_core)

    def pass_corner(self, q, e):
        on_core = partners()[2]
        index = route_partner(q, e)[1]
        self.arrived(1, q, e)
        here = self.dst.at[self.rows(index, 1), :]
        self.start(3, q, e, here, self.dst.at[self.rows(index, 3), :], on_core)

    def finish(self):
        for (what, q, e), copy in self.copies.items():
            if (what, q, e) != (0, 0, 0):
                copy.wait_send()
            if what in (2, 3) or not self.spread:
                self.arrived(what, q, e)


PIECES = 8


class Pieces:
    def __init__(self, buffer, send_sem, recv_sem):
        self.buffer, self.send_sem, self.recv_sem, self.used = buffer, send_sem, recv_sem, []
        self.quarter = buffer.shape[0] // 4
        self.step = self.quarter // PIECES
        self.on_hi = route_partner(1, 0)[0]
        self.on_dp = route_partner(2, 0)[0]

    def copy(self, what, piece):
        group, place = lax.axis_index(DP), lax.axis_index(CONTEXT)
        low, high = place % 2, place // 2
        high = 1 - high if what == 2 else high
        half = low if piece < PIECES // 2 else 1 - low
        first = (2 * group + high) * self.quarter + half * (self.quarter // 2)
        first = pl.multiple_of(first + piece % (PIECES // 2) * self.step, 16)
        at = self.buffer.at[pl.ds(first, self.step), :]
        return pltpu.make_async_remote_copy(
            src_ref=at,
            dst_ref=at,
            send_sem=self.send_sem.at[what, piece],
            recv_sem=self.recv_sem.at[what, piece],
            device_id=self.on_dp if what else self.on_hi,
            device_id_type=MESH_IDS,
        )

    def send(self, piece):
        self.copy(0, piece).start()
        self.copy(1, piece).start()
        self.used.append(piece)

    def pass_on(self, piece):
        self.copy(0, piece).wait_recv()
        self.copy(2, piece).start()

    def finish(self):
        for piece in self.used:
            for what in range(3):
                copy = self.copy(what, piece)
                copy.wait_send()
                if what > 0:
                    copy.wait_recv()


def piece_scratch():
    return [pltpu.SemaphoreType.DMA((3, PIECES))] * 2


def route_scratch(parts):
    return [
        pltpu.SemaphoreType.DMA((parts * len(ROUTES),)),
        pltpu.SemaphoreType.DMA((parts * len(ROUTES),)),
        pltpu.SemaphoreType.DMA(()),
    ]


def greet(devices):
    barrier = pltpu.get_barrier_semaphore()
    for device in devices:
        pl.semaphore_signal(barrier, inc=1, device_id=device, device_id_type=MESH_IDS)
    pl.semaphore_wait(barrier, len(devices))


def root_of(value):
    return lax.rsqrt(jnp.mean(value * value, axis=-1, keepdims=True) + EPS)


def norm_gradient(value, gain, grad):
    root = root_of(value)
    weighted = grad * gain
    return root * weighted - value * (root * root * root) * jnp.mean(
        weighted * value, axis=-1, keepdims=True
    ), jnp.sum(grad * value * root, axis=0, keepdims=True)


def token_kernel(*refs, kind, scatter, gather, pieces):
    refs = list(refs)
    take = lambda count: [refs.pop(0) for unused in range(count)]
    if scatter:
        (parts,) = take(1)
    (x_ref,) = take(1)
    if kind in (FIRST, LAST):
        (gain,) = take(1)
    if kind == LAST:
        (add_ref,) = take(1)
    if kind == LAST:
        aside, total_grad, other_gain = take(3)
    (bulk,) = take(1)
    if gather:
        (everyone,) = take(1)
    if kind == SUM:
        (sum_out,) = take(1)
    if kind == LAST:
        grad_out, gains_out, aside_out, keep_out, got_out = take(5)
    (bulk_out,) = take(1)
    if scatter:
        from_core, send_y, keep_y, got_y, send_lo, got_lo, mine, mine_sem = take(8)
    if gather:
        ready, local_sem = take(2)
    if kind == LAST:
        (ready,) = take(1)
    if kind == LAST:
        aside_router = Router(aside, aside_out, *take(3), spread=True)
        grad_router = Router(ready, grad_out, *take(3), spread=True)
        gain_acc, gain_sent, gain_got, own_half, from_dp, from_hi = take(6)
        hi_keep, hi_send, lo_send, side_local, side_send, side_recv = take(6)
    bulk_send, bulk_recv = take(2)
    send_sem, recv_sem = refs
    size, width = x_ref.shape
    step = size // ROUNDS
    on_y, on_lo, on_core = partners()
    on_hi, on_dp = route_partner(1, 0)[0], route_partner(2, 0)[0]
    if kind == LAST:
        greet((on_y, on_core, *(route_partner(q, e)[0] for q, e in ROUTES[1:])))
        for q, e in ROUTES:
            aside_router.send(q, e)
    else:
        greet((on_y, on_lo, on_core, on_hi, on_dp) if gather else (on_y, on_lo, on_core, on_hi))
    if gather:
        weights = Pieces(bulk_out, bulk_send, bulk_recv)
    bulk_copies = []

    def bulk_send_piece(index):
        if gather:
            weights.send(pieces[index])
            return
        count = bulk.shape[0] // pieces
        rows = pl.ds(index * count, count)
        copy = pltpu.make_async_remote_copy(
            src_ref=bulk.at[rows, :],
            dst_ref=bulk_out.at[rows, :],
            send_sem=bulk_send.at[0, index],
            recv_sem=bulk_recv.at[0, index],
            device_id=on_hi,
            device_id_type=MESH_IDS,
        )
        copy.start()
        bulk_copies.append(copy)

    copies = {}

    def start(what, q, src, dst, device):
        copies[what, q] = pltpu.make_async_remote_copy(
            src_ref=src,
            dst_ref=dst,
            send_sem=send_sem.at[what, q],
            recv_sem=recv_sem.at[what, q],
            device_id=device,
            device_id_type=MESH_IDS,
        )
        copies[what, q].start()

    def arrived(what, q):
        copies[what, q].wait_recv()

    def rows_of(q):
        return pl.ds(pl.multiple_of(order(q) * step, step), step)

    def order(q):
        return route_partner(q, 0)[1] // 2 if kind == LAST else q

    def sum_core(q):
        rows = rows_of(q)
        arrived(CORE, q)
        copies["mine", q].wait()
        for lo in range(2):
            at = 2 * lo
            keep_y[lo, rows, :] = mine[at, rows, :].astype(F32) + from_core[at, rows, :].astype(F32)
            at = 2 * lo + 1
            total = mine[at, rows, :].astype(F32) + from_core[at, rows, :].astype(F32)
            send_y[lo, rows, :] = total.astype(BF)
        start(RY, q, send_y.at[:, rows, :], got_y.at[:, rows, :], on_y)

    def sum_y(q):
        rows = rows_of(q)
        arrived(RY, q)
        send_lo[rows, :] = (keep_y[1, rows, :] + got_y[1, rows, :].astype(F32)).astype(BF)
        start(RL, q, send_lo.at[rows, :], got_lo.at[rows, :], on_lo)

    def sum_lo(q):
        rows = rows_of(q)
        arrived(RL, q)
        return keep_y[0, rows, :] + got_y[0, rows, :].astype(F32) + got_lo[rows, :].astype(F32)

    def finish(q):
        rows = rows_of(q)
        total = sum_lo(q) if scatter else None
        value = x_ref[rows, :]
        if kind == SUM:
            sum_out[rows, :] = (value.astype(F32) + total).astype(sum_out.dtype)
            return
        if kind == PLAIN:
            low = value
        elif kind == FIRST:
            value = value.astype(F32)
            low = (value * root_of(value) * gain[...]).astype(BF)
        else:
            grad, gain_grad = norm_gradient(value.astype(F32), gain[...], total)
            grad = grad + add_ref[rows, :].astype(F32)
            ready[rows, :] = grad.astype(BF)
            if q == 0:
                gain_acc[...] = gain_grad
            else:
                gain_acc[...] += gain_grad
        if kind == LAST:
            grad_router.send(q, 0)
            grad_router.send(q, 1)
        if gather:
            ready[rows, :] = low
            keep = pltpu.make_async_copy(ready.at[rows, :], everyone.at[rows, :], local_sem.at[q])
            keep.start()
            copies["local", q] = keep
            start(GY, q, ready.at[rows, :], everyone.at[block(1, q), :], on_y)
            start(GL, q, ready.at[rows, :], everyone.at[block(2, q), :], on_lo)
            start(GC, q, ready.at[rows, :], everyone.at[block(4, q), :], on_core)

    def block(index, q):
        return pl.ds(index * size + q * step, step)

    def forward(q):
        arrived(GL, q)
        start(FY, q, everyone.at[block(2, q), :], everyone.at[block(3, q), :], on_y)
        start(CL, q, everyone.at[block(2, q), :], everyone.at[block(6, q), :], on_core)
        arrived(GY, q)
        start(CY, q, everyone.at[block(1, q), :], everyone.at[block(5, q), :], on_core)

    def corner(q):
        arrived(FY, q)
        start(CC, q, everyone.at[block(3, q), :], everyone.at[block(7, q), :], on_core)

    def pass_on(q):
        for router in routers:
            router.pass_on(q, 0)
            router.pass_on(q, 1)

    def pass_corner(q):
        for router in routers:
            router.pass_corner(q, 0)
            router.pass_corner(q, 1)

    side_copies = []

    def side(src, dst, device):
        at = len(side_copies)
        copy = pltpu.make_async_remote_copy(
            src_ref=src,
            dst_ref=dst,
            send_sem=side_send.at[at],
            recv_sem=side_recv.at[at],
            device_id=device,
            device_id_type=MESH_IDS,
        )
        copy.start()
        side_copies.append(copy)
        return copy

    def share(index, count):
        return pl.ds(pl.multiple_of(index * count, 16), count)

    waiting = {}

    def grad_to_dp():
        group = lax.axis_index(DP)
        count = own_half.shape[0]
        waiting["own"] = pltpu.make_async_copy(
            total_grad.at[share(group, count), :], own_half, side_local
        )
        waiting["own"].start()
        waiting["dp"] = side(total_grad.at[share(1 - group, count), :], from_dp, on_dp)

    def grad_to_hi():
        high = lax.axis_index(CONTEXT) // 2
        waiting["own"].wait()
        waiting["dp"].wait_recv()
        count = hi_keep.shape[0]
        rows, others = share(high, count), share(1 - high, count)
        hi_keep[...] = own_half[rows, :].astype(F32) + from_dp[rows, :].astype(F32)
        hi_send[...] = (own_half[others, :].astype(F32) + from_dp[others, :].astype(F32)).astype(BF)
        waiting["hi"] = side(hi_send, from_hi, on_hi)

    def grad_to_lo():
        low = lax.axis_index(CONTEXT) % 2
        waiting["hi"].wait_recv()
        count = lo_send.shape[0]
        rows, others = share(low, count), share(1 - low, count)
        keep_out[...] = hi_keep[rows, :] + from_hi[rows, :].astype(F32)
        lo_send[...] = (hi_keep[others, :] + from_hi[others, :].astype(F32)).astype(BF)
        waiting["lo"] = side(lo_send, got_out, on_lo)

    def gain_hop(index):
        if index == 0:
            total = jnp.concatenate([gain_acc[...], other_gain[...]], axis=0)
        else:
            waiting["gain"].wait_recv()
            total = gain_sent[index - 1] + gain_got[index - 1]
        if index == 5:
            gains_out[...] = total
        else:
            gain_sent[index] = total
            device = (on_core, on_y, on_lo, on_dp, on_hi)[index]
            waiting["gain"] = side(gain_sent.at[index], gain_got.at[index], device)

    def beside(tick):
        if tick == 0:
            grad_to_dp()
        if tick == 3:
            grad_to_hi()
        if tick == 6:
            grad_to_lo()
        if 5 <= tick < 8:
            gain_hop(tick - 5)
        if tick == 7:
            for index in range(3, 6):
                gain_hop(index)

    routers = [aside_router, grad_router] if kind == LAST else []
    stages = []
    if scatter:
        for q in range(ROUNDS):
            rows = rows_of(q)
            start(CORE, q, parts.at[pl.ds(4, 4), rows, :], from_core.at[:, rows, :], on_core)
            copies["mine", q] = pltpu.make_async_copy(
                parts.at[pl.ds(0, 4), rows, :], mine.at[:, rows, :], mine_sem.at[q]
            )
            copies["mine", q].start()
        stages += [sum_core, sum_y]
    stages.append(finish)
    if gather:
        stages += [forward, corner]
    if routers:
        stages += [pass_on, pass_corner]
    for tick in range(ROUNDS + len(stages) - 1):
        for index, stage in enumerate(stages):
            if 0 <= tick - index < ROUNDS:
                stage(tick - index)
        if tick < (len(pieces) if gather else pieces):
            bulk_send_piece(tick)
        if kind == LAST:
            beside(tick)
        if gather and 0 <= tick - 2 < len(pieces):
            weights.pass_on(pieces[tick - 2])
    for (what, q), copy in copies.items():
        if what == "local":
            copy.wait()
        elif what != "mine":
            copy.wait_send()
            if what in (GC, CY, CL, CC):
                copy.wait_recv()
    if gather:
        weights.finish()
    for copy in bulk_copies:
        copy.wait()
    if kind == LAST:
        aside_router.finish()
        grad_router.finish()
        for copy in side_copies:
            copy.wait_send()
        waiting["lo"].wait_recv()


def call_tokens(
    kind, ident, part, x, bulk, pieces, gain=None, add=None, aside=None, total_grad=None, other_gain=None
):
    size, width = x.shape
    scatter, gather = part is not None, kind not in (LAST, SUM)
    vmem = pl.BlockSpec(memory_space=pltpu.VMEM)
    anywhere = pl.BlockSpec(memory_space=pl.ANY)
    operands, in_specs, out_specs, out_shape, scratch = [], [], [], [], []
    if scatter:
        operands.append(part.reshape(8, size, width))
        in_specs.append(anywhere)
    operands.append(x)
    in_specs.append(vmem)
    if gain is not None:
        operands.append(gain.reshape(1, width))
        in_specs.append(vmem)
    if add is not None:
        operands.append(add)
        in_specs.append(vmem)
    if aside is not None:
        operands += [aside, total_grad, other_gain]
        in_specs += [anywhere, anywhere, vmem]
        grad_rows, grad_width = total_grad.shape
        halves = [grad_rows // 2 ** (at + 1) for at in range(3)]
    operands.append(bulk)
    in_specs.append(anywhere)
    if gather:
        out_specs.append(anywhere)
        out_shape.append(jax.ShapeDtypeStruct((8 * size, width), BF))
    if kind == SUM:
        out_specs.append(vmem)
        out_shape.append(jax.ShapeDtypeStruct((size, width), BF))
    if kind == LAST:
        out_specs.append(anywhere)
        out_shape.append(jax.ShapeDtypeStruct((4 * size, width), BF))
    if kind == LAST:
        out_specs.append(vmem)
        out_shape.append(jax.ShapeDtypeStruct((2, width), F32))
        out_specs += [anywhere, vmem, anywhere]
        out_shape += [
            jax.ShapeDtypeStruct((4 * size, width), BF),
            jax.ShapeDtypeStruct((halves[2], grad_width), F32),
            jax.ShapeDtypeStruct((halves[2], grad_width), BF),
        ]
    out_specs.append(anywhere)
    out_shape.append(jax.ShapeDtypeStruct(bulk.shape, BF))
    if scatter:
        scratch.append(pltpu.VMEM((4, size, width), BF))
        pair = (2, size, width)
        scratch += [pltpu.VMEM(pair, BF), pltpu.VMEM(pair, F32), pltpu.VMEM(pair, BF)]
        scratch += [pltpu.VMEM((size, width), BF)] * 2
        scratch += [pltpu.VMEM((4, size, width), BF), pltpu.SemaphoreType.DMA((ROUNDS,))]
    if gather:
        scratch += [pltpu.VMEM((size, width), BF), pltpu.SemaphoreType.DMA((ROUNDS,))]
    if kind == LAST:
        scratch.append(pltpu.VMEM((size, width), BF))
        scratch += route_scratch(4) + route_scratch(4)
        scratch += [pltpu.VMEM((1, width), F32)] + [pltpu.VMEM((5, 2, width), F32)] * 2
        scratch += [pltpu.VMEM((halves[0], grad_width), BF)] * 2
        scratch += [pltpu.VMEM((halves[1], grad_width), BF)]
        scratch += [pltpu.VMEM((halves[1], grad_width), F32)]
        scratch += [pltpu.VMEM((halves[1], grad_width), BF)]
        scratch += [pltpu.VMEM((halves[2], grad_width), BF)]
        scratch += [pltpu.SemaphoreType.DMA(())] + [pltpu.SemaphoreType.DMA((8,))] * 2
    scratch += piece_scratch()
    scratch += [pltpu.SemaphoreType.DMA((KINDS, ROUNDS))] * 2
    return pl.pallas_call(
        functools.partial(
            token_kernel, kind=kind, scatter=scatter, gather=gather, pieces=pieces
        ),
        in_specs=in_specs,
        out_specs=out_specs,
        out_shape=out_shape,
        scratch_shapes=scratch,
        input_output_aliases={len(operands) - 1: len(out_shape) - 1} if gather else {},
        compiler_params=pltpu.CompilerParams(
            collective_id=ident, has_side_effects=True, vmem_limit_bytes=48 * 2**20
        ),
        cost_estimate=QUICK,
        name="tokens_%d" % kind,
    )(*operands)


def ffn_kernel(
    parts,
    x_ref,
    gain,
    d_y,
    d_y_all,
    large,
    two_all,
    grad_all,
    inner_out,
    both_out,
    y_out,
    mid_out,
    grad_out,
    gain_out,
    large_out,
    weights,
    summed,
    got_a,
    got_b,
    got_c,
    got_d,
    mine,
    two_ready,
    grad_ready,
    two_block,
    d_y_block,
    inner_block,
    both_block,
    y_block,
    d_two,
    weight_sem,
    mine_sem,
    ready_sem,
    load_sem,
    store_sem,
    send_sem,
    recv_sem,
    piece_send,
    piece_recv,
    *,
    pieces,
):
    size, width = x_ref.shape
    units = inner_out.shape[2]
    cut = width // 2
    step = size // ROUNDS
    half = step // 2
    on_y, on_lo, on_core = partners()
    arriving = Pieces(large_out, piece_send, piece_recv)
    greet((on_y, on_lo, on_core, arriving.on_hi, arriving.on_dp))
    left, right = pl.ds(0, cut), pl.ds(cut, width - cut)

    def rows_of(q):
        return pl.ds(pl.multiple_of(q * step, step), step)

    def block(index, q, first=0, count=None):
        start = pl.multiple_of(index * size + q * step + first, half)
        return pl.ds(start, step if count is None else count)

    def remote(base, what, q):
        rows = rows_of(q)
        ready, everyone = (two_ready, two_all) if base == 0 else (grad_ready, grad_all)
        part_of = lambda *place: everyone.at[block(*place), :]
        if what == CORE:
            src = parts.at[1, :, :, rows, :] if base == 0 else d_two.at[lax.rem(q, 2), 1]
            ends = src, summed.at[:, :, rows, :], on_core
        elif what == RY:
            ends = summed.at[:, 1, rows, left], got_a.at[:, rows, :], on_y
        elif what == RL:
            ends = summed.at[1, :, rows, right], got_b.at[:, rows, :], on_lo
        elif what == SL:
            ends = summed.at[1, 0, rows, left], got_c.at[rows, :], on_lo
        elif what == SY:
            ends = summed.at[0, 1, rows, right], got_d.at[rows, :], on_y
        elif what in (GY, GL, GC):
            index, device = {GY: (1, on_y), GL: (2, on_lo), GC: (4, on_core)}[what]
            ends = ready.at[rows, :], part_of(index, q), device
        elif what == FL:
            ends = part_of(1, q, 0, half), part_of(3, q, 0, half), on_lo
        elif what == FY:
            ends = part_of(2, q, half, half), part_of(3, q, half, half), on_y
        else:
            index = {CY: 1, CL: 2, CC: 3}[what]
            ends = part_of(index, q), part_of(index + 4, q), on_core
        return pltpu.make_async_remote_copy(
            src_ref=ends[0],
            dst_ref=ends[1],
            send_sem=send_sem.at[base + what, q],
            recv_sem=recv_sem.at[base + what, q],
            device_id=ends[2],
            device_id_type=MESH_IDS,
        )

    def arrived(base, what, q):
        remote(base, what, q).wait_recv()

    def sum_core(base, q, value):
        rows = rows_of(q)
        arrived(base, CORE, q)
        for lo in range(2):
            for y in range(2):
                total = value(lo, y).astype(F32) + summed[lo, y, rows, :].astype(F32)
                summed[lo, y, rows, :] = total.astype(BF)
        remote(base, RY, q).start()
        remote(base, RL, q).start()

    def sum_first(base, q):
        rows = rows_of(q)
        arrived(base, RY, q)
        total = summed[1, 0, rows, :cut].astype(F32) + got_a[1, rows, :].astype(F32)
        summed[1, 0, rows, :cut] = total.astype(BF)
        remote(base, SL, q).start()
        arrived(base, RL, q)
        total = summed[0, 1, rows, cut:].astype(F32) + got_b[1, rows, :].astype(F32)
        summed[0, 1, rows, cut:] = total.astype(BF)
        remote(base, SY, q).start()

    def sum_second(base, q):
        rows = rows_of(q)
        arrived(base, SL, q)
        arrived(base, SY, q)
        first = summed[0, 0, rows, :cut].astype(F32) + got_a[0, rows, :].astype(F32)
        second = summed[0, 0, rows, cut:].astype(F32) + got_b[0, rows, :].astype(F32)
        first = first + got_c[rows, :].astype(F32)
        second = second + got_d[rows, :].astype(F32)
        for what in (RY, RL, SL, SY):
            remote(base, what, q).wait_send()
        return jnp.concatenate([first, second], axis=1)

    def own_rows(base, q):
        ready, everyone = (two_ready, two_all) if base == 0 else (grad_ready, grad_all)
        rows = rows_of(q)
        sem = ready_sem.at[base // KINDS, q]
        return pltpu.make_async_copy(ready.at[rows, :], everyone.at[rows, :], sem)

    def spread(base, q):
        own_rows(base, q).start()
        for what in (GY, GL, GC):
            remote(base, what, q).start()

    def forward(base, q):
        arrived(base, GY, q)
        remote(base, FL, q).start()
        remote(base, CY, q).start()
        arrived(base, GL, q)
        remote(base, FY, q).start()
        remote(base, CL, q).start()

    def corner(base, q):
        arrived(base, FL, q)
        arrived(base, FY, q)
        remote(base, CC, q).start()

    def fetch_mine(q):
        src = parts.at[0, :, :, rows_of(q), :]
        slot = lax.rem(q, 2)
        return pltpu.make_async_copy(src, mine.at[slot], mine_sem.at[slot])

    def middle_core(q):
        fetch_mine(q).wait()
        sum_core(0, q, lambda lo, y: mine[lax.rem(q, 2), lo, y])

        @pl.when(q + 2 < ROUNDS)
        def _():
            fetch_mine(q + 2).start()

    def middle_norm(q):
        rows = rows_of(q)
        value = x_ref[rows, :].astype(F32) + sum_second(0, q)
        mid_out[rows, :] = value
        two_ready[rows, :] = (value * root_of(value) * gain[...]).astype(BF)
        spread(0, q)

    def loads(part, q):
        for index, (src, dst) in enumerate(((two_all, two_block), (d_y_all, d_y_block))):
            for at in range(4):
                yield pltpu.make_async_copy(
                    src.at[block(4 * part + at, q), :],
                    dst.at[part, pl.ds(at * step, step), :],
                    load_sem.at[index, part, at],
                )

    def stores(part, q):
        pairs = ((inner_block, inner_out), (both_block, both_out), (y_block, y_out))
        for index, (src, dst) in enumerate(pairs):
            for at in range(4):
                yield pltpu.make_async_copy(
                    src.at[part, pl.ds(at * step, step), :],
                    dst.at[4 * part + at, rows_of(q), :],
                    store_sem.at[index, part, at],
                )

    def feed_forward(q):
        own_rows(0, q).wait()
        for what in (GC, CY, CL, CC):
            arrived(0, what, q)

        @pl.when(q == 0)
        def _():
            pltpu.make_async_copy(large_out, weights, weight_sem.at[0]).wait()

        @pl.when(q >= 2)
        def _():
            remote(KINDS, CORE, q - 2).wait_send()

        for part in (1, 0):
            for copy in loads(part, q):
                copy.start()

        @pl.loop(0, 2)
        def _(turn_index):
            part = 1 - turn_index
            for copy in loads(part, q):
                copy.wait()

            @pl.when(q > 0)
            def _():
                for copy in stores(part, q - 1):
                    copy.wait()

            both = mm(two_block[part], weights[:, : 2 * units])
            gate, up = both[:, :units], both[:, units:]
            d_inner = mm(d_y_block[part], weights[:, 2 * units :])
            sigma = 1.0 / (1.0 + jnp.exp(-gate))
            silu_gate = gate * sigma
            inner_block[part] = (silu_gate * up).astype(BF)
            d_gate = d_inner * up * sigma * (1.0 + gate * (1.0 - sigma))
            both_block[part, :, :units] = d_gate.astype(BF)
            both_block[part, :, units:] = (d_inner * silu_gate).astype(BF)
            d_two[lax.rem(q, 2), part] = (
                times_t(both_block[part], weights[:, : 2 * units])
                .astype(BF)
                .reshape(2, 2, step, width)
            )

            @pl.when(part == 1)
            def _():
                remote(KINDS, CORE, q).start()

            y_block[part] = times_t(inner_block[part], weights[:, 2 * units :]).astype(BF)
            for copy in stores(part, q):
                copy.start()

    def back_core(q):
        sum_core(KINDS, q, lambda lo, y: d_two[lax.rem(q, 2), 0, lo, y])

    def back_norm(q):
        rows = rows_of(q)
        grad, gain_grad = norm_gradient(mid_out[rows, :], gain[...], sum_second(KINDS, q))
        grad = grad + d_y[rows, :].astype(F32)
        grad_out[rows, :] = grad
        gain_out[...] += gain_grad
        grad_ready[rows, :] = grad.astype(BF)
        spread(KINDS, q)

    gain_out[...] = jnp.zeros_like(gain_out)
    for q in range(ROUNDS):
        remote(0, CORE, q).start()
        if q < 2:
            fetch_mine(q).start()
    stages = [
        middle_core,
        functools.partial(sum_first, 0),
        middle_norm,
        functools.partial(forward, 0),
        functools.partial(corner, 0),
        feed_forward,
        back_core,
        functools.partial(sum_first, KINDS),
        back_norm,
        functools.partial(forward, KINDS),
        functools.partial(corner, KINDS),
    ]

    @pl.loop(0, ROUNDS + len(stages) - 1)
    def _(tick):
        for index, stage in enumerate(stages):
            pl.when((tick >= index) & (tick < index + ROUNDS))(
                functools.partial(stage, tick - index)
            )
        for index, piece in enumerate(pieces):
            pl.when(tick == index)(functools.partial(arriving.send, piece))
            pl.when(tick == index + 2)(functools.partial(arriving.pass_on, piece))

        @pl.when(tick == len(pieces) + 2)
        def _():
            arriving.finish()
            pltpu.make_async_copy(large_out, weights, weight_sem.at[0]).start()

    for q in range(ROUNDS):
        for base in (0, KINDS):
            for what in range(KINDS):
                if what in (RY, RL, SL, SY) or (what == CORE and base and q < ROUNDS - 2):
                    continue
                remote(base, what, q).wait_send()
        for what in (GC, CY, CL, CC):
            arrived(KINDS, what, q)
        own_rows(KINDS, q).wait()
    for part in range(2):
        for copy in stores(part, ROUNDS - 1):
            copy.wait()


def call_ffn(parts, x, gain, d_y, d_y_all, large, pieces):
    size, width = x.shape
    units = large.shape[1] // 3
    cut = width // 2
    step = size // ROUNDS
    vmem = pl.BlockSpec(memory_space=pltpu.VMEM)
    anywhere = pl.BlockSpec(memory_space=pl.ANY)
    everyone = jax.ShapeDtypeStruct((8 * size, width), BF)
    shape = lambda n: jax.ShapeDtypeStruct((8, size, n), BF)
    local = jax.ShapeDtypeStruct((size, width), F32)
    dma = pltpu.SemaphoreType.DMA
    half = pltpu.VMEM((2, size, cut), BF)
    quarter = pltpu.VMEM((size, cut), BF)
    ready = pltpu.VMEM((size, width), BF)
    block = lambda n: pltpu.VMEM((2, 4 * step, n), BF)
    return pl.pallas_call(
        functools.partial(ffn_kernel, pieces=pieces),
        in_specs=[anywhere, vmem, vmem, vmem, anywhere, anywhere],
        out_specs=[anywhere] * 5 + [vmem] * 3 + [anywhere],
        input_output_aliases={5: 8},
        out_shape=[
            everyone,
            everyone,
            shape(units),
            shape(2 * units),
            shape(width),
            local,
            local,
            jax.ShapeDtypeStruct((1, width), F32),
            jax.ShapeDtypeStruct(large.shape, BF),
        ],
        scratch_shapes=[
            pltpu.VMEM((width, 3 * units), BF),
            pltpu.VMEM((2, 2, size, width), BF),
            half,
            half,
            quarter,
            quarter,
            pltpu.VMEM((2, 2, 2, step, width), BF),
            ready,
            ready,
            block(width),
            block(width),
            block(units),
            block(2 * units),
            block(width),
            pltpu.VMEM((2, 2, 2, 2, step, width), BF),
            dma((1,)),
            dma((2,)),
            dma((2, ROUNDS)),
            dma((2, 2, 4)),
            dma((3, 2, 4)),
            dma((2 * KINDS, ROUNDS)),
            dma((2 * KINDS, ROUNDS)),
            *piece_scratch(),
        ],
        compiler_params=pltpu.CompilerParams(
            collective_id=8, has_side_effects=True, vmem_limit_bytes=62 * 2**20
        ),
        cost_estimate=QUICK,
        name="feed_forward",
    )(parts.reshape(2, 2, 2, size, width), x, gain.reshape(1, width), d_y, d_y_all, large)


CHUNKS = 2


def weights_kernel(
    small_keep,
    small_give,
    large_keep,
    large_give,
    rows,
    late_rows,
    small,
    large,
    rows_out,
    late_out,
    local,
    send,
    recv,
    *rest,
    pieces,
):
    group, place, shard = (lax.axis_index(name) for name in MESH_AXES)
    low, high = place % 2, place // 2
    on_lo = (group, place + 1 - 2 * low, shard)
    on_hi = (group, place + 2 - 4 * high, shard)
    on_dp = (1 - group, place, shard)
    eighth = small_keep.shape[0]
    step = eighth // CHUNKS
    greet([route_partner(q, e)[0] for q, e in ROUTES[1:]])
    copies = []
    router, late = Router(rows, rows_out, *rest[:3]), Router(late_rows, late_out, *rest[3:6])
    weights = Pieces(large, *rest[6:])
    for q, e in ROUTES:
        router.send(q, e)

    def start(src, dst, device):
        at = len(copies)
        copy = pltpu.make_async_remote_copy(
            src_ref=src,
            dst_ref=dst,
            send_sem=send.at[at],
            recv_sem=recv.at[at],
            device_id=device,
            device_id_type=MESH_IDS,
        )
        copy.start()
        copies.append(copy)
        return copy

    def span(index, first, count):
        return pl.ds(pl.multiple_of(index * eighth + first, 16), count)

    own = (group * 2 + high) * 2
    across = (group * 2 + 1 - high) * 2
    from_low = []
    for q in range(CHUNKS):
        src = small_give.at[pl.ds(q * step, step), :]
        from_low.append(start(src, small.at[span(own + low, q * step, step), :], on_lo))
    stay = [
        pltpu.make_async_copy(small_keep, small.at[span(own + low, 0, eighth), :], local.at[0]),
        pltpu.make_async_copy(large_keep, large.at[span(own + low, 0, eighth), :], local.at[1]),
    ]
    for copy in stay:
        copy.start()
    from_high = []
    for q in range(CHUNKS):
        src = small_keep.at[pl.ds(q * step, step), :]
        dst = small.at[span(own + low, q * step, step), :]
        from_high.append(start(src, dst, on_hi))
        start(src, dst, on_dp)
    start(large_give, large.at[span(own + low, 0, eighth), :], on_lo)
    for q in range(CHUNKS):
        from_low[q].wait_recv()
        at = small.at[span(own + 1 - low, q * step, step), :]
        from_high.append(start(at, at, on_hi))
        start(at, at, on_dp)
    for q in range(2 * CHUNKS):
        half = low if q < CHUNKS else 1 - low
        from_high[q].wait_recv()
        at = small.at[span(across + half, q % CHUNKS * step, step), :]
        start(at, at, on_dp)
        if q == 0:
            for pair in ROUTES:
                late.send(*pair)
            stay[1].wait()
        if 0 <= q - 1 < len(pieces):
            weights.send(pieces[q - 1])
    for piece in pieces:
        weights.pass_on(piece)
    weights.finish()
    waited = from_low + from_high
    for copy in copies:
        copy.wait_send()
        if not any(copy is item for item in waited):
            copy.wait_recv()
    stay[0].wait()
    router.finish()
    late.finish()


def call_weights(small_keep, small_give, large_keep, large_give, rows, late_rows, parts, pieces):
    eighth = small_keep.shape[0]
    anywhere = pl.BlockSpec(memory_space=pl.ANY)
    count = 7 * CHUNKS + 1
    return pl.pallas_call(
        functools.partial(weights_kernel, pieces=pieces),
        in_specs=[anywhere] * 6,
        out_specs=[anywhere] * 4,
        out_shape=[
            jax.ShapeDtypeStruct((2 * parts * eighth, small_keep.shape[1]), BF),
            jax.ShapeDtypeStruct((2 * parts * eighth, large_keep.shape[1]), BF),
            jax.ShapeDtypeStruct(rows.shape, BF),
            jax.ShapeDtypeStruct(rows.shape, BF),
        ],
        scratch_shapes=[
            pltpu.SemaphoreType.DMA((2,)),
            pltpu.SemaphoreType.DMA((count,)),
            pltpu.SemaphoreType.DMA((count,)),
            *route_scratch(1),
            *route_scratch(1),
            *piece_scratch(),
        ],
        compiler_params=pltpu.CompilerParams(collective_id=1, has_side_effects=True),
        cost_estimate=QUICK,
        name="weights_first",
    )(small_keep, small_give, large_keep, large_give, rows, late_rows)


def head_columns(part, base):
    half = part // 2
    entry = np.arange(part)
    return base + np.where(entry < half, entry, LANES // 2 + entry - half)


def after(value, *events):
    return lax.optimization_barrier((value, *events))[0]


def on_device_paired(
    tokens,
    gain_attn,
    w_query,
    key_weight,
    value_weight,
    w_out,
    gain_mlp,
    w_gate,
    w_up,
    w_down,
    cotangent,
    lengths,
    order_perm,
    block_order,
):
    names = MESH_AXES
    n_dp, n_ctx, n_ten = (lax.axis_size(name) for name in names)
    devices = n_dp * n_ctx * n_ten
    on_core, on_y, on_lo, on_hi, on_dp = 1, 2, n_ten, 2 * n_ten, n_ctx * n_ten
    group = lax.axis_index(DP)
    place = lax.axis_index(CONTEXT)
    shard = lax.axis_index(TENSOR)
    high, low = place // 2, place % 2
    row, core = shard // 2, shard % 2
    groups = n_dp * n_ctx
    my_index = group * n_ctx + place
    rows, width = tokens.shape
    share = rows // groups
    part = share // n_ten
    local = rows // n_ten
    block_rows = rows // MB
    half_rows = block_rows // 2
    pack = block_rows * n_ctx
    n_blocks = block_order.shape[0]
    blocks = n_blocks // 2
    scale = HEAD_SIZE ** (-0.5)
    quarter = width // (2 * n_dp)
    eighth = quarter // 2

    def swap(value, bit):
        return lax.ppermute(value, names, [(i, i ^ bit) for i in range(devices)])

    def pick(flag, yes, no):
        return jnp.where(flag == 1, yes, no)

    def by_low(mine, partner, axis):
        return jnp.concatenate(
            [pick(low, partner, mine), pick(low, mine, partner)], axis=axis
        )

    quads = [
        [g * n_ctx + 2 * h + l for g in range(n_dp) for h in range(n_ctx // 2)] for l in range(2)
    ]

    def scatter_quads(total):
        own = lax.psum_scatter(
            total, names[:2], scatter_dimension=0, tiled=True, axis_index_groups=quads
        )
        got = swap(pick(low, own[:eighth], own[eighth:]), on_lo)
        return pick(low, own[eighth:], own[:eighth]), got

    places = order_perm.reshape(groups, rows)
    source = places // rows
    is_mine = source == my_index
    below = jnp.arange(rows, dtype=jnp.int32)
    ahead = one_hot(1, (below[:, None] <= below[None, :]).astype(jnp.int32))
    all_sources = jnp.arange(groups, dtype=jnp.int32)
    runs = [
        lax.dynamic_index_in_dim(source, group * n_ctx + 2 * high + (low ^ d), 0, keepdims=False)
        for d in range(2)
    ]
    from_each = [run[None, :] == all_sources[:, None] for run in runs]
    flags = jnp.concatenate([is_mine, *from_each], axis=0)
    counted = mm(flags.astype(BF), ahead).astype(jnp.int32) - 1
    rank = counted[:groups]
    row_at = jnp.where(is_mine, places % rows, 0)

    def rows_sent(slots):
        hits = is_mine[:, None, :] & (rank[:, None, :] == slots[None, :, None])
        return jnp.sum(jnp.where(hits, row_at[:, None, :], 0), axis=2)

    send_index = rows_sent(shard * part + jnp.arange(part, dtype=jnp.int32)).reshape(local, 1)
    send_rows = one_hot(send_index, below[None, :])

    def arrivals(d):
        known = counted[(d + 1) * groups : (d + 2) * groups]
        own_rank = jnp.sum(jnp.where(from_each[d], known, 0), axis=0)
        holder = own_rank // part
        device = ((holder % 2) ^ core) * 2 + ((holder // 2) ^ row)
        return (device * groups + runs[d]) * part + own_rank % part

    index = jnp.stack([arrivals(d) for d in range(2)])
    index_col, index_row = index[:, :, None], index[:, None, :]

    def lookup(table, at):
        hits = at[..., None] == jnp.arange(table.shape[0], dtype=jnp.int32)
        return jnp.sum(jnp.where(hits, table, 0), axis=-1)

    slot_of = invert(block_order)
    query = jnp.arange(2 * MB * 2, dtype=jnp.int32)
    run_of, micro_of, half_of = query // (2 * MB), query // 2 % MB, query % 2
    which = lookup(block_order, 2 * (2 * high + (low ^ run_of)) + half_of)
    upper = which // blocks
    item = jnp.arange(blocks, dtype=jnp.int32)
    slot = lookup(slot_of, upper[:, None] * blocks + item)
    where = ((slot // 4) ^ high) * 2 + (((slot // 2) % 2) ^ low)
    starts = ((where * MB + micro_of[:, None]) * 2 + slot % 2) * half_rows
    first = lookup(lengths[:, 0], group * MB + micro_of)
    second = first + lookup(lengths[:, 1], group * MB + micro_of)
    limit = jnp.where(upper == 0, pack // 2, second - pack // 2)
    meta = jnp.concatenate([(which % blocks)[:, None], limit[:, None], starts], axis=1)
    at = which[:, None] * half_rows + jnp.arange(half_rows, dtype=jnp.int32)
    first, second = first[:, None], second[:, None]
    at = at - jnp.where(at < first, 0, jnp.where(at < second, first, second))
    position = at.reshape(2, rows)
    hit = index[:, :, None] == jnp.arange(rows, dtype=jnp.int32)[None, None, :]
    position_arrived = jnp.sum(jnp.where(hit, position[:, :, None], 0), axis=1)

    lane = np.arange(LANES)
    entry_of = lane % (LANES // 2)
    used = entry_of < HEAD_SIZE // 2
    freq = np.where(used, THETA ** (-2.0 * entry_of / HEAD_SIZE), 0.0).astype(np.float32)
    sign = np.where(used, np.where(lane < LANES // 2, -1.0, 1.0), 0.0).astype(np.float32)

    def tables(pos):
        angle = pos.astype(F32)[..., None] * freq
        return jnp.cos(angle), jnp.sin(angle) * sign

    cos_arrived, sin_arrived = tables(position_arrived)
    cos_place, sin_place = tables(position)

    q_width, kv_width = GROUP * HEAD_SIZE, HEAD_SIZE
    all_width = q_width + 2 * kv_width
    target = np.concatenate(
        [head_columns(HEAD_SIZE, h * LANES) for h in range(GROUP + 1)]
        + [(GROUP + 1) * LANES + np.arange(HEAD_SIZE)]
    )
    spread_np = np.zeros((all_width, (GROUP + 2) * LANES), np.float32)
    spread_np[np.arange(all_width), target] = 1.0
    spread = jnp.asarray(spread_np, BF)
    out_target = np.concatenate([h * LANES + np.arange(HEAD_SIZE) for h in range(GROUP)])
    out_np = np.zeros((q_width, GROUP * LANES), np.float32)
    out_np[np.arange(q_width), out_target] = 1.0
    out_spread = jnp.asarray(out_np, BF)

    def halves(value):
        size = value.shape[1] // 2
        return pick(low, value[:, size:], value[:, :size]), pick(low, value[:, :size], value[:, size:])

    def together(values):
        keeps, gives = zip(*(halves(value) for value in values), strict=True)
        return list(keeps), list(gives)

    x_send = mm(send_rows, tokens).astype(BF)
    cot_send = mm(send_rows, cotangent).astype(BF)
    w_out_t, w_down_t = w_out.T, w_down.T
    keeps, gives = together([w_query, key_weight, value_weight])
    keep_out, give_out = halves(w_out_t)
    gains = jnp.stack([gain_attn, gain_mlp], axis=1)
    out_at, gain_at = 4 * LANES, 4 * LANES + q_width
    gap = jnp.zeros((eighth, out_at - all_width), BF)
    end = jnp.zeros((eighth, 7 * LANES - gain_at - 2), BF)
    small_keep = jnp.concatenate([*keeps, gap, keep_out, gains, end], axis=1)
    small_give = jnp.concatenate([*gives, gap, give_out, gains, end], axis=1)
    keeps, gives = together([w_gate, w_up, w_down_t])
    small, large, x_low, cot_low = call_weights(
        small_keep,
        small_give,
        jnp.concatenate(keeps, axis=1),
        jnp.concatenate(gives, axis=1),
        x_send,
        cot_send,
        2 * n_dp,
        (0,),
    )
    w_qkv = small[:, :all_width]
    w_o_t = small[:, out_at:gain_at]
    gain_a = small[:, gain_at].astype(F32)
    gain_m = small[:, gain_at + 1].astype(F32)

    one_all, large = call_tokens(FIRST, 2, None, x_low, large, (1, 2, 3), gain_a)

    w_qkv_wide = mm(w_qkv, spread).astype(BF)
    w_o_wide = mm(w_o_t, out_spread).astype(BF)
    split = GROUP * LANES
    kv_own = call_sort(mm(one_all, w_qkv_wide[:, split:]), cos_arrived, sin_arrived, index_col, 1)
    kv_got = swap(kv_own, on_hi)
    q_sorted = call_sort(mm(one_all, w_qkv_wide[:, :split]), cos_arrived, sin_arrived, index_col, 2)
    dy_all, large = call_tokens(PLAIN, 3, None, after(cot_low, q_sorted), large, (4, 5))
    kv_all = jnp.concatenate([kv_own, kv_got], axis=0)
    kv_all, dy_all = lax.optimization_barrier((kv_all, dy_all))
    o_all = call_forward(meta, q_sorted, kv_all, index_row, out_spread.T, scale)
    o_part = times_t(o_all, w_o_t).astype(BF)
    two_all, dh_all, inner_all, d_both_all, y_part, mid, d_mid, gain_grad_m, unused = call_ffn(
        o_part, x_low, gain_m, cot_low, dy_all, large, (6, 7)
    )
    units = inner_all.shape[2]
    inner_all = inner_all.reshape(2 * rows, units)
    d_both_all = d_both_all.reshape(2 * rows, 2 * units)

    def rows_at(value, index, size):
        return lax.dynamic_slice_in_dim(value, index * size, size, 0)

    def other_dp(total):
        return swap(rows_at(total, 1 - group, 2 * quarter), on_dp)

    def dp_sum(total, came):
        kept = rows_at(total, group, 2 * quarter).astype(F32) + came.astype(F32)
        return rows_at(kept, high, quarter), rows_at(kept, 1 - high, quarter).astype(BF)

    def quad_sum(kept, came):
        kept = kept + came.astype(F32)
        return rows_at(kept, low, eighth), rows_at(kept, 1 - low, eighth).astype(BF)

    down_part = t_times(dy_all, inner_all).astype(BF)
    down_came = other_dp(down_part)
    two_late = after(two_all, down_part)
    gate_part = t_times(two_late, d_both_all[:, :units]).astype(BF)
    gate_came = other_dp(gate_part)
    two_late = after(two_late, gate_part)
    up_part = t_times(two_late, d_both_all[:, units:]).astype(BF)
    up_came = other_dp(up_part)
    out_part = t_times(dh_all, o_all).astype(BF)
    d_o = mm(dh_all, w_o_wide).astype(BF)
    d_o, down_part, gate_part, up_part, out_part = lax.optimization_barrier(
        (d_o, down_part, gate_part, up_part, out_part)
    )
    down_keep, down_send = dp_sum(down_part, down_came)
    d_o, down_send = lax.optimization_barrier((d_o, down_send))
    down_came = swap(down_send, on_hi)
    keep, got = scatter_quads(out_part)
    grad_out_t = by_low(keep, got, 1)
    dq_all, dkv_own, dkv_sent = call_backward(
        meta,
        q_sorted,
        kv_all,
        d_o,
        index_col,
        index_row,
        cos_place.reshape(2 * rows, LANES),
        sin_place.reshape(2 * rows, LANES),
        scale,
    )

    dkv_got = swap(dkv_sent, on_hi)
    gate_keep, gate_send = dp_sum(gate_part, gate_came)
    down_keep, down_give = quad_sum(down_keep, down_came)
    y_part, gate_send, down_give, dkv_sent = lax.optimization_barrier(
        (y_part, gate_send, down_give, dkv_sent)
    )
    grad_down_t = by_low(down_keep, swap(down_give, on_lo).astype(F32), 1)
    y_local, gate_came = call_tokens(SUM, 6, y_part, mid, gate_send, 5)
    dkv_got, y_local = lax.optimization_barrier((dkv_got, y_local))
    d_all = call_unsort(
        dkv_own, dkv_got, cos_place, sin_place, index_row, dq_all, spread.T, scale
    )
    one_part = t_times(one_all, d_all).astype(BF)
    up_keep, up_send = dp_sum(up_part, after(up_came, y_local))
    gate_keep, gate_give = quad_sum(gate_keep, gate_came)
    d_one_part, one_part, up_send, gate_give = lax.optimization_barrier(
        (times_t(d_all, w_qkv).astype(BF), one_part, up_send, gate_give)
    )
    grad_gate = by_low(gate_keep, swap(gate_give, on_lo).astype(F32), 1)
    x_grad_rows, both_gains, y_rows, keep, got, up_came = call_tokens(
        LAST,
        7,
        d_one_part,
        x_low,
        up_send,
        8,
        gain_a,
        d_mid,
        y_local,
        one_part,
        gain_grad_m,
    )
    got = got.astype(F32)
    up_keep, up_give = quad_sum(up_keep, up_came)
    grad_up = by_low(up_keep, swap(up_give, on_lo).astype(F32), 1)
    qkv_parts = []
    for first, last in ((0, q_width), (q_width, q_width + kv_width), (q_width + kv_width, all_width)):
        qkv_parts.append(by_low(keep[:, first:last], got[:, first:last], 1))
    grad_query, grad_key, grad_value = qkv_parts
    own_gains = lax.dynamic_slice_in_dim(both_gains, my_index * eighth, eighth, 1)

    send_all = rows_sent(jnp.arange(share, dtype=jnp.int32))
    held = [row * 2 + core, (row ^ 1) * 2 + core, row * 2 + (core ^ 1), (row ^ 1) * 2 + (core ^ 1)]
    from_slot = jnp.concatenate(
        [
            lax.dynamic_slice_in_dim(send_all, device * part, part, 1).reshape(local)
            for device in held
        ]
    )
    data_rows = one_hot(below[:, None], from_slot[None, :])
    output = mm(data_rows, y_rows).astype(BF)
    input_grad = mm(data_rows, x_grad_rows).astype(BF)
    return (
        output,
        input_grad,
        own_gains[0],
        grad_query,
        grad_key,
        grad_value,
        grad_out_t.astype(F32).T,
        own_gains[1],
        grad_gate,
        grad_up,
        grad_down_t.T,
    )


def solution(mesh):
    placed = (
        P(TOKEN_AXES, None),
        P(TOKEN_AXES),
        P(TOKEN_AXES, TENSOR),
        P(TOKEN_AXES, TENSOR),
        P(TOKEN_AXES, TENSOR),
        P(TENSOR, TOKEN_AXES),
        P(TOKEN_AXES),
        P(TOKEN_AXES, TENSOR),
        P(TOKEN_AXES, TENSOR),
        P(TENSOR, TOKEN_AXES),
        P(TOKEN_AXES, None),
        P(),
        P(),
        P(),
    )
    paired = tuple(mesh.shape[name] for name in MESH_AXES) == (2, 4, 4)
    return jax.shard_map(
        on_device_paired if paired else on_device,
        mesh=mesh,
        in_specs=placed,
        out_specs=(
            P(TOKEN_AXES, None),
            P(TOKEN_AXES, None),
            P(TOKEN_AXES),
            P(TOKEN_AXES, TENSOR),
            P(TOKEN_AXES, TENSOR),
            P(TOKEN_AXES, TENSOR),
            P(TENSOR, TOKEN_AXES),
            P(TOKEN_AXES),
            P(TOKEN_AXES, TENSOR),
            P(TOKEN_AXES, TENSOR),
            P(TENSOR, TOKEN_AXES),
        ),
        check_vma=False,
    )
```

```python
import functools

import jax
import jax.numpy as jnp
import numpy as np
from jax import lax
from jax.experimental import pallas as pl
from jax.experimental.pallas import tpu as pltpu
from jax.sharding import PartitionSpec as P

HEAD_SIZE = 80
MB = 2


EPS = 1e-05
THETA = 1000000.0
MASKED = -1e30
DP, CONTEXT, TENSOR = "dp", "context", "tensor"
TOKEN_AXES, MESH_AXES = (DP, CONTEXT), (DP, CONTEXT, TENSOR)


def rotate(field, positions, sign):
    half_width = field.shape[-1] // 2
    freq = THETA ** (-2.0 * jnp.arange(half_width, dtype=jnp.float32) / field.shape[-1])
    angle = positions.astype(jnp.float32)[:, None] * freq[None, :]
    cosine = jnp.cos(angle)[:, None, :]
    sine = sign * jnp.sin(angle)[:, None, :]
    first = field[..., :half_width]
    second = field[..., half_width:]
    return jnp.concatenate(
        [first * cosine - second * sine, second * cosine + first * sine], axis=-1
    )


def times_t(left, right):
    return lax.dot_general(
        left, right, (((1,), (1,)), ((), ())), preferred_element_type=jnp.float32
    )


def t_times(left, right):
    return lax.dot_general(
        left, right, (((0,), (0,)), ((), ())), preferred_element_type=jnp.float32
    )


def invert(index):
    count = index.shape[0]
    iota = jnp.arange(count, dtype=jnp.int32)
    return jnp.sum(iota[None, :] * (index[None, :] == iota[:, None]).astype(jnp.int32), axis=1)


def route_plan(order_perm, groups, rows, my_index):
    share = rows // groups
    places = order_perm.reshape(groups, rows)
    source = places // rows
    mine = (source == my_index).astype(jnp.int32)
    rank = jnp.cumsum(mine, axis=1) - 1
    slots = jnp.arange(share, dtype=jnp.int32)
    pick = mine[:, :, None] * (rank[:, :, None] == slots[None, None, :]).astype(jnp.int32)
    send_index = jnp.sum(pick * (places % rows)[:, :, None], axis=1).reshape(rows)
    own = lax.dynamic_index_in_dim(places, my_index, 0, keepdims=False)
    own_source = own // rows
    onehot = (own_source[:, None] == jnp.arange(groups, dtype=jnp.int32)[None, :]).astype(jnp.int32)
    own_rank = jnp.sum((jnp.cumsum(onehot, axis=0) - 1) * onehot, axis=1)
    return (send_index, own_source * share + own_rank)


def pack_places(count, block_rows, half_rows, block_order):
    index = jnp.arange(count, dtype=jnp.int32)
    slot = 2 * (index // block_rows) + index % block_rows // half_rows
    table = (slot[:, None] == jnp.arange(block_order.shape[0], dtype=jnp.int32)[None, :]).astype(
        jnp.int32
    )
    which = jnp.sum(table * block_order[None, :], axis=1)
    return which * half_rows + index % half_rows


def segment_info(places, seq_lengths):
    first = seq_lengths[0]
    second = seq_lengths[0] + seq_lengths[1]
    segment = (places >= first).astype(jnp.int32) + (places >= second).astype(jnp.int32)
    start = jnp.where(segment == 0, 0, jnp.where(segment == 1, first, second))
    return (segment, places - start)


def norm_forward(value_tensor, gain):
    root = lax.rsqrt(jnp.mean(value_tensor * value_tensor, axis=-1, keepdims=True) + EPS)
    return (root, (value_tensor * root * gain).astype(jnp.bfloat16))


def norm_backward(value_tensor, root, gain, grad):
    weighted = grad * gain
    cubed = root * root * root
    d_values = root * weighted - value_tensor * cubed * jnp.mean(
        weighted * value_tensor, axis=-1, keepdims=True
    )
    return (d_values, jnp.sum(grad * value_tensor * root, axis=0))


def key_split(count):
    step = 512
    return (count // step, step)


def block_scores(q_group, key_block, pos_block, seg_block, q_pos, q_seg, scale):
    scores = (
        jnp.einsum("qgrd,kgd->grqk", q_group, key_block, preferred_element_type=jnp.float32) * scale
    )
    allowed = (q_seg[:, None] == seg_block[None, :]) & (pos_block[None, :] <= q_pos[:, None])
    return (jnp.where(allowed, scores, MASKED), allowed)


def key_items(key_tensor, value_tensor, k_pos, k_seg, heads_kv):
    count, step = key_split(key_tensor.shape[0])
    return (
        key_tensor.reshape(count, step, heads_kv, HEAD_SIZE),
        value_tensor.reshape(count, step, heads_kv, HEAD_SIZE),
        k_pos.reshape(count, step),
        k_seg.reshape(count, step),
    )


def attention_forward(q_group, key_tensor, value_tensor, q_pos, q_seg, k_pos, k_seg, scale):
    heads_kv = q_group.shape[1]
    items = key_items(key_tensor, value_tensor, k_pos, k_seg, heads_kv)
    stat_shape = (heads_kv, q_group.shape[2], q_group.shape[0])

    def measure(carry, item):
        top, total = carry
        scores, allowed = block_scores(q_group, item[0], item[2], item[3], q_pos, q_seg, scale)
        new_top = jnp.maximum(top, jnp.max(scores, axis=-1))
        kept = jnp.where(allowed, jnp.exp(scores - new_top[..., None]), 0.0)
        return ((new_top, total * jnp.exp(top - new_top) + jnp.sum(kept, axis=-1)), None)

    start = (jnp.full(stat_shape, MASKED, jnp.float32), jnp.zeros(stat_shape, jnp.float32))
    (top, total), unused = lax.scan(measure, start, items)

    def mix(acc, item):
        scores, allowed = block_scores(q_group, item[0], item[2], item[3], q_pos, q_seg, scale)
        probs = jnp.where(allowed, jnp.exp(scores - top[..., None]) / total[..., None], 0.0).astype(
            jnp.bfloat16
        )
        return (
            acc + jnp.einsum("grqk,kgd->qgrd", probs, item[1], preferred_element_type=jnp.float32),
            None,
        )

    attended, unused = lax.scan(mix, jnp.zeros(q_group.shape, jnp.float32), items)
    return (attended, top, total)


def attention_backward(
    q_group, key_tensor, value_tensor, q_pos, q_seg, k_pos, k_seg, top, total, d_out, delta, scale
):
    heads_kv = q_group.shape[1]
    items = key_items(key_tensor, value_tensor, k_pos, k_seg, heads_kv)
    step = items[2].shape[1]

    def visit(d_query, item):
        scores, allowed = block_scores(q_group, item[0], item[2], item[3], q_pos, q_seg, scale)
        weight = jnp.where(allowed, jnp.exp(scores - top[..., None]) / total[..., None], 0.0)
        d_prob = jnp.einsum("qgrd,kgd->grqk", d_out, item[1], preferred_element_type=jnp.float32)
        d_score = (weight * (d_prob - delta[..., None])).astype(jnp.bfloat16)
        d_query = d_query + jnp.einsum(
            "grqk,kgd->qgrd", d_score, item[0], preferred_element_type=jnp.float32
        )
        d_key = (
            jnp.einsum("grqk,qgrd->kgd", d_score, q_group, preferred_element_type=jnp.float32)
            * scale
        )
        d_value = jnp.einsum(
            "grqk,qgrd->kgd", weight.astype(jnp.bfloat16), d_out, preferred_element_type=jnp.float32
        )
        return (d_query, (d_key.reshape(step, -1), d_value.reshape(step, -1)))

    d_query, (d_keys, d_values) = lax.scan(visit, jnp.zeros(q_group.shape, jnp.float32), items)
    return (
        d_query * scale,
        d_keys.reshape(key_tensor.shape[0], -1),
        d_values.reshape(key_tensor.shape[0], -1),
    )


def fetch_attention(gain_attn, w_query, key_weight, value_weight, w_out):
    return (
        lax.all_gather(gain_attn, TOKEN_AXES, axis=0, tiled=True),
        lax.all_gather(w_query, TOKEN_AXES, axis=0, tiled=True),
        lax.all_gather(key_weight, TOKEN_AXES, axis=0, tiled=True),
        lax.all_gather(value_weight, TOKEN_AXES, axis=0, tiled=True),
        lax.all_gather(w_out, TOKEN_AXES, axis=1, tiled=True),
    )


def fetch_mlp(gain_mlp, w_gate, w_up, w_down):
    return (
        lax.all_gather(gain_mlp, TOKEN_AXES, axis=0, tiled=True),
        lax.all_gather(w_gate, TOKEN_AXES, axis=0, tiled=True),
        lax.all_gather(w_up, TOKEN_AXES, axis=0, tiled=True),
        lax.all_gather(w_down, TOKEN_AXES, axis=1, tiled=True),
    )


def head_sum(partial_sum):
    return lax.psum(partial_sum.astype(jnp.bfloat16), TENSOR).astype(jnp.float32)


def on_device(
    tokens,
    gain_attn,
    w_query,
    key_weight,
    value_weight,
    w_out,
    gain_mlp,
    w_gate,
    w_up,
    w_down,
    cotangent,
    lengths,
    order_perm,
    block_order,
):
    devices_ctx = lax.axis_size(CONTEXT)
    groups = lax.axis_size(DP) * devices_ctx
    group_id = lax.axis_index(DP)
    place = lax.axis_index(CONTEXT)
    my_index = group_id * devices_ctx + place
    rows = tokens.shape[0]
    width = tokens.shape[1]
    block_rows = rows // MB
    half_rows = block_rows // 2
    share = rows // groups
    scale = HEAD_SIZE ** (-0.5)
    send_index, recv_index = route_plan(order_perm, groups, rows, my_index)
    arrived = (
        lax.all_to_all(
            tokens[send_index].reshape(groups, share, width),
            TOKEN_AXES,
            split_axis=0,
            concat_axis=0,
            tiled=True,
        ),
        lax.all_to_all(
            cotangent[send_index].reshape(groups, share, width),
            TOKEN_AXES,
            split_axis=0,
            concat_axis=0,
            tiled=True,
        ),
    )
    seq_tokens = arrived[0].reshape(rows, width)[recv_index]
    seq_cot = arrived[1].reshape(rows, width)[recv_index]
    whole_place = pack_places(block_rows * devices_ctx, block_rows, half_rows, block_order)
    acc_gain_a = jnp.zeros((width,), jnp.float32)
    acc_query = jnp.zeros((width, w_query.shape[1]), jnp.float32)
    acc_key = jnp.zeros((width, key_weight.shape[1]), jnp.float32)
    acc_value = jnp.zeros((width, value_weight.shape[1]), jnp.float32)
    acc_out = jnp.zeros((w_out.shape[0], width), jnp.float32)
    acc_gain_m = jnp.zeros((width,), jnp.float32)
    acc_gate = jnp.zeros((width, w_gate.shape[1]), jnp.float32)
    acc_up = jnp.zeros((width, w_up.shape[1]), jnp.float32)
    acc_down = jnp.zeros((w_down.shape[0], width), jnp.float32)
    outputs = []
    input_grads = []
    for micro in range(MB):
        seq_lengths = lax.dynamic_index_in_dim(lengths, group_id * MB + micro, 0, keepdims=False)
        key_seg, key_pos = segment_info(whole_place, seq_lengths)
        q_seg = lax.dynamic_slice_in_dim(key_seg, place * block_rows, block_rows)
        q_pos = lax.dynamic_slice_in_dim(key_pos, place * block_rows, block_rows)
        inputs_f = seq_tokens[micro * block_rows : (micro + 1) * block_rows].astype(jnp.float32)
        d_y = seq_cot[micro * block_rows : (micro + 1) * block_rows]
        attn_now = fetch_attention(gain_attn, w_query, key_weight, value_weight, w_out)
        gain_a, w_q, w_k, w_v, w_o = attn_now
        root_a, normed_one = norm_forward(inputs_f, gain_a.astype(jnp.float32))
        q_lin = jnp.dot(normed_one, w_q, preferred_element_type=jnp.float32)
        k_lin = jnp.dot(normed_one, w_k, preferred_element_type=jnp.float32)
        v_lin = jnp.dot(normed_one, w_v, preferred_element_type=jnp.float32)
        heads_kv = k_lin.shape[1] // HEAD_SIZE
        q_group = rotate(q_lin.reshape(block_rows, -1, HEAD_SIZE), q_pos, 1.0).astype(jnp.bfloat16)
        q_group = q_group.reshape(block_rows, heads_kv, -1, HEAD_SIZE)
        k_in = (
            rotate(k_lin.reshape(block_rows, heads_kv, HEAD_SIZE), q_pos, 1.0)
            .astype(jnp.bfloat16)
            .reshape(block_rows, -1)
        )
        v_in = v_lin.astype(jnp.bfloat16)
        key_tensor, value_tensor = (
            lax.all_gather(k_in, CONTEXT, axis=0, tiled=True),
            lax.all_gather(v_in, CONTEXT, axis=0, tiled=True),
        )
        attended, top, total = attention_forward(
            q_group, key_tensor, value_tensor, q_pos, q_seg, key_pos, key_seg, scale
        )
        o_in = attended.reshape(block_rows, -1).astype(jnp.bfloat16)
        mid_state = inputs_f + head_sum(jnp.dot(o_in, w_o, preferred_element_type=jnp.float32))
        mlp_now = fetch_mlp(gain_mlp, w_gate, w_up, w_down)
        gain_m, w_g, w_u, w_d = mlp_now
        root_m, normed_two = norm_forward(mid_state, gain_m.astype(jnp.float32))
        gate = jnp.dot(normed_two, w_g, preferred_element_type=jnp.float32)
        up_proj = jnp.dot(normed_two, w_u, preferred_element_type=jnp.float32)
        sigma = jax.nn.sigmoid(gate)
        silu_gate = gate * sigma
        inner = (silu_gate * up_proj).astype(jnp.bfloat16)
        result = mid_state + head_sum(jnp.dot(inner, w_d, preferred_element_type=jnp.float32))
        outputs.append(result.astype(jnp.bfloat16))
        mlp_back = fetch_mlp(gain_mlp, w_gate, w_up, w_down)
        gain_m, w_g, w_u, w_d = mlp_back
        d_inner = times_t(d_y, w_d)
        acc_down = acc_down + t_times(inner, d_y)
        d_gate = (d_inner * up_proj * sigma * (1.0 + gate * (1.0 - sigma))).astype(jnp.bfloat16)
        d_up = (d_inner * silu_gate).astype(jnp.bfloat16)
        d_two = head_sum(times_t(d_gate, w_g) + times_t(d_up, w_u))
        acc_gate = acc_gate + t_times(normed_two, d_gate)
        acc_up = acc_up + t_times(normed_two, d_up)
        d_mid, gain_grad_m = norm_backward(mid_state, root_m, gain_m.astype(jnp.float32), d_two)
        acc_gain_m = acc_gain_m + gain_grad_m
        d_mid = d_y.astype(jnp.float32) + d_mid
        d_mid_low = d_mid.astype(jnp.bfloat16)
        attn_back = fetch_attention(gain_attn, w_query, key_weight, value_weight, w_out)
        gain_a, w_q, w_k, w_v, w_o = attn_back
        acc_out = acc_out + t_times(o_in, d_mid_low)
        d_out = times_t(d_mid_low, w_o).astype(jnp.bfloat16).reshape(q_group.shape)
        delta = jnp.sum(d_out.astype(jnp.float32) * attended, axis=-1).transpose(1, 2, 0)
        d_query, d_keys, d_values = attention_backward(
            q_group,
            key_tensor,
            value_tensor,
            q_pos,
            q_seg,
            key_pos,
            key_seg,
            top,
            total,
            d_out,
            delta,
            scale,
        )
        own_keys, own_values = (
            lax.psum_scatter(
                d_keys.astype(jnp.bfloat16), CONTEXT, scatter_dimension=0, tiled=True
            ).astype(jnp.float32),
            lax.psum_scatter(
                d_values.astype(jnp.bfloat16), CONTEXT, scatter_dimension=0, tiled=True
            ).astype(jnp.float32),
        )
        d_q_low = (
            rotate(d_query.reshape(block_rows, -1, HEAD_SIZE), q_pos, -1.0)
            .astype(jnp.bfloat16)
            .reshape(block_rows, -1)
        )
        d_k_low = (
            rotate(own_keys.reshape(block_rows, -1, HEAD_SIZE), q_pos, -1.0)
            .astype(jnp.bfloat16)
            .reshape(block_rows, -1)
        )
        d_v_low = own_values.astype(jnp.bfloat16)
        d_one = head_sum(times_t(d_q_low, w_q) + times_t(d_k_low, w_k) + times_t(d_v_low, w_v))
        acc_query = acc_query + t_times(normed_one, d_q_low)
        acc_key = acc_key + t_times(normed_one, d_k_low)
        acc_value = acc_value + t_times(normed_one, d_v_low)
        d_inputs, gain_grad_a = norm_backward(inputs_f, root_a, gain_a.astype(jnp.float32), d_one)
        acc_gain_a = acc_gain_a + gain_grad_a
        input_grads.append((d_mid + d_inputs).astype(jnp.bfloat16))
    grads_attn = (
        lax.psum_scatter(
            acc_gain_a.astype(jnp.bfloat16), TOKEN_AXES, scatter_dimension=0, tiled=True
        ).astype(jnp.float32),
        lax.psum_scatter(
            acc_query.astype(jnp.bfloat16), TOKEN_AXES, scatter_dimension=0, tiled=True
        ).astype(jnp.float32),
        lax.psum_scatter(
            acc_key.astype(jnp.bfloat16), TOKEN_AXES, scatter_dimension=0, tiled=True
        ).astype(jnp.float32),
        lax.psum_scatter(
            acc_value.astype(jnp.bfloat16), TOKEN_AXES, scatter_dimension=0, tiled=True
        ).astype(jnp.float32),
        lax.psum_scatter(
            acc_out.astype(jnp.bfloat16), TOKEN_AXES, scatter_dimension=1, tiled=True
        ).astype(jnp.float32),
    )
    grads_mlp = (
        lax.psum_scatter(
            acc_gain_m.astype(jnp.bfloat16), TOKEN_AXES, scatter_dimension=0, tiled=True
        ).astype(jnp.float32),
        lax.psum_scatter(
            acc_gate.astype(jnp.bfloat16), TOKEN_AXES, scatter_dimension=0, tiled=True
        ).astype(jnp.float32),
        lax.psum_scatter(
            acc_up.astype(jnp.bfloat16), TOKEN_AXES, scatter_dimension=0, tiled=True
        ).astype(jnp.float32),
        lax.psum_scatter(
            acc_down.astype(jnp.bfloat16), TOKEN_AXES, scatter_dimension=1, tiled=True
        ).astype(jnp.float32),
    )
    seq_out = jnp.concatenate(outputs, axis=0)
    seq_grad = jnp.concatenate(input_grads, axis=0)
    back_index = invert(recv_index)
    returned = (
        lax.all_to_all(
            seq_out[back_index].reshape(groups, share, width),
            TOKEN_AXES,
            split_axis=0,
            concat_axis=0,
            tiled=True,
        ),
        lax.all_to_all(
            seq_grad[back_index].reshape(groups, share, width),
            TOKEN_AXES,
            split_axis=0,
            concat_axis=0,
            tiled=True,
        ),
    )
    data_index = invert(send_index)
    output = returned[0].reshape(rows, width)[data_index]
    input_grad = returned[1].reshape(rows, width)[data_index]
    return (
        output,
        input_grad,
        grads_attn[0],
        grads_attn[1],
        grads_attn[2],
        grads_attn[3],
        grads_attn[4],
        grads_mlp[0],
        grads_mlp[1],
        grads_mlp[2],
        grads_mlp[3],
    )


BF = jnp.bfloat16
F32 = jnp.float32
TILE = 256
LANES = 128
GROUP = 4
QUICK = pl.CostEstimate(flops=10**6, bytes_accessed=10**5, transcendentals=0)


def mm(left, right):
    return jnp.dot(left, right, preferred_element_type=F32)


def one_hot(rows, columns):
    return jnp.where(rows == columns, 1.0, 0.0).astype(BF)


def turn(u, cosine, sine):
    return u * cosine + pltpu.roll(u, LANES // 2, 1) * sine


def place_rows(index_col_ref, count):
    column = index_col_ref[0]
    lanes = lax.broadcasted_iota(jnp.int32, (column.shape[0], count), 1)
    return one_hot(lanes, column)


def arrival_rows(index_row_ref, count):
    row = index_row_ref[0]
    rows = lax.broadcasted_iota(jnp.int32, (count, row.shape[1]), 0)
    return one_hot(rows, row)


FLAG = HEAD_SIZE // 2


def flagged(value, flag):
    lanes = lax.broadcasted_iota(jnp.int32, value.shape, 1)
    return jnp.where(lanes % LANES == FLAG, flag, value)


def sort_kernel(mine, other, weight, cosine, sine, index_col, flag, out, picks, *, turned):
    @pl.when(pl.program_id(1) == 0)
    def _():
        picks[...] = place_rows(index_col, picks.shape[1])

    u = jnp.concatenate([mm(mine[...], weight[...]), mm(other[...], weight[...])], axis=0)
    cos_t, sin_t = cosine[0], sine[0]
    parts = [turn(u[:, :LANES], cos_t, sin_t), u[:, LANES:]]
    if turned == 2:
        parts[1] = turn(parts[1], cos_t, sin_t)
    moved = mm(picks[...], jnp.concatenate(parts, axis=1).astype(BF))
    if turned == 2:
        out[...] = flagged(moved, flag[0]).astype(BF)
    else:
        out[:, :LANES] = flagged(moved[:, :LANES], flag[0]).astype(BF)
        out[:, LANES:] = moved[:, LANES:].astype(BF)


def causal_bias():
    rows = lax.broadcasted_iota(jnp.int32, (TILE, TILE), 0)
    lanes = lax.broadcasted_iota(jnp.int32, (TILE, TILE), 1)
    return jnp.where(lanes <= rows, 0.0, MASKED)


def probabilities(q_head, keys, bias, scale):
    scores = times_t(q_head, keys)
    last = scores[:, -TILE:] + bias
    scores = jnp.concatenate([scores[:, :-TILE], last], axis=1) if keys.shape[0] > TILE else last
    top = jnp.max(scores, axis=1, keepdims=True)
    raised = jnp.exp2((scores - top) * (scale * 1.4426950408889634))
    return raised * (1.0 / jnp.sum(raised, axis=1, keepdims=True))


def fetch_keys(meta, block, kv, keys, values, count):
    for item in range(count):
        start = pl.multiple_of(meta[block, 1 + item], TILE)
        rows = pl.ds(item * TILE, TILE)
        keys[rows, :] = kv[pl.ds(start, TILE), :LANES]
        values[rows, :] = kv[pl.ds(start, TILE), LANES:]


def head_of(index):
    return slice(index * LANES, (index + 1) * LANES)


def forward_kernel(
    meta, q, kv, index_row, unpad, out, total, bias, keys, values, *, scale, blocks, per_run
):
    block = pl.program_id(0)
    part = lax.rem(block, per_run)
    run_rows = total.shape[0]

    @pl.when(block == 0)
    def _():
        bias[...] = causal_bias()

    def attend(count):
        fetch_keys(meta, block, kv, keys, values, count)
        size = count * TILE
        mixed = []
        for head in range(GROUP):
            probs = probabilities(q[:, head_of(head)], keys[:size, :], bias[...], scale)
            mixed.append(mm(probs.astype(BF), values[:size, :]).astype(BF))
        moved = mm(arrival_rows(index_row, run_rows), jnp.concatenate(mixed, axis=1))

        @pl.when(part == 0)
        def _():
            total[...] = moved

        @pl.when(part > 0)
        def _():
            total[...] += moved

    for count in range(1, blocks + 1):
        pl.when(meta[block, 0] == count - 1)(functools.partial(attend, count))

    @pl.when(part == per_run - 1)
    def _():
        packed = mm(total[...].astype(BF), unpad[...]).astype(BF)
        half = run_rows // 2
        first = pl.multiple_of(block // per_run * half, TILE)
        out[pl.ds(first, half), :] = packed[:half]
        out[pl.ds(2 * half + first, half), :] = packed[half:]


def backward_kernel(
    meta,
    q,
    kv,
    d_mine,
    d_other,
    index_col,
    index_row,
    cosine,
    sine,
    q_grad,
    own,
    sent,
    total,
    bias,
    keys,
    values,
    probs_all,
    scores_all,
    keys_grad,
    *,
    scale,
    blocks,
    per_run,
):
    block = pl.program_id(0)
    part = lax.rem(block, per_run)
    run_rows = total.shape[0]
    half = run_rows // 2

    @pl.when(block == 0)
    def _():
        keys_grad[...] = jnp.zeros_like(keys_grad)
        bias[...] = causal_bias()

    def attend(count):
        fetch_keys(meta, block, kv, keys, values, count)
        size = count * TILE
        places = place_rows(index_col, run_rows)
        d_out = mm(places[:, :half], d_mine[...]) + mm(places[:, half:], d_other[...])
        d_out = d_out.astype(BF)
        turned = []
        for head in range(GROUP):
            rows = pl.ds(head * TILE, TILE)
            probs = probabilities(q[:, head_of(head)], keys[:size, :], bias[...], scale)
            probs_all[rows, :size] = probs.astype(BF)
            d_probs = times_t(d_out[:, head_of(head)], values[:size, :])
            delta = jnp.sum(probs * d_probs, axis=1, keepdims=True)
            d_score = (probs * (d_probs - delta)).astype(BF)
            scores_all[rows, :size] = d_score
            d_query = flagged(mm(d_score, keys[:size, :]) * scale, 0.0)
            turned.append(turn(d_query, cosine[...], -sine[...]).astype(BF))
        heads = [head_of(head) for head in range(GROUP)]
        q_all = jnp.concatenate([q[:, at] for at in heads], axis=0)
        d_all = jnp.concatenate([d_out[:, at] for at in heads], axis=0)
        d_keys = t_times(scores_all[:, :size], q_all)
        d_values = t_times(probs_all[:, :size], d_all)
        for item in range(count):
            rows = pl.ds(pl.multiple_of(meta[block, 1 + item], TILE), TILE)
            keys_grad[rows, :LANES] += d_keys[item * TILE : (item + 1) * TILE]
            keys_grad[rows, LANES:] += d_values[item * TILE : (item + 1) * TILE]
        moved = mm(arrival_rows(index_row, run_rows), jnp.concatenate(turned, axis=1))

        @pl.when(part == 0)
        def _():
            total[...] = moved

        @pl.when(part > 0)
        def _():
            total[...] += moved

    for count in range(1, blocks + 1):
        pl.when(meta[block, 0] == count - 1)(functools.partial(attend, count))

    @pl.when(part == per_run - 1)
    def _():
        first = pl.multiple_of(block // per_run * half, TILE)
        q_grad[pl.ds(first, half), :] = total[:half].astype(BF)
        q_grad[pl.ds(2 * half + first, half), :] = total[half:].astype(BF)

    @pl.when(block == pl.num_programs(0) - 1)
    def _():
        count = own.shape[0]
        own[...] = keys_grad[:count]
        sent[...] = keys_grad[count:].astype(BF)


def unsort_kernel(own, got, cosine, sine, index_row, q_mine, q_other, unpad, out, *, scale):
    both = own[...] + got[...].astype(F32)
    d_keys = turn(both[:, :LANES] * scale, cosine[0], -sine[0])
    low = jnp.concatenate([d_keys, both[:, LANES:]], axis=1).astype(BF)
    moved = mm(arrival_rows(index_row, low.shape[0]), low).astype(BF)
    half = moved.shape[0] // 2
    split = q_mine.shape[1]
    first = pl.multiple_of(pl.program_id(0) * half, TILE)
    for rows, d_query, at in (
        (moved[:half], q_mine, first),
        (moved[half:], q_other, 2 * half + first),
    ):
        packed = mm(d_query[...], unpad[:split]) + mm(rows, unpad[split:])
        out[pl.ds(at, half), :] = packed.astype(BF)


def resident(shape):
    return pl.BlockSpec(shape, lambda *unused: (0,) * len(shape))


def call_sort(tokens, weight, cosine, sine, index_col, flag, turned):
    count, width = tokens.shape
    run_rows = count // 2
    half = run_rows // 2
    wide = 2 * LANES
    steps = weight.shape[1] // wide
    table = pl.BlockSpec((1, run_rows, LANES), lambda d, g: (d, 0, 0))
    column = pl.BlockSpec((1, run_rows, 1), lambda d, g: (d, 0, 0))
    return pl.pallas_call(
        functools.partial(sort_kernel, turned=turned),
        grid=(2, steps),
        in_specs=[
            pl.BlockSpec((half, width), lambda d, g: (d, 0)),
            pl.BlockSpec((half, width), lambda d, g: (2 + d, 0)),
            pl.BlockSpec((width, wide), lambda d, g: (0, g)),
            table,
            table,
            column,
            column,
        ],
        out_specs=pl.BlockSpec((run_rows, wide), lambda d, g: (d, g)),
        out_shape=jax.ShapeDtypeStruct((count, weight.shape[1]), BF),
        scratch_shapes=[pltpu.VMEM((run_rows, run_rows), BF)],
        compiler_params=pltpu.CompilerParams(vmem_limit_bytes=48 * 2**20),
        cost_estimate=QUICK,
        name="sort_tokens",
    )(tokens, tokens, weight, cosine, sine, index_col, flag)


def call_forward(meta, q, kv, index_row, unpad, scale):
    tokens = q.shape[0]
    run_rows = tokens // 2
    per_run = run_rows // TILE
    blocks = meta.shape[1] - 1
    body = functools.partial(forward_kernel, scale=scale, blocks=blocks, per_run=per_run)
    out = jax.ShapeDtypeStruct((tokens, unpad.shape[1]), BF)
    return pl.pallas_call(
        body,
        grid=(2 * per_run,),
        in_specs=[
            pl.BlockSpec(memory_space=pltpu.SMEM),
            pl.BlockSpec((TILE, GROUP * LANES), lambda b: (b, 0)),
            resident(kv.shape),
            pl.BlockSpec((1, 1, TILE), lambda b: (b // per_run, 0, b % per_run)),
            resident(unpad.shape),
        ],
        out_specs=resident(out.shape),
        out_shape=out,
        scratch_shapes=[
            pltpu.VMEM((run_rows, GROUP * LANES), F32),
            pltpu.VMEM((TILE, TILE), F32),
            pltpu.VMEM((blocks * TILE, LANES), BF),
            pltpu.VMEM((blocks * TILE, LANES), BF),
        ],
        compiler_params=pltpu.CompilerParams(vmem_limit_bytes=48 * 2**20),
        cost_estimate=QUICK,
        name="attention_forward",
    )(meta, q, kv, index_row, unpad)


def call_backward(meta, q, kv, d_out, index_col, index_row, cosine, sine, scale):
    tokens = q.shape[0]
    run_rows = tokens // 2
    per_run = run_rows // TILE
    blocks = meta.shape[1] - 1
    body = functools.partial(backward_kernel, scale=scale, blocks=blocks, per_run=per_run)
    run_half = run_rows // 2
    shape = (tokens, 2 * LANES)
    table = pl.BlockSpec((TILE, LANES), lambda b: (b, 0))
    return pl.pallas_call(
        body,
        grid=(2 * per_run,),
        in_specs=[
            pl.BlockSpec(memory_space=pltpu.SMEM),
            pl.BlockSpec((TILE, GROUP * LANES), lambda b: (b, 0)),
            resident(kv.shape),
            pl.BlockSpec((run_half, GROUP * LANES), lambda b: (b // per_run, 0)),
            pl.BlockSpec((run_half, GROUP * LANES), lambda b: (2 + b // per_run, 0)),
            pl.BlockSpec((1, TILE, 1), lambda b: (b // per_run, b % per_run, 0)),
            pl.BlockSpec((1, 1, TILE), lambda b: (b // per_run, 0, b % per_run)),
            table,
            table,
        ],
        out_specs=[resident(q.shape), resident(shape), resident(shape)],
        out_shape=[
            jax.ShapeDtypeStruct(q.shape, BF),
            jax.ShapeDtypeStruct(shape, F32),
            jax.ShapeDtypeStruct(shape, BF),
        ],
        scratch_shapes=[
            pltpu.VMEM((run_rows, GROUP * LANES), F32),
            pltpu.VMEM((TILE, TILE), F32),
            pltpu.VMEM((blocks * TILE, LANES), BF),
            pltpu.VMEM((blocks * TILE, LANES), BF),
            pltpu.VMEM((GROUP * TILE, blocks * TILE), BF),
            pltpu.VMEM((GROUP * TILE, blocks * TILE), BF),
            pltpu.VMEM((kv.shape[0], 2 * LANES), F32),
        ],
        compiler_params=pltpu.CompilerParams(vmem_limit_bytes=56 * 2**20),
        cost_estimate=QUICK,
        name="attention_backward",
    )(meta, q, kv, d_out, d_out, index_col, index_row, cosine, sine)


def call_unsort(own, got, cosine, sine, index_row, q_grad, unpad, scale):
    tokens, wide = own.shape
    run_rows = tokens // 2
    half = run_rows // 2
    table = pl.BlockSpec((1, run_rows, LANES), lambda d: (d, 0, 0))
    out = jax.ShapeDtypeStruct((tokens, unpad.shape[1]), BF)
    return pl.pallas_call(
        functools.partial(unsort_kernel, scale=scale),
        grid=(2,),
        in_specs=[
            pl.BlockSpec((run_rows, wide), lambda d: (d, 0)),
            pl.BlockSpec((run_rows, wide), lambda d: (d, 0)),
            table,
            table,
            pl.BlockSpec((1, 1, run_rows), lambda d: (d, 0, 0)),
            pl.BlockSpec((half, q_grad.shape[1]), lambda d: (d, 0)),
            pl.BlockSpec((half, q_grad.shape[1]), lambda d: (2 + d, 0)),
            resident(unpad.shape),
        ],
        out_specs=resident(out.shape),
        out_shape=out,
        compiler_params=pltpu.CompilerParams(vmem_limit_bytes=40 * 2**20),
        cost_estimate=QUICK,
        name="unsort_tokens",
    )(own, got, cosine, sine, index_row, q_grad, q_grad, unpad)


def product_kernel(left, right, *outs, form, spread):
    contract = ((1,), (0,)) if form == 0 else ((1,), (1,)) if form == 1 else ((0,), (0,))
    value = lax.dot_general(
        left[...], right[...], (contract, ((), ())), preferred_element_type=F32
    ).astype(BF)
    if spread:
        outs[0][...] = mm(value, outs[-1][...]).astype(BF)
        return
    first = 0
    for out in outs:
        out[...] = value[:, first : first + out.shape[1]]
        first += out.shape[1]


def spread_kernel(left, right, lanes, out, *, form):
    product_kernel(left, right, out, lanes, form=form, spread=True)


def product(left, right, form, cuts=1, lanes=None):
    block = 2 * TILE
    count = left.shape[1 if form == 2 else 0]
    columns = right.shape[0 if form == 1 else 1]
    whole = lambda value: pl.BlockSpec(value.shape, lambda i: (0, 0))
    if form == 2:
        left_spec = pl.BlockSpec((left.shape[0], block), lambda i: (0, i))
    else:
        left_spec = pl.BlockSpec((block, left.shape[1]), lambda i: (i, 0))
    operands, in_specs = [left, right], [left_spec, whole(right)]
    body = functools.partial(product_kernel, form=form, spread=False)
    if lanes is not None:
        operands.append(lanes)
        in_specs.append(whole(lanes))
        body = functools.partial(spread_kernel, form=form)
        columns = lanes.shape[1]
    width = columns // cuts
    outs = pl.pallas_call(
        body,
        grid=(count // block,),
        in_specs=in_specs,
        out_specs=[pl.BlockSpec((block, width), lambda i: (i, 0))] * cuts,
        out_shape=[jax.ShapeDtypeStruct((count, width), BF)] * cuts,
        compiler_params=pltpu.CompilerParams(vmem_limit_bytes=48 * 2**20),
        cost_estimate=QUICK,
        name="product",
    )(*operands)
    return outs if cuts > 1 else outs[0]


ROUNDS = 4
FIRST, MIDDLE, BACK, LAST, PLAIN, SUM = range(6)
KINDS = 13
CORE, RY, RL, SL, SY, GY, GL, GC, FL, FY, CY, CL, CC = range(KINDS)
MESH_IDS = pl.DeviceIdType.MESH


def partners():
    group, place, shard = (lax.axis_index(name) for name in MESH_AXES)
    return (
        (group, place, shard + 2 - 4 * (shard // 2)),
        (group, place + 1 - 2 * (place % 2), shard),
        (group, place, shard + 1 - 2 * (shard % 2)),
    )


def route_partner(q, e):
    group, place, shard = (lax.axis_index(name) for name in MESH_AXES)
    high, low = place // 2, place % 2
    group = 1 - group if q // 2 else group
    high = 1 - high if q % 2 else high
    low = 1 - low if e else low
    return (group, 2 * high + low, shard), 4 * group + 2 * high + low


ROUTES = [(q, e) for q in range(4) for e in range(2)]


class Router:
    def __init__(self, src, dst, send_sem, recv_sem, local_sem, spread=False):
        self.src, self.dst, self.copies, self.spread = src, dst, {}, spread
        self.send_sem, self.recv_sem, self.local_sem = send_sem, recv_sem, local_sem
        self.size = src.shape[0]
        self.share = self.size // len(ROUTES)

    def rows(self, index, slot=0):
        return pl.ds(pl.multiple_of(slot * self.size + index * self.share, 16), self.share)

    def start(self, what, q, e, src, dst, device):
        at = what * len(ROUTES) + 2 * q + e
        copy = pltpu.make_async_remote_copy(
            src_ref=src,
            dst_ref=dst,
            send_sem=self.send_sem.at[at],
            recv_sem=self.recv_sem.at[at],
            device_id=device,
            device_id_type=MESH_IDS,
        )
        copy.start()
        self.copies[what, q, e] = copy

    def send(self, q, e):
        device, index = route_partner(q, e)
        own = route_partner(0, 0)[1]
        if (q, e) == (0, 0):
            copy = pltpu.make_async_copy(
                self.src.at[self.rows(own), :], self.dst.at[self.rows(own), :], self.local_sem
            )
            copy.start()
            self.copies[0, 0, 0] = copy
        else:
            self.start(
                0, q, e, self.src.at[self.rows(index), :], self.dst.at[self.rows(own), :], device
            )

    def arrived(self, what, q, e):
        copy = self.copies[what, q, e]
        if (what, q, e) == (0, 0, 0):
            copy.wait()
        else:
            copy.wait_recv()

    def pass_on(self, q, e):
        on_y, unused, on_core = partners()
        index = route_partner(q, e)[1]
        self.arrived(0, q, e)
        here = self.dst.at[self.rows(index), :]
        self.start(1, q, e, here, self.dst.at[self.rows(index, 1), :], on_y)
        self.start(2, q, e, here, self.dst.at[self.rows(index, 2), :], on_core)

    def pass_corner(self, q, e):
        on_core = partners()[2]
        index = route_partner(q, e)[1]
        self.arrived(1, q, e)
        here = self.dst.at[self.rows(index, 1), :]
        self.start(3, q, e, here, self.dst.at[self.rows(index, 3), :], on_core)

    def finish(self):
        for (what, q, e), copy in self.copies.items():
            if (what, q, e) != (0, 0, 0):
                copy.wait_send()
            if what in (2, 3) or not self.spread:
                self.arrived(what, q, e)


PIECES = 8


class Pieces:
    def __init__(self, buffer, send_sem, recv_sem):
        self.buffer, self.send_sem, self.recv_sem = buffer, send_sem, recv_sem
        self.used, self.near = [], []
        self.quarter = buffer.shape[0] // 4
        self.step = self.quarter // PIECES
        self.on_hi = route_partner(1, 0)[0]
        self.on_dp = route_partner(2, 0)[0]

    def copy(self, what, piece):
        group, place = lax.axis_index(DP), lax.axis_index(CONTEXT)
        low, high = place % 2, place // 2
        high = 1 - high if what == 2 else high
        half = low if piece < PIECES // 2 else 1 - low
        first = (2 * group + high) * self.quarter + half * (self.quarter // 2)
        first = pl.multiple_of(first + piece % (PIECES // 2) * self.step, 16)
        at = self.buffer.at[pl.ds(first, self.step), :]
        return pltpu.make_async_remote_copy(
            src_ref=at,
            dst_ref=at,
            send_sem=self.send_sem.at[what, piece],
            recv_sem=self.recv_sem.at[what, piece],
            device_id=self.on_dp if what else self.on_hi,
            device_id_type=MESH_IDS,
        )

    def send(self, piece):
        self.copy(0, piece).start()
        self.copy(1, piece).start()
        self.used.append(piece)

    def pass_on(self, piece):
        self.copy(0, piece).wait_recv()
        self.copy(2, piece).start()

    def spread(self, piece):
        self.copy(1, piece).start()
        self.copy(2, piece).start()
        self.near.append(piece)

    def finish(self):
        for piece in self.used + self.near:
            for what in range(3):
                if what == 0 and piece in self.near:
                    continue
                copy = self.copy(what, piece)
                copy.wait_send()
                if what > 0:
                    copy.wait_recv()


def piece_scratch():
    return [pltpu.SemaphoreType.DMA((3, PIECES))] * 2


def route_scratch(parts):
    return [
        pltpu.SemaphoreType.DMA((parts * len(ROUTES),)),
        pltpu.SemaphoreType.DMA((parts * len(ROUTES),)),
        pltpu.SemaphoreType.DMA(()),
    ]


def greet(devices):
    barrier = pltpu.get_barrier_semaphore()
    for device in devices:
        pl.semaphore_signal(barrier, inc=1, device_id=device, device_id_type=MESH_IDS)
    pl.semaphore_wait(barrier, len(devices))


def root_of(value):
    return lax.rsqrt(jnp.mean(value * value, axis=-1, keepdims=True) + EPS)


def norm_gradient(value, gain, grad):
    root = root_of(value)
    weighted = grad * gain
    return root * weighted - value * (root * root * root) * jnp.mean(
        weighted * value, axis=-1, keepdims=True
    ), jnp.sum(grad * value * root, axis=0, keepdims=True)


def token_kernel(*refs, kind, scatter, gather, pieces):
    refs = list(refs)
    take = lambda count: [refs.pop(0) for unused in range(count)]
    if scatter:
        (parts,) = take(1)
    (x_ref,) = take(1)
    if kind in (FIRST, LAST):
        (gain,) = take(1)
    if kind == PLAIN:
        (own_kv,) = take(1)
    if kind == LAST:
        (add_ref,) = take(1)
    if kind == LAST:
        aside, other_gain = take(2)
        near_send, near_keep, total = take(3)
    else:
        (bulk,) = take(1)
    if kind == PLAIN:
        (all_kv,) = take(1)
    if gather:
        (everyone,) = take(1)
    if kind == LAST:
        grad_out, gains_out, aside_out = take(3)
        kept, gotten = take(2), take(2)
    else:
        (bulk_out,) = take(1)
    if scatter:
        from_core, send_y, keep_y, got_y, send_lo, got_lo, mine, mine_sem = take(8)
    if gather:
        ready, local_sem = take(2)
    if kind == LAST:
        (ready,) = take(1)
    if kind == LAST:
        aside_router = Router(aside, aside_out, *take(3), spread=True)
        grad_router = Router(ready, grad_out, *take(3), spread=True)
        gain_acc, gain_sent, gain_got, side_local, side_send, side_recv = take(6)
        from_his, lo_sends = take(2), take(2)
        own_half, from_dp, total_keep, total_send = take(4)
    else:
        bulk_send, bulk_recv = take(2)
    if kind == PLAIN:
        kv_local, kv_send, kv_recv = take(3)
    send_sem, recv_sem = refs
    size, width = x_ref.shape
    step = size // ROUNDS
    on_y, on_lo, on_core = partners()
    on_hi, on_dp = route_partner(1, 0)[0], route_partner(2, 0)[0]
    if kind == LAST:
        greet((on_y, on_core, *(route_partner(q, e)[0] for q, e in ROUTES[1:])))
        for q, e in ROUTES:
            aside_router.send(q, e)
    else:
        greet((on_y, on_lo, on_core, on_hi, on_dp))
    kv_copies = []
    if kind == PLAIN:
        count = own_kv.shape[0]
        kv_copies.append(pltpu.make_async_copy(own_kv, all_kv.at[pl.ds(0, count), :], kv_local))
        kv_copies.append(
            pltpu.make_async_remote_copy(
                src_ref=own_kv,
                dst_ref=all_kv.at[pl.ds(count, count), :],
                send_sem=kv_send,
                recv_sem=kv_recv,
                device_id=on_hi,
                device_id_type=MESH_IDS,
            )
        )
        for copy in kv_copies:
            copy.start()
    if gather:
        weights = Pieces(bulk_out, bulk_send, bulk_recv)
    copies = {}

    def start(what, q, src, dst, device):
        copies[what, q] = pltpu.make_async_remote_copy(
            src_ref=src,
            dst_ref=dst,
            send_sem=send_sem.at[what, q],
            recv_sem=recv_sem.at[what, q],
            device_id=device,
            device_id_type=MESH_IDS,
        )
        copies[what, q].start()

    def arrived(what, q):
        copies[what, q].wait_recv()

    def rows_of(q):
        return pl.ds(pl.multiple_of(order(q) * step, step), step)

    def order(q):
        return route_partner(q, 0)[1] // 2 if kind == LAST else q

    def sum_core(q):
        rows = rows_of(q)
        arrived(CORE, q)
        copies["mine", q].wait()
        for lo in range(2):
            at = 2 * lo
            keep_y[lo, rows, :] = mine[at, rows, :].astype(F32) + from_core[at, rows, :].astype(F32)
            at = 2 * lo + 1
            total = mine[at, rows, :].astype(F32) + from_core[at, rows, :].astype(F32)
            send_y[lo, rows, :] = total.astype(BF)
        start(RY, q, send_y.at[:, rows, :], got_y.at[:, rows, :], on_y)

    def sum_y(q):
        rows = rows_of(q)
        arrived(RY, q)
        send_lo[rows, :] = (keep_y[1, rows, :] + got_y[1, rows, :].astype(F32)).astype(BF)
        start(RL, q, send_lo.at[rows, :], got_lo.at[rows, :], on_lo)

    def sum_lo(q):
        rows = rows_of(q)
        arrived(RL, q)
        return keep_y[0, rows, :] + got_y[0, rows, :].astype(F32) + got_lo[rows, :].astype(F32)

    def finish(q):
        rows = rows_of(q)
        total = sum_lo(q) if scatter else None
        value = x_ref[rows, :]
        if kind == PLAIN:
            low = value
        elif kind == FIRST:
            value = value.astype(F32)
            low = (value * root_of(value) * gain[...]).astype(BF)
        else:
            grad, gain_grad = norm_gradient(value.astype(F32), gain[...], total)
            grad = grad + add_ref[rows, :].astype(F32)
            ready[rows, :] = grad.astype(BF)
            if q == 0:
                gain_acc[...] = gain_grad
            else:
                gain_acc[...] += gain_grad
        if kind == LAST:
            grad_router.send(q, 0)
            grad_router.send(q, 1)
        if gather:
            ready[rows, :] = low
            keep = pltpu.make_async_copy(ready.at[rows, :], everyone.at[rows, :], local_sem.at[q])
            keep.start()
            copies["local", q] = keep
            start(GY, q, ready.at[rows, :], everyone.at[block(1, q), :], on_y)
            start(GL, q, ready.at[rows, :], everyone.at[block(2, q), :], on_lo)
            start(GC, q, ready.at[rows, :], everyone.at[block(4, q), :], on_core)

    def block(index, q):
        return pl.ds(index * size + q * step, step)

    def forward(q):
        arrived(GL, q)
        start(FY, q, everyone.at[block(2, q), :], everyone.at[block(3, q), :], on_y)
        start(CL, q, everyone.at[block(2, q), :], everyone.at[block(6, q), :], on_core)
        arrived(GY, q)
        start(CY, q, everyone.at[block(1, q), :], everyone.at[block(5, q), :], on_core)

    def corner(q):
        arrived(FY, q)
        start(CC, q, everyone.at[block(3, q), :], everyone.at[block(7, q), :], on_core)

    def pass_on(q):
        for router in routers:
            router.pass_on(q, 0)
            router.pass_on(q, 1)

    def pass_corner(q):
        for router in routers:
            router.pass_corner(q, 0)
            router.pass_corner(q, 1)

    side_copies = []

    def side(src, dst, device):
        at = len(side_copies)
        copy = pltpu.make_async_remote_copy(
            src_ref=src,
            dst_ref=dst,
            send_sem=side_send.at[at],
            recv_sem=side_recv.at[at],
            device_id=device,
            device_id_type=MESH_IDS,
        )
        copy.start()
        side_copies.append(copy)
        return copy

    waiting = {}

    def unit_rows(unit):
        low = lax.axis_index(CONTEXT) % 2
        count = from_his[unit // 2].shape[0] // 2
        index = low if unit % 2 else 1 - low
        return pl.ds(pl.multiple_of(index * count, 16), count)

    def unit_to_dp(unit):
        group = lax.axis_index(DP)
        rows = unit_rows(unit)
        waiting["own", unit] = pltpu.make_async_copy(
            total.at[group, :, rows, :], own_half.at[:, rows, :], side_local.at[unit]
        )
        waiting["own", unit].start()
        waiting["dp", unit] = side(
            total.at[1 - group, :, rows, :], from_dp.at[:, rows, :], on_dp
        )

    def unit_to_hi(unit):
        high = lax.axis_index(CONTEXT) // 2
        rows = unit_rows(unit)
        send = near_send if unit < 2 else total_send
        if unit >= 2:
            waiting["own", unit].wait()
            waiting["dp", unit].wait_recv()
            total_keep[rows, :] = own_half[high, rows, :].astype(F32) + from_dp[
                high, rows, :
            ].astype(F32)
            send[rows, :] = (
                own_half[1 - high, rows, :].astype(F32) + from_dp[1 - high, rows, :].astype(F32)
            ).astype(BF)
        waiting["hi", unit] = side(send.at[rows, :], from_his[unit // 2].at[rows, :], on_hi)

    def unit_to_lo(unit):
        rows = unit_rows(unit)
        keep = near_keep if unit < 2 else total_keep
        waiting["hi", unit].wait_recv()
        value = keep[rows, :] + from_his[unit // 2][rows, :].astype(F32)
        if unit % 2:
            kept[unit // 2][...] = value
        else:
            lo_sends[unit // 2][...] = value.astype(BF)
            waiting["lo", unit] = side(lo_sends[unit // 2], gotten[unit // 2], on_lo)

    def gain_hop(index):
        if index == 0:
            total = jnp.concatenate([gain_acc[...], other_gain[...]], axis=0)
        else:
            waiting["gain"].wait_recv()
            total = gain_sent[index - 1] + gain_got[index - 1]
        if index == 5:
            gains_out[...] = total
        else:
            gain_sent[index] = total
            device = (on_core, on_y, on_lo, on_dp, on_hi)[index]
            waiting["gain"] = side(gain_sent.at[index], gain_got.at[index], device)

    def beside(tick):
        if tick == 0:
            unit_to_dp(2)
            unit_to_dp(3)
        if tick < 2:
            unit_to_hi(tick)
        if tick in (3, 4):
            unit_to_hi(tick - 1)
        if tick in (5, 6):
            unit_to_lo(tick - 5)
        if 5 <= tick < 8:
            gain_hop(tick - 5)
        if tick == 7:
            for index in range(3, 6):
                gain_hop(index)
            unit_to_lo(2)
            unit_to_lo(3)

    routers = [aside_router, grad_router] if kind == LAST else []
    stages = []
    if scatter:
        for q in range(ROUNDS):
            rows = rows_of(q)
            start(CORE, q, parts.at[pl.ds(4, 4), rows, :], from_core.at[:, rows, :], on_core)
            copies["mine", q] = pltpu.make_async_copy(
                parts.at[pl.ds(0, 4), rows, :], mine.at[:, rows, :], mine_sem.at[q]
            )
            copies["mine", q].start()
        stages += [sum_core, sum_y]
    stages.append(finish)
    if gather:
        stages += [forward, corner]
    if routers:
        stages += [pass_on, pass_corner]
    ordered = list(enumerate(stages))
    if scatter:
        ordered.reverse()
    for tick in range(ROUNDS + len(stages) - 1):
        for index, stage in ordered:
            if 0 <= tick - index < ROUNDS:
                stage(tick - index)
        if gather and tick < len(pieces):
            weights.send(pieces[tick])
        if kind == LAST:
            beside(tick)
        if gather and 0 <= tick - 2 < len(pieces):
            weights.pass_on(pieces[tick - 2])
    for (what, q), copy in copies.items():
        if what == "local":
            copy.wait()
        elif what != "mine":
            copy.wait_send()
            if what in (GC, CY, CL, CC):
                copy.wait_recv()
    if gather:
        weights.finish()
    for copy in kv_copies:
        copy.wait()
    if kind == LAST:
        aside_router.finish()
        grad_router.finish()
        for copy in side_copies:
            copy.wait_send()
        for unit in (0, 2):
            waiting["lo", unit].wait_recv()


def call_tokens(
    kind, ident, part, x, bulk, pieces, gain=None, add=None, aside=None, other_gain=None, grads=None
):
    size, width = x.shape
    scatter, gather = part is not None, kind != LAST
    vmem = pl.BlockSpec(memory_space=pltpu.VMEM)
    anywhere = pl.BlockSpec(memory_space=pl.ANY)
    operands, in_specs, out_specs, out_shape, scratch = [], [], [], [], []
    if scatter:
        operands.append(part.reshape(8, size, width))
        in_specs.append(anywhere)
    operands.append(x)
    in_specs.append(vmem)
    if gain is not None:
        operands.append(gain.reshape(1, width))
        in_specs.append(vmem)
    if kind == PLAIN:
        operands.append(add)
        in_specs.append(anywhere)
        out_specs.append(anywhere)
        out_shape.append(jax.ShapeDtypeStruct((2 * add.shape[0], add.shape[1]), BF))
    elif add is not None:
        operands.append(add)
        in_specs.append(vmem)
    if aside is not None:
        send, keep, total = grads
        cuts = [keep.shape, (total.shape[0] // 4, total.shape[1])]
        operands += [aside, other_gain, send, keep, total.reshape(2, 2, *cuts[1])]
        in_specs += [anywhere, vmem, anywhere, vmem, anywhere]
    if bulk is not None:
        operands.append(bulk)
        in_specs.append(anywhere)
    if gather:
        out_specs.append(anywhere)
        out_shape.append(jax.ShapeDtypeStruct((8 * size, width), BF))
    if kind == LAST:
        out_specs.append(anywhere)
        out_shape.append(jax.ShapeDtypeStruct((4 * size, width), BF))
    if kind == LAST:
        out_specs.append(vmem)
        out_shape.append(jax.ShapeDtypeStruct((2, width), F32))
        out_specs += [anywhere] + [vmem] * 2 + [anywhere] * 2
        out_shape.append(jax.ShapeDtypeStruct((4 * size, width), BF))
        out_shape += [jax.ShapeDtypeStruct((count // 2, n), F32) for count, n in cuts]
        out_shape += [jax.ShapeDtypeStruct((count // 2, n), BF) for count, n in cuts]
    if bulk is not None:
        out_specs.append(anywhere)
        out_shape.append(jax.ShapeDtypeStruct(bulk.shape, BF))
    if scatter:
        scratch.append(pltpu.VMEM((4, size, width), BF))
        pair = (2, size, width)
        scratch += [pltpu.VMEM(pair, BF), pltpu.VMEM(pair, F32), pltpu.VMEM(pair, BF)]
        scratch += [pltpu.VMEM((size, width), BF)] * 2
        scratch += [pltpu.VMEM((4, size, width), BF), pltpu.SemaphoreType.DMA((ROUNDS,))]
    if gather:
        scratch += [pltpu.VMEM((size, width), BF), pltpu.SemaphoreType.DMA((ROUNDS,))]
    if kind == LAST:
        scratch.append(pltpu.VMEM((size, width), BF))
        scratch += route_scratch(4) + route_scratch(4)
        scratch += [pltpu.VMEM((1, width), F32)] + [pltpu.VMEM((5, 2, width), F32)] * 2
        scratch.append(pltpu.SemaphoreType.DMA((6,)))
        scratch += [pltpu.SemaphoreType.DMA((20,))] * 2
        scratch += [pltpu.VMEM(cut, BF) for cut in cuts]
        scratch += [pltpu.VMEM((count // 2, n), BF) for count, n in cuts]
        scratch += [pltpu.VMEM((2, *cuts[1]), BF)] * 2
        scratch += [pltpu.VMEM(cuts[1], F32), pltpu.VMEM(cuts[1], BF)]
    else:
        scratch += piece_scratch()
    if kind == PLAIN:
        scratch += [pltpu.SemaphoreType.DMA(())] * 3
    scratch += [pltpu.SemaphoreType.DMA((KINDS, ROUNDS))] * 2
    return pl.pallas_call(
        functools.partial(
            token_kernel, kind=kind, scatter=scatter, gather=gather, pieces=pieces
        ),
        in_specs=in_specs,
        out_specs=out_specs,
        out_shape=out_shape,
        scratch_shapes=scratch,
        input_output_aliases={len(operands) - 1: len(out_shape) - 1} if gather else {},
        compiler_params=pltpu.CompilerParams(
            collective_id=ident, has_side_effects=True, vmem_limit_bytes=62 * 2**20
        ),
        cost_estimate=QUICK,
        name="tokens_%d" % kind,
    )(*operands)


def ffn_kernel(
    parts,
    x_ref,
    gain,
    d_y,
    d_y_all,
    large,
    two_all,
    grad_all,
    inner_out,
    both_out,
    y_out,
    mid_out,
    grad_out,
    gain_out,
    large_out,
    weights,
    summed,
    got_a,
    got_b,
    got_c,
    got_d,
    mine,
    two_ready,
    grad_ready,
    two_block,
    d_y_block,
    inner_block,
    both_block,
    y_block,
    d_two,
    weight_sem,
    mine_sem,
    ready_sem,
    load_sem,
    store_sem,
    send_sem,
    recv_sem,
    piece_send,
    piece_recv,
    *,
    pieces,
):
    size, width = x_ref.shape
    units = inner_out.shape[2]
    cut = width // 2
    step = size // ROUNDS
    half = step // 2
    on_y, on_lo, on_core = partners()
    arriving = Pieces(large_out, piece_send, piece_recv)
    greet((on_y, on_lo, on_core, arriving.on_dp))
    left, right = pl.ds(0, cut), pl.ds(cut, width - cut)

    def rows_of(q):
        return pl.ds(pl.multiple_of(q * step, step), step)

    def block(index, q, first=0, count=None):
        start = pl.multiple_of(index * size + q * step + first, half)
        return pl.ds(start, step if count is None else count)

    def remote(base, what, q):
        rows = rows_of(q)
        ready, everyone = (two_ready, two_all) if base == 0 else (grad_ready, grad_all)
        part_of = lambda *place: everyone.at[block(*place), :]
        if what == CORE:
            src = parts.at[1, :, :, rows, :] if base == 0 else d_two.at[lax.rem(q, 2), 1]
            ends = src, summed.at[:, :, rows, :], on_core
        elif what == RY:
            ends = summed.at[:, 1, rows, left], got_a.at[:, rows, :], on_y
        elif what == RL:
            ends = summed.at[1, :, rows, right], got_b.at[:, rows, :], on_lo
        elif what == SL:
            ends = summed.at[1, 0, rows, left], got_c.at[rows, :], on_lo
        elif what == SY:
            ends = summed.at[0, 1, rows, right], got_d.at[rows, :], on_y
        elif what in (GY, GL, GC):
            index, device = {GY: (1, on_y), GL: (2, on_lo), GC: (4, on_core)}[what]
            ends = ready.at[rows, :], part_of(index, q), device
        elif what == FL:
            ends = part_of(1, q, 0, half), part_of(3, q, 0, half), on_lo
        elif what == FY:
            ends = part_of(2, q, half, half), part_of(3, q, half, half), on_y
        else:
            index = {CY: 1, CL: 2, CC: 3}[what]
            ends = part_of(index, q), part_of(index + 4, q), on_core
        return pltpu.make_async_remote_copy(
            src_ref=ends[0],
            dst_ref=ends[1],
            send_sem=send_sem.at[base + what, q],
            recv_sem=recv_sem.at[base + what, q],
            device_id=ends[2],
            device_id_type=MESH_IDS,
        )

    def arrived(base, what, q):
        remote(base, what, q).wait_recv()

    def sum_core(base, q, value):
        rows = rows_of(q)
        arrived(base, CORE, q)
        for lo in range(2):
            for y in range(2):
                total = value(lo, y).astype(F32) + summed[lo, y, rows, :].astype(F32)
                summed[lo, y, rows, :] = total.astype(BF)
        remote(base, RY, q).start()
        remote(base, RL, q).start()

    def sum_first(base, q):
        rows = rows_of(q)
        arrived(base, RY, q)
        total = summed[1, 0, rows, :cut].astype(F32) + got_a[1, rows, :].astype(F32)
        summed[1, 0, rows, :cut] = total.astype(BF)
        remote(base, SL, q).start()
        arrived(base, RL, q)
        total = summed[0, 1, rows, cut:].astype(F32) + got_b[1, rows, :].astype(F32)
        summed[0, 1, rows, cut:] = total.astype(BF)
        remote(base, SY, q).start()

    def sum_second(base, q):
        rows = rows_of(q)
        arrived(base, SL, q)
        arrived(base, SY, q)
        first = summed[0, 0, rows, :cut].astype(F32) + got_a[0, rows, :].astype(F32)
        second = summed[0, 0, rows, cut:].astype(F32) + got_b[0, rows, :].astype(F32)
        first = first + got_c[rows, :].astype(F32)
        second = second + got_d[rows, :].astype(F32)
        for what in (RY, RL, SL, SY):
            remote(base, what, q).wait_send()
        return jnp.concatenate([first, second], axis=1)

    def own_rows(base, q):
        ready, everyone = (two_ready, two_all) if base == 0 else (grad_ready, grad_all)
        rows = rows_of(q)
        sem = ready_sem.at[base // KINDS, q]
        return pltpu.make_async_copy(ready.at[rows, :], everyone.at[rows, :], sem)

    def spread(base, q):
        own_rows(base, q).start()
        for what in (GY, GL, GC):
            remote(base, what, q).start()

    def forward(base, q):
        arrived(base, GY, q)
        remote(base, FL, q).start()
        remote(base, CY, q).start()
        arrived(base, GL, q)
        remote(base, FY, q).start()
        remote(base, CL, q).start()

    def corner(base, q):
        arrived(base, FL, q)
        arrived(base, FY, q)
        remote(base, CC, q).start()

    def fetch_mine(q):
        src = parts.at[0, :, :, rows_of(q), :]
        slot = lax.rem(q, 2)
        return pltpu.make_async_copy(src, mine.at[slot], mine_sem.at[slot])

    def middle_core(q):
        fetch_mine(q).wait()
        sum_core(0, q, lambda lo, y: mine[lax.rem(q, 2), lo, y])

        @pl.when(q + 2 < ROUNDS)
        def _():
            fetch_mine(q + 2).start()

    def middle_norm(q):
        rows = rows_of(q)
        value = x_ref[rows, :].astype(F32) + sum_second(0, q)
        mid_out[rows, :] = value
        two_ready[rows, :] = (value * root_of(value) * gain[...]).astype(BF)
        spread(0, q)

    def loads(part, q):
        for index, (src, dst) in enumerate(((two_all, two_block), (d_y_all, d_y_block))):
            for at in range(4):
                yield pltpu.make_async_copy(
                    src.at[block(4 * part + at, q), :],
                    dst.at[part, pl.ds(at * step, step), :],
                    load_sem.at[index, part, at],
                )

    def stores(part, q):
        pairs = ((inner_block, inner_out), (both_block, both_out), (y_block, y_out))
        for index, (src, dst) in enumerate(pairs):
            for at in range(4):
                yield pltpu.make_async_copy(
                    src.at[part, pl.ds(at * step, step), :],
                    dst.at[4 * part + at, rows_of(q), :],
                    store_sem.at[index, part, at],
                )

    def feed_forward(q):
        own_rows(0, q).wait()
        for what in (GC, CY, CL, CC):
            arrived(0, what, q)

        @pl.when(q == 0)
        def _():
            pltpu.make_async_copy(large_out, weights, weight_sem.at[0]).wait()

        @pl.when(q >= 2)
        def _():
            remote(KINDS, CORE, q - 2).wait_send()

        for part in (1, 0):
            for copy in loads(part, q):
                copy.start()

        @pl.loop(0, 2)
        def _(turn_index):
            part = 1 - turn_index
            for copy in loads(part, q):
                copy.wait()

            @pl.when(q > 0)
            def _():
                for copy in stores(part, q - 1):
                    copy.wait()

            both = mm(two_block[part], weights[:, : 2 * units])
            gate, up = both[:, :units], both[:, units:]
            d_inner = mm(d_y_block[part], weights[:, 2 * units :])
            sigma = 1.0 / (1.0 + jnp.exp(-gate))
            silu_gate = gate * sigma
            inner_block[part] = (silu_gate * up).astype(BF)
            d_gate = d_inner * up * sigma * (1.0 + gate * (1.0 - sigma))
            both_block[part, :, :units] = d_gate.astype(BF)
            both_block[part, :, units:] = (d_inner * silu_gate).astype(BF)
            d_two[lax.rem(q, 2), part] = (
                times_t(both_block[part], weights[:, : 2 * units])
                .astype(BF)
                .reshape(2, 2, step, width)
            )

            @pl.when(part == 1)
            def _():
                remote(KINDS, CORE, q).start()

            y_block[part] = times_t(inner_block[part], weights[:, 2 * units :]).astype(BF)
            for copy in stores(part, q):
                copy.start()

    def back_core(q):
        sum_core(KINDS, q, lambda lo, y: d_two[lax.rem(q, 2), 0, lo, y])

    def back_norm(q):
        rows = rows_of(q)
        grad, gain_grad = norm_gradient(mid_out[rows, :], gain[...], sum_second(KINDS, q))
        grad = grad + d_y[rows, :].astype(F32)
        grad_out[rows, :] = grad
        gain_out[...] += gain_grad
        grad_ready[rows, :] = grad.astype(BF)
        spread(KINDS, q)

    gain_out[...] = jnp.zeros_like(gain_out)
    for q in range(ROUNDS):
        remote(0, CORE, q).start()
        if q < 2:
            fetch_mine(q).start()
    stages = [
        middle_core,
        functools.partial(sum_first, 0),
        middle_norm,
        functools.partial(forward, 0),
        functools.partial(corner, 0),
        feed_forward,
        back_core,
        functools.partial(sum_first, KINDS),
        back_norm,
        functools.partial(forward, KINDS),
        functools.partial(corner, KINDS),
    ]

    @pl.loop(0, ROUNDS + len(stages) - 1)
    def _(tick):
        for index, stage in reversed(list(enumerate(stages))):
            pl.when((tick >= index) & (tick < index + ROUNDS))(
                functools.partial(stage, tick - index)
            )

        @pl.when(tick == 0)
        def _():
            for piece in pieces:
                arriving.spread(piece)

        @pl.when(tick == 4)
        def _():
            arriving.finish()
            pltpu.make_async_copy(large_out, weights, weight_sem.at[0]).start()

    for q in range(ROUNDS):
        for base in (0, KINDS):
            for what in range(KINDS):
                if what in (RY, RL, SL, SY) or (what == CORE and base and q < ROUNDS - 2):
                    continue
                remote(base, what, q).wait_send()
        for what in (GC, CY, CL, CC):
            arrived(KINDS, what, q)
        own_rows(KINDS, q).wait()
    for part in range(2):
        for copy in stores(part, ROUNDS - 1):
            copy.wait()


def call_ffn(parts, x, gain, d_y, d_y_all, large, pieces):
    size, width = x.shape
    units = large.shape[1] // 3
    cut = width // 2
    step = size // ROUNDS
    vmem = pl.BlockSpec(memory_space=pltpu.VMEM)
    anywhere = pl.BlockSpec(memory_space=pl.ANY)
    everyone = jax.ShapeDtypeStruct((8 * size, width), BF)
    shape = lambda n: jax.ShapeDtypeStruct((8, size, n), BF)
    local = jax.ShapeDtypeStruct((size, width), F32)
    dma = pltpu.SemaphoreType.DMA
    half = pltpu.VMEM((2, size, cut), BF)
    quarter = pltpu.VMEM((size, cut), BF)
    ready = pltpu.VMEM((size, width), BF)
    block = lambda n: pltpu.VMEM((2, 4 * step, n), BF)
    return pl.pallas_call(
        functools.partial(ffn_kernel, pieces=pieces),
        in_specs=[anywhere, vmem, vmem, vmem, anywhere, anywhere],
        out_specs=[anywhere] * 5 + [vmem] * 3 + [anywhere],
        input_output_aliases={5: 8},
        out_shape=[
            everyone,
            everyone,
            shape(units),
            shape(2 * units),
            shape(width),
            local,
            local,
            jax.ShapeDtypeStruct((1, width), F32),
            jax.ShapeDtypeStruct(large.shape, BF),
        ],
        scratch_shapes=[
            pltpu.VMEM((width, 3 * units), BF),
            pltpu.VMEM((2, 2, size, width), BF),
            half,
            half,
            quarter,
            quarter,
            pltpu.VMEM((2, 2, 2, step, width), BF),
            ready,
            ready,
            block(width),
            block(width),
            block(units),
            block(2 * units),
            block(width),
            pltpu.VMEM((2, 2, 2, 2, step, width), BF),
            dma((1,)),
            dma((2,)),
            dma((2, ROUNDS)),
            dma((2, 2, 4)),
            dma((3, 2, 4)),
            dma((2 * KINDS, ROUNDS)),
            dma((2 * KINDS, ROUNDS)),
            *piece_scratch(),
        ],
        compiler_params=pltpu.CompilerParams(
            collective_id=8, has_side_effects=True, vmem_limit_bytes=62 * 2**20
        ),
        cost_estimate=QUICK,
        name="feed_forward",
    )(parts.reshape(2, 2, 2, size, width), x, gain.reshape(1, width), d_y, d_y_all, large)


CHUNKS = 2


def weights_kernel(
    small_keep,
    small_give,
    large_keep,
    rows,
    late_rows,
    small,
    large,
    rows_out,
    late_out,
    local,
    send,
    recv,
    *rest,
):
    group, place, shard = (lax.axis_index(name) for name in MESH_AXES)
    low, high = place % 2, place // 2
    on_lo = (group, place + 1 - 2 * low, shard)
    on_hi = (group, place + 2 - 4 * high, shard)
    on_dp = (1 - group, place, shard)
    eighth = small_keep.shape[0]
    step = eighth // CHUNKS
    greet([route_partner(q, e)[0] for q, e in ROUTES[1:]])
    copies = []
    router, late = Router(rows, rows_out, *rest[:3]), Router(late_rows, late_out, *rest[3:6])
    for q, e in ROUTES:
        router.send(q, e)

    def start(src, dst, device):
        at = len(copies)
        copy = pltpu.make_async_remote_copy(
            src_ref=src,
            dst_ref=dst,
            send_sem=send.at[at],
            recv_sem=recv.at[at],
            device_id=device,
            device_id_type=MESH_IDS,
        )
        copy.start()
        copies.append(copy)
        return copy

    def span(index, first, count):
        return pl.ds(pl.multiple_of(index * eighth + first, 16), count)

    own = (group * 2 + high) * 2
    across = (group * 2 + 1 - high) * 2
    from_low = []
    for q in range(CHUNKS):
        src = small_give.at[pl.ds(q * step, step), :]
        from_low.append(start(src, small.at[span(own + low, q * step, step), :], on_lo))
    stay = [
        pltpu.make_async_copy(small_keep, small.at[span(own + low, 0, eighth), :], local.at[0]),
        pltpu.make_async_copy(large_keep, large.at[span(own + low, 0, eighth), :], local.at[1]),
    ]
    for copy in stay:
        copy.start()
    from_high = []
    for q in range(CHUNKS):
        src = small_keep.at[pl.ds(q * step, step), :]
        dst = small.at[span(own + low, q * step, step), :]
        from_high.append(start(src, dst, on_hi))
        start(src, dst, on_dp)
    for q in range(CHUNKS):
        from_low[q].wait_recv()
        at = small.at[span(own + 1 - low, q * step, step), :]
        from_high.append(start(at, at, on_hi))
        start(at, at, on_dp)
    for q in range(2 * CHUNKS):
        half = low if q < CHUNKS else 1 - low
        from_high[q].wait_recv()
        at = small.at[span(across + half, q % CHUNKS * step, step), :]
        start(at, at, on_dp)
        if q == 0:
            for pair in ROUTES:
                late.send(*pair)
    waited = from_low + from_high
    for copy in copies:
        copy.wait_send()
        if not any(copy is item for item in waited):
            copy.wait_recv()
    for copy in stay:
        copy.wait()
    router.finish()
    late.finish()


def call_weights(small_keep, small_give, large_keep, rows, late_rows, parts):
    eighth = small_keep.shape[0]
    anywhere = pl.BlockSpec(memory_space=pl.ANY)
    count = 7 * CHUNKS
    return pl.pallas_call(
        weights_kernel,
        in_specs=[anywhere] * 5,
        out_specs=[anywhere] * 4,
        out_shape=[
            jax.ShapeDtypeStruct((2 * parts * eighth, small_keep.shape[1]), BF),
            jax.ShapeDtypeStruct((2 * parts * eighth, large_keep.shape[1]), BF),
            jax.ShapeDtypeStruct(rows.shape, BF),
            jax.ShapeDtypeStruct(rows.shape, BF),
        ],
        scratch_shapes=[
            pltpu.SemaphoreType.DMA((2,)),
            pltpu.SemaphoreType.DMA((count,)),
            pltpu.SemaphoreType.DMA((count,)),
            *route_scratch(1),
            *route_scratch(1),
        ],
        compiler_params=pltpu.CompilerParams(collective_id=1, has_side_effects=True),
        cost_estimate=QUICK,
        name="weights_first",
    )(small_keep, small_give, large_keep, rows, late_rows)


def head_columns(part, base):
    half = part // 2
    entry = np.arange(part)
    return base + np.where(entry < half, entry, LANES // 2 + entry - half)


def after(value, *events):
    return lax.optimization_barrier((value, *events))[0]


def on_device_paired(
    tokens,
    gain_attn,
    w_query,
    key_weight,
    value_weight,
    w_out,
    gain_mlp,
    w_gate,
    w_up,
    w_down,
    cotangent,
    lengths,
    order_perm,
    block_order,
):
    names = MESH_AXES
    n_dp, n_ctx, n_ten = (lax.axis_size(name) for name in names)
    devices = n_dp * n_ctx * n_ten
    on_core, on_y, on_lo, on_hi, on_dp = 1, 2, n_ten, 2 * n_ten, n_ctx * n_ten
    group = lax.axis_index(DP)
    place = lax.axis_index(CONTEXT)
    shard = lax.axis_index(TENSOR)
    high, low = place // 2, place % 2
    row, core = shard // 2, shard % 2
    groups = n_dp * n_ctx
    my_index = group * n_ctx + place
    rows, width = tokens.shape
    share = rows // groups
    part = share // n_ten
    local = rows // n_ten
    block_rows = rows // MB
    half_rows = block_rows // 2
    pack = block_rows * n_ctx
    n_blocks = block_order.shape[0]
    blocks = n_blocks // 2
    scale = HEAD_SIZE ** (-0.5)
    quarter = width // (2 * n_dp)
    eighth = quarter // 2

    def swap(value, bit):
        return lax.ppermute(value, names, [(i, i ^ bit) for i in range(devices)])

    def pick(flag, yes, no):
        return jnp.where(flag == 1, yes, no)

    def by_low(mine, partner, axis):
        return jnp.concatenate(
            [pick(low, partner, mine), pick(low, mine, partner)], axis=axis
        )

    places = order_perm.reshape(groups, rows)
    source = places // rows
    is_mine = source == my_index
    below = jnp.arange(rows, dtype=jnp.int32)
    ahead = one_hot(1, (below[:, None] <= below[None, :]).astype(jnp.int32))
    all_sources = jnp.arange(groups, dtype=jnp.int32)
    runs = [
        lax.dynamic_index_in_dim(source, group * n_ctx + 2 * high + (low ^ d), 0, keepdims=False)
        for d in range(2)
    ]
    from_each = [run[None, :] == all_sources[:, None] for run in runs]
    flags = jnp.concatenate([is_mine, *from_each], axis=0)
    counted = mm(flags.astype(BF), ahead).astype(jnp.int32) - 1
    rank = counted[:groups]
    row_at = jnp.where(is_mine, places % rows, 0)

    def rows_sent(slots):
        hits = is_mine[:, None, :] & (rank[:, None, :] == slots[None, :, None])
        return jnp.sum(jnp.where(hits, row_at[:, None, :], 0), axis=2)

    send_index = rows_sent(shard * part + jnp.arange(part, dtype=jnp.int32)).reshape(local, 1)
    send_rows = one_hot(send_index, below[None, :])

    def arrivals(d):
        known = counted[(d + 1) * groups : (d + 2) * groups]
        own_rank = jnp.sum(jnp.where(from_each[d], known, 0), axis=0)
        holder = own_rank // part
        device = ((holder % 2) ^ core) * 2 + ((holder // 2) ^ row)
        return (device * groups + runs[d]) * part + own_rank % part

    index = jnp.stack([arrivals(d) for d in range(2)])
    index_col, index_row = index[:, :, None], index[:, None, :]

    def lookup(table, at):
        hits = at[..., None] == jnp.arange(table.shape[0], dtype=jnp.int32)
        return jnp.sum(jnp.where(hits, table, 0), axis=-1)

    slot_of = invert(block_order)
    query = jnp.arange(2 * MB * 2, dtype=jnp.int32)
    run_of, micro_of, half_of = query // (2 * MB), query // 2 % MB, query % 2
    which = lookup(block_order, 2 * (2 * high + (low ^ run_of)) + half_of)
    upper = which // blocks
    item = jnp.arange(blocks, dtype=jnp.int32)
    slot = lookup(slot_of, upper[:, None] * blocks + item)
    where = ((slot // 4) ^ high) * 2 + (((slot // 2) % 2) ^ low)
    starts = ((where * MB + micro_of[:, None]) * 2 + slot % 2) * half_rows
    first = lookup(lengths[:, 0], group * MB + micro_of)
    second = first + lookup(lengths[:, 1], group * MB + micro_of)
    meta = jnp.concatenate([(which % blocks)[:, None], starts], axis=1)
    at = which[:, None] * half_rows + jnp.arange(half_rows, dtype=jnp.int32)
    first, second = first[:, None], second[:, None]
    in_last = at >= second
    q_flag = jnp.where(in_last, 1.0, 0.0).reshape(2, rows, 1)
    k_flag = jnp.where(in_last, 0.0, MASKED).reshape(2, rows, 1)
    at = at - jnp.where(at < first, 0, jnp.where(at < second, first, second))
    position = at.reshape(2, rows)
    hit = index[:, :, None] == jnp.arange(rows, dtype=jnp.int32)[None, None, :]
    position_arrived = jnp.sum(jnp.where(hit, position[:, :, None], 0), axis=1)

    half_head = HEAD_SIZE // 2
    entry_of = np.arange(half_head)
    freq = (THETA ** (-2.0 * entry_of / HEAD_SIZE)).astype(np.float32)
    to_lanes = np.zeros((2, half_head, LANES), np.float32)
    to_lanes[:, entry_of, entry_of + LANES // 2] = 1.0
    to_lanes[0, entry_of, entry_of] = 1.0
    to_lanes[1, entry_of, entry_of] = -1.0

    def tables(pos):
        angle = freq[:, None] * pos.reshape(-1).astype(F32)[None, :]
        return [
            lax.dot_general(
                value,
                jnp.asarray(lanes),
                (((0,), (0,)), ((), ())),
                precision=lax.Precision.HIGHEST,
                preferred_element_type=F32,
            ).reshape(2, rows, LANES)
            for value, lanes in zip((jnp.cos(angle), jnp.sin(angle)), to_lanes, strict=True)
        ]

    cos_arrived, sin_arrived = tables(position_arrived)
    cos_place, sin_place = tables(position)

    q_width, kv_width = GROUP * HEAD_SIZE, HEAD_SIZE
    all_width = q_width + 2 * kv_width
    target = np.concatenate(
        [head_columns(HEAD_SIZE, h * LANES) for h in range(GROUP + 1)]
        + [(GROUP + 1) * LANES + np.arange(HEAD_SIZE)]
    )
    spread_np = np.zeros((all_width, (GROUP + 2) * LANES), np.float32)
    spread_np[np.arange(all_width), target] = 1.0
    spread = jnp.asarray(spread_np, BF)
    out_target = np.concatenate([h * LANES + np.arange(HEAD_SIZE) for h in range(GROUP)])
    out_np = np.zeros((q_width, GROUP * LANES), np.float32)
    out_np[np.arange(q_width), out_target] = 1.0
    out_spread = jnp.asarray(out_np, BF)

    def halves(value):
        size = value.shape[1] // 2
        return pick(low, value[:, size:], value[:, :size]), pick(low, value[:, :size], value[:, size:])

    def together(values):
        keeps, gives = zip(*(halves(value) for value in values), strict=True)
        return list(keeps), list(gives)

    x_send = mm(send_rows, tokens).astype(BF)
    cot_send = mm(send_rows, cotangent).astype(BF)
    w_out_t, w_down_t = w_out.T, w_down.T
    keeps, gives = together([w_query, key_weight, value_weight])
    keep_out, give_out = halves(w_out_t)
    gains = jnp.stack([gain_attn, gain_mlp], axis=1)
    out_at, gain_at = 4 * LANES, 4 * LANES + q_width
    gap = jnp.zeros((eighth, out_at - all_width), BF)
    end = jnp.zeros((eighth, 7 * LANES - gain_at - 2), BF)
    small_keep = jnp.concatenate([*keeps, gap, keep_out, gains, end], axis=1)
    small_give = jnp.concatenate([*gives, gap, give_out, gains, end], axis=1)
    keeps, gives = together([w_gate, w_up, w_down_t])
    small, large, x_low, cot_low = call_weights(
        small_keep,
        small_give,
        jnp.concatenate(keeps, axis=1),
        x_send,
        cot_send,
        2 * n_dp,
    )
    large_give = jnp.concatenate(gives, axis=1)
    w_qkv = small[:, :all_width]
    w_o_t = small[:, out_at:gain_at]
    gain_a = small[:, gain_at].astype(F32)
    gain_m = small[:, gain_at + 1].astype(F32)

    one_all, large = call_tokens(FIRST, 2, None, x_low, large, (0, 1, 2, 3), gain_a)
    large_got = swap(after(large_give, one_all), on_lo)

    w_qkv_wide = mm(w_qkv, spread).astype(BF)
    split = GROUP * LANES
    kv_own = call_sort(
        one_all, w_qkv_wide[:, split:], cos_arrived, sin_arrived, index_col, k_flag, 1
    )
    block_first = (2 * group + high) * quarter
    across_first = (2 * group + 1 - high) * quarter
    large = lax.dynamic_update_slice_in_dim(large, large_got, block_first + (1 - low) * eighth, 0)
    kv_all, dy_all, large = call_tokens(PLAIN, 3, None, cot_low, large, (4,), None, kv_own)
    late_first, late_count = (1 - low) * eighth + eighth // 4, eighth - eighth // 4
    late = lax.dynamic_slice_in_dim(large, block_first + late_first, late_count, 0)
    late = swap(late, on_hi)
    q_sorted = call_sort(
        after(one_all, dy_all), w_qkv_wide[:, :split], cos_arrived, sin_arrived, index_col, q_flag, 2
    )
    o_all = call_forward(meta, q_sorted, kv_all, index_row, out_spread.T, scale)
    o_part = product(o_all, w_o_t, 1)
    o_part, late = lax.optimization_barrier((o_part, late))
    large = lax.dynamic_update_slice_in_dim(large, late, across_first + late_first, 0)
    two_all, dh_all, inner_all, d_both_all, y_part, mid, d_mid, gain_grad_m, unused = call_ffn(
        o_part, x_low, gain_m, cot_low, dy_all, large, (5, 6, 7)
    )
    units = inner_all.shape[2]
    inner_all = inner_all.reshape(2 * rows, units)
    d_both_all = d_both_all.reshape(2 * rows, 2 * units)

    def rows_at(value, index, size):
        return lax.dynamic_slice_in_dim(value, index * size, size, 0)

    def other_dp(total):
        return swap(rows_at(total, 1 - group, 2 * quarter), on_dp)

    def dp_sum(total, came):
        kept = rows_at(total, group, 2 * quarter).astype(F32) + came.astype(F32)
        return rows_at(kept, high, quarter), rows_at(kept, 1 - high, quarter).astype(BF)

    def quad_sum(kept, came):
        kept = kept + came.astype(F32)
        return rows_at(kept, low, eighth), rows_at(kept, 1 - low, eighth).astype(BF)

    y_part = y_part.reshape(8, local, width)
    y_came = swap(y_part[4:], on_core)
    down_part = product(dy_all, inner_all, 2)
    y_came, down_part = lax.optimization_barrier((y_came, down_part))
    y_sum = (y_part[:4].astype(F32) + y_came.astype(F32)).reshape(2, 2, local, width)
    y_sent, y_kept = y_sum[:, 1].astype(BF), y_sum[:, 0]
    y_came = swap(y_sent, on_y)
    down_came = other_dp(down_part)
    gate_part, up_part = product(after(two_all, y_sent), d_both_all, 2, cuts=2)
    d_o = product(after(dh_all, gate_part), w_o_t, 0, lanes=out_spread)
    d_o, down_came = lax.optimization_barrier((d_o, down_came))
    gate_came = other_dp(after(gate_part, down_came))
    down_keep, down_send = dp_sum(down_part, down_came)
    d_o, down_send = lax.optimization_barrier((d_o, down_send))
    down_came = swap(down_send, on_hi)
    dq_all, dkv_own, dkv_sent = call_backward(
        meta,
        q_sorted,
        kv_all,
        d_o,
        index_col,
        index_row,
        cos_place.reshape(2 * rows, LANES),
        sin_place.reshape(2 * rows, LANES),
        scale,
    )

    dkv_got = swap(dkv_sent, on_hi)
    y_came, dkv_own = lax.optimization_barrier((y_came, dkv_own))
    y_pair = y_kept + y_came.astype(F32)
    y_sent = y_pair[1].astype(BF)
    y_came = swap(y_sent, on_lo)
    dh_late, y_sent, down_came = lax.optimization_barrier((dh_all, y_sent, down_came))
    out_part = product(dh_late, o_all, 2)
    gate_came, out_part = lax.optimization_barrier((gate_came, out_part))
    up_came = other_dp(after(up_part, gate_came))
    gate_keep, gate_send = dp_sum(gate_part, gate_came)
    gate_send, y_came, dkv_got = lax.optimization_barrier((gate_send, y_came, dkv_got))
    gate_came = swap(gate_send, on_hi)
    y_local = (mid + y_pair[0] + y_came.astype(F32)).astype(BF)
    d_all = call_unsort(
        dkv_own, dkv_got, cos_place, sin_place, index_row, dq_all, spread.T, scale
    )
    total_part = jnp.concatenate([product(one_all, d_all, 2), out_part], axis=1)
    up_keep, up_send = dp_sum(up_part, after(up_came, d_all))
    d_one_part, total_part, up_send, gate_came = lax.optimization_barrier(
        (product(d_all, w_qkv, 1), total_part, up_send, gate_came)
    )
    x_grad_rows, both_gains, y_rows, *grads = call_tokens(
        LAST,
        7,
        d_one_part,
        x_low,
        None,
        (),
        gain_a,
        d_mid,
        y_local,
        gain_grad_m,
        (up_send, up_keep, total_part),
    )
    x_grad_rows, down_came, gate_came = lax.optimization_barrier(
        (x_grad_rows, down_came, gate_came)
    )
    down_keep, down_give = quad_sum(down_keep, down_came)
    gate_keep, gate_give = quad_sum(gate_keep, gate_came)
    grad_down_t = by_low(down_keep, swap(down_give, on_lo).astype(F32), 1)
    grad_gate = by_low(gate_keep, swap(gate_give, on_lo).astype(F32), 1)
    grad_up = by_low(grads[0], grads[2].astype(F32), 1)
    keep, got = grads[1], grads[3].astype(F32)
    grad_out_t = by_low(keep[:, all_width:], got[:, all_width:], 1)
    qkv_parts = []
    for first, last in ((0, q_width), (q_width, q_width + kv_width), (q_width + kv_width, all_width)):
        qkv_parts.append(by_low(keep[:, first:last], got[:, first:last], 1))
    grad_query, grad_key, grad_value = qkv_parts
    own_gains = lax.dynamic_slice_in_dim(both_gains, my_index * eighth, eighth, 1)

    send_all = rows_sent(jnp.arange(share, dtype=jnp.int32))
    held = [row * 2 + core, (row ^ 1) * 2 + core, row * 2 + (core ^ 1), (row ^ 1) * 2 + (core ^ 1)]
    from_slot = jnp.concatenate(
        [
            lax.dynamic_slice_in_dim(send_all, device * part, part, 1).reshape(local)
            for device in held
        ]
    )
    data_rows = one_hot(below[:, None], from_slot[None, :])
    output = mm(data_rows, y_rows).astype(BF)
    input_grad = mm(data_rows, x_grad_rows).astype(BF)
    return (
        output,
        input_grad,
        own_gains[0],
        grad_query,
        grad_key,
        grad_value,
        grad_out_t.T,
        own_gains[1],
        grad_gate,
        grad_up,
        grad_down_t.T,
    )


def solution(mesh):
    placed = (
        P(TOKEN_AXES, None),
        P(TOKEN_AXES),
        P(TOKEN_AXES, TENSOR),
        P(TOKEN_AXES, TENSOR),
        P(TOKEN_AXES, TENSOR),
        P(TENSOR, TOKEN_AXES),
        P(TOKEN_AXES),
        P(TOKEN_AXES, TENSOR),
        P(TOKEN_AXES, TENSOR),
        P(TENSOR, TOKEN_AXES),
        P(TOKEN_AXES, None),
        P(),
        P(),
        P(),
    )
    paired = tuple(mesh.shape[name] for name in MESH_AXES) == (2, 4, 4)
    return jax.shard_map(
        on_device_paired if paired else on_device,
        mesh=mesh,
        in_specs=placed,
        out_specs=(
            P(TOKEN_AXES, None),
            P(TOKEN_AXES, None),
            P(TOKEN_AXES),
            P(TOKEN_AXES, TENSOR),
            P(TOKEN_AXES, TENSOR),
            P(TOKEN_AXES, TENSOR),
            P(TENSOR, TOKEN_AXES),
            P(TOKEN_AXES),
            P(TOKEN_AXES, TENSOR),
            P(TOKEN_AXES, TENSOR),
            P(TENSOR, TOKEN_AXES),
        ),
        check_vma=False,
    )
```

```python
import functools

import jax
import jax.numpy as jnp
import numpy as np
from jax import lax
from jax.experimental import pallas as pl
from jax.experimental.pallas import tpu as pltpu
from jax.sharding import PartitionSpec as P

HEAD_SIZE = 80
MB = 2


EPS = 1e-05
THETA = 1000000.0
MASKED = -1e30
DP, CONTEXT, TENSOR = "dp", "context", "tensor"
TOKEN_AXES, MESH_AXES = (DP, CONTEXT), (DP, CONTEXT, TENSOR)


def rotate(field, positions, sign):
    half_width = field.shape[-1] // 2
    freq = THETA ** (-2.0 * jnp.arange(half_width, dtype=jnp.float32) / field.shape[-1])
    angle = positions.astype(jnp.float32)[:, None] * freq[None, :]
    cosine = jnp.cos(angle)[:, None, :]
    sine = sign * jnp.sin(angle)[:, None, :]
    first = field[..., :half_width]
    second = field[..., half_width:]
    return jnp.concatenate(
        [first * cosine - second * sine, second * cosine + first * sine], axis=-1
    )


def times_t(left, right):
    return lax.dot_general(
        left, right, (((1,), (1,)), ((), ())), preferred_element_type=jnp.float32
    )


def t_times(left, right):
    return lax.dot_general(
        left, right, (((0,), (0,)), ((), ())), preferred_element_type=jnp.float32
    )


def invert(index):
    count = index.shape[0]
    iota = jnp.arange(count, dtype=jnp.int32)
    return jnp.sum(iota[None, :] * (index[None, :] == iota[:, None]).astype(jnp.int32), axis=1)


def route_plan(order_perm, groups, rows, my_index):
    share = rows // groups
    places = order_perm.reshape(groups, rows)
    source = places // rows
    mine = (source == my_index).astype(jnp.int32)
    rank = jnp.cumsum(mine, axis=1) - 1
    slots = jnp.arange(share, dtype=jnp.int32)
    pick = mine[:, :, None] * (rank[:, :, None] == slots[None, None, :]).astype(jnp.int32)
    send_index = jnp.sum(pick * (places % rows)[:, :, None], axis=1).reshape(rows)
    own = lax.dynamic_index_in_dim(places, my_index, 0, keepdims=False)
    own_source = own // rows
    onehot = (own_source[:, None] == jnp.arange(groups, dtype=jnp.int32)[None, :]).astype(jnp.int32)
    own_rank = jnp.sum((jnp.cumsum(onehot, axis=0) - 1) * onehot, axis=1)
    return (send_index, own_source * share + own_rank)


def pack_places(count, block_rows, half_rows, block_order):
    index = jnp.arange(count, dtype=jnp.int32)
    slot = 2 * (index // block_rows) + index % block_rows // half_rows
    table = (slot[:, None] == jnp.arange(block_order.shape[0], dtype=jnp.int32)[None, :]).astype(
        jnp.int32
    )
    which = jnp.sum(table * block_order[None, :], axis=1)
    return which * half_rows + index % half_rows


def segment_info(places, seq_lengths):
    first = seq_lengths[0]
    second = seq_lengths[0] + seq_lengths[1]
    segment = (places >= first).astype(jnp.int32) + (places >= second).astype(jnp.int32)
    start = jnp.where(segment == 0, 0, jnp.where(segment == 1, first, second))
    return (segment, places - start)


def norm_forward(value_tensor, gain):
    root = lax.rsqrt(jnp.mean(value_tensor * value_tensor, axis=-1, keepdims=True) + EPS)
    return (root, (value_tensor * root * gain).astype(jnp.bfloat16))


def norm_backward(value_tensor, root, gain, grad):
    weighted = grad * gain
    cubed = root * root * root
    d_values = root * weighted - value_tensor * cubed * jnp.mean(
        weighted * value_tensor, axis=-1, keepdims=True
    )
    return (d_values, jnp.sum(grad * value_tensor * root, axis=0))


def key_split(count):
    step = 512
    return (count // step, step)


def block_scores(q_group, key_block, pos_block, seg_block, q_pos, q_seg, scale):
    scores = (
        jnp.einsum("qgrd,kgd->grqk", q_group, key_block, preferred_element_type=jnp.float32) * scale
    )
    allowed = (q_seg[:, None] == seg_block[None, :]) & (pos_block[None, :] <= q_pos[:, None])
    return (jnp.where(allowed, scores, MASKED), allowed)


def key_items(key_tensor, value_tensor, k_pos, k_seg, heads_kv):
    count, step = key_split(key_tensor.shape[0])
    return (
        key_tensor.reshape(count, step, heads_kv, HEAD_SIZE),
        value_tensor.reshape(count, step, heads_kv, HEAD_SIZE),
        k_pos.reshape(count, step),
        k_seg.reshape(count, step),
    )


def attention_forward(q_group, key_tensor, value_tensor, q_pos, q_seg, k_pos, k_seg, scale):
    heads_kv = q_group.shape[1]
    items = key_items(key_tensor, value_tensor, k_pos, k_seg, heads_kv)
    stat_shape = (heads_kv, q_group.shape[2], q_group.shape[0])

    def measure(carry, item):
        top, total = carry
        scores, allowed = block_scores(q_group, item[0], item[2], item[3], q_pos, q_seg, scale)
        new_top = jnp.maximum(top, jnp.max(scores, axis=-1))
        kept = jnp.where(allowed, jnp.exp(scores - new_top[..., None]), 0.0)
        return ((new_top, total * jnp.exp(top - new_top) + jnp.sum(kept, axis=-1)), None)

    start = (jnp.full(stat_shape, MASKED, jnp.float32), jnp.zeros(stat_shape, jnp.float32))
    (top, total), unused = lax.scan(measure, start, items)

    def mix(acc, item):
        scores, allowed = block_scores(q_group, item[0], item[2], item[3], q_pos, q_seg, scale)
        probs = jnp.where(allowed, jnp.exp(scores - top[..., None]) / total[..., None], 0.0).astype(
            jnp.bfloat16
        )
        return (
            acc + jnp.einsum("grqk,kgd->qgrd", probs, item[1], preferred_element_type=jnp.float32),
            None,
        )

    attended, unused = lax.scan(mix, jnp.zeros(q_group.shape, jnp.float32), items)
    return (attended, top, total)


def attention_backward(
    q_group, key_tensor, value_tensor, q_pos, q_seg, k_pos, k_seg, top, total, d_out, delta, scale
):
    heads_kv = q_group.shape[1]
    items = key_items(key_tensor, value_tensor, k_pos, k_seg, heads_kv)
    step = items[2].shape[1]

    def visit(d_query, item):
        scores, allowed = block_scores(q_group, item[0], item[2], item[3], q_pos, q_seg, scale)
        weight = jnp.where(allowed, jnp.exp(scores - top[..., None]) / total[..., None], 0.0)
        d_prob = jnp.einsum("qgrd,kgd->grqk", d_out, item[1], preferred_element_type=jnp.float32)
        d_score = (weight * (d_prob - delta[..., None])).astype(jnp.bfloat16)
        d_query = d_query + jnp.einsum(
            "grqk,kgd->qgrd", d_score, item[0], preferred_element_type=jnp.float32
        )
        d_key = (
            jnp.einsum("grqk,qgrd->kgd", d_score, q_group, preferred_element_type=jnp.float32)
            * scale
        )
        d_value = jnp.einsum(
            "grqk,qgrd->kgd", weight.astype(jnp.bfloat16), d_out, preferred_element_type=jnp.float32
        )
        return (d_query, (d_key.reshape(step, -1), d_value.reshape(step, -1)))

    d_query, (d_keys, d_values) = lax.scan(visit, jnp.zeros(q_group.shape, jnp.float32), items)
    return (
        d_query * scale,
        d_keys.reshape(key_tensor.shape[0], -1),
        d_values.reshape(key_tensor.shape[0], -1),
    )


def fetch_attention(gain_attn, w_query, key_weight, value_weight, w_out):
    return (
        lax.all_gather(gain_attn, TOKEN_AXES, axis=0, tiled=True),
        lax.all_gather(w_query, TOKEN_AXES, axis=0, tiled=True),
        lax.all_gather(key_weight, TOKEN_AXES, axis=0, tiled=True),
        lax.all_gather(value_weight, TOKEN_AXES, axis=0, tiled=True),
        lax.all_gather(w_out, TOKEN_AXES, axis=1, tiled=True),
    )


def fetch_mlp(gain_mlp, w_gate, w_up, w_down):
    return (
        lax.all_gather(gain_mlp, TOKEN_AXES, axis=0, tiled=True),
        lax.all_gather(w_gate, TOKEN_AXES, axis=0, tiled=True),
        lax.all_gather(w_up, TOKEN_AXES, axis=0, tiled=True),
        lax.all_gather(w_down, TOKEN_AXES, axis=1, tiled=True),
    )


def head_sum(partial_sum):
    return lax.psum(partial_sum.astype(jnp.bfloat16), TENSOR).astype(jnp.float32)


def on_device(
    tokens,
    gain_attn,
    w_query,
    key_weight,
    value_weight,
    w_out,
    gain_mlp,
    w_gate,
    w_up,
    w_down,
    cotangent,
    lengths,
    order_perm,
    block_order,
):
    devices_ctx = lax.axis_size(CONTEXT)
    groups = lax.axis_size(DP) * devices_ctx
    group_id = lax.axis_index(DP)
    place = lax.axis_index(CONTEXT)
    my_index = group_id * devices_ctx + place
    rows = tokens.shape[0]
    width = tokens.shape[1]
    block_rows = rows // MB
    half_rows = block_rows // 2
    share = rows // groups
    scale = HEAD_SIZE ** (-0.5)
    send_index, recv_index = route_plan(order_perm, groups, rows, my_index)
    arrived = (
        lax.all_to_all(
            tokens[send_index].reshape(groups, share, width),
            TOKEN_AXES,
            split_axis=0,
            concat_axis=0,
            tiled=True,
        ),
        lax.all_to_all(
            cotangent[send_index].reshape(groups, share, width),
            TOKEN_AXES,
            split_axis=0,
            concat_axis=0,
            tiled=True,
        ),
    )
    seq_tokens = arrived[0].reshape(rows, width)[recv_index]
    seq_cot = arrived[1].reshape(rows, width)[recv_index]
    whole_place = pack_places(block_rows * devices_ctx, block_rows, half_rows, block_order)
    acc_gain_a = jnp.zeros((width,), jnp.float32)
    acc_query = jnp.zeros((width, w_query.shape[1]), jnp.float32)
    acc_key = jnp.zeros((width, key_weight.shape[1]), jnp.float32)
    acc_value = jnp.zeros((width, value_weight.shape[1]), jnp.float32)
    acc_out = jnp.zeros((w_out.shape[0], width), jnp.float32)
    acc_gain_m = jnp.zeros((width,), jnp.float32)
    acc_gate = jnp.zeros((width, w_gate.shape[1]), jnp.float32)
    acc_up = jnp.zeros((width, w_up.shape[1]), jnp.float32)
    acc_down = jnp.zeros((w_down.shape[0], width), jnp.float32)
    outputs = []
    input_grads = []
    for micro in range(MB):
        seq_lengths = lax.dynamic_index_in_dim(lengths, group_id * MB + micro, 0, keepdims=False)
        key_seg, key_pos = segment_info(whole_place, seq_lengths)
        q_seg = lax.dynamic_slice_in_dim(key_seg, place * block_rows, block_rows)
        q_pos = lax.dynamic_slice_in_dim(key_pos, place * block_rows, block_rows)
        inputs_f = seq_tokens[micro * block_rows : (micro + 1) * block_rows].astype(jnp.float32)
        d_y = seq_cot[micro * block_rows : (micro + 1) * block_rows]
        attn_now = fetch_attention(gain_attn, w_query, key_weight, value_weight, w_out)
        gain_a, w_q, w_k, w_v, w_o = attn_now
        root_a, normed_one = norm_forward(inputs_f, gain_a.astype(jnp.float32))
        q_lin = jnp.dot(normed_one, w_q, preferred_element_type=jnp.float32)
        k_lin = jnp.dot(normed_one, w_k, preferred_element_type=jnp.float32)
        v_lin = jnp.dot(normed_one, w_v, preferred_element_type=jnp.float32)
        heads_kv = k_lin.shape[1] // HEAD_SIZE
        q_group = rotate(q_lin.reshape(block_rows, -1, HEAD_SIZE), q_pos, 1.0).astype(jnp.bfloat16)
        q_group = q_group.reshape(block_rows, heads_kv, -1, HEAD_SIZE)
        k_in = (
            rotate(k_lin.reshape(block_rows, heads_kv, HEAD_SIZE), q_pos, 1.0)
            .astype(jnp.bfloat16)
            .reshape(block_rows, -1)
        )
        v_in = v_lin.astype(jnp.bfloat16)
        key_tensor, value_tensor = (
            lax.all_gather(k_in, CONTEXT, axis=0, tiled=True),
            lax.all_gather(v_in, CONTEXT, axis=0, tiled=True),
        )
        attended, top, total = attention_forward(
            q_group, key_tensor, value_tensor, q_pos, q_seg, key_pos, key_seg, scale
        )
        o_in = attended.reshape(block_rows, -1).astype(jnp.bfloat16)
        mid_state = inputs_f + head_sum(jnp.dot(o_in, w_o, preferred_element_type=jnp.float32))
        mlp_now = fetch_mlp(gain_mlp, w_gate, w_up, w_down)
        gain_m, w_g, w_u, w_d = mlp_now
        root_m, normed_two = norm_forward(mid_state, gain_m.astype(jnp.float32))
        gate = jnp.dot(normed_two, w_g, preferred_element_type=jnp.float32)
        up_proj = jnp.dot(normed_two, w_u, preferred_element_type=jnp.float32)
        sigma = jax.nn.sigmoid(gate)
        silu_gate = gate * sigma
        inner = (silu_gate * up_proj).astype(jnp.bfloat16)
        result = mid_state + head_sum(jnp.dot(inner, w_d, preferred_element_type=jnp.float32))
        outputs.append(result.astype(jnp.bfloat16))
        mlp_back = fetch_mlp(gain_mlp, w_gate, w_up, w_down)
        gain_m, w_g, w_u, w_d = mlp_back
        d_inner = times_t(d_y, w_d)
        acc_down = acc_down + t_times(inner, d_y)
        d_gate = (d_inner * up_proj * sigma * (1.0 + gate * (1.0 - sigma))).astype(jnp.bfloat16)
        d_up = (d_inner * silu_gate).astype(jnp.bfloat16)
        d_two = head_sum(times_t(d_gate, w_g) + times_t(d_up, w_u))
        acc_gate = acc_gate + t_times(normed_two, d_gate)
        acc_up = acc_up + t_times(normed_two, d_up)
        d_mid, gain_grad_m = norm_backward(mid_state, root_m, gain_m.astype(jnp.float32), d_two)
        acc_gain_m = acc_gain_m + gain_grad_m
        d_mid = d_y.astype(jnp.float32) + d_mid
        d_mid_low = d_mid.astype(jnp.bfloat16)
        attn_back = fetch_attention(gain_attn, w_query, key_weight, value_weight, w_out)
        gain_a, w_q, w_k, w_v, w_o = attn_back
        acc_out = acc_out + t_times(o_in, d_mid_low)
        d_out = times_t(d_mid_low, w_o).astype(jnp.bfloat16).reshape(q_group.shape)
        delta = jnp.sum(d_out.astype(jnp.float32) * attended, axis=-1).transpose(1, 2, 0)
        d_query, d_keys, d_values = attention_backward(
            q_group,
            key_tensor,
            value_tensor,
            q_pos,
            q_seg,
            key_pos,
            key_seg,
            top,
            total,
            d_out,
            delta,
            scale,
        )
        own_keys, own_values = (
            lax.psum_scatter(
                d_keys.astype(jnp.bfloat16), CONTEXT, scatter_dimension=0, tiled=True
            ).astype(jnp.float32),
            lax.psum_scatter(
                d_values.astype(jnp.bfloat16), CONTEXT, scatter_dimension=0, tiled=True
            ).astype(jnp.float32),
        )
        d_q_low = (
            rotate(d_query.reshape(block_rows, -1, HEAD_SIZE), q_pos, -1.0)
            .astype(jnp.bfloat16)
            .reshape(block_rows, -1)
        )
        d_k_low = (
            rotate(own_keys.reshape(block_rows, -1, HEAD_SIZE), q_pos, -1.0)
            .astype(jnp.bfloat16)
            .reshape(block_rows, -1)
        )
        d_v_low = own_values.astype(jnp.bfloat16)
        d_one = head_sum(times_t(d_q_low, w_q) + times_t(d_k_low, w_k) + times_t(d_v_low, w_v))
        acc_query = acc_query + t_times(normed_one, d_q_low)
        acc_key = acc_key + t_times(normed_one, d_k_low)
        acc_value = acc_value + t_times(normed_one, d_v_low)
        d_inputs, gain_grad_a = norm_backward(inputs_f, root_a, gain_a.astype(jnp.float32), d_one)
        acc_gain_a = acc_gain_a + gain_grad_a
        input_grads.append((d_mid + d_inputs).astype(jnp.bfloat16))
    grads_attn = (
        lax.psum_scatter(
            acc_gain_a.astype(jnp.bfloat16), TOKEN_AXES, scatter_dimension=0, tiled=True
        ).astype(jnp.float32),
        lax.psum_scatter(
            acc_query.astype(jnp.bfloat16), TOKEN_AXES, scatter_dimension=0, tiled=True
        ).astype(jnp.float32),
        lax.psum_scatter(
            acc_key.astype(jnp.bfloat16), TOKEN_AXES, scatter_dimension=0, tiled=True
        ).astype(jnp.float32),
        lax.psum_scatter(
            acc_value.astype(jnp.bfloat16), TOKEN_AXES, scatter_dimension=0, tiled=True
        ).astype(jnp.float32),
        lax.psum_scatter(
            acc_out.astype(jnp.bfloat16), TOKEN_AXES, scatter_dimension=1, tiled=True
        ).astype(jnp.float32),
    )
    grads_mlp = (
        lax.psum_scatter(
            acc_gain_m.astype(jnp.bfloat16), TOKEN_AXES, scatter_dimension=0, tiled=True
        ).astype(jnp.float32),
        lax.psum_scatter(
            acc_gate.astype(jnp.bfloat16), TOKEN_AXES, scatter_dimension=0, tiled=True
        ).astype(jnp.float32),
        lax.psum_scatter(
            acc_up.astype(jnp.bfloat16), TOKEN_AXES, scatter_dimension=0, tiled=True
        ).astype(jnp.float32),
        lax.psum_scatter(
            acc_down.astype(jnp.bfloat16), TOKEN_AXES, scatter_dimension=1, tiled=True
        ).astype(jnp.float32),
    )
    seq_out = jnp.concatenate(outputs, axis=0)
    seq_grad = jnp.concatenate(input_grads, axis=0)
    back_index = invert(recv_index)
    returned = (
        lax.all_to_all(
            seq_out[back_index].reshape(groups, share, width),
            TOKEN_AXES,
            split_axis=0,
            concat_axis=0,
            tiled=True,
        ),
        lax.all_to_all(
            seq_grad[back_index].reshape(groups, share, width),
            TOKEN_AXES,
            split_axis=0,
            concat_axis=0,
            tiled=True,
        ),
    )
    data_index = invert(send_index)
    output = returned[0].reshape(rows, width)[data_index]
    input_grad = returned[1].reshape(rows, width)[data_index]
    return (
        output,
        input_grad,
        grads_attn[0],
        grads_attn[1],
        grads_attn[2],
        grads_attn[3],
        grads_attn[4],
        grads_mlp[0],
        grads_mlp[1],
        grads_mlp[2],
        grads_mlp[3],
    )


BF = jnp.bfloat16
F32 = jnp.float32
TILE = 256
LANES = 128
GROUP = 4
QUICK = pl.CostEstimate(flops=10**6, bytes_accessed=10**5, transcendentals=0)


def mm(left, right):
    return jnp.dot(left, right, preferred_element_type=F32)


def one_hot(rows, columns):
    return jnp.where(rows == columns, 1.0, 0.0).astype(BF)


def turn(u, cosine, sine):
    return u * cosine + pltpu.roll(u, LANES // 2, 1) * sine


def place_rows(index_col_ref, count):
    column = index_col_ref[0]
    lanes = lax.broadcasted_iota(jnp.int32, (column.shape[0], count), 1)
    return one_hot(lanes, column)


def arrival_rows(index_row_ref, count):
    row = index_row_ref[0]
    rows = lax.broadcasted_iota(jnp.int32, (count, row.shape[1]), 0)
    return one_hot(rows, row)


FLAG = HEAD_SIZE // 2


def flagged(value, flag):
    lanes = lax.broadcasted_iota(jnp.int32, value.shape, 1)
    return jnp.where(lanes % LANES == FLAG, flag, value)


def sort_kernel(mine, other, weight, cosine, sine, index_col, flag, out, picks, *, turned):
    @pl.when(pl.program_id(1) == 0)
    def _():
        picks[...] = place_rows(index_col, picks.shape[1])

    u = jnp.concatenate([mm(mine[...], weight[...]), mm(other[...], weight[...])], axis=0)
    cos_t, sin_t = cosine[0], sine[0]
    parts = [turn(u[:, :LANES], cos_t, sin_t), u[:, LANES:]]
    if turned == 2:
        parts[1] = turn(parts[1], cos_t, sin_t)
    moved = mm(picks[...], jnp.concatenate(parts, axis=1).astype(BF))
    if turned == 2:
        out[...] = flagged(moved, flag[0]).astype(BF)
    else:
        out[:, :LANES] = flagged(moved[:, :LANES], flag[0]).astype(BF)
        out[:, LANES:] = moved[:, LANES:].astype(BF)


def causal_bias():
    rows = lax.broadcasted_iota(jnp.int32, (TILE, TILE), 0)
    lanes = lax.broadcasted_iota(jnp.int32, (TILE, TILE), 1)
    return jnp.where(lanes <= rows, 0.0, MASKED)


def probabilities(q_head, keys, bias, scale):
    scores = times_t(q_head, keys)
    last = scores[:, -TILE:] + bias
    scores = jnp.concatenate([scores[:, :-TILE], last], axis=1) if keys.shape[0] > TILE else last
    top = jnp.max(scores, axis=1, keepdims=True)
    raised = jnp.exp2((scores - top) * (scale * 1.4426950408889634))
    return raised * (1.0 / jnp.sum(raised, axis=1, keepdims=True))


def fetch_keys(meta, block, kv, keys, values, count):
    for item in range(count):
        start = pl.multiple_of(meta[block, 1 + item], TILE)
        rows = pl.ds(item * TILE, TILE)
        keys[rows, :] = kv[pl.ds(start, TILE), :LANES]
        values[rows, :] = kv[pl.ds(start, TILE), LANES:]


def head_of(index):
    return slice(index * LANES, (index + 1) * LANES)


def forward_kernel(
    meta, q, kv, index_row, unpad, out, total, bias, keys, values, *, scale, blocks, per_run
):
    block = pl.program_id(0)
    part = lax.rem(block, per_run)
    run_rows = total.shape[0]

    @pl.when(block == 0)
    def _():
        bias[...] = causal_bias()

    def attend(count):
        fetch_keys(meta, block, kv, keys, values, count)
        size = count * TILE
        mixed = []
        for head in range(GROUP):
            probs = probabilities(q[:, head_of(head)], keys[:size, :], bias[...], scale)
            mixed.append(mm(probs.astype(BF), values[:size, :]).astype(BF))
        moved = mm(arrival_rows(index_row, run_rows), jnp.concatenate(mixed, axis=1))

        @pl.when(part == 0)
        def _():
            total[...] = moved

        @pl.when(part > 0)
        def _():
            total[...] += moved

    for count in range(1, blocks + 1):
        pl.when(meta[block, 0] == count - 1)(functools.partial(attend, count))

    @pl.when(part == per_run - 1)
    def _():
        packed = mm(total[...].astype(BF), unpad[...]).astype(BF)
        half = run_rows // 2
        first = pl.multiple_of(block // per_run * half, TILE)
        out[pl.ds(first, half), :] = packed[:half]
        out[pl.ds(2 * half + first, half), :] = packed[half:]


def backward_kernel(
    meta,
    q,
    kv,
    d_mine,
    d_other,
    index_col,
    index_row,
    cosine,
    sine,
    q_grad,
    own,
    sent,
    total,
    bias,
    keys,
    values,
    probs_all,
    scores_all,
    keys_grad,
    *,
    scale,
    blocks,
    per_run,
):
    block = pl.program_id(0)
    part = lax.rem(block, per_run)
    run_rows = total.shape[0]
    half = run_rows // 2

    @pl.when(block == 0)
    def _():
        keys_grad[...] = jnp.zeros_like(keys_grad)
        bias[...] = causal_bias()

    def attend(count):
        fetch_keys(meta, block, kv, keys, values, count)
        size = count * TILE
        places = place_rows(index_col, run_rows)
        d_out = mm(places[:, :half], d_mine[...]) + mm(places[:, half:], d_other[...])
        d_out = d_out.astype(BF)
        turned = []
        for head in range(GROUP):
            rows = pl.ds(head * TILE, TILE)
            probs = probabilities(q[:, head_of(head)], keys[:size, :], bias[...], scale)
            probs_all[rows, :size] = probs.astype(BF)
            d_probs = times_t(d_out[:, head_of(head)], values[:size, :])
            delta = jnp.sum(probs * d_probs, axis=1, keepdims=True)
            d_score = (probs * (d_probs - delta)).astype(BF)
            scores_all[rows, :size] = d_score
            d_query = flagged(mm(d_score, keys[:size, :]) * scale, 0.0)
            turned.append(turn(d_query, cosine[...], -sine[...]).astype(BF))
        heads = [head_of(head) for head in range(GROUP)]
        q_all = jnp.concatenate([q[:, at] for at in heads], axis=0)
        d_all = jnp.concatenate([d_out[:, at] for at in heads], axis=0)
        d_keys = t_times(scores_all[:, :size], q_all)
        d_values = t_times(probs_all[:, :size], d_all)
        for item in range(count):
            rows = pl.ds(pl.multiple_of(meta[block, 1 + item], TILE), TILE)
            keys_grad[rows, :LANES] += d_keys[item * TILE : (item + 1) * TILE]
            keys_grad[rows, LANES:] += d_values[item * TILE : (item + 1) * TILE]
        moved = mm(arrival_rows(index_row, run_rows), jnp.concatenate(turned, axis=1))

        @pl.when(part == 0)
        def _():
            total[...] = moved

        @pl.when(part > 0)
        def _():
            total[...] += moved

    for count in range(1, blocks + 1):
        pl.when(meta[block, 0] == count - 1)(functools.partial(attend, count))

    @pl.when(part == per_run - 1)
    def _():
        first = pl.multiple_of(block // per_run * half, TILE)
        q_grad[pl.ds(first, half), :] = total[:half].astype(BF)
        q_grad[pl.ds(2 * half + first, half), :] = total[half:].astype(BF)

    @pl.when(block == pl.num_programs(0) - 1)
    def _():
        count = own.shape[0]
        own[...] = keys_grad[:count]
        sent[...] = keys_grad[count:].astype(BF)


def unsort_kernel(own, got, cosine, sine, index_row, q_mine, q_other, unpad, out, *, scale):
    both = own[...] + got[...].astype(F32)
    d_keys = turn(both[:, :LANES] * scale, cosine[0], -sine[0])
    low = jnp.concatenate([d_keys, both[:, LANES:]], axis=1).astype(BF)
    moved = mm(arrival_rows(index_row, low.shape[0]), low).astype(BF)
    half = moved.shape[0] // 2
    split = q_mine.shape[1]
    first = pl.multiple_of(pl.program_id(0) * half, TILE)
    for rows, d_query, at in (
        (moved[:half], q_mine, first),
        (moved[half:], q_other, 2 * half + first),
    ):
        packed = mm(d_query[...], unpad[:split]) + mm(rows, unpad[split:])
        out[pl.ds(at, half), :] = packed.astype(BF)


def resident(shape):
    return pl.BlockSpec(shape, lambda *unused: (0,) * len(shape))


def call_sort(tokens, weight, cosine, sine, index_col, flag, turned):
    count, width = tokens.shape
    run_rows = count // 2
    half = run_rows // 2
    wide = 2 * LANES
    steps = weight.shape[1] // wide
    table = pl.BlockSpec((1, run_rows, LANES), lambda d, g: (d, 0, 0))
    column = pl.BlockSpec((1, run_rows, 1), lambda d, g: (d, 0, 0))
    return pl.pallas_call(
        functools.partial(sort_kernel, turned=turned),
        grid=(2, steps),
        in_specs=[
            pl.BlockSpec((half, width), lambda d, g: (d, 0)),
            pl.BlockSpec((half, width), lambda d, g: (2 + d, 0)),
            pl.BlockSpec((width, wide), lambda d, g: (0, g)),
            table,
            table,
            column,
            column,
        ],
        out_specs=pl.BlockSpec((run_rows, wide), lambda d, g: (d, g)),
        out_shape=jax.ShapeDtypeStruct((count, weight.shape[1]), BF),
        scratch_shapes=[pltpu.VMEM((run_rows, run_rows), BF)],
        compiler_params=pltpu.CompilerParams(vmem_limit_bytes=48 * 2**20),
        cost_estimate=QUICK,
        name="sort_tokens",
    )(tokens, tokens, weight, cosine, sine, index_col, flag)


def call_forward(meta, q, kv, index_row, unpad, scale):
    tokens = q.shape[0]
    run_rows = tokens // 2
    per_run = run_rows // TILE
    blocks = meta.shape[1] - 1
    body = functools.partial(forward_kernel, scale=scale, blocks=blocks, per_run=per_run)
    out = jax.ShapeDtypeStruct((tokens, unpad.shape[1]), BF)
    return pl.pallas_call(
        body,
        grid=(2 * per_run,),
        in_specs=[
            pl.BlockSpec(memory_space=pltpu.SMEM),
            pl.BlockSpec((TILE, GROUP * LANES), lambda b: (b, 0)),
            resident(kv.shape),
            pl.BlockSpec((1, 1, TILE), lambda b: (b // per_run, 0, b % per_run)),
            resident(unpad.shape),
        ],
        out_specs=resident(out.shape),
        out_shape=out,
        scratch_shapes=[
            pltpu.VMEM((run_rows, GROUP * LANES), F32),
            pltpu.VMEM((TILE, TILE), F32),
            pltpu.VMEM((blocks * TILE, LANES), BF),
            pltpu.VMEM((blocks * TILE, LANES), BF),
        ],
        compiler_params=pltpu.CompilerParams(vmem_limit_bytes=48 * 2**20),
        cost_estimate=QUICK,
        name="attention_forward",
    )(meta, q, kv, index_row, unpad)


def call_backward(meta, q, kv, d_out, index_col, index_row, cosine, sine, scale):
    tokens = q.shape[0]
    run_rows = tokens // 2
    per_run = run_rows // TILE
    blocks = meta.shape[1] - 1
    body = functools.partial(backward_kernel, scale=scale, blocks=blocks, per_run=per_run)
    run_half = run_rows // 2
    shape = (tokens, 2 * LANES)
    table = pl.BlockSpec((TILE, LANES), lambda b: (b, 0))
    return pl.pallas_call(
        body,
        grid=(2 * per_run,),
        in_specs=[
            pl.BlockSpec(memory_space=pltpu.SMEM),
            pl.BlockSpec((TILE, GROUP * LANES), lambda b: (b, 0)),
            resident(kv.shape),
            pl.BlockSpec((run_half, GROUP * LANES), lambda b: (b // per_run, 0)),
            pl.BlockSpec((run_half, GROUP * LANES), lambda b: (2 + b // per_run, 0)),
            pl.BlockSpec((1, TILE, 1), lambda b: (b // per_run, b % per_run, 0)),
            pl.BlockSpec((1, 1, TILE), lambda b: (b // per_run, 0, b % per_run)),
            table,
            table,
        ],
        out_specs=[resident(q.shape), resident(shape), resident(shape)],
        out_shape=[
            jax.ShapeDtypeStruct(q.shape, BF),
            jax.ShapeDtypeStruct(shape, F32),
            jax.ShapeDtypeStruct(shape, BF),
        ],
        scratch_shapes=[
            pltpu.VMEM((run_rows, GROUP * LANES), F32),
            pltpu.VMEM((TILE, TILE), F32),
            pltpu.VMEM((blocks * TILE, LANES), BF),
            pltpu.VMEM((blocks * TILE, LANES), BF),
            pltpu.VMEM((GROUP * TILE, blocks * TILE), BF),
            pltpu.VMEM((GROUP * TILE, blocks * TILE), BF),
            pltpu.VMEM((kv.shape[0], 2 * LANES), F32),
        ],
        compiler_params=pltpu.CompilerParams(vmem_limit_bytes=56 * 2**20),
        cost_estimate=QUICK,
        name="attention_backward",
    )(meta, q, kv, d_out, d_out, index_col, index_row, cosine, sine)


def call_unsort(own, got, cosine, sine, index_row, q_grad, unpad, scale):
    tokens, wide = own.shape
    run_rows = tokens // 2
    half = run_rows // 2
    table = pl.BlockSpec((1, run_rows, LANES), lambda d: (d, 0, 0))
    out = jax.ShapeDtypeStruct((tokens, unpad.shape[1]), BF)
    return pl.pallas_call(
        functools.partial(unsort_kernel, scale=scale),
        grid=(2,),
        in_specs=[
            pl.BlockSpec((run_rows, wide), lambda d: (d, 0)),
            pl.BlockSpec((run_rows, wide), lambda d: (d, 0)),
            table,
            table,
            pl.BlockSpec((1, 1, run_rows), lambda d: (d, 0, 0)),
            pl.BlockSpec((half, q_grad.shape[1]), lambda d: (d, 0)),
            pl.BlockSpec((half, q_grad.shape[1]), lambda d: (2 + d, 0)),
            resident(unpad.shape),
        ],
        out_specs=resident(out.shape),
        out_shape=out,
        compiler_params=pltpu.CompilerParams(vmem_limit_bytes=40 * 2**20),
        cost_estimate=QUICK,
        name="unsort_tokens",
    )(own, got, cosine, sine, index_row, q_grad, q_grad, unpad)


def product_kernel(left, right, *outs, form, spread):
    contract = ((1,), (0,)) if form == 0 else ((1,), (1,)) if form == 1 else ((0,), (0,))
    value = lax.dot_general(
        left[...], right[...], (contract, ((), ())), preferred_element_type=F32
    ).astype(BF)
    if spread:
        outs[0][...] = mm(value, outs[-1][...]).astype(BF)
        return
    first = 0
    for out in outs:
        out[...] = value[:, first : first + out.shape[1]]
        first += out.shape[1]


def spread_kernel(left, right, lanes, out, *, form):
    product_kernel(left, right, out, lanes, form=form, spread=True)


def product(left, right, form, cuts=1, lanes=None):
    block = 2 * TILE
    count = left.shape[1 if form == 2 else 0]
    columns = right.shape[0 if form == 1 else 1]
    whole = lambda value: pl.BlockSpec(value.shape, lambda i: (0, 0))
    if form == 2:
        left_spec = pl.BlockSpec((left.shape[0], block), lambda i: (0, i))
    else:
        left_spec = pl.BlockSpec((block, left.shape[1]), lambda i: (i, 0))
    operands, in_specs = [left, right], [left_spec, whole(right)]
    body = functools.partial(product_kernel, form=form, spread=False)
    if lanes is not None:
        operands.append(lanes)
        in_specs.append(whole(lanes))
        body = functools.partial(spread_kernel, form=form)
        columns = lanes.shape[1]
    width = columns // cuts
    outs = pl.pallas_call(
        body,
        grid=(count // block,),
        in_specs=in_specs,
        out_specs=[pl.BlockSpec((block, width), lambda i: (i, 0))] * cuts,
        out_shape=[jax.ShapeDtypeStruct((count, width), BF)] * cuts,
        compiler_params=pltpu.CompilerParams(vmem_limit_bytes=48 * 2**20),
        cost_estimate=QUICK,
        name="product",
    )(*operands)
    return outs if cuts > 1 else outs[0]


def pick_kernel(index, first, second, first_out, second_out, *, by_column):
    count = first.shape[0]
    if by_column:
        lanes = lax.broadcasted_iota(jnp.int32, (first_out.shape[0], count), 1)
        hits = one_hot(lanes, index[...])
    else:
        rows = lax.broadcasted_iota(jnp.int32, (first_out.shape[0], count), 0)
        hits = one_hot(rows + pl.program_id(0) * first_out.shape[0], index[...])
    first_out[...] = mm(hits, first[...]).astype(BF)
    second_out[...] = mm(hits, second[...]).astype(BF)


def pick_rows(index, first, second, by_column):
    count, width = first.shape
    total = index.shape[0 if by_column else 1]
    block = min(total, TILE)
    whole = pl.BlockSpec((count, width), lambda i: (0, 0))
    if by_column:
        index_spec = pl.BlockSpec((block, 1), lambda i: (i, 0))
    else:
        index_spec = pl.BlockSpec((1, total), lambda i: (0, 0))
    out = jax.ShapeDtypeStruct((total, width), BF)
    return pl.pallas_call(
        functools.partial(pick_kernel, by_column=by_column),
        grid=(total // block,),
        in_specs=[index_spec, whole, whole],
        out_specs=[pl.BlockSpec((block, width), lambda i: (i, 0))] * 2,
        out_shape=[out, out],
        compiler_params=pltpu.CompilerParams(vmem_limit_bytes=48 * 2**20),
        cost_estimate=QUICK,
        name="pick_rows",
    )(index, first, second)


ROUNDS = 4
FIRST, MIDDLE, BACK, LAST, PLAIN, SUM = range(6)
KINDS = 13
CORE, RY, RL, SL, SY, GY, GL, GC, FL, FY, CY, CL, CC = range(KINDS)
MESH_IDS = pl.DeviceIdType.MESH


def partners():
    group, place, shard = (lax.axis_index(name) for name in MESH_AXES)
    return (
        (group, place, shard + 2 - 4 * (shard // 2)),
        (group, place + 1 - 2 * (place % 2), shard),
        (group, place, shard + 1 - 2 * (shard % 2)),
    )


def route_partner(q, e):
    group, place, shard = (lax.axis_index(name) for name in MESH_AXES)
    high, low = place // 2, place % 2
    group = 1 - group if q // 2 else group
    high = 1 - high if q % 2 else high
    low = 1 - low if e else low
    return (group, 2 * high + low, shard), 4 * group + 2 * high + low


ROUTES = [(q, e) for q in range(4) for e in range(2)]


class Router:
    def __init__(self, src, dst, send_sem, recv_sem, local_sem, spread=False):
        self.src, self.dst, self.copies, self.spread = src, dst, {}, spread
        self.send_sem, self.recv_sem, self.local_sem = send_sem, recv_sem, local_sem
        self.size = src.shape[0]
        self.share = self.size // len(ROUTES)

    def rows(self, index, slot=0):
        return pl.ds(pl.multiple_of(slot * self.size + index * self.share, 16), self.share)

    def start(self, what, q, e, src, dst, device):
        at = what * len(ROUTES) + 2 * q + e
        copy = pltpu.make_async_remote_copy(
            src_ref=src,
            dst_ref=dst,
            send_sem=self.send_sem.at[at],
            recv_sem=self.recv_sem.at[at],
            device_id=device,
            device_id_type=MESH_IDS,
        )
        copy.start()
        self.copies[what, q, e] = copy

    def send(self, q, e):
        device, index = route_partner(q, e)
        own = route_partner(0, 0)[1]
        if (q, e) == (0, 0):
            copy = pltpu.make_async_copy(
                self.src.at[self.rows(own), :], self.dst.at[self.rows(own), :], self.local_sem
            )
            copy.start()
            self.copies[0, 0, 0] = copy
        else:
            self.start(
                0, q, e, self.src.at[self.rows(index), :], self.dst.at[self.rows(own), :], device
            )

    def arrived(self, what, q, e):
        copy = self.copies[what, q, e]
        if (what, q, e) == (0, 0, 0):
            copy.wait()
        else:
            copy.wait_recv()

    def pass_on(self, q, e):
        on_y, unused, on_core = partners()
        index = route_partner(q, e)[1]
        self.arrived(0, q, e)
        here = self.dst.at[self.rows(index), :]
        self.start(1, q, e, here, self.dst.at[self.rows(index, 1), :], on_y)
        self.start(2, q, e, here, self.dst.at[self.rows(index, 2), :], on_core)

    def pass_corner(self, q, e):
        on_core = partners()[2]
        index = route_partner(q, e)[1]
        self.arrived(1, q, e)
        here = self.dst.at[self.rows(index, 1), :]
        self.start(3, q, e, here, self.dst.at[self.rows(index, 3), :], on_core)

    def finish(self):
        for (what, q, e), copy in self.copies.items():
            if (what, q, e) != (0, 0, 0):
                copy.wait_send()
            if what in (2, 3) or not self.spread:
                self.arrived(what, q, e)


PIECES = 8


class Pieces:
    def __init__(self, buffer, send_sem, recv_sem):
        self.buffer, self.send_sem, self.recv_sem = buffer, send_sem, recv_sem
        self.used, self.near = [], []
        self.quarter = buffer.shape[0] // 4
        self.step = self.quarter // PIECES
        self.on_hi = route_partner(1, 0)[0]
        self.on_dp = route_partner(2, 0)[0]

    def copy(self, what, piece):
        group, place = lax.axis_index(DP), lax.axis_index(CONTEXT)
        low, high = place % 2, place // 2
        high = 1 - high if what == 2 else high
        half = low if piece < PIECES // 2 else 1 - low
        first = (2 * group + high) * self.quarter + half * (self.quarter // 2)
        first = pl.multiple_of(first + piece % (PIECES // 2) * self.step, 16)
        at = self.buffer.at[pl.ds(first, self.step), :]
        return pltpu.make_async_remote_copy(
            src_ref=at,
            dst_ref=at,
            send_sem=self.send_sem.at[what, piece],
            recv_sem=self.recv_sem.at[what, piece],
            device_id=self.on_dp if what else self.on_hi,
            device_id_type=MESH_IDS,
        )

    def send(self, piece):
        self.copy(0, piece).start()
        self.copy(1, piece).start()
        self.used.append(piece)

    def pass_on(self, piece):
        self.copy(0, piece).wait_recv()
        self.copy(2, piece).start()

    def spread(self, piece):
        self.copy(1, piece).start()
        self.copy(2, piece).start()
        self.near.append(piece)

    def finish(self):
        for piece in self.used + self.near:
            for what in range(3):
                if what == 0 and piece in self.near:
                    continue
                copy = self.copy(what, piece)
                copy.wait_send()
                if what > 0:
                    copy.wait_recv()


def piece_scratch():
    return [pltpu.SemaphoreType.DMA((3, PIECES))] * 2


def route_scratch(parts):
    return [
        pltpu.SemaphoreType.DMA((parts * len(ROUTES),)),
        pltpu.SemaphoreType.DMA((parts * len(ROUTES),)),
        pltpu.SemaphoreType.DMA(()),
    ]


def greet(devices):
    barrier = pltpu.get_barrier_semaphore()
    for device in devices:
        pl.semaphore_signal(barrier, inc=1, device_id=device, device_id_type=MESH_IDS)
    pl.semaphore_wait(barrier, len(devices))


def root_of(value):
    return lax.rsqrt(jnp.mean(value * value, axis=-1, keepdims=True) + EPS)


def norm_gradient(value, gain, grad):
    root = root_of(value)
    weighted = grad * gain
    return root * weighted - value * (root * root * root) * jnp.mean(
        weighted * value, axis=-1, keepdims=True
    ), jnp.sum(grad * value * root, axis=0, keepdims=True)


def token_kernel(*refs, kind, scatter, gather, pieces):
    refs = list(refs)
    take = lambda count: [refs.pop(0) for unused in range(count)]
    if scatter:
        (parts,) = take(1)
    (x_ref,) = take(1)
    if kind in (FIRST, LAST):
        (gain,) = take(1)
    if kind == PLAIN:
        (own_kv,) = take(1)
    if kind == LAST:
        (add_ref,) = take(1)
    if kind == LAST:
        aside, other_gain = take(2)
        near_send, near_keep, total = take(3)
    else:
        (bulk,) = take(1)
    if kind == PLAIN:
        (all_kv,) = take(1)
    if gather:
        (everyone,) = take(1)
    if kind == LAST:
        grad_out, gains_out, aside_out = take(3)
        kept, gotten = take(2), take(2)
    else:
        (bulk_out,) = take(1)
    if scatter:
        from_core, send_y, keep_y, got_y, send_lo, got_lo, mine, mine_sem = take(8)
    if gather:
        ready, local_sem = take(2)
    if kind == LAST:
        (ready,) = take(1)
    if kind == LAST:
        aside_router = Router(aside, aside_out, *take(3), spread=True)
        grad_router = Router(ready, grad_out, *take(3), spread=True)
        gain_acc, gain_sent, gain_got, side_local, side_send, side_recv = take(6)
        from_his, lo_sends = take(2), take(2)
        own_half, from_dp, total_keep, total_send = take(4)
    else:
        bulk_send, bulk_recv = take(2)
    if kind == PLAIN:
        kv_local, kv_send, kv_recv = take(3)
    send_sem, recv_sem = refs
    size, width = x_ref.shape
    step = size // ROUNDS
    on_y, on_lo, on_core = partners()
    on_hi, on_dp = route_partner(1, 0)[0], route_partner(2, 0)[0]
    if kind == LAST:
        greet((on_y, on_core, *(route_partner(q, e)[0] for q, e in ROUTES[1:])))
        for q, e in ROUTES:
            aside_router.send(q, e)
    else:
        greet((on_y, on_lo, on_core, on_hi, on_dp))
    kv_copies = []
    if kind == PLAIN:
        count = own_kv.shape[0]
        kv_copies.append(pltpu.make_async_copy(own_kv, all_kv.at[pl.ds(0, count), :], kv_local))
        kv_copies.append(
            pltpu.make_async_remote_copy(
                src_ref=own_kv,
                dst_ref=all_kv.at[pl.ds(count, count), :],
                send_sem=kv_send,
                recv_sem=kv_recv,
                device_id=on_hi,
                device_id_type=MESH_IDS,
            )
        )
        for copy in kv_copies:
            copy.start()
    if gather:
        weights = Pieces(bulk_out, bulk_send, bulk_recv)
    copies = {}

    def start(what, q, src, dst, device):
        copies[what, q] = pltpu.make_async_remote_copy(
            src_ref=src,
            dst_ref=dst,
            send_sem=send_sem.at[what, q],
            recv_sem=recv_sem.at[what, q],
            device_id=device,
            device_id_type=MESH_IDS,
        )
        copies[what, q].start()

    def arrived(what, q):
        copies[what, q].wait_recv()

    def rows_of(q):
        return pl.ds(pl.multiple_of(order(q) * step, step), step)

    def order(q):
        return route_partner(q, 0)[1] // 2 if kind == LAST else q

    def sum_core(q):
        rows = rows_of(q)
        arrived(CORE, q)
        copies["mine", q].wait()
        for lo in range(2):
            at = 2 * lo
            keep_y[lo, rows, :] = mine[at, rows, :].astype(F32) + from_core[at, rows, :].astype(F32)
            at = 2 * lo + 1
            total = mine[at, rows, :].astype(F32) + from_core[at, rows, :].astype(F32)
            send_y[lo, rows, :] = total.astype(BF)
        start(RY, q, send_y.at[:, rows, :], got_y.at[:, rows, :], on_y)

    def sum_y(q):
        rows = rows_of(q)
        arrived(RY, q)
        send_lo[rows, :] = (keep_y[1, rows, :] + got_y[1, rows, :].astype(F32)).astype(BF)
        start(RL, q, send_lo.at[rows, :], got_lo.at[rows, :], on_lo)

    def sum_lo(q):
        rows = rows_of(q)
        arrived(RL, q)
        return keep_y[0, rows, :] + got_y[0, rows, :].astype(F32) + got_lo[rows, :].astype(F32)

    def finish(q):
        rows = rows_of(q)
        total = sum_lo(q) if scatter else None
        value = x_ref[rows, :]
        if kind == PLAIN:
            low = value
        elif kind == FIRST:
            value = value.astype(F32)
            low = (value * root_of(value) * gain[...]).astype(BF)
        else:
            grad, gain_grad = norm_gradient(value.astype(F32), gain[...], total)
            grad = grad + add_ref[rows, :].astype(F32)
            ready[rows, :] = grad.astype(BF)
            if q == 0:
                gain_acc[...] = gain_grad
            else:
                gain_acc[...] += gain_grad
        if kind == LAST:
            grad_router.send(q, 0)
            grad_router.send(q, 1)
        if gather:
            ready[rows, :] = low
            keep = pltpu.make_async_copy(ready.at[rows, :], everyone.at[rows, :], local_sem.at[q])
            keep.start()
            copies["local", q] = keep
            start(GY, q, ready.at[rows, :], everyone.at[block(1, q), :], on_y)
            start(GL, q, ready.at[rows, :], everyone.at[block(2, q), :], on_lo)
            start(GC, q, ready.at[rows, :], everyone.at[block(4, q), :], on_core)

    def block(index, q):
        return pl.ds(index * size + q * step, step)

    def forward(q):
        arrived(GL, q)
        start(FY, q, everyone.at[block(2, q), :], everyone.at[block(3, q), :], on_y)
        start(CL, q, everyone.at[block(2, q), :], everyone.at[block(6, q), :], on_core)
        arrived(GY, q)
        start(CY, q, everyone.at[block(1, q), :], everyone.at[block(5, q), :], on_core)

    def corner(q):
        arrived(FY, q)
        start(CC, q, everyone.at[block(3, q), :], everyone.at[block(7, q), :], on_core)

    def pass_on(q):
        for router in routers:
            router.pass_on(q, 0)
            router.pass_on(q, 1)

    def pass_corner(q):
        for router in routers:
            router.pass_corner(q, 0)
            router.pass_corner(q, 1)

    side_copies = []

    def side(src, dst, device):
        at = len(side_copies)
        copy = pltpu.make_async_remote_copy(
            src_ref=src,
            dst_ref=dst,
            send_sem=side_send.at[at],
            recv_sem=side_recv.at[at],
            device_id=device,
            device_id_type=MESH_IDS,
        )
        copy.start()
        side_copies.append(copy)
        return copy

    waiting = {}

    def unit_rows(unit):
        low = lax.axis_index(CONTEXT) % 2
        count = from_his[unit // 2].shape[0] // 2
        index = low if unit % 2 else 1 - low
        return pl.ds(pl.multiple_of(index * count, 16), count)

    def unit_to_dp(unit):
        group = lax.axis_index(DP)
        rows = unit_rows(unit)
        waiting["own", unit] = pltpu.make_async_copy(
            total.at[group, :, rows, :], own_half.at[:, rows, :], side_local.at[unit]
        )
        waiting["own", unit].start()
        waiting["dp", unit] = side(
            total.at[1 - group, :, rows, :], from_dp.at[:, rows, :], on_dp
        )

    def unit_to_hi(unit):
        high = lax.axis_index(CONTEXT) // 2
        rows = unit_rows(unit)
        send = total_send
        if unit >= 2:
            waiting["own", unit].wait()
            waiting["dp", unit].wait_recv()
            total_keep[rows, :] = own_half[high, rows, :].astype(F32) + from_dp[
                high, rows, :
            ].astype(F32)
            send[rows, :] = (
                own_half[1 - high, rows, :].astype(F32) + from_dp[1 - high, rows, :].astype(F32)
            ).astype(BF)
        waiting["hi", unit] = side(send.at[rows, :], from_his[unit // 2].at[rows, :], on_hi)

    def near_to_hi(index):
        low = lax.axis_index(CONTEXT) % 2
        count = near_send.shape[0] // 8
        first = (1 - low if index < 4 else low) * 4 * count + index % 4 * count
        rows = pl.ds(pl.multiple_of(first, 16), count)
        waiting["near", index] = side(near_send.at[rows, :], from_his[0].at[rows, :], on_hi)

    def unit_to_lo(unit):
        rows = unit_rows(unit)
        keep = near_keep if unit < 2 else total_keep
        if unit < 2:
            for index in range(4 * unit, 4 * unit + 4):
                waiting["near", index].wait_recv()
        else:
            waiting["hi", unit].wait_recv()
        value = keep[rows, :] + from_his[unit // 2][rows, :].astype(F32)
        if unit % 2:
            kept[unit // 2][...] = value
        else:
            lo_sends[unit // 2][...] = value.astype(BF)
            waiting["lo", unit] = side(lo_sends[unit // 2], gotten[unit // 2], on_lo)

    def gain_hop(index):
        if index == 0:
            total = jnp.concatenate([gain_acc[...], other_gain[...]], axis=0)
        else:
            waiting["gain"].wait_recv()
            total = gain_sent[index - 1] + gain_got[index - 1]
        if index == 5:
            gains_out[...] = total
        else:
            gain_sent[index] = total
            device = (on_core, on_y, on_lo, on_dp, on_hi)[index]
            waiting["gain"] = side(gain_sent.at[index], gain_got.at[index], device)

    def beside(tick):
        if tick == 0:
            unit_to_dp(2)
            unit_to_dp(3)
        if tick < 8:
            near_to_hi(tick)
        if tick in (3, 4):
            unit_to_hi(tick - 1)
        if tick == 6:
            unit_to_lo(0)
        if 5 <= tick < 8:
            gain_hop(tick - 5)
        if tick == 7:
            for index in range(3, 6):
                gain_hop(index)
            for unit in range(1, 4):
                unit_to_lo(unit)

    routers = [aside_router, grad_router] if kind == LAST else []
    stages = []
    if scatter:
        for q in range(ROUNDS):
            rows = rows_of(q)
            start(CORE, q, parts.at[pl.ds(4, 4), rows, :], from_core.at[:, rows, :], on_core)
            copies["mine", q] = pltpu.make_async_copy(
                parts.at[pl.ds(0, 4), rows, :], mine.at[:, rows, :], mine_sem.at[q]
            )
            copies["mine", q].start()
        stages += [sum_core, sum_y]
    stages.append(finish)
    if gather:
        stages += [forward, corner]
    if routers:
        stages += [pass_on, pass_corner]
    ordered = list(enumerate(stages))
    if scatter:
        ordered.reverse()
    elif kind == PLAIN:
        for q in range(ROUNDS):
            finish(q)
        ordered = ordered[1:]
    for tick in range(ROUNDS + len(stages) - 1):
        for index, stage in ordered:
            if 0 <= tick - index < ROUNDS:
                stage(tick - index)
        if gather and tick < len(pieces):
            weights.send(pieces[tick])
        if kind == LAST:
            beside(tick)
        if gather and 0 <= tick - 2 < len(pieces):
            weights.pass_on(pieces[tick - 2])
    for (what, q), copy in copies.items():
        if what == "local":
            copy.wait()
        elif what != "mine":
            copy.wait_send()
            if what in (GC, CY, CL, CC):
                copy.wait_recv()
    if gather:
        weights.finish()
    for copy in kv_copies:
        copy.wait()
    if kind == LAST:
        aside_router.finish()
        grad_router.finish()
        for copy in side_copies:
            copy.wait_send()
        for unit in (0, 2):
            waiting["lo", unit].wait_recv()


def call_tokens(
    kind, ident, part, x, bulk, pieces, gain=None, add=None, aside=None, other_gain=None, grads=None
):
    size, width = x.shape
    scatter, gather = part is not None, kind != LAST
    vmem = pl.BlockSpec(memory_space=pltpu.VMEM)
    anywhere = pl.BlockSpec(memory_space=pl.ANY)
    operands, in_specs, out_specs, out_shape, scratch = [], [], [], [], []
    if scatter:
        operands.append(part.reshape(8, size, width))
        in_specs.append(anywhere)
    operands.append(x)
    in_specs.append(vmem)
    if gain is not None:
        operands.append(gain.reshape(1, width))
        in_specs.append(vmem)
    if kind == PLAIN:
        operands.append(add)
        in_specs.append(anywhere)
        out_specs.append(anywhere)
        out_shape.append(jax.ShapeDtypeStruct((2 * add.shape[0], add.shape[1]), BF))
    elif add is not None:
        operands.append(add)
        in_specs.append(vmem)
    if aside is not None:
        send, keep, total = grads
        cuts = [keep.shape, (total.shape[0] // 4, total.shape[1])]
        operands += [aside, other_gain, send, keep, total.reshape(2, 2, *cuts[1])]
        in_specs += [anywhere, vmem, anywhere, vmem, anywhere]
    if bulk is not None:
        operands.append(bulk)
        in_specs.append(anywhere)
    if gather:
        out_specs.append(anywhere)
        out_shape.append(jax.ShapeDtypeStruct((8 * size, width), BF))
    if kind == LAST:
        out_specs.append(anywhere)
        out_shape.append(jax.ShapeDtypeStruct((4 * size, width), BF))
    if kind == LAST:
        out_specs.append(vmem)
        out_shape.append(jax.ShapeDtypeStruct((2, width), F32))
        out_specs += [anywhere] + [vmem] * 2 + [anywhere] * 2
        out_shape.append(jax.ShapeDtypeStruct((4 * size, width), BF))
        out_shape += [jax.ShapeDtypeStruct((count // 2, n), F32) for count, n in cuts]
        out_shape += [jax.ShapeDtypeStruct((count // 2, n), BF) for count, n in cuts]
    if bulk is not None:
        out_specs.append(anywhere)
        out_shape.append(jax.ShapeDtypeStruct(bulk.shape, BF))
    if scatter:
        scratch.append(pltpu.VMEM((4, size, width), BF))
        pair = (2, size, width)
        scratch += [pltpu.VMEM(pair, BF), pltpu.VMEM(pair, F32), pltpu.VMEM(pair, BF)]
        scratch += [pltpu.VMEM((size, width), BF)] * 2
        scratch += [pltpu.VMEM((4, size, width), BF), pltpu.SemaphoreType.DMA((ROUNDS,))]
    if gather:
        scratch += [pltpu.VMEM((size, width), BF), pltpu.SemaphoreType.DMA((ROUNDS,))]
    if kind == LAST:
        scratch.append(pltpu.VMEM((size, width), BF))
        scratch += route_scratch(4) + route_scratch(4)
        scratch += [pltpu.VMEM((1, width), F32)] + [pltpu.VMEM((5, 2, width), F32)] * 2
        scratch.append(pltpu.SemaphoreType.DMA((6,)))
        scratch += [pltpu.SemaphoreType.DMA((20,))] * 2
        scratch += [pltpu.VMEM(cut, BF) for cut in cuts]
        scratch += [pltpu.VMEM((count // 2, n), BF) for count, n in cuts]
        scratch += [pltpu.VMEM((2, *cuts[1]), BF)] * 2
        scratch += [pltpu.VMEM(cuts[1], F32), pltpu.VMEM(cuts[1], BF)]
    else:
        scratch += piece_scratch()
    if kind == PLAIN:
        scratch += [pltpu.SemaphoreType.DMA(())] * 3
    scratch += [pltpu.SemaphoreType.DMA((KINDS, ROUNDS))] * 2
    return pl.pallas_call(
        functools.partial(
            token_kernel, kind=kind, scatter=scatter, gather=gather, pieces=pieces
        ),
        in_specs=in_specs,
        out_specs=out_specs,
        out_shape=out_shape,
        scratch_shapes=scratch,
        input_output_aliases={len(operands) - 1: len(out_shape) - 1} if gather else {},
        compiler_params=pltpu.CompilerParams(
            collective_id=ident, has_side_effects=True, vmem_limit_bytes=62 * 2**20
        ),
        cost_estimate=QUICK,
        name="tokens_%d" % kind,
    )(*operands)


def ffn_kernel(
    parts,
    x_ref,
    gain,
    d_y,
    d_y_all,
    large,
    two_all,
    grad_all,
    inner_out,
    both_out,
    y_mine,
    y_other,
    mid_out,
    grad_out,
    gain_out,
    large_out,
    weights,
    summed,
    got_a,
    got_b,
    got_c,
    got_d,
    mine,
    two_ready,
    grad_ready,
    two_block,
    d_y_block,
    inner_block,
    both_block,
    y_block,
    d_two,
    weight_sem,
    mine_sem,
    ready_sem,
    load_sem,
    store_sem,
    send_sem,
    recv_sem,
    piece_send,
    piece_recv,
    *,
    pieces,
):
    size, width = x_ref.shape
    units = inner_out.shape[2]
    cut = width // 2
    step = size // ROUNDS
    half = step // 2
    on_y, on_lo, on_core = partners()
    arriving = Pieces(large_out, piece_send, piece_recv)
    greet((on_y, on_lo, on_core, arriving.on_dp))
    left, right = pl.ds(0, cut), pl.ds(cut, width - cut)

    def rows_of(q):
        return pl.ds(pl.multiple_of(q * step, step), step)

    def block(index, q, first=0, count=None):
        start = pl.multiple_of(index * size + q * step + first, half)
        return pl.ds(start, step if count is None else count)

    def remote(base, what, q):
        rows = rows_of(q)
        ready, everyone = (two_ready, two_all) if base == 0 else (grad_ready, grad_all)
        part_of = lambda *place: everyone.at[block(*place), :]
        if what == CORE:
            src = parts.at[1, :, :, rows, :] if base == 0 else d_two.at[lax.rem(q, 2), 1]
            ends = src, summed.at[:, :, rows, :], on_core
        elif what == RY:
            ends = summed.at[:, 1, rows, left], got_a.at[:, rows, :], on_y
        elif what == RL:
            ends = summed.at[1, :, rows, right], got_b.at[:, rows, :], on_lo
        elif what == SL:
            ends = summed.at[1, 0, rows, left], got_c.at[rows, :], on_lo
        elif what == SY:
            ends = summed.at[0, 1, rows, right], got_d.at[rows, :], on_y
        elif what in (GY, GL, GC):
            index, device = {GY: (1, on_y), GL: (2, on_lo), GC: (4, on_core)}[what]
            ends = ready.at[rows, :], part_of(index, q), device
        elif what == FL:
            ends = part_of(1, q, 0, half), part_of(3, q, 0, half), on_lo
        elif what == FY:
            ends = part_of(2, q, half, half), part_of(3, q, half, half), on_y
        else:
            index = {CY: 1, CL: 2, CC: 3}[what]
            ends = part_of(index, q), part_of(index + 4, q), on_core
        return pltpu.make_async_remote_copy(
            src_ref=ends[0],
            dst_ref=ends[1],
            send_sem=send_sem.at[base + what, q],
            recv_sem=recv_sem.at[base + what, q],
            device_id=ends[2],
            device_id_type=MESH_IDS,
        )

    def arrived(base, what, q):
        remote(base, what, q).wait_recv()

    def sum_core(base, q, value):
        rows = rows_of(q)
        arrived(base, CORE, q)
        for lo in range(2):
            for y in range(2):
                total = value(lo, y).astype(F32) + summed[lo, y, rows, :].astype(F32)
                summed[lo, y, rows, :] = total.astype(BF)
        remote(base, RY, q).start()
        remote(base, RL, q).start()

    def sum_first(base, q):
        rows = rows_of(q)
        arrived(base, RY, q)
        total = summed[1, 0, rows, :cut].astype(F32) + got_a[1, rows, :].astype(F32)
        summed[1, 0, rows, :cut] = total.astype(BF)
        remote(base, SL, q).start()
        arrived(base, RL, q)
        total = summed[0, 1, rows, cut:].astype(F32) + got_b[1, rows, :].astype(F32)
        summed[0, 1, rows, cut:] = total.astype(BF)
        remote(base, SY, q).start()

    def sum_second(base, q):
        rows = rows_of(q)
        arrived(base, SL, q)
        arrived(base, SY, q)
        first = summed[0, 0, rows, :cut].astype(F32) + got_a[0, rows, :].astype(F32)
        second = summed[0, 0, rows, cut:].astype(F32) + got_b[0, rows, :].astype(F32)
        first = first + got_c[rows, :].astype(F32)
        second = second + got_d[rows, :].astype(F32)
        for what in (RY, RL, SL, SY):
            remote(base, what, q).wait_send()
        return jnp.concatenate([first, second], axis=1)

    def own_rows(base, q):
        ready, everyone = (two_ready, two_all) if base == 0 else (grad_ready, grad_all)
        rows = rows_of(q)
        sem = ready_sem.at[base // KINDS, q]
        return pltpu.make_async_copy(ready.at[rows, :], everyone.at[rows, :], sem)

    def spread(base, q):
        own_rows(base, q).start()
        for what in (GY, GL, GC):
            remote(base, what, q).start()

    def forward(base, q):
        arrived(base, GY, q)
        remote(base, FL, q).start()
        remote(base, CY, q).start()
        arrived(base, GL, q)
        remote(base, FY, q).start()
        remote(base, CL, q).start()

    def corner(base, q):
        arrived(base, FL, q)
        arrived(base, FY, q)
        remote(base, CC, q).start()

    def fetch_mine(q):
        src = parts.at[0, :, :, rows_of(q), :]
        slot = lax.rem(q, 2)
        return pltpu.make_async_copy(src, mine.at[slot], mine_sem.at[slot])

    def middle_core(q):
        fetch_mine(q).wait()
        sum_core(0, q, lambda lo, y: mine[lax.rem(q, 2), lo, y])

        @pl.when(q + 2 < ROUNDS)
        def _():
            fetch_mine(q + 2).start()

    def middle_norm(q):
        rows = rows_of(q)
        value = x_ref[rows, :].astype(F32) + sum_second(0, q)
        mid_out[rows, :] = value
        two_ready[rows, :] = (value * root_of(value) * gain[...]).astype(BF)
        spread(0, q)

    def loads(part, q):
        for index, (src, dst) in enumerate(((two_all, two_block), (d_y_all, d_y_block))):
            for at in range(4):
                yield pltpu.make_async_copy(
                    src.at[block(4 * part + at, q), :],
                    dst.at[part, pl.ds(at * step, step), :],
                    load_sem.at[index, part, at],
                )

    def stores(part, q):
        for index, (src, dst) in enumerate(((inner_block, inner_out), (both_block, both_out))):
            for at in range(4):
                yield pltpu.make_async_copy(
                    src.at[part, pl.ds(at * step, step), :],
                    dst.at[4 * part + at, rows_of(q), :],
                    store_sem.at[index, part, at],
                )

    def y_stores(part, q, act):
        for index, dst in enumerate((y_mine, y_other)):

            @pl.when(part == index)
            def _():
                for at in range(4):
                    copy = pltpu.make_async_copy(
                        y_block.at[index, pl.ds(at * step, step), :],
                        dst.at[at, rows_of(q), :],
                        store_sem.at[2, index, at],
                    )
                    act(copy)

    def feed_forward(q):
        own_rows(0, q).wait()
        for what in (GC, CY, CL, CC):
            arrived(0, what, q)

        @pl.when(q == 0)
        def _():
            pltpu.make_async_copy(large_out, weights, weight_sem.at[0]).wait()

        @pl.when(q >= 2)
        def _():
            remote(KINDS, CORE, q - 2).wait_send()

        for part in (1, 0):
            for copy in loads(part, q):
                copy.start()

        @pl.loop(0, 2)
        def _(turn_index):
            part = 1 - turn_index
            for copy in loads(part, q):
                copy.wait()

            @pl.when(q > 0)
            def _():
                for copy in stores(part, q - 1):
                    copy.wait()
                y_stores(part, q - 1, lambda copy: copy.wait())

            both = mm(two_block[part], weights[:, : 2 * units])
            gate, up = both[:, :units], both[:, units:]
            d_inner = mm(d_y_block[part], weights[:, 2 * units :])
            sigma = 1.0 / (1.0 + jnp.exp(-gate))
            silu_gate = gate * sigma
            inner_block[part] = (silu_gate * up).astype(BF)
            d_gate = d_inner * up * sigma * (1.0 + gate * (1.0 - sigma))
            both_block[part, :, :units] = d_gate.astype(BF)
            both_block[part, :, units:] = (d_inner * silu_gate).astype(BF)
            d_two[lax.rem(q, 2), part] = (
                times_t(both_block[part], weights[:, : 2 * units])
                .astype(BF)
                .reshape(2, 2, step, width)
            )

            @pl.when(part == 1)
            def _():
                remote(KINDS, CORE, q).start()

            y_block[part] = times_t(inner_block[part], weights[:, 2 * units :]).astype(BF)
            for copy in stores(part, q):
                copy.start()
            y_stores(part, q, lambda copy: copy.start())

    def back_core(q):
        sum_core(KINDS, q, lambda lo, y: d_two[lax.rem(q, 2), 0, lo, y])

    def back_norm(q):
        rows = rows_of(q)
        grad, gain_grad = norm_gradient(mid_out[rows, :], gain[...], sum_second(KINDS, q))
        grad = grad + d_y[rows, :].astype(F32)
        grad_out[rows, :] = grad
        gain_out[...] += gain_grad
        grad_ready[rows, :] = grad.astype(BF)
        spread(KINDS, q)

    gain_out[...] = jnp.zeros_like(gain_out)
    for q in range(ROUNDS):
        remote(0, CORE, q).start()
        if q < 2:
            fetch_mine(q).start()
    stages = [
        middle_core,
        functools.partial(sum_first, 0),
        middle_norm,
        functools.partial(forward, 0),
        functools.partial(corner, 0),
        feed_forward,
        back_core,
        functools.partial(sum_first, KINDS),
        back_norm,
        functools.partial(forward, KINDS),
        functools.partial(corner, KINDS),
    ]

    @pl.loop(0, ROUNDS + len(stages) - 1)
    def _(tick):
        for index, stage in reversed(list(enumerate(stages))):
            pl.when((tick >= index) & (tick < index + ROUNDS))(
                functools.partial(stage, tick - index)
            )

        @pl.when(tick == 0)
        def _():
            for piece in pieces:
                arriving.spread(piece)

        @pl.when(tick == 4)
        def _():
            arriving.finish()
            pltpu.make_async_copy(large_out, weights, weight_sem.at[0]).start()

    for q in range(ROUNDS):
        for base in (0, KINDS):
            for what in range(KINDS):
                if what in (RY, RL, SL, SY) or (what == CORE and base and q < ROUNDS - 2):
                    continue
                remote(base, what, q).wait_send()
        for what in (GC, CY, CL, CC):
            arrived(KINDS, what, q)
        own_rows(KINDS, q).wait()
    for part in range(2):
        for copy in stores(part, ROUNDS - 1):
            copy.wait()
        y_stores(part, ROUNDS - 1, lambda copy: copy.wait())


def call_ffn(parts, x, gain, d_y, d_y_all, large, pieces):
    size, width = x.shape
    units = large.shape[1] // 3
    cut = width // 2
    step = size // ROUNDS
    vmem = pl.BlockSpec(memory_space=pltpu.VMEM)
    anywhere = pl.BlockSpec(memory_space=pl.ANY)
    everyone = jax.ShapeDtypeStruct((8 * size, width), BF)
    shape = lambda n: jax.ShapeDtypeStruct((8, size, n), BF)
    local = jax.ShapeDtypeStruct((size, width), F32)
    dma = pltpu.SemaphoreType.DMA
    half = pltpu.VMEM((2, size, cut), BF)
    quarter = pltpu.VMEM((size, cut), BF)
    ready = pltpu.VMEM((size, width), BF)
    block = lambda n: pltpu.VMEM((2, 4 * step, n), BF)
    return pl.pallas_call(
        functools.partial(ffn_kernel, pieces=pieces),
        in_specs=[anywhere, vmem, vmem, vmem, anywhere, anywhere],
        out_specs=[anywhere] * 6 + [vmem] * 3 + [anywhere],
        input_output_aliases={5: 9},
        out_shape=[
            everyone,
            everyone,
            shape(units),
            shape(2 * units),
            jax.ShapeDtypeStruct((4, size, width), BF),
            jax.ShapeDtypeStruct((4, size, width), BF),
            local,
            local,
            jax.ShapeDtypeStruct((1, width), F32),
            jax.ShapeDtypeStruct(large.shape, BF),
        ],
        scratch_shapes=[
            pltpu.VMEM((width, 3 * units), BF),
            pltpu.VMEM((2, 2, size, width), BF),
            half,
            half,
            quarter,
            quarter,
            pltpu.VMEM((2, 2, 2, step, width), BF),
            ready,
            ready,
            block(width),
            block(width),
            block(units),
            block(2 * units),
            block(width),
            pltpu.VMEM((2, 2, 2, 2, step, width), BF),
            dma((1,)),
            dma((2,)),
            dma((2, ROUNDS)),
            dma((2, 2, 4)),
            dma((3, 2, 4)),
            dma((2 * KINDS, ROUNDS)),
            dma((2 * KINDS, ROUNDS)),
            *piece_scratch(),
        ],
        compiler_params=pltpu.CompilerParams(
            collective_id=8, has_side_effects=True, vmem_limit_bytes=62 * 2**20
        ),
        cost_estimate=QUICK,
        name="feed_forward",
    )(parts.reshape(2, 2, 2, size, width), x, gain.reshape(1, width), d_y, d_y_all, large)


CHUNKS = 2


def weights_kernel(
    small_keep,
    small_give,
    large_keep,
    rows,
    late_rows,
    small,
    large,
    rows_out,
    late_out,
    local,
    send,
    recv,
    *rest,
):
    group, place, shard = (lax.axis_index(name) for name in MESH_AXES)
    low, high = place % 2, place // 2
    on_lo = (group, place + 1 - 2 * low, shard)
    on_hi = (group, place + 2 - 4 * high, shard)
    on_dp = (1 - group, place, shard)
    eighth = small_keep.shape[0]
    step = eighth // CHUNKS
    greet([route_partner(q, e)[0] for q, e in ROUTES[1:]])
    copies = []
    router, late = Router(rows, rows_out, *rest[:3]), Router(late_rows, late_out, *rest[3:6])
    for q, e in ROUTES:
        router.send(q, e)

    def start(src, dst, device):
        at = len(copies)
        copy = pltpu.make_async_remote_copy(
            src_ref=src,
            dst_ref=dst,
            send_sem=send.at[at],
            recv_sem=recv.at[at],
            device_id=device,
            device_id_type=MESH_IDS,
        )
        copy.start()
        copies.append(copy)
        return copy

    def span(index, first, count):
        return pl.ds(pl.multiple_of(index * eighth + first, 16), count)

    own = (group * 2 + high) * 2
    across = (group * 2 + 1 - high) * 2
    from_low = []
    for q in range(CHUNKS):
        src = small_give.at[pl.ds(q * step, step), :]
        from_low.append(start(src, small.at[span(own + low, q * step, step), :], on_lo))
    stay = [
        pltpu.make_async_copy(small_keep, small.at[span(own + low, 0, eighth), :], local.at[0]),
        pltpu.make_async_copy(large_keep, large.at[span(own + low, 0, eighth), :], local.at[1]),
    ]
    for copy in stay:
        copy.start()
    from_high = []
    for q in range(CHUNKS):
        src = small_keep.at[pl.ds(q * step, step), :]
        dst = small.at[span(own + low, q * step, step), :]
        from_high.append(start(src, dst, on_hi))
        start(src, dst, on_dp)
    for q in range(CHUNKS):
        from_low[q].wait_recv()
        at = small.at[span(own + 1 - low, q * step, step), :]
        from_high.append(start(at, at, on_hi))
        start(at, at, on_dp)
    for q in range(2 * CHUNKS):
        half = low if q < CHUNKS else 1 - low
        from_high[q].wait_recv()
        at = small.at[span(across + half, q % CHUNKS * step, step), :]
        start(at, at, on_dp)
        if q == 0:
            for pair in ROUTES:
                late.send(*pair)
    waited = from_low + from_high
    for copy in copies:
        copy.wait_send()
        if not any(copy is item for item in waited):
            copy.wait_recv()
    for copy in stay:
        copy.wait()
    router.finish()
    late.finish()


def call_weights(small_keep, small_give, large_keep, rows, late_rows, parts):
    eighth = small_keep.shape[0]
    anywhere = pl.BlockSpec(memory_space=pl.ANY)
    count = 7 * CHUNKS
    return pl.pallas_call(
        weights_kernel,
        in_specs=[anywhere] * 5,
        out_specs=[anywhere] * 4,
        out_shape=[
            jax.ShapeDtypeStruct((2 * parts * eighth, small_keep.shape[1]), BF),
            jax.ShapeDtypeStruct((2 * parts * eighth, large_keep.shape[1]), BF),
            jax.ShapeDtypeStruct(rows.shape, BF),
            jax.ShapeDtypeStruct(rows.shape, BF),
        ],
        scratch_shapes=[
            pltpu.SemaphoreType.DMA((2,)),
            pltpu.SemaphoreType.DMA((count,)),
            pltpu.SemaphoreType.DMA((count,)),
            *route_scratch(1),
            *route_scratch(1),
        ],
        compiler_params=pltpu.CompilerParams(collective_id=1, has_side_effects=True),
        cost_estimate=QUICK,
        name="weights_first",
    )(small_keep, small_give, large_keep, rows, late_rows)


def head_columns(part, base):
    half = part // 2
    entry = np.arange(part)
    return base + np.where(entry < half, entry, LANES // 2 + entry - half)


def after(value, *events):
    return lax.optimization_barrier((value, *events))[0]


def on_device_paired(
    tokens,
    gain_attn,
    w_query,
    key_weight,
    value_weight,
    w_out,
    gain_mlp,
    w_gate,
    w_up,
    w_down,
    cotangent,
    lengths,
    order_perm,
    block_order,
):
    names = MESH_AXES
    n_dp, n_ctx, n_ten = (lax.axis_size(name) for name in names)
    devices = n_dp * n_ctx * n_ten
    on_core, on_y, on_lo, on_hi, on_dp = 1, 2, n_ten, 2 * n_ten, n_ctx * n_ten
    group = lax.axis_index(DP)
    place = lax.axis_index(CONTEXT)
    shard = lax.axis_index(TENSOR)
    high, low = place // 2, place % 2
    row, core = shard // 2, shard % 2
    groups = n_dp * n_ctx
    my_index = group * n_ctx + place
    rows, width = tokens.shape
    share = rows // groups
    part = share // n_ten
    local = rows // n_ten
    block_rows = rows // MB
    half_rows = block_rows // 2
    pack = block_rows * n_ctx
    n_blocks = block_order.shape[0]
    blocks = n_blocks // 2
    scale = HEAD_SIZE ** (-0.5)
    quarter = width // (2 * n_dp)
    eighth = quarter // 2

    def swap(value, bit):
        return lax.ppermute(value, names, [(i, i ^ bit) for i in range(devices)])

    def pick(flag, yes, no):
        return jnp.where(flag == 1, yes, no)

    def by_low(mine, partner, axis):
        return jnp.concatenate(
            [pick(low, partner, mine), pick(low, mine, partner)], axis=axis
        )

    places = order_perm.reshape(groups, rows)
    source = places // rows
    is_mine = source == my_index
    below = jnp.arange(rows, dtype=jnp.int32)
    ahead = one_hot(1, (below[:, None] <= below[None, :]).astype(jnp.int32))
    all_sources = jnp.arange(groups, dtype=jnp.int32)
    runs = [
        lax.dynamic_index_in_dim(source, group * n_ctx + 2 * high + (low ^ d), 0, keepdims=False)
        for d in range(2)
    ]
    from_each = [run[None, :] == all_sources[:, None] for run in runs]
    flags = jnp.concatenate([is_mine, *from_each], axis=0)
    counted = mm(flags.astype(BF), ahead).astype(jnp.int32) - 1
    rank = counted[:groups]
    row_at = jnp.where(is_mine, places % rows, 0)

    def rows_sent(slots):
        hits = is_mine[:, None, :] & (rank[:, None, :] == slots[None, :, None])
        return jnp.sum(jnp.where(hits, row_at[:, None, :], 0), axis=2)

    send_index = rows_sent(shard * part + jnp.arange(part, dtype=jnp.int32)).reshape(local, 1)

    def arrivals(d):
        known = counted[(d + 1) * groups : (d + 2) * groups]
        own_rank = jnp.sum(jnp.where(from_each[d], known, 0), axis=0)
        holder = own_rank // part
        device = ((holder % 2) ^ core) * 2 + ((holder // 2) ^ row)
        return (device * groups + runs[d]) * part + own_rank % part

    index = jnp.stack([arrivals(d) for d in range(2)])
    index_col, index_row = index[:, :, None], index[:, None, :]

    def lookup(table, at):
        hits = at[..., None] == jnp.arange(table.shape[0], dtype=jnp.int32)
        return jnp.sum(jnp.where(hits, table, 0), axis=-1)

    slot_of = invert(block_order)
    query = jnp.arange(2 * MB * 2, dtype=jnp.int32)
    run_of, micro_of, half_of = query // (2 * MB), query // 2 % MB, query % 2
    which = lookup(block_order, 2 * (2 * high + (low ^ run_of)) + half_of)
    upper = which // blocks
    item = jnp.arange(blocks, dtype=jnp.int32)
    slot = lookup(slot_of, upper[:, None] * blocks + item)
    where = ((slot // 4) ^ high) * 2 + (((slot // 2) % 2) ^ low)
    starts = ((where * MB + micro_of[:, None]) * 2 + slot % 2) * half_rows
    first = lookup(lengths[:, 0], group * MB + micro_of)
    second = first + lookup(lengths[:, 1], group * MB + micro_of)
    meta = jnp.concatenate([(which % blocks)[:, None], starts], axis=1)
    at = which[:, None] * half_rows + jnp.arange(half_rows, dtype=jnp.int32)
    first, second = first[:, None], second[:, None]
    in_last = at >= second
    q_flag = jnp.where(in_last, 1.0, 0.0).reshape(2, rows, 1)
    k_flag = jnp.where(in_last, 0.0, MASKED).reshape(2, rows, 1)
    at = at - jnp.where(at < first, 0, jnp.where(at < second, first, second))
    position = at.reshape(2, rows)
    hit = index[:, :, None] == jnp.arange(rows, dtype=jnp.int32)[None, None, :]
    position_arrived = jnp.sum(jnp.where(hit, position[:, :, None], 0), axis=1)

    half_head = HEAD_SIZE // 2
    entry_of = np.arange(half_head)
    freq = (THETA ** (-2.0 * entry_of / HEAD_SIZE)).astype(np.float32)
    to_lanes = np.zeros((2, half_head, LANES), np.float32)
    to_lanes[:, entry_of, entry_of + LANES // 2] = 1.0
    to_lanes[0, entry_of, entry_of] = 1.0
    to_lanes[1, entry_of, entry_of] = -1.0

    def tables(pos):
        angle = freq[:, None] * pos.reshape(-1).astype(F32)[None, :]
        return [
            lax.dot_general(
                value,
                jnp.asarray(lanes),
                (((0,), (0,)), ((), ())),
                precision=lax.Precision.HIGHEST,
                preferred_element_type=F32,
            ).reshape(2, rows, LANES)
            for value, lanes in zip((jnp.cos(angle), jnp.sin(angle)), to_lanes, strict=True)
        ]

    cos_arrived, sin_arrived = tables(position_arrived)
    cos_place, sin_place = tables(position)

    q_width, kv_width = GROUP * HEAD_SIZE, HEAD_SIZE
    all_width = q_width + 2 * kv_width
    target = np.concatenate(
        [head_columns(HEAD_SIZE, h * LANES) for h in range(GROUP + 1)]
        + [(GROUP + 1) * LANES + np.arange(HEAD_SIZE)]
    )
    spread_np = np.zeros((all_width, (GROUP + 2) * LANES), np.float32)
    spread_np[np.arange(all_width), target] = 1.0
    spread = jnp.asarray(spread_np, BF)
    out_target = np.concatenate([h * LANES + np.arange(HEAD_SIZE) for h in range(GROUP)])
    out_np = np.zeros((q_width, GROUP * LANES), np.float32)
    out_np[np.arange(q_width), out_target] = 1.0
    out_spread = jnp.asarray(out_np, BF)

    def halves(value):
        size = value.shape[1] // 2
        return pick(low, value[:, size:], value[:, :size]), pick(low, value[:, :size], value[:, size:])

    def together(values):
        keeps, gives = zip(*(halves(value) for value in values), strict=True)
        return list(keeps), list(gives)

    x_send, cot_send = pick_rows(send_index, tokens, cotangent, True)
    w_out_t, w_down_t = w_out.T, w_down.T
    keeps, gives = together([w_query, key_weight, value_weight])
    keep_out, give_out = halves(w_out_t)
    gains = jnp.stack([gain_attn, gain_mlp], axis=1)
    out_at, gain_at = 4 * LANES, 4 * LANES + q_width
    gap = jnp.zeros((eighth, out_at - all_width), BF)
    end = jnp.zeros((eighth, 7 * LANES - gain_at - 2), BF)
    small_keep = jnp.concatenate([*keeps, gap, keep_out, gains, end], axis=1)
    small_give = jnp.concatenate([*gives, gap, give_out, gains, end], axis=1)
    keeps, gives = together([w_gate, w_up, w_down_t])
    small, large, x_low, cot_low = call_weights(
        small_keep,
        small_give,
        jnp.concatenate(keeps, axis=1),
        x_send,
        cot_send,
        2 * n_dp,
    )
    large_give = jnp.concatenate(gives, axis=1)
    w_qkv = small[:, :all_width]
    w_o_t = small[:, out_at:gain_at]
    gain_a = small[:, gain_at].astype(F32)
    gain_m = small[:, gain_at + 1].astype(F32)

    one_all, large = call_tokens(FIRST, 2, None, x_low, large, (0, 1, 2, 3), gain_a)
    large_got = swap(after(large_give, one_all), on_lo)

    split = GROUP * LANES
    kv_own = call_sort(
        one_all, mm(w_qkv, spread[:, split:]).astype(BF), cos_arrived, sin_arrived, index_col, k_flag, 1
    )
    block_first = (2 * group + high) * quarter
    across_first = (2 * group + 1 - high) * quarter
    large = lax.dynamic_update_slice_in_dim(large, large_got, block_first + (1 - low) * eighth, 0)
    kv_all, dy_all, large = call_tokens(PLAIN, 3, None, cot_low, large, (4,), None, kv_own)
    late_first, late_count = (1 - low) * eighth + eighth // 4, eighth - eighth // 4
    late = lax.dynamic_slice_in_dim(large, block_first + late_first, late_count, 0)
    late = swap(late, on_hi)
    q_sorted = call_sort(
        after(one_all, dy_all),
        mm(w_qkv, spread[:, :split]).astype(BF),
        cos_arrived,
        sin_arrived,
        index_col,
        q_flag,
        2,
    )
    o_all = call_forward(meta, q_sorted, kv_all, index_row, out_spread.T, scale)
    o_part = product(o_all, w_o_t, 1)
    o_part, late = lax.optimization_barrier((o_part, late))
    large = lax.dynamic_update_slice_in_dim(large, late, across_first + late_first, 0)
    two_all, dh_all, inner_all, d_both_all, y_part, y_other, mid, d_mid, gain_grad_m, unused = call_ffn(
        o_part, x_low, gain_m, cot_low, dy_all, large, (5, 6, 7)
    )
    units = inner_all.shape[2]
    inner_all = inner_all.reshape(2 * rows, units)
    d_both_all = d_both_all.reshape(2 * rows, 2 * units)

    def rows_at(value, index, size):
        return lax.dynamic_slice_in_dim(value, index * size, size, 0)

    def other_dp(total):
        return swap(rows_at(total, 1 - group, 2 * quarter), on_dp)

    def dp_sum(total, came):
        kept = rows_at(total, group, 2 * quarter).astype(F32) + came.astype(F32)
        return rows_at(kept, high, quarter), rows_at(kept, 1 - high, quarter).astype(BF)

    def quad_sum(kept, came):
        kept = kept + came.astype(F32)
        return rows_at(kept, low, eighth), rows_at(kept, 1 - low, eighth).astype(BF)

    y_came = swap(y_other, on_core)
    down_part = product(dy_all, inner_all, 2)
    y_came, down_part = lax.optimization_barrier((y_came, down_part))
    y_sum = (y_part.astype(F32) + y_came.astype(F32)).reshape(2, 2, local, width)
    y_sent, y_kept = y_sum[:, 1].astype(BF), y_sum[:, 0]
    y_came = swap(y_sent, on_y)
    down_came = other_dp(down_part)
    gate_part, up_part = product(after(two_all, y_sent), d_both_all, 2, cuts=2)
    d_o = product(after(dh_all, gate_part), w_o_t, 0, lanes=out_spread)
    d_o, down_came, y_came = lax.optimization_barrier((d_o, down_came, y_came))
    y_pair = y_kept + y_came.astype(F32)
    y_sent = y_pair[1].astype(BF)
    gate_came = other_dp(after(gate_part, down_came))
    down_keep, down_send = dp_sum(down_part, down_came)
    d_o, down_send, y_sent = lax.optimization_barrier((d_o, down_send, y_sent))
    y_came = swap(y_sent, on_lo)
    down_came = swap(down_send, on_hi)
    dq_all, dkv_own, dkv_sent = call_backward(
        meta,
        q_sorted,
        kv_all,
        d_o,
        index_col,
        index_row,
        cos_place.reshape(2 * rows, LANES),
        sin_place.reshape(2 * rows, LANES),
        scale,
    )

    dkv_got = swap(dkv_sent, on_hi)
    dh_late, dkv_own, down_came = lax.optimization_barrier((dh_all, dkv_own, down_came))
    out_part = product(dh_late, o_all, 2)
    gate_came, out_part = lax.optimization_barrier((gate_came, out_part))
    up_came = other_dp(after(up_part, gate_came))
    gate_keep, gate_send = dp_sum(gate_part, gate_came)
    gate_send, y_came, dkv_got = lax.optimization_barrier((gate_send, y_came, dkv_got))
    gate_came = swap(gate_send, on_hi)
    y_local = (mid + y_pair[0] + y_came.astype(F32)).astype(BF)
    d_all = call_unsort(
        dkv_own, dkv_got, cos_place, sin_place, index_row, dq_all, spread.T, scale
    )
    total_part = jnp.concatenate([product(one_all, d_all, 2), out_part], axis=1)
    up_keep, up_send = dp_sum(up_part, after(up_came, d_all))
    d_one_part, total_part, up_send, gate_came = lax.optimization_barrier(
        (product(d_all, w_qkv, 1), total_part, up_send, gate_came)
    )
    x_grad_rows, both_gains, y_rows, *grads = call_tokens(
        LAST,
        7,
        d_one_part,
        x_low,
        None,
        (),
        gain_a,
        d_mid,
        y_local,
        gain_grad_m,
        (up_send, up_keep, total_part),
    )
    x_grad_rows, down_came, gate_came = lax.optimization_barrier(
        (x_grad_rows, down_came, gate_came)
    )
    down_keep, down_give = quad_sum(down_keep, down_came)
    gate_keep, gate_give = quad_sum(gate_keep, gate_came)
    grad_down_t = by_low(down_keep, swap(down_give, on_lo).astype(F32), 1)
    grad_gate = by_low(gate_keep, swap(gate_give, on_lo).astype(F32), 1)
    grad_up = by_low(grads[0], grads[2].astype(F32), 1)
    keep, got = grads[1], grads[3].astype(F32)
    grad_out_t = by_low(keep[:, all_width:], got[:, all_width:], 1)
    qkv_parts = []
    for first, last in ((0, q_width), (q_width, q_width + kv_width), (q_width + kv_width, all_width)):
        qkv_parts.append(by_low(keep[:, first:last], got[:, first:last], 1))
    grad_query, grad_key, grad_value = qkv_parts
    own_gains = lax.dynamic_slice_in_dim(both_gains, my_index * eighth, eighth, 1)

    send_all = rows_sent(jnp.arange(share, dtype=jnp.int32))
    held = [row * 2 + core, (row ^ 1) * 2 + core, row * 2 + (core ^ 1), (row ^ 1) * 2 + (core ^ 1)]
    from_slot = jnp.concatenate(
        [
            lax.dynamic_slice_in_dim(send_all, device * part, part, 1).reshape(local)
            for device in held
        ]
    )
    output, input_grad = pick_rows(from_slot[None, :], y_rows, x_grad_rows, False)
    return (
        output,
        input_grad,
        own_gains[0],
        grad_query,
        grad_key,
        grad_value,
        grad_out_t.T,
        own_gains[1],
        grad_gate,
        grad_up,
        grad_down_t.T,
    )


def solution(mesh):
    placed = (
        P(TOKEN_AXES, None),
        P(TOKEN_AXES),
        P(TOKEN_AXES, TENSOR),
        P(TOKEN_AXES, TENSOR),
        P(TOKEN_AXES, TENSOR),
        P(TENSOR, TOKEN_AXES),
        P(TOKEN_AXES),
        P(TOKEN_AXES, TENSOR),
        P(TOKEN_AXES, TENSOR),
        P(TENSOR, TOKEN_AXES),
        P(TOKEN_AXES, None),
        P(),
        P(),
        P(),
    )
    paired = tuple(mesh.shape[name] for name in MESH_AXES) == (2, 4, 4)
    return jax.shard_map(
        on_device_paired if paired else on_device,
        mesh=mesh,
        in_specs=placed,
        out_specs=(
            P(TOKEN_AXES, None),
            P(TOKEN_AXES, None),
            P(TOKEN_AXES),
            P(TOKEN_AXES, TENSOR),
            P(TOKEN_AXES, TENSOR),
            P(TOKEN_AXES, TENSOR),
            P(TENSOR, TOKEN_AXES),
            P(TOKEN_AXES),
            P(TOKEN_AXES, TENSOR),
            P(TOKEN_AXES, TENSOR),
            P(TENSOR, TOKEN_AXES),
        ),
        check_vma=False,
    )
```

```python
import functools

import jax
import jax.numpy as jnp
import numpy as np
from jax import lax
from jax.experimental import pallas as pl
from jax.experimental.pallas import tpu as pltpu
from jax.sharding import PartitionSpec as P

HEAD_SIZE = 80
MB = 2


EPS = 1e-05
THETA = 1000000.0
MASKED = -1e30
DP, CONTEXT, TENSOR = "dp", "context", "tensor"
TOKEN_AXES, MESH_AXES = (DP, CONTEXT), (DP, CONTEXT, TENSOR)


def rotate(field, positions, sign):
    half_width = field.shape[-1] // 2
    freq = THETA ** (-2.0 * jnp.arange(half_width, dtype=jnp.float32) / field.shape[-1])
    angle = positions.astype(jnp.float32)[:, None] * freq[None, :]
    cosine = jnp.cos(angle)[:, None, :]
    sine = sign * jnp.sin(angle)[:, None, :]
    first = field[..., :half_width]
    second = field[..., half_width:]
    return jnp.concatenate(
        [first * cosine - second * sine, second * cosine + first * sine], axis=-1
    )


def times_t(left, right):
    return lax.dot_general(
        left, right, (((1,), (1,)), ((), ())), preferred_element_type=jnp.float32
    )


def t_times(left, right):
    return lax.dot_general(
        left, right, (((0,), (0,)), ((), ())), preferred_element_type=jnp.float32
    )


def invert(index):
    count = index.shape[0]
    iota = jnp.arange(count, dtype=jnp.int32)
    return jnp.sum(iota[None, :] * (index[None, :] == iota[:, None]).astype(jnp.int32), axis=1)


def route_plan(order_perm, groups, rows, my_index):
    share = rows // groups
    places = order_perm.reshape(groups, rows)
    source = places // rows
    mine = (source == my_index).astype(jnp.int32)
    rank = jnp.cumsum(mine, axis=1) - 1
    slots = jnp.arange(share, dtype=jnp.int32)
    pick = mine[:, :, None] * (rank[:, :, None] == slots[None, None, :]).astype(jnp.int32)
    send_index = jnp.sum(pick * (places % rows)[:, :, None], axis=1).reshape(rows)
    own = lax.dynamic_index_in_dim(places, my_index, 0, keepdims=False)
    own_source = own // rows
    onehot = (own_source[:, None] == jnp.arange(groups, dtype=jnp.int32)[None, :]).astype(jnp.int32)
    own_rank = jnp.sum((jnp.cumsum(onehot, axis=0) - 1) * onehot, axis=1)
    return (send_index, own_source * share + own_rank)


def pack_places(count, block_rows, half_rows, block_order):
    index = jnp.arange(count, dtype=jnp.int32)
    slot = 2 * (index // block_rows) + index % block_rows // half_rows
    table = (slot[:, None] == jnp.arange(block_order.shape[0], dtype=jnp.int32)[None, :]).astype(
        jnp.int32
    )
    which = jnp.sum(table * block_order[None, :], axis=1)
    return which * half_rows + index % half_rows


def segment_info(places, seq_lengths):
    first = seq_lengths[0]
    second = seq_lengths[0] + seq_lengths[1]
    segment = (places >= first).astype(jnp.int32) + (places >= second).astype(jnp.int32)
    start = jnp.where(segment == 0, 0, jnp.where(segment == 1, first, second))
    return (segment, places - start)


def norm_forward(value_tensor, gain):
    root = lax.rsqrt(jnp.mean(value_tensor * value_tensor, axis=-1, keepdims=True) + EPS)
    return (root, (value_tensor * root * gain).astype(jnp.bfloat16))


def norm_backward(value_tensor, root, gain, grad):
    weighted = grad * gain
    cubed = root * root * root
    d_values = root * weighted - value_tensor * cubed * jnp.mean(
        weighted * value_tensor, axis=-1, keepdims=True
    )
    return (d_values, jnp.sum(grad * value_tensor * root, axis=0))


def key_split(count):
    step = 512
    return (count // step, step)


def block_scores(q_group, key_block, pos_block, seg_block, q_pos, q_seg, scale):
    scores = (
        jnp.einsum("qgrd,kgd->grqk", q_group, key_block, preferred_element_type=jnp.float32) * scale
    )
    allowed = (q_seg[:, None] == seg_block[None, :]) & (pos_block[None, :] <= q_pos[:, None])
    return (jnp.where(allowed, scores, MASKED), allowed)


def key_items(key_tensor, value_tensor, k_pos, k_seg, heads_kv):
    count, step = key_split(key_tensor.shape[0])
    return (
        key_tensor.reshape(count, step, heads_kv, HEAD_SIZE),
        value_tensor.reshape(count, step, heads_kv, HEAD_SIZE),
        k_pos.reshape(count, step),
        k_seg.reshape(count, step),
    )


def attention_forward(q_group, key_tensor, value_tensor, q_pos, q_seg, k_pos, k_seg, scale):
    heads_kv = q_group.shape[1]
    items = key_items(key_tensor, value_tensor, k_pos, k_seg, heads_kv)
    stat_shape = (heads_kv, q_group.shape[2], q_group.shape[0])

    def measure(carry, item):
        top, total = carry
        scores, allowed = block_scores(q_group, item[0], item[2], item[3], q_pos, q_seg, scale)
        new_top = jnp.maximum(top, jnp.max(scores, axis=-1))
        kept = jnp.where(allowed, jnp.exp(scores - new_top[..., None]), 0.0)
        return ((new_top, total * jnp.exp(top - new_top) + jnp.sum(kept, axis=-1)), None)

    start = (jnp.full(stat_shape, MASKED, jnp.float32), jnp.zeros(stat_shape, jnp.float32))
    (top, total), unused = lax.scan(measure, start, items)

    def mix(acc, item):
        scores, allowed = block_scores(q_group, item[0], item[2], item[3], q_pos, q_seg, scale)
        probs = jnp.where(allowed, jnp.exp(scores - top[..., None]) / total[..., None], 0.0).astype(
            jnp.bfloat16
        )
        return (
            acc + jnp.einsum("grqk,kgd->qgrd", probs, item[1], preferred_element_type=jnp.float32),
            None,
        )

    attended, unused = lax.scan(mix, jnp.zeros(q_group.shape, jnp.float32), items)
    return (attended, top, total)


def attention_backward(
    q_group, key_tensor, value_tensor, q_pos, q_seg, k_pos, k_seg, top, total, d_out, delta, scale
):
    heads_kv = q_group.shape[1]
    items = key_items(key_tensor, value_tensor, k_pos, k_seg, heads_kv)
    step = items[2].shape[1]

    def visit(d_query, item):
        scores, allowed = block_scores(q_group, item[0], item[2], item[3], q_pos, q_seg, scale)
        weight = jnp.where(allowed, jnp.exp(scores - top[..., None]) / total[..., None], 0.0)
        d_prob = jnp.einsum("qgrd,kgd->grqk", d_out, item[1], preferred_element_type=jnp.float32)
        d_score = (weight * (d_prob - delta[..., None])).astype(jnp.bfloat16)
        d_query = d_query + jnp.einsum(
            "grqk,kgd->qgrd", d_score, item[0], preferred_element_type=jnp.float32
        )
        d_key = (
            jnp.einsum("grqk,qgrd->kgd", d_score, q_group, preferred_element_type=jnp.float32)
            * scale
        )
        d_value = jnp.einsum(
            "grqk,qgrd->kgd", weight.astype(jnp.bfloat16), d_out, preferred_element_type=jnp.float32
        )
        return (d_query, (d_key.reshape(step, -1), d_value.reshape(step, -1)))

    d_query, (d_keys, d_values) = lax.scan(visit, jnp.zeros(q_group.shape, jnp.float32), items)
    return (
        d_query * scale,
        d_keys.reshape(key_tensor.shape[0], -1),
        d_values.reshape(key_tensor.shape[0], -1),
    )


def fetch_attention(gain_attn, w_query, key_weight, value_weight, w_out):
    return (
        lax.all_gather(gain_attn, TOKEN_AXES, axis=0, tiled=True),
        lax.all_gather(w_query, TOKEN_AXES, axis=0, tiled=True),
        lax.all_gather(key_weight, TOKEN_AXES, axis=0, tiled=True),
        lax.all_gather(value_weight, TOKEN_AXES, axis=0, tiled=True),
        lax.all_gather(w_out, TOKEN_AXES, axis=1, tiled=True),
    )


def fetch_mlp(gain_mlp, w_gate, w_up, w_down):
    return (
        lax.all_gather(gain_mlp, TOKEN_AXES, axis=0, tiled=True),
        lax.all_gather(w_gate, TOKEN_AXES, axis=0, tiled=True),
        lax.all_gather(w_up, TOKEN_AXES, axis=0, tiled=True),
        lax.all_gather(w_down, TOKEN_AXES, axis=1, tiled=True),
    )


def head_sum(partial_sum):
    return lax.psum(partial_sum.astype(jnp.bfloat16), TENSOR).astype(jnp.float32)


def on_device(
    tokens,
    gain_attn,
    w_query,
    key_weight,
    value_weight,
    w_out,
    gain_mlp,
    w_gate,
    w_up,
    w_down,
    cotangent,
    lengths,
    order_perm,
    block_order,
):
    devices_ctx = lax.axis_size(CONTEXT)
    groups = lax.axis_size(DP) * devices_ctx
    group_id = lax.axis_index(DP)
    place = lax.axis_index(CONTEXT)
    my_index = group_id * devices_ctx + place
    rows = tokens.shape[0]
    width = tokens.shape[1]
    block_rows = rows // MB
    half_rows = block_rows // 2
    share = rows // groups
    scale = HEAD_SIZE ** (-0.5)
    send_index, recv_index = route_plan(order_perm, groups, rows, my_index)
    arrived = (
        lax.all_to_all(
            tokens[send_index].reshape(groups, share, width),
            TOKEN_AXES,
            split_axis=0,
            concat_axis=0,
            tiled=True,
        ),
        lax.all_to_all(
            cotangent[send_index].reshape(groups, share, width),
            TOKEN_AXES,
            split_axis=0,
            concat_axis=0,
            tiled=True,
        ),
    )
    seq_tokens = arrived[0].reshape(rows, width)[recv_index]
    seq_cot = arrived[1].reshape(rows, width)[recv_index]
    whole_place = pack_places(block_rows * devices_ctx, block_rows, half_rows, block_order)
    acc_gain_a = jnp.zeros((width,), jnp.float32)
    acc_query = jnp.zeros((width, w_query.shape[1]), jnp.float32)
    acc_key = jnp.zeros((width, key_weight.shape[1]), jnp.float32)
    acc_value = jnp.zeros((width, value_weight.shape[1]), jnp.float32)
    acc_out = jnp.zeros((w_out.shape[0], width), jnp.float32)
    acc_gain_m = jnp.zeros((width,), jnp.float32)
    acc_gate = jnp.zeros((width, w_gate.shape[1]), jnp.float32)
    acc_up = jnp.zeros((width, w_up.shape[1]), jnp.float32)
    acc_down = jnp.zeros((w_down.shape[0], width), jnp.float32)
    outputs = []
    input_grads = []
    for micro in range(MB):
        seq_lengths = lax.dynamic_index_in_dim(lengths, group_id * MB + micro, 0, keepdims=False)
        key_seg, key_pos = segment_info(whole_place, seq_lengths)
        q_seg = lax.dynamic_slice_in_dim(key_seg, place * block_rows, block_rows)
        q_pos = lax.dynamic_slice_in_dim(key_pos, place * block_rows, block_rows)
        inputs_f = seq_tokens[micro * block_rows : (micro + 1) * block_rows].astype(jnp.float32)
        d_y = seq_cot[micro * block_rows : (micro + 1) * block_rows]
        attn_now = fetch_attention(gain_attn, w_query, key_weight, value_weight, w_out)
        gain_a, w_q, w_k, w_v, w_o = attn_now
        root_a, normed_one = norm_forward(inputs_f, gain_a.astype(jnp.float32))
        q_lin = jnp.dot(normed_one, w_q, preferred_element_type=jnp.float32)
        k_lin = jnp.dot(normed_one, w_k, preferred_element_type=jnp.float32)
        v_lin = jnp.dot(normed_one, w_v, preferred_element_type=jnp.float32)
        heads_kv = k_lin.shape[1] // HEAD_SIZE
        q_group = rotate(q_lin.reshape(block_rows, -1, HEAD_SIZE), q_pos, 1.0).astype(jnp.bfloat16)
        q_group = q_group.reshape(block_rows, heads_kv, -1, HEAD_SIZE)
        k_in = (
            rotate(k_lin.reshape(block_rows, heads_kv, HEAD_SIZE), q_pos, 1.0)
            .astype(jnp.bfloat16)
            .reshape(block_rows, -1)
        )
        v_in = v_lin.astype(jnp.bfloat16)
        key_tensor, value_tensor = (
            lax.all_gather(k_in, CONTEXT, axis=0, tiled=True),
            lax.all_gather(v_in, CONTEXT, axis=0, tiled=True),
        )
        attended, top, total = attention_forward(
            q_group, key_tensor, value_tensor, q_pos, q_seg, key_pos, key_seg, scale
        )
        o_in = attended.reshape(block_rows, -1).astype(jnp.bfloat16)
        mid_state = inputs_f + head_sum(jnp.dot(o_in, w_o, preferred_element_type=jnp.float32))
        mlp_now = fetch_mlp(gain_mlp, w_gate, w_up, w_down)
        gain_m, w_g, w_u, w_d = mlp_now
        root_m, normed_two = norm_forward(mid_state, gain_m.astype(jnp.float32))
        gate = jnp.dot(normed_two, w_g, preferred_element_type=jnp.float32)
        up_proj = jnp.dot(normed_two, w_u, preferred_element_type=jnp.float32)
        sigma = jax.nn.sigmoid(gate)
        silu_gate = gate * sigma
        inner = (silu_gate * up_proj).astype(jnp.bfloat16)
        result = mid_state + head_sum(jnp.dot(inner, w_d, preferred_element_type=jnp.float32))
        outputs.append(result.astype(jnp.bfloat16))
        mlp_back = fetch_mlp(gain_mlp, w_gate, w_up, w_down)
        gain_m, w_g, w_u, w_d = mlp_back
        d_inner = times_t(d_y, w_d)
        acc_down = acc_down + t_times(inner, d_y)
        d_gate = (d_inner * up_proj * sigma * (1.0 + gate * (1.0 - sigma))).astype(jnp.bfloat16)
        d_up = (d_inner * silu_gate).astype(jnp.bfloat16)
        d_two = head_sum(times_t(d_gate, w_g) + times_t(d_up, w_u))
        acc_gate = acc_gate + t_times(normed_two, d_gate)
        acc_up = acc_up + t_times(normed_two, d_up)
        d_mid, gain_grad_m = norm_backward(mid_state, root_m, gain_m.astype(jnp.float32), d_two)
        acc_gain_m = acc_gain_m + gain_grad_m
        d_mid = d_y.astype(jnp.float32) + d_mid
        d_mid_low = d_mid.astype(jnp.bfloat16)
        attn_back = fetch_attention(gain_attn, w_query, key_weight, value_weight, w_out)
        gain_a, w_q, w_k, w_v, w_o = attn_back
        acc_out = acc_out + t_times(o_in, d_mid_low)
        d_out = times_t(d_mid_low, w_o).astype(jnp.bfloat16).reshape(q_group.shape)
        delta = jnp.sum(d_out.astype(jnp.float32) * attended, axis=-1).transpose(1, 2, 0)
        d_query, d_keys, d_values = attention_backward(
            q_group,
            key_tensor,
            value_tensor,
            q_pos,
            q_seg,
            key_pos,
            key_seg,
            top,
            total,
            d_out,
            delta,
            scale,
        )
        own_keys, own_values = (
            lax.psum_scatter(
                d_keys.astype(jnp.bfloat16), CONTEXT, scatter_dimension=0, tiled=True
            ).astype(jnp.float32),
            lax.psum_scatter(
                d_values.astype(jnp.bfloat16), CONTEXT, scatter_dimension=0, tiled=True
            ).astype(jnp.float32),
        )
        d_q_low = (
            rotate(d_query.reshape(block_rows, -1, HEAD_SIZE), q_pos, -1.0)
            .astype(jnp.bfloat16)
            .reshape(block_rows, -1)
        )
        d_k_low = (
            rotate(own_keys.reshape(block_rows, -1, HEAD_SIZE), q_pos, -1.0)
            .astype(jnp.bfloat16)
            .reshape(block_rows, -1)
        )
        d_v_low = own_values.astype(jnp.bfloat16)
        d_one = head_sum(times_t(d_q_low, w_q) + times_t(d_k_low, w_k) + times_t(d_v_low, w_v))
        acc_query = acc_query + t_times(normed_one, d_q_low)
        acc_key = acc_key + t_times(normed_one, d_k_low)
        acc_value = acc_value + t_times(normed_one, d_v_low)
        d_inputs, gain_grad_a = norm_backward(inputs_f, root_a, gain_a.astype(jnp.float32), d_one)
        acc_gain_a = acc_gain_a + gain_grad_a
        input_grads.append((d_mid + d_inputs).astype(jnp.bfloat16))
    grads_attn = (
        lax.psum_scatter(
            acc_gain_a.astype(jnp.bfloat16), TOKEN_AXES, scatter_dimension=0, tiled=True
        ).astype(jnp.float32),
        lax.psum_scatter(
            acc_query.astype(jnp.bfloat16), TOKEN_AXES, scatter_dimension=0, tiled=True
        ).astype(jnp.float32),
        lax.psum_scatter(
            acc_key.astype(jnp.bfloat16), TOKEN_AXES, scatter_dimension=0, tiled=True
        ).astype(jnp.float32),
        lax.psum_scatter(
            acc_value.astype(jnp.bfloat16), TOKEN_AXES, scatter_dimension=0, tiled=True
        ).astype(jnp.float32),
        lax.psum_scatter(
            acc_out.astype(jnp.bfloat16), TOKEN_AXES, scatter_dimension=1, tiled=True
        ).astype(jnp.float32),
    )
    grads_mlp = (
        lax.psum_scatter(
            acc_gain_m.astype(jnp.bfloat16), TOKEN_AXES, scatter_dimension=0, tiled=True
        ).astype(jnp.float32),
        lax.psum_scatter(
            acc_gate.astype(jnp.bfloat16), TOKEN_AXES, scatter_dimension=0, tiled=True
        ).astype(jnp.float32),
        lax.psum_scatter(
            acc_up.astype(jnp.bfloat16), TOKEN_AXES, scatter_dimension=0, tiled=True
        ).astype(jnp.float32),
        lax.psum_scatter(
            acc_down.astype(jnp.bfloat16), TOKEN_AXES, scatter_dimension=1, tiled=True
        ).astype(jnp.float32),
    )
    seq_out = jnp.concatenate(outputs, axis=0)
    seq_grad = jnp.concatenate(input_grads, axis=0)
    back_index = invert(recv_index)
    returned = (
        lax.all_to_all(
            seq_out[back_index].reshape(groups, share, width),
            TOKEN_AXES,
            split_axis=0,
            concat_axis=0,
            tiled=True,
        ),
        lax.all_to_all(
            seq_grad[back_index].reshape(groups, share, width),
            TOKEN_AXES,
            split_axis=0,
            concat_axis=0,
            tiled=True,
        ),
    )
    data_index = invert(send_index)
    output = returned[0].reshape(rows, width)[data_index]
    input_grad = returned[1].reshape(rows, width)[data_index]
    return (
        output,
        input_grad,
        grads_attn[0],
        grads_attn[1],
        grads_attn[2],
        grads_attn[3],
        grads_attn[4],
        grads_mlp[0],
        grads_mlp[1],
        grads_mlp[2],
        grads_mlp[3],
    )


BF = jnp.bfloat16
F32 = jnp.float32
TILE = 256
LANES = 128
GROUP = 4
QUICK = pl.CostEstimate(flops=10**6, bytes_accessed=10**5, transcendentals=0)


def mm(left, right):
    return jnp.dot(left, right, preferred_element_type=F32)


def one_hot(rows, columns):
    return jnp.where(rows == columns, 1.0, 0.0).astype(BF)


def turn(u, cosine, sine):
    return u * cosine + pltpu.roll(u, LANES // 2, 1) * sine


def place_rows(index_col_ref, count):
    column = index_col_ref[0]
    lanes = lax.broadcasted_iota(jnp.int32, (column.shape[0], count), 1)
    return one_hot(lanes, column)


def arrival_rows(index_row_ref, count):
    row = index_row_ref[0]
    rows = lax.broadcasted_iota(jnp.int32, (count, row.shape[1]), 0)
    return one_hot(rows, row)


FLAG = HEAD_SIZE // 2


def flagged(value, flag):
    lanes = lax.broadcasted_iota(jnp.int32, value.shape, 1)
    return jnp.where(lanes % LANES == FLAG, flag, value)


def sort_kernel(mine, other, weight, cosine, sine, index_col, flag, out, picks, *, turned):
    @pl.when(pl.program_id(1) == 0)
    def _():
        picks[...] = place_rows(index_col, picks.shape[1])

    u = jnp.concatenate([mm(mine[...], weight[...]), mm(other[...], weight[...])], axis=0)
    cos_t, sin_t = cosine[0], sine[0]
    parts = [turn(u[:, :LANES], cos_t, sin_t), u[:, LANES:]]
    if turned == 2:
        parts[1] = turn(parts[1], cos_t, sin_t)
    moved = mm(picks[...], jnp.concatenate(parts, axis=1).astype(BF))
    if turned == 2:
        out[...] = flagged(moved, flag[0]).astype(BF)
    else:
        out[:, :LANES] = flagged(moved[:, :LANES], flag[0]).astype(BF)
        out[:, LANES:] = moved[:, LANES:].astype(BF)


def causal_bias():
    rows = lax.broadcasted_iota(jnp.int32, (TILE, TILE), 0)
    lanes = lax.broadcasted_iota(jnp.int32, (TILE, TILE), 1)
    return jnp.where(lanes <= rows, 0.0, MASKED)


def probabilities(q_head, keys, bias, scale):
    scores = times_t(q_head, keys)
    last = scores[:, -TILE:] + bias
    scores = jnp.concatenate([scores[:, :-TILE], last], axis=1) if keys.shape[0] > TILE else last
    top = jnp.max(scores, axis=1, keepdims=True)
    raised = jnp.exp2((scores - top) * (scale * 1.4426950408889634))
    return raised * (1.0 / jnp.sum(raised, axis=1, keepdims=True))


def fetch_keys(meta, block, kv, keys, values, count):
    for item in range(count):
        start = pl.multiple_of(meta[block, 1 + item], TILE)
        rows = pl.ds(item * TILE, TILE)
        keys[rows, :] = kv[pl.ds(start, TILE), :LANES]
        values[rows, :] = kv[pl.ds(start, TILE), LANES:]


def head_of(index):
    return slice(index * LANES, (index + 1) * LANES)


def forward_kernel(
    meta, q, kv, index_row, unpad, out, total, bias, keys, values, *, scale, blocks, per_run
):
    block = pl.program_id(0)
    part = lax.rem(block, per_run)
    run_rows = total.shape[0]

    @pl.when(block == 0)
    def _():
        bias[...] = causal_bias()

    def attend(count):
        fetch_keys(meta, block, kv, keys, values, count)
        size = count * TILE
        mixed = []
        for head in range(GROUP):
            probs = probabilities(q[:, head_of(head)], keys[:size, :], bias[...], scale)
            mixed.append(mm(probs.astype(BF), values[:size, :]).astype(BF))
        moved = mm(arrival_rows(index_row, run_rows), jnp.concatenate(mixed, axis=1))

        @pl.when(part == 0)
        def _():
            total[...] = moved

        @pl.when(part > 0)
        def _():
            total[...] += moved

    for count in range(1, blocks + 1):
        pl.when(meta[block, 0] == count - 1)(functools.partial(attend, count))

    @pl.when(part == per_run - 1)
    def _():
        packed = mm(total[...].astype(BF), unpad[...]).astype(BF)
        half = run_rows // 2
        first = pl.multiple_of(block // per_run * half, TILE)
        out[pl.ds(first, half), :] = packed[:half]
        out[pl.ds(2 * half + first, half), :] = packed[half:]


def backward_kernel(
    meta,
    q,
    kv,
    d_mine,
    d_other,
    index_col,
    index_row,
    cosine,
    sine,
    q_grad,
    own,
    sent,
    total,
    bias,
    keys,
    values,
    probs_all,
    scores_all,
    keys_grad,
    *,
    scale,
    blocks,
    per_run,
):
    block = pl.program_id(0)
    part = lax.rem(block, per_run)
    run_rows = total.shape[0]
    half = run_rows // 2

    @pl.when(block == 0)
    def _():
        keys_grad[...] = jnp.zeros_like(keys_grad)
        bias[...] = causal_bias()

    def attend(count):
        fetch_keys(meta, block, kv, keys, values, count)
        size = count * TILE
        places = place_rows(index_col, run_rows)
        d_out = mm(places[:, :half], d_mine[...]) + mm(places[:, half:], d_other[...])
        d_out = d_out.astype(BF)
        turned = []
        for head in range(GROUP):
            rows = pl.ds(head * TILE, TILE)
            probs = probabilities(q[:, head_of(head)], keys[:size, :], bias[...], scale)
            probs_all[rows, :size] = probs.astype(BF)
            d_probs = times_t(d_out[:, head_of(head)], values[:size, :])
            delta = jnp.sum(probs * d_probs, axis=1, keepdims=True)
            d_score = (probs * (d_probs - delta)).astype(BF)
            scores_all[rows, :size] = d_score
            d_query = flagged(mm(d_score, keys[:size, :]) * scale, 0.0)
            turned.append(turn(d_query, cosine[...], -sine[...]).astype(BF))
        heads = [head_of(head) for head in range(GROUP)]
        q_all = jnp.concatenate([q[:, at] for at in heads], axis=0)
        d_all = jnp.concatenate([d_out[:, at] for at in heads], axis=0)
        d_keys = t_times(scores_all[:, :size], q_all)
        d_values = t_times(probs_all[:, :size], d_all)
        for item in range(count):
            rows = pl.ds(pl.multiple_of(meta[block, 1 + item], TILE), TILE)
            keys_grad[rows, :LANES] += d_keys[item * TILE : (item + 1) * TILE]
            keys_grad[rows, LANES:] += d_values[item * TILE : (item + 1) * TILE]
        moved = mm(arrival_rows(index_row, run_rows), jnp.concatenate(turned, axis=1))

        @pl.when(part == 0)
        def _():
            total[...] = moved

        @pl.when(part > 0)
        def _():
            total[...] += moved

    for count in range(1, blocks + 1):
        pl.when(meta[block, 0] == count - 1)(functools.partial(attend, count))

    @pl.when(part == per_run - 1)
    def _():
        first = pl.multiple_of(block // per_run * half, TILE)
        q_grad[pl.ds(first, half), :] = total[:half].astype(BF)
        q_grad[pl.ds(2 * half + first, half), :] = total[half:].astype(BF)

    @pl.when(block == pl.num_programs(0) - 1)
    def _():
        count = own.shape[0]
        own[...] = keys_grad[:count]
        sent[...] = keys_grad[count:].astype(BF)


def unsort_kernel(own, got, cosine, sine, index_row, q_mine, q_other, unpad, out, *, scale):
    both = own[...] + got[...].astype(F32)
    d_keys = turn(both[:, :LANES] * scale, cosine[0], -sine[0])
    low = jnp.concatenate([d_keys, both[:, LANES:]], axis=1).astype(BF)
    moved = mm(arrival_rows(index_row, low.shape[0]), low).astype(BF)
    half = moved.shape[0] // 2
    split = q_mine.shape[1]
    first = pl.multiple_of(pl.program_id(0) * half, TILE)
    for rows, d_query, at in (
        (moved[:half], q_mine, first),
        (moved[half:], q_other, 2 * half + first),
    ):
        packed = mm(d_query[...], unpad[:split]) + mm(rows, unpad[split:])
        out[pl.ds(at, half), :] = packed.astype(BF)


def resident(shape):
    return pl.BlockSpec(shape, lambda *unused: (0,) * len(shape))


def call_sort(tokens, weight, cosine, sine, index_col, flag, turned):
    count, width = tokens.shape
    run_rows = count // 2
    half = run_rows // 2
    wide = 2 * LANES
    steps = weight.shape[1] // wide
    table = pl.BlockSpec((1, run_rows, LANES), lambda d, g: (d, 0, 0))
    column = pl.BlockSpec((1, run_rows, 1), lambda d, g: (d, 0, 0))
    return pl.pallas_call(
        functools.partial(sort_kernel, turned=turned),
        grid=(2, steps),
        in_specs=[
            pl.BlockSpec((half, width), lambda d, g: (d, 0)),
            pl.BlockSpec((half, width), lambda d, g: (2 + d, 0)),
            pl.BlockSpec((width, wide), lambda d, g: (0, g)),
            table,
            table,
            column,
            column,
        ],
        out_specs=pl.BlockSpec((run_rows, wide), lambda d, g: (d, g)),
        out_shape=jax.ShapeDtypeStruct((count, weight.shape[1]), BF),
        scratch_shapes=[pltpu.VMEM((run_rows, run_rows), BF)],
        compiler_params=pltpu.CompilerParams(vmem_limit_bytes=48 * 2**20),
        cost_estimate=QUICK,
        name="sort_tokens",
    )(tokens, tokens, weight, cosine, sine, index_col, flag)


def call_forward(meta, q, kv, index_row, unpad, scale):
    tokens = q.shape[0]
    run_rows = tokens // 2
    per_run = run_rows // TILE
    blocks = meta.shape[1] - 1
    body = functools.partial(forward_kernel, scale=scale, blocks=blocks, per_run=per_run)
    out = jax.ShapeDtypeStruct((tokens, unpad.shape[1]), BF)
    return pl.pallas_call(
        body,
        grid=(2 * per_run,),
        in_specs=[
            pl.BlockSpec(memory_space=pltpu.SMEM),
            pl.BlockSpec((TILE, GROUP * LANES), lambda b: (b, 0)),
            resident(kv.shape),
            pl.BlockSpec((1, 1, TILE), lambda b: (b // per_run, 0, b % per_run)),
            resident(unpad.shape),
        ],
        out_specs=resident(out.shape),
        out_shape=out,
        scratch_shapes=[
            pltpu.VMEM((run_rows, GROUP * LANES), F32),
            pltpu.VMEM((TILE, TILE), F32),
            pltpu.VMEM((blocks * TILE, LANES), BF),
            pltpu.VMEM((blocks * TILE, LANES), BF),
        ],
        compiler_params=pltpu.CompilerParams(vmem_limit_bytes=48 * 2**20),
        cost_estimate=QUICK,
        name="attention_forward",
    )(meta, q, kv, index_row, unpad)


def call_backward(meta, q, kv, d_out, index_col, index_row, cosine, sine, scale):
    tokens = q.shape[0]
    run_rows = tokens // 2
    per_run = run_rows // TILE
    blocks = meta.shape[1] - 1
    body = functools.partial(backward_kernel, scale=scale, blocks=blocks, per_run=per_run)
    run_half = run_rows // 2
    shape = (tokens, 2 * LANES)
    table = pl.BlockSpec((TILE, LANES), lambda b: (b, 0))
    return pl.pallas_call(
        body,
        grid=(2 * per_run,),
        in_specs=[
            pl.BlockSpec(memory_space=pltpu.SMEM),
            pl.BlockSpec((TILE, GROUP * LANES), lambda b: (b, 0)),
            resident(kv.shape),
            pl.BlockSpec((run_half, GROUP * LANES), lambda b: (b // per_run, 0)),
            pl.BlockSpec((run_half, GROUP * LANES), lambda b: (2 + b // per_run, 0)),
            pl.BlockSpec((1, TILE, 1), lambda b: (b // per_run, b % per_run, 0)),
            pl.BlockSpec((1, 1, TILE), lambda b: (b // per_run, 0, b % per_run)),
            table,
            table,
        ],
        out_specs=[resident(q.shape), resident(shape), resident(shape)],
        out_shape=[
            jax.ShapeDtypeStruct(q.shape, BF),
            jax.ShapeDtypeStruct(shape, F32),
            jax.ShapeDtypeStruct(shape, BF),
        ],
        scratch_shapes=[
            pltpu.VMEM((run_rows, GROUP * LANES), F32),
            pltpu.VMEM((TILE, TILE), F32),
            pltpu.VMEM((blocks * TILE, LANES), BF),
            pltpu.VMEM((blocks * TILE, LANES), BF),
            pltpu.VMEM((GROUP * TILE, blocks * TILE), BF),
            pltpu.VMEM((GROUP * TILE, blocks * TILE), BF),
            pltpu.VMEM((kv.shape[0], 2 * LANES), F32),
        ],
        compiler_params=pltpu.CompilerParams(vmem_limit_bytes=56 * 2**20),
        cost_estimate=QUICK,
        name="attention_backward",
    )(meta, q, kv, d_out, d_out, index_col, index_row, cosine, sine)


def call_unsort(own, got, cosine, sine, index_row, q_grad, unpad, scale):
    tokens, wide = own.shape
    run_rows = tokens // 2
    half = run_rows // 2
    table = pl.BlockSpec((1, run_rows, LANES), lambda d: (d, 0, 0))
    out = jax.ShapeDtypeStruct((tokens, unpad.shape[1]), BF)
    return pl.pallas_call(
        functools.partial(unsort_kernel, scale=scale),
        grid=(2,),
        in_specs=[
            pl.BlockSpec((run_rows, wide), lambda d: (d, 0)),
            pl.BlockSpec((run_rows, wide), lambda d: (d, 0)),
            table,
            table,
            pl.BlockSpec((1, 1, run_rows), lambda d: (d, 0, 0)),
            pl.BlockSpec((half, q_grad.shape[1]), lambda d: (d, 0)),
            pl.BlockSpec((half, q_grad.shape[1]), lambda d: (2 + d, 0)),
            resident(unpad.shape),
        ],
        out_specs=resident(out.shape),
        out_shape=out,
        compiler_params=pltpu.CompilerParams(vmem_limit_bytes=40 * 2**20),
        cost_estimate=QUICK,
        name="unsort_tokens",
    )(own, got, cosine, sine, index_row, q_grad, q_grad, unpad)


def product_kernel(left, right, *outs, form, spread):
    contract = ((1,), (0,)) if form == 0 else ((1,), (1,)) if form == 1 else ((0,), (0,))
    value = lax.dot_general(
        left[...], right[...], (contract, ((), ())), preferred_element_type=F32
    ).astype(BF)
    if spread:
        outs[0][...] = mm(value, outs[-1][...]).astype(BF)
        return
    first = 0
    for out in outs:
        out[...] = value[:, first : first + out.shape[1]]
        first += out.shape[1]


def spread_kernel(left, right, lanes, out, *, form):
    product_kernel(left, right, out, lanes, form=form, spread=True)


def product(left, right, form, cuts=1, lanes=None):
    block = 2 * TILE
    count = left.shape[1 if form == 2 else 0]
    columns = right.shape[0 if form == 1 else 1]
    whole = lambda value: pl.BlockSpec(value.shape, lambda i: (0, 0))
    if form == 2:
        left_spec = pl.BlockSpec((left.shape[0], block), lambda i: (0, i))
    else:
        left_spec = pl.BlockSpec((block, left.shape[1]), lambda i: (i, 0))
    operands, in_specs = [left, right], [left_spec, whole(right)]
    body = functools.partial(product_kernel, form=form, spread=False)
    if lanes is not None:
        operands.append(lanes)
        in_specs.append(whole(lanes))
        body = functools.partial(spread_kernel, form=form)
        columns = lanes.shape[1]
    width = columns // cuts
    outs = pl.pallas_call(
        body,
        grid=(count // block,),
        in_specs=in_specs,
        out_specs=[pl.BlockSpec((block, width), lambda i: (i, 0))] * cuts,
        out_shape=[jax.ShapeDtypeStruct((count, width), BF)] * cuts,
        compiler_params=pltpu.CompilerParams(vmem_limit_bytes=48 * 2**20),
        cost_estimate=QUICK,
        name="product",
    )(*operands)
    return outs if cuts > 1 else outs[0]


def pick_kernel(index, first, second, first_out, second_out, *, by_column):
    count = first.shape[0]
    if by_column:
        lanes = lax.broadcasted_iota(jnp.int32, (first_out.shape[0], count), 1)
        hits = one_hot(lanes, index[...])
    else:
        rows = lax.broadcasted_iota(jnp.int32, (first_out.shape[0], count), 0)
        hits = one_hot(rows + pl.program_id(0) * first_out.shape[0], index[...])
    first_out[...] = mm(hits, first[...]).astype(BF)
    second_out[...] = mm(hits, second[...]).astype(BF)


def pick_rows(index, first, second, by_column):
    count, width = first.shape
    total = index.shape[0 if by_column else 1]
    block = min(total, TILE)
    whole = pl.BlockSpec((count, width), lambda i: (0, 0))
    if by_column:
        index_spec = pl.BlockSpec((block, 1), lambda i: (i, 0))
    else:
        index_spec = pl.BlockSpec((1, total), lambda i: (0, 0))
    out = jax.ShapeDtypeStruct((total, width), BF)
    return pl.pallas_call(
        functools.partial(pick_kernel, by_column=by_column),
        grid=(total // block,),
        in_specs=[index_spec, whole, whole],
        out_specs=[pl.BlockSpec((block, width), lambda i: (i, 0))] * 2,
        out_shape=[out, out],
        compiler_params=pltpu.CompilerParams(vmem_limit_bytes=48 * 2**20),
        cost_estimate=QUICK,
        name="pick_rows",
    )(index, first, second)


ROUNDS = 4
FIRST, MIDDLE, BACK, LAST, PLAIN, SUM = range(6)
KINDS = 13
CORE, RY, RL, SL, SY, GY, GL, GC, FL, FY, CY, CL, CC = range(KINDS)
MESH_IDS = pl.DeviceIdType.MESH


def partners():
    group, place, shard = (lax.axis_index(name) for name in MESH_AXES)
    return (
        (group, place, shard + 2 - 4 * (shard // 2)),
        (group, place + 1 - 2 * (place % 2), shard),
        (group, place, shard + 1 - 2 * (shard % 2)),
    )


def route_partner(q, e):
    group, place, shard = (lax.axis_index(name) for name in MESH_AXES)
    high, low = place // 2, place % 2
    group = 1 - group if q // 2 else group
    high = 1 - high if q % 2 else high
    low = 1 - low if e else low
    return (group, 2 * high + low, shard), 4 * group + 2 * high + low


ROUTES = [(q, e) for q in range(4) for e in range(2)]


class Router:
    def __init__(self, src, dst, send_sem, recv_sem, local_sem, spread=False):
        self.src, self.dst, self.copies, self.spread = src, dst, {}, spread
        self.send_sem, self.recv_sem, self.local_sem = send_sem, recv_sem, local_sem
        self.size = src.shape[0]
        self.share = self.size // len(ROUTES)

    def rows(self, index, slot=0):
        return pl.ds(pl.multiple_of(slot * self.size + index * self.share, 16), self.share)

    def start(self, what, q, e, src, dst, device):
        at = what * len(ROUTES) + 2 * q + e
        copy = pltpu.make_async_remote_copy(
            src_ref=src,
            dst_ref=dst,
            send_sem=self.send_sem.at[at],
            recv_sem=self.recv_sem.at[at],
            device_id=device,
            device_id_type=MESH_IDS,
        )
        copy.start()
        self.copies[what, q, e] = copy

    def send(self, q, e):
        device, index = route_partner(q, e)
        own = route_partner(0, 0)[1]
        if (q, e) == (0, 0):
            copy = pltpu.make_async_copy(
                self.src.at[self.rows(own), :], self.dst.at[self.rows(own), :], self.local_sem
            )
            copy.start()
            self.copies[0, 0, 0] = copy
        else:
            self.start(
                0, q, e, self.src.at[self.rows(index), :], self.dst.at[self.rows(own), :], device
            )

    def arrived(self, what, q, e):
        copy = self.copies[what, q, e]
        if (what, q, e) == (0, 0, 0):
            copy.wait()
        else:
            copy.wait_recv()

    def pass_on(self, q, e):
        on_y, unused, on_core = partners()
        index = route_partner(q, e)[1]
        self.arrived(0, q, e)
        here = self.dst.at[self.rows(index), :]
        self.start(1, q, e, here, self.dst.at[self.rows(index, 1), :], on_y)
        self.start(2, q, e, here, self.dst.at[self.rows(index, 2), :], on_core)

    def pass_corner(self, q, e):
        on_core = partners()[2]
        index = route_partner(q, e)[1]
        self.arrived(1, q, e)
        here = self.dst.at[self.rows(index, 1), :]
        self.start(3, q, e, here, self.dst.at[self.rows(index, 3), :], on_core)

    def finish(self):
        for (what, q, e), copy in self.copies.items():
            if (what, q, e) != (0, 0, 0):
                copy.wait_send()
            if what in (2, 3) or not self.spread:
                self.arrived(what, q, e)


PIECES = 8


class Pieces:
    def __init__(self, buffer, send_sem, recv_sem):
        self.buffer, self.send_sem, self.recv_sem = buffer, send_sem, recv_sem
        self.used, self.near = [], []
        self.quarter = buffer.shape[0] // 4
        self.step = self.quarter // PIECES
        self.on_hi = route_partner(1, 0)[0]
        self.on_dp = route_partner(2, 0)[0]

    def copy(self, what, piece):
        group, place = lax.axis_index(DP), lax.axis_index(CONTEXT)
        low, high = place % 2, place // 2
        high = 1 - high if what == 2 else high
        half = low if piece < PIECES // 2 else 1 - low
        first = (2 * group + high) * self.quarter + half * (self.quarter // 2)
        first = pl.multiple_of(first + piece % (PIECES // 2) * self.step, 16)
        at = self.buffer.at[pl.ds(first, self.step), :]
        return pltpu.make_async_remote_copy(
            src_ref=at,
            dst_ref=at,
            send_sem=self.send_sem.at[what, piece],
            recv_sem=self.recv_sem.at[what, piece],
            device_id=self.on_dp if what else self.on_hi,
            device_id_type=MESH_IDS,
        )

    def send(self, piece):
        self.copy(0, piece).start()
        self.copy(1, piece).start()
        self.used.append(piece)

    def pass_on(self, piece):
        self.copy(0, piece).wait_recv()
        self.copy(2, piece).start()

    def spread(self, piece):
        self.copy(1, piece).start()
        self.copy(2, piece).start()
        self.near.append(piece)

    def finish(self):
        for piece in self.used + self.near:
            for what in range(3):
                if what == 0 and piece in self.near:
                    continue
                copy = self.copy(what, piece)
                copy.wait_send()
                if what > 0:
                    copy.wait_recv()


def piece_scratch():
    return [pltpu.SemaphoreType.DMA((3, PIECES))] * 2


def route_scratch(parts):
    return [
        pltpu.SemaphoreType.DMA((parts * len(ROUTES),)),
        pltpu.SemaphoreType.DMA((parts * len(ROUTES),)),
        pltpu.SemaphoreType.DMA(()),
    ]


def greet(devices):
    barrier = pltpu.get_barrier_semaphore()
    for device in devices:
        pl.semaphore_signal(barrier, inc=1, device_id=device, device_id_type=MESH_IDS)
    pl.semaphore_wait(barrier, len(devices))


def root_of(value):
    return lax.rsqrt(jnp.mean(value * value, axis=-1, keepdims=True) + EPS)


def norm_gradient(value, gain, grad):
    root = root_of(value)
    weighted = grad * gain
    return root * weighted - value * (root * root * root) * jnp.mean(
        weighted * value, axis=-1, keepdims=True
    ), jnp.sum(grad * value * root, axis=0, keepdims=True)


def token_kernel(*refs, kind, scatter, gather, pieces):
    refs = list(refs)
    take = lambda count: [refs.pop(0) for unused in range(count)]
    if scatter:
        (parts,) = take(1)
    (x_ref,) = take(1)
    if kind in (FIRST, LAST):
        (gain,) = take(1)
    if kind == PLAIN:
        (own_kv,) = take(1)
    if kind == LAST:
        (add_ref,) = take(1)
    if kind == LAST:
        aside, other_gain = take(2)
        near_send, near_keep, total = take(3)
    else:
        (bulk,) = take(1)
    if kind == PLAIN:
        (all_kv,) = take(1)
    if gather:
        (everyone,) = take(1)
    if kind == LAST:
        grad_out, gains_out, aside_out = take(3)
        kept, gotten = take(2), take(2)
    else:
        (bulk_out,) = take(1)
    if scatter:
        from_core, send_y, keep_y, got_y, send_lo, got_lo, mine, mine_sem = take(8)
    if gather:
        ready, local_sem = take(2)
    if kind == LAST:
        (ready,) = take(1)
    if kind == LAST:
        aside_router = Router(aside, aside_out, *take(3), spread=True)
        grad_router = Router(ready, grad_out, *take(3), spread=True)
        gain_acc, gain_sent, gain_got, side_local, side_send, side_recv = take(6)
        from_his, lo_sends = take(2), take(2)
        own_half, from_dp, total_keep, total_send = take(4)
    else:
        bulk_send, bulk_recv = take(2)
    if kind == PLAIN:
        kv_local, kv_send, kv_recv = take(3)
    send_sem, recv_sem = refs
    size, width = x_ref.shape
    step = size // ROUNDS
    on_y, on_lo, on_core = partners()
    on_hi, on_dp = route_partner(1, 0)[0], route_partner(2, 0)[0]
    if kind == LAST:
        greet((on_y, on_core, *(route_partner(q, e)[0] for q, e in ROUTES[1:])))
        for q, e in ROUTES:
            aside_router.send(q, e)
    else:
        greet((on_y, on_lo, on_core, on_hi, on_dp))
    kv_copies = []
    if kind == PLAIN:
        count = own_kv.shape[0]
        kv_copies.append(pltpu.make_async_copy(own_kv, all_kv.at[pl.ds(0, count), :], kv_local))
        kv_copies.append(
            pltpu.make_async_remote_copy(
                src_ref=own_kv,
                dst_ref=all_kv.at[pl.ds(count, count), :],
                send_sem=kv_send,
                recv_sem=kv_recv,
                device_id=on_hi,
                device_id_type=MESH_IDS,
            )
        )
        for copy in kv_copies:
            copy.start()
    if gather:
        weights = Pieces(bulk_out, bulk_send, bulk_recv)
    copies = {}

    def start(what, q, src, dst, device):
        copies[what, q] = pltpu.make_async_remote_copy(
            src_ref=src,
            dst_ref=dst,
            send_sem=send_sem.at[what, q],
            recv_sem=recv_sem.at[what, q],
            device_id=device,
            device_id_type=MESH_IDS,
        )
        copies[what, q].start()

    def arrived(what, q):
        copies[what, q].wait_recv()

    def rows_of(q):
        return pl.ds(pl.multiple_of(order(q) * step, step), step)

    def order(q):
        return route_partner(q, 0)[1] // 2 if kind == LAST else q

    def sum_core(q):
        rows = rows_of(q)
        arrived(CORE, q)
        copies["mine", q].wait()
        for lo in range(2):
            at = 2 * lo
            keep_y[lo, rows, :] = mine[at, rows, :].astype(F32) + from_core[at, rows, :].astype(F32)
            at = 2 * lo + 1
            total = mine[at, rows, :].astype(F32) + from_core[at, rows, :].astype(F32)
            send_y[lo, rows, :] = total.astype(BF)
        start(RY, q, send_y.at[:, rows, :], got_y.at[:, rows, :], on_y)

    def sum_y(q):
        rows = rows_of(q)
        arrived(RY, q)
        send_lo[rows, :] = (keep_y[1, rows, :] + got_y[1, rows, :].astype(F32)).astype(BF)
        start(RL, q, send_lo.at[rows, :], got_lo.at[rows, :], on_lo)

    def sum_lo(q):
        rows = rows_of(q)
        arrived(RL, q)
        return keep_y[0, rows, :] + got_y[0, rows, :].astype(F32) + got_lo[rows, :].astype(F32)

    def finish(q):
        rows = rows_of(q)
        total = sum_lo(q) if scatter else None
        value = x_ref[rows, :]
        if kind == PLAIN:
            low = value
        elif kind == FIRST:
            value = value.astype(F32)
            low = (value * root_of(value) * gain[...]).astype(BF)
        else:
            grad, gain_grad = norm_gradient(value.astype(F32), gain[...], total)
            grad = grad + add_ref[rows, :].astype(F32)
            ready[rows, :] = grad.astype(BF)
            if q == 0:
                gain_acc[...] = gain_grad
            else:
                gain_acc[...] += gain_grad
        if kind == LAST:
            grad_router.send(q, 0)
            grad_router.send(q, 1)
        if gather:
            ready[rows, :] = low
            keep = pltpu.make_async_copy(ready.at[rows, :], everyone.at[rows, :], local_sem.at[q])
            keep.start()
            copies["local", q] = keep
            start(GY, q, ready.at[rows, :], everyone.at[block(1, q), :], on_y)
            start(GL, q, ready.at[rows, :], everyone.at[block(2, q), :], on_lo)
            start(GC, q, ready.at[rows, :], everyone.at[block(4, q), :], on_core)

    def block(index, q):
        return pl.ds(index * size + q * step, step)

    def forward(q):
        arrived(GL, q)
        start(FY, q, everyone.at[block(2, q), :], everyone.at[block(3, q), :], on_y)
        start(CL, q, everyone.at[block(2, q), :], everyone.at[block(6, q), :], on_core)
        arrived(GY, q)
        start(CY, q, everyone.at[block(1, q), :], everyone.at[block(5, q), :], on_core)

    def corner(q):
        arrived(FY, q)
        start(CC, q, everyone.at[block(3, q), :], everyone.at[block(7, q), :], on_core)

    def pass_on(q):
        for router in routers:
            router.pass_on(q, 0)
            router.pass_on(q, 1)

    def pass_corner(q):
        for router in routers:
            router.pass_corner(q, 0)
            router.pass_corner(q, 1)

    side_copies = []

    def side(src, dst, device):
        at = len(side_copies)
        copy = pltpu.make_async_remote_copy(
            src_ref=src,
            dst_ref=dst,
            send_sem=side_send.at[at],
            recv_sem=side_recv.at[at],
            device_id=device,
            device_id_type=MESH_IDS,
        )
        copy.start()
        side_copies.append(copy)
        return copy

    waiting = {}

    def unit_rows(unit):
        low = lax.axis_index(CONTEXT) % 2
        count = from_his[unit // 2].shape[0] // 2
        index = low if unit % 2 else 1 - low
        return pl.ds(pl.multiple_of(index * count, 16), count)

    def unit_to_dp(unit):
        group = lax.axis_index(DP)
        rows = unit_rows(unit)
        waiting["own", unit] = pltpu.make_async_copy(
            total.at[group, :, rows, :], own_half.at[:, rows, :], side_local.at[unit]
        )
        waiting["own", unit].start()
        waiting["dp", unit] = side(
            total.at[1 - group, :, rows, :], from_dp.at[:, rows, :], on_dp
        )

    def unit_to_hi(unit):
        high = lax.axis_index(CONTEXT) // 2
        rows = unit_rows(unit)
        send = total_send
        if unit >= 2:
            waiting["own", unit].wait()
            waiting["dp", unit].wait_recv()
            total_keep[rows, :] = own_half[high, rows, :].astype(F32) + from_dp[
                high, rows, :
            ].astype(F32)
            send[rows, :] = (
                own_half[1 - high, rows, :].astype(F32) + from_dp[1 - high, rows, :].astype(F32)
            ).astype(BF)
        waiting["hi", unit] = side(send.at[rows, :], from_his[unit // 2].at[rows, :], on_hi)

    def near_to_hi(index):
        low = lax.axis_index(CONTEXT) % 2
        count = near_send.shape[0] // 8
        first = (1 - low if index < 4 else low) * 4 * count + index % 4 * count
        rows = pl.ds(pl.multiple_of(first, 16), count)
        waiting["near", index] = side(near_send.at[rows, :], from_his[0].at[rows, :], on_hi)

    def unit_to_lo(unit):
        rows = unit_rows(unit)
        keep = near_keep if unit < 2 else total_keep
        if unit < 2:
            for index in range(4 * unit, 4 * unit + 4):
                waiting["near", index].wait_recv()
        else:
            waiting["hi", unit].wait_recv()
        value = keep[rows, :] + from_his[unit // 2][rows, :].astype(F32)
        if unit % 2:
            kept[unit // 2][...] = value
        else:
            lo_sends[unit // 2][...] = value.astype(BF)
            waiting["lo", unit] = side(lo_sends[unit // 2], gotten[unit // 2], on_lo)

    def gain_hop(index):
        if index == 0:
            total = jnp.concatenate([gain_acc[...], other_gain[...]], axis=0)
        else:
            waiting["gain"].wait_recv()
            total = gain_sent[index - 1] + gain_got[index - 1]
        if index == 5:
            gains_out[...] = total
        else:
            gain_sent[index] = total
            device = (on_core, on_y, on_lo, on_dp, on_hi)[index]
            waiting["gain"] = side(gain_sent.at[index], gain_got.at[index], device)

    def beside(tick):
        if tick == 0:
            unit_to_dp(2)
            unit_to_dp(3)
        if tick < 8:
            near_to_hi(tick)
        if tick in (3, 4):
            unit_to_hi(tick - 1)
        if tick == 6:
            unit_to_lo(0)
        if 5 <= tick < 8:
            gain_hop(tick - 5)
        if tick == 7:
            for index in range(3, 6):
                gain_hop(index)
            for unit in range(1, 4):
                unit_to_lo(unit)

    routers = [aside_router, grad_router] if kind == LAST else []
    stages = []
    if scatter:
        for q in range(ROUNDS):
            rows = rows_of(q)
            start(CORE, q, parts.at[pl.ds(4, 4), rows, :], from_core.at[:, rows, :], on_core)
            copies["mine", q] = pltpu.make_async_copy(
                parts.at[pl.ds(0, 4), rows, :], mine.at[:, rows, :], mine_sem.at[q]
            )
            copies["mine", q].start()
        stages += [sum_core, sum_y]
    stages.append(finish)
    if gather:
        stages += [forward, corner]
    if routers:
        stages += [pass_on, pass_corner]
    ordered = list(enumerate(stages))
    if scatter:
        ordered.reverse()
    elif kind == PLAIN:
        for q in range(ROUNDS):
            finish(q)
        ordered = ordered[1:]
    for tick in range(ROUNDS + len(stages) - 1):
        for index, stage in ordered:
            if 0 <= tick - index < ROUNDS:
                stage(tick - index)
        if gather and tick < len(pieces):
            weights.send(pieces[tick])
        if kind == LAST:
            beside(tick)
        if gather and 0 <= tick - 2 < len(pieces):
            weights.pass_on(pieces[tick - 2])
    for (what, q), copy in copies.items():
        if what == "local":
            copy.wait()
        elif what != "mine":
            copy.wait_send()
            if what in (GC, CY, CL, CC):
                copy.wait_recv()
    if gather:
        weights.finish()
    for copy in kv_copies:
        copy.wait()
    if kind == LAST:
        aside_router.finish()
        grad_router.finish()
        for copy in side_copies:
            copy.wait_send()
        for unit in (0, 2):
            waiting["lo", unit].wait_recv()


def call_tokens(
    kind, ident, part, x, bulk, pieces, gain=None, add=None, aside=None, other_gain=None, grads=None
):
    size, width = x.shape
    scatter, gather = part is not None, kind != LAST
    vmem = pl.BlockSpec(memory_space=pltpu.VMEM)
    anywhere = pl.BlockSpec(memory_space=pl.ANY)
    operands, in_specs, out_specs, out_shape, scratch = [], [], [], [], []
    if scatter:
        operands.append(part.reshape(8, size, width))
        in_specs.append(anywhere)
    operands.append(x)
    in_specs.append(vmem)
    if gain is not None:
        operands.append(gain.reshape(1, width))
        in_specs.append(vmem)
    if kind == PLAIN:
        operands.append(add)
        in_specs.append(anywhere)
        out_specs.append(anywhere)
        out_shape.append(jax.ShapeDtypeStruct((2 * add.shape[0], add.shape[1]), BF))
    elif add is not None:
        operands.append(add)
        in_specs.append(vmem)
    if aside is not None:
        send, keep, total = grads
        cuts = [keep.shape, (total.shape[0] // 4, total.shape[1])]
        operands += [aside, other_gain, send, keep, total.reshape(2, 2, *cuts[1])]
        in_specs += [anywhere, vmem, anywhere, vmem, anywhere]
    if bulk is not None:
        operands.append(bulk)
        in_specs.append(anywhere)
    if gather:
        out_specs.append(anywhere)
        out_shape.append(jax.ShapeDtypeStruct((8 * size, width), BF))
    if kind == LAST:
        out_specs.append(anywhere)
        out_shape.append(jax.ShapeDtypeStruct((4 * size, width), BF))
    if kind == LAST:
        out_specs.append(vmem)
        out_shape.append(jax.ShapeDtypeStruct((2, width), F32))
        out_specs += [anywhere] + [vmem] * 2 + [anywhere] * 2
        out_shape.append(jax.ShapeDtypeStruct((4 * size, width), BF))
        out_shape += [jax.ShapeDtypeStruct((count // 2, n), F32) for count, n in cuts]
        out_shape += [jax.ShapeDtypeStruct((count // 2, n), BF) for count, n in cuts]
    if bulk is not None:
        out_specs.append(anywhere)
        out_shape.append(jax.ShapeDtypeStruct(bulk.shape, BF))
    if scatter:
        scratch.append(pltpu.VMEM((4, size, width), BF))
        pair = (2, size, width)
        scratch += [pltpu.VMEM(pair, BF), pltpu.VMEM(pair, F32), pltpu.VMEM(pair, BF)]
        scratch += [pltpu.VMEM((size, width), BF)] * 2
        scratch += [pltpu.VMEM((4, size, width), BF), pltpu.SemaphoreType.DMA((ROUNDS,))]
    if gather:
        scratch += [pltpu.VMEM((size, width), BF), pltpu.SemaphoreType.DMA((ROUNDS,))]
    if kind == LAST:
        scratch.append(pltpu.VMEM((size, width), BF))
        scratch += route_scratch(4) + route_scratch(4)
        scratch += [pltpu.VMEM((1, width), F32)] + [pltpu.VMEM((5, 2, width), F32)] * 2
        scratch.append(pltpu.SemaphoreType.DMA((6,)))
        scratch += [pltpu.SemaphoreType.DMA((20,))] * 2
        scratch += [pltpu.VMEM(cut, BF) for cut in cuts]
        scratch += [pltpu.VMEM((count // 2, n), BF) for count, n in cuts]
        scratch += [pltpu.VMEM((2, *cuts[1]), BF)] * 2
        scratch += [pltpu.VMEM(cuts[1], F32), pltpu.VMEM(cuts[1], BF)]
    else:
        scratch += piece_scratch()
    if kind == PLAIN:
        scratch += [pltpu.SemaphoreType.DMA(())] * 3
    scratch += [pltpu.SemaphoreType.DMA((KINDS, ROUNDS))] * 2
    return pl.pallas_call(
        functools.partial(
            token_kernel, kind=kind, scatter=scatter, gather=gather, pieces=pieces
        ),
        in_specs=in_specs,
        out_specs=out_specs,
        out_shape=out_shape,
        scratch_shapes=scratch,
        input_output_aliases={len(operands) - 1: len(out_shape) - 1} if gather else {},
        compiler_params=pltpu.CompilerParams(
            collective_id=ident, has_side_effects=True, vmem_limit_bytes=62 * 2**20
        ),
        cost_estimate=QUICK,
        name="tokens_%d" % kind,
    )(*operands)


def ffn_kernel(
    parts,
    x_ref,
    gain,
    d_y,
    d_y_all,
    large,
    two_all,
    grad_all,
    inner_out,
    both_out,
    y_mine,
    y_other,
    mid_out,
    grad_out,
    gain_out,
    large_out,
    weights,
    summed,
    got_a,
    got_b,
    got_c,
    got_d,
    mine,
    two_ready,
    grad_ready,
    two_block,
    d_y_block,
    inner_block,
    both_block,
    y_block,
    d_two,
    weight_sem,
    mine_sem,
    ready_sem,
    load_sem,
    store_sem,
    send_sem,
    recv_sem,
    piece_send,
    piece_recv,
    *,
    pieces,
):
    size, width = x_ref.shape
    units = inner_out.shape[2]
    cut = width // 2
    step = size // ROUNDS
    half = step // 2
    on_y, on_lo, on_core = partners()
    arriving = Pieces(large_out, piece_send, piece_recv)
    greet((on_y, on_lo, on_core, arriving.on_dp))
    left, right = pl.ds(0, cut), pl.ds(cut, width - cut)

    def rows_of(q):
        return pl.ds(pl.multiple_of(q * step, step), step)

    def block(index, q, first=0, count=None):
        start = pl.multiple_of(index * size + q * step + first, half)
        return pl.ds(start, step if count is None else count)

    def remote(base, what, q):
        rows = rows_of(q)
        ready, everyone = (two_ready, two_all) if base == 0 else (grad_ready, grad_all)
        part_of = lambda *place: everyone.at[block(*place), :]
        if what == CORE:
            src = parts.at[1, :, :, rows, :] if base == 0 else d_two.at[lax.rem(q, 2), 1]
            ends = src, summed.at[:, :, rows, :], on_core
        elif what == RY:
            ends = summed.at[:, 1, rows, left], got_a.at[:, rows, :], on_y
        elif what == RL:
            ends = summed.at[1, :, rows, right], got_b.at[:, rows, :], on_lo
        elif what == SL:
            ends = summed.at[1, 0, rows, left], got_c.at[rows, :], on_lo
        elif what == SY:
            ends = summed.at[0, 1, rows, right], got_d.at[rows, :], on_y
        elif what in (GY, GL, GC):
            index, device = {GY: (1, on_y), GL: (2, on_lo), GC: (4, on_core)}[what]
            ends = ready.at[rows, :], part_of(index, q), device
        elif what == FL:
            ends = part_of(1, q, 0, half), part_of(3, q, 0, half), on_lo
        elif what == FY:
            ends = part_of(2, q, half, half), part_of(3, q, half, half), on_y
        else:
            index = {CY: 1, CL: 2, CC: 3}[what]
            ends = part_of(index, q), part_of(index + 4, q), on_core
        return pltpu.make_async_remote_copy(
            src_ref=ends[0],
            dst_ref=ends[1],
            send_sem=send_sem.at[base + what, q],
            recv_sem=recv_sem.at[base + what, q],
            device_id=ends[2],
            device_id_type=MESH_IDS,
        )

    def arrived(base, what, q):
        remote(base, what, q).wait_recv()

    def sum_core(base, q, value):
        rows = rows_of(q)
        arrived(base, CORE, q)
        for lo in range(2):
            for y in range(2):
                total = value(lo, y).astype(F32) + summed[lo, y, rows, :].astype(F32)
                summed[lo, y, rows, :] = total.astype(BF)
        remote(base, RY, q).start()
        remote(base, RL, q).start()

    def sum_first(base, q):
        rows = rows_of(q)
        arrived(base, RY, q)
        total = summed[1, 0, rows, :cut].astype(F32) + got_a[1, rows, :].astype(F32)
        summed[1, 0, rows, :cut] = total.astype(BF)
        remote(base, SL, q).start()
        arrived(base, RL, q)
        total = summed[0, 1, rows, cut:].astype(F32) + got_b[1, rows, :].astype(F32)
        summed[0, 1, rows, cut:] = total.astype(BF)
        remote(base, SY, q).start()

    def sum_second(base, q):
        rows = rows_of(q)
        arrived(base, SL, q)
        arrived(base, SY, q)
        first = summed[0, 0, rows, :cut].astype(F32) + got_a[0, rows, :].astype(F32)
        second = summed[0, 0, rows, cut:].astype(F32) + got_b[0, rows, :].astype(F32)
        first = first + got_c[rows, :].astype(F32)
        second = second + got_d[rows, :].astype(F32)
        for what in (RY, RL, SL, SY):
            remote(base, what, q).wait_send()
        return jnp.concatenate([first, second], axis=1)

    def own_rows(base, q):
        ready, everyone = (two_ready, two_all) if base == 0 else (grad_ready, grad_all)
        rows = rows_of(q)
        sem = ready_sem.at[base // KINDS, q]
        return pltpu.make_async_copy(ready.at[rows, :], everyone.at[rows, :], sem)

    def spread(base, q):
        own_rows(base, q).start()
        for what in (GY, GL, GC):
            remote(base, what, q).start()

    def forward(base, q):
        arrived(base, GY, q)
        remote(base, FL, q).start()
        remote(base, CY, q).start()
        arrived(base, GL, q)
        remote(base, FY, q).start()
        remote(base, CL, q).start()

    def corner(base, q):
        arrived(base, FL, q)
        arrived(base, FY, q)
        remote(base, CC, q).start()

    def fetch_mine(q):
        src = parts.at[0, :, :, rows_of(q), :]
        slot = lax.rem(q, 2)
        return pltpu.make_async_copy(src, mine.at[slot], mine_sem.at[slot])

    def middle_core(q):
        fetch_mine(q).wait()
        sum_core(0, q, lambda lo, y: mine[lax.rem(q, 2), lo, y])

        @pl.when(q + 2 < ROUNDS)
        def _():
            fetch_mine(q + 2).start()

    def middle_norm(q):
        rows = rows_of(q)
        value = x_ref[rows, :].astype(F32) + sum_second(0, q)
        mid_out[rows, :] = value
        two_ready[rows, :] = (value * root_of(value) * gain[...]).astype(BF)
        spread(0, q)

    def loads(part, q):
        for index, (src, dst) in enumerate(((two_all, two_block), (d_y_all, d_y_block))):
            for at in range(4):
                yield pltpu.make_async_copy(
                    src.at[block(4 * part + at, q), :],
                    dst.at[part, pl.ds(at * step, step), :],
                    load_sem.at[index, part, at],
                )

    def stores(part, q):
        for index, (src, dst) in enumerate(((inner_block, inner_out), (both_block, both_out))):
            for at in range(4):
                yield pltpu.make_async_copy(
                    src.at[part, pl.ds(at * step, step), :],
                    dst.at[4 * part + at, rows_of(q), :],
                    store_sem.at[index, part, at],
                )

    def y_stores(part, q, act):
        for index, dst in enumerate((y_mine, y_other)):

            @pl.when(part == index)
            def _():
                for at in range(4):
                    copy = pltpu.make_async_copy(
                        y_block.at[index, pl.ds(at * step, step), :],
                        dst.at[at, rows_of(q), :],
                        store_sem.at[2, index, at],
                    )
                    act(copy)

    def feed_forward(q):
        own_rows(0, q).wait()
        for what in (GC, CY, CL, CC):
            arrived(0, what, q)

        @pl.when(q == 0)
        def _():
            pltpu.make_async_copy(large_out, weights, weight_sem.at[0]).wait()

        @pl.when(q >= 2)
        def _():
            remote(KINDS, CORE, q - 2).wait_send()

        for part in (1, 0):
            for copy in loads(part, q):
                copy.start()

        @pl.loop(0, 2)
        def _(turn_index):
            part = 1 - turn_index
            for copy in loads(part, q):
                copy.wait()

            @pl.when(q > 0)
            def _():
                for copy in stores(part, q - 1):
                    copy.wait()
                y_stores(part, q - 1, lambda copy: copy.wait())

            both = mm(two_block[part], weights[:, : 2 * units])
            gate, up = both[:, :units], both[:, units:]
            d_inner = mm(d_y_block[part], weights[:, 2 * units :])
            sigma = 1.0 / (1.0 + jnp.exp(-gate))
            silu_gate = gate * sigma
            inner_block[part] = (silu_gate * up).astype(BF)
            d_gate = d_inner * up * sigma * (1.0 + gate * (1.0 - sigma))
            both_block[part, :, :units] = d_gate.astype(BF)
            both_block[part, :, units:] = (d_inner * silu_gate).astype(BF)
            d_two[lax.rem(q, 2), part] = (
                times_t(both_block[part], weights[:, : 2 * units])
                .astype(BF)
                .reshape(2, 2, step, width)
            )

            @pl.when(part == 1)
            def _():
                remote(KINDS, CORE, q).start()

            y_block[part] = times_t(inner_block[part], weights[:, 2 * units :]).astype(BF)
            for copy in stores(part, q):
                copy.start()
            y_stores(part, q, lambda copy: copy.start())

    def back_core(q):
        sum_core(KINDS, q, lambda lo, y: d_two[lax.rem(q, 2), 0, lo, y])

    def back_norm(q):
        rows = rows_of(q)
        grad, gain_grad = norm_gradient(mid_out[rows, :], gain[...], sum_second(KINDS, q))
        grad = grad + d_y[rows, :].astype(F32)
        grad_out[rows, :] = grad
        gain_out[...] += gain_grad
        grad_ready[rows, :] = grad.astype(BF)
        spread(KINDS, q)

    gain_out[...] = jnp.zeros_like(gain_out)
    for q in range(ROUNDS):
        remote(0, CORE, q).start()
        if q < 2:
            fetch_mine(q).start()
    stages = [
        middle_core,
        functools.partial(sum_first, 0),
        middle_norm,
        functools.partial(forward, 0),
        functools.partial(corner, 0),
        feed_forward,
        back_core,
        functools.partial(sum_first, KINDS),
        back_norm,
        functools.partial(forward, KINDS),
        functools.partial(corner, KINDS),
    ]

    @pl.loop(0, ROUNDS + len(stages) - 1)
    def _(tick):
        for index, stage in reversed(list(enumerate(stages))):
            pl.when((tick >= index) & (tick < index + ROUNDS))(
                functools.partial(stage, tick - index)
            )

        @pl.when(tick == 0)
        def _():
            for piece in pieces:
                arriving.spread(piece)

        @pl.when(tick == 4)
        def _():
            arriving.finish()
            pltpu.make_async_copy(large_out, weights, weight_sem.at[0]).start()

    for q in range(ROUNDS):
        for base in (0, KINDS):
            for what in range(KINDS):
                if what in (RY, RL, SL, SY) or (what == CORE and base and q < ROUNDS - 2):
                    continue
                remote(base, what, q).wait_send()
        for what in (GC, CY, CL, CC):
            arrived(KINDS, what, q)
        own_rows(KINDS, q).wait()
    for part in range(2):
        for copy in stores(part, ROUNDS - 1):
            copy.wait()
        y_stores(part, ROUNDS - 1, lambda copy: copy.wait())


def call_ffn(parts, x, gain, d_y, d_y_all, large, pieces):
    size, width = x.shape
    units = large.shape[1] // 3
    cut = width // 2
    step = size // ROUNDS
    vmem = pl.BlockSpec(memory_space=pltpu.VMEM)
    anywhere = pl.BlockSpec(memory_space=pl.ANY)
    everyone = jax.ShapeDtypeStruct((8 * size, width), BF)
    shape = lambda n: jax.ShapeDtypeStruct((8, size, n), BF)
    local = jax.ShapeDtypeStruct((size, width), F32)
    dma = pltpu.SemaphoreType.DMA
    half = pltpu.VMEM((2, size, cut), BF)
    quarter = pltpu.VMEM((size, cut), BF)
    ready = pltpu.VMEM((size, width), BF)
    block = lambda n: pltpu.VMEM((2, 4 * step, n), BF)
    return pl.pallas_call(
        functools.partial(ffn_kernel, pieces=pieces),
        in_specs=[anywhere, vmem, vmem, vmem, anywhere, anywhere],
        out_specs=[anywhere] * 6 + [vmem] * 3 + [anywhere],
        input_output_aliases={5: 9},
        out_shape=[
            everyone,
            everyone,
            shape(units),
            shape(2 * units),
            jax.ShapeDtypeStruct((4, size, width), BF),
            jax.ShapeDtypeStruct((4, size, width), BF),
            local,
            local,
            jax.ShapeDtypeStruct((1, width), F32),
            jax.ShapeDtypeStruct(large.shape, BF),
        ],
        scratch_shapes=[
            pltpu.VMEM((width, 3 * units), BF),
            pltpu.VMEM((2, 2, size, width), BF),
            half,
            half,
            quarter,
            quarter,
            pltpu.VMEM((2, 2, 2, step, width), BF),
            ready,
            ready,
            block(width),
            block(width),
            block(units),
            block(2 * units),
            block(width),
            pltpu.VMEM((2, 2, 2, 2, step, width), BF),
            dma((1,)),
            dma((2,)),
            dma((2, ROUNDS)),
            dma((2, 2, 4)),
            dma((3, 2, 4)),
            dma((2 * KINDS, ROUNDS)),
            dma((2 * KINDS, ROUNDS)),
            *piece_scratch(),
        ],
        compiler_params=pltpu.CompilerParams(
            collective_id=8, has_side_effects=True, vmem_limit_bytes=62 * 2**20
        ),
        cost_estimate=QUICK,
        name="feed_forward",
    )(parts.reshape(2, 2, 2, size, width), x, gain.reshape(1, width), d_y, d_y_all, large)


CHUNKS = 2


def weights_kernel(
    small_keep,
    small_give,
    large_keep,
    rows,
    late_rows,
    small,
    large,
    rows_out,
    late_out,
    local,
    send,
    recv,
    *rest,
):
    group, place, shard = (lax.axis_index(name) for name in MESH_AXES)
    low, high = place % 2, place // 2
    on_lo = (group, place + 1 - 2 * low, shard)
    on_hi = (group, place + 2 - 4 * high, shard)
    on_dp = (1 - group, place, shard)
    eighth = small_keep.shape[0]
    step = eighth // CHUNKS
    greet([route_partner(q, e)[0] for q, e in ROUTES[1:]])
    copies = []
    router, late = Router(rows, rows_out, *rest[:3]), Router(late_rows, late_out, *rest[3:6])
    for q, e in ROUTES:
        router.send(q, e)

    def start(src, dst, device):
        at = len(copies)
        copy = pltpu.make_async_remote_copy(
            src_ref=src,
            dst_ref=dst,
            send_sem=send.at[at],
            recv_sem=recv.at[at],
            device_id=device,
            device_id_type=MESH_IDS,
        )
        copy.start()
        copies.append(copy)
        return copy

    def span(index, first, count):
        return pl.ds(pl.multiple_of(index * eighth + first, 16), count)

    own = (group * 2 + high) * 2
    across = (group * 2 + 1 - high) * 2
    from_low = []
    for q in range(CHUNKS):
        src = small_give.at[pl.ds(q * step, step), :]
        from_low.append(start(src, small.at[span(own + low, q * step, step), :], on_lo))
    stay = [
        pltpu.make_async_copy(small_keep, small.at[span(own + low, 0, eighth), :], local.at[0]),
        pltpu.make_async_copy(large_keep, large.at[span(own + low, 0, eighth), :], local.at[1]),
    ]
    for copy in stay:
        copy.start()
    from_high = []
    for q in range(CHUNKS):
        src = small_keep.at[pl.ds(q * step, step), :]
        dst = small.at[span(own + low, q * step, step), :]
        from_high.append(start(src, dst, on_hi))
        start(src, dst, on_dp)
    for q in range(CHUNKS):
        from_low[q].wait_recv()
        at = small.at[span(own + 1 - low, q * step, step), :]
        from_high.append(start(at, at, on_hi))
        start(at, at, on_dp)
    for q in range(2 * CHUNKS):
        half = low if q < CHUNKS else 1 - low
        from_high[q].wait_recv()
        at = small.at[span(across + half, q % CHUNKS * step, step), :]
        start(at, at, on_dp)
        if q == 0:
            for pair in ROUTES:
                late.send(*pair)
    waited = from_low + from_high
    for copy in copies:
        copy.wait_send()
        if not any(copy is item for item in waited):
            copy.wait_recv()
    for copy in stay:
        copy.wait()
    router.finish()
    late.finish()


def call_weights(small_keep, small_give, large_keep, rows, late_rows, parts):
    eighth = small_keep.shape[0]
    anywhere = pl.BlockSpec(memory_space=pl.ANY)
    count = 7 * CHUNKS
    return pl.pallas_call(
        weights_kernel,
        in_specs=[anywhere] * 5,
        out_specs=[anywhere] * 4,
        out_shape=[
            jax.ShapeDtypeStruct((2 * parts * eighth, small_keep.shape[1]), BF),
            jax.ShapeDtypeStruct((2 * parts * eighth, large_keep.shape[1]), BF),
            jax.ShapeDtypeStruct(rows.shape, BF),
            jax.ShapeDtypeStruct(rows.shape, BF),
        ],
        scratch_shapes=[
            pltpu.SemaphoreType.DMA((2,)),
            pltpu.SemaphoreType.DMA((count,)),
            pltpu.SemaphoreType.DMA((count,)),
            *route_scratch(1),
            *route_scratch(1),
        ],
        compiler_params=pltpu.CompilerParams(collective_id=1, has_side_effects=True),
        cost_estimate=QUICK,
        name="weights_first",
    )(small_keep, small_give, large_keep, rows, late_rows)


def head_columns(part, base):
    half = part // 2
    entry = np.arange(part)
    return base + np.where(entry < half, entry, LANES // 2 + entry - half)


def after(value, *events):
    return lax.optimization_barrier((value, *events))[0]


def on_device_paired(
    tokens,
    gain_attn,
    w_query,
    key_weight,
    value_weight,
    w_out,
    gain_mlp,
    w_gate,
    w_up,
    w_down,
    cotangent,
    lengths,
    order_perm,
    block_order,
):
    names = MESH_AXES
    n_dp, n_ctx, n_ten = (lax.axis_size(name) for name in names)
    devices = n_dp * n_ctx * n_ten
    on_core, on_y, on_lo, on_hi, on_dp = 1, 2, n_ten, 2 * n_ten, n_ctx * n_ten
    group = lax.axis_index(DP)
    place = lax.axis_index(CONTEXT)
    shard = lax.axis_index(TENSOR)
    high, low = place // 2, place % 2
    row, core = shard // 2, shard % 2
    groups = n_dp * n_ctx
    my_index = group * n_ctx + place
    rows, width = tokens.shape
    share = rows // groups
    part = share // n_ten
    local = rows // n_ten
    block_rows = rows // MB
    half_rows = block_rows // 2
    pack = block_rows * n_ctx
    n_blocks = block_order.shape[0]
    blocks = n_blocks // 2
    scale = HEAD_SIZE ** (-0.5)
    quarter = width // (2 * n_dp)
    eighth = quarter // 2

    def swap(value, bit):
        return lax.ppermute(value, names, [(i, i ^ bit) for i in range(devices)])

    def pick(flag, yes, no):
        return jnp.where(flag == 1, yes, no)

    def by_low(mine, partner, axis):
        return jnp.concatenate(
            [pick(low, partner, mine), pick(low, mine, partner)], axis=axis
        )

    places = order_perm.reshape(groups, rows)
    source = places // rows
    is_mine = source == my_index
    below = jnp.arange(rows, dtype=jnp.int32)
    ahead = one_hot(1, (below[:, None] <= below[None, :]).astype(jnp.int32))
    all_sources = jnp.arange(groups, dtype=jnp.int32)
    runs = [
        lax.dynamic_index_in_dim(source, group * n_ctx + 2 * high + (low ^ d), 0, keepdims=False)
        for d in range(2)
    ]
    from_each = [run[None, :] == all_sources[:, None] for run in runs]
    flags = jnp.concatenate([is_mine, *from_each], axis=0)
    counted = mm(flags.astype(BF), ahead).astype(jnp.int32) - 1
    rank = counted[:groups]
    row_at = jnp.where(is_mine, places % rows, 0)

    def rows_sent(slots):
        hits = is_mine[:, None, :] & (rank[:, None, :] == slots[None, :, None])
        return jnp.sum(jnp.where(hits, row_at[:, None, :], 0), axis=2)

    send_index = rows_sent(shard * part + jnp.arange(part, dtype=jnp.int32)).reshape(local, 1)

    def arrivals(d):
        known = counted[(d + 1) * groups : (d + 2) * groups]
        own_rank = jnp.sum(jnp.where(from_each[d], known, 0), axis=0)
        holder = own_rank // part
        device = ((holder % 2) ^ core) * 2 + ((holder // 2) ^ row)
        return (device * groups + runs[d]) * part + own_rank % part

    index = jnp.stack([arrivals(d) for d in range(2)])
    index_col, index_row = index[:, :, None], index[:, None, :]

    def lookup(table, at):
        hits = at[..., None] == jnp.arange(table.shape[0], dtype=jnp.int32)
        return jnp.sum(jnp.where(hits, table, 0), axis=-1)

    slot_of = invert(block_order)
    query = jnp.arange(2 * MB * 2, dtype=jnp.int32)
    run_of, micro_of, half_of = query // (2 * MB), query // 2 % MB, query % 2
    which = lookup(block_order, 2 * (2 * high + (low ^ run_of)) + half_of)
    upper = which // blocks
    item = jnp.arange(blocks, dtype=jnp.int32)
    slot = lookup(slot_of, upper[:, None] * blocks + item)
    where = ((slot // 4) ^ high) * 2 + (((slot // 2) % 2) ^ low)
    starts = ((where * MB + micro_of[:, None]) * 2 + slot % 2) * half_rows
    first = lookup(lengths[:, 0], group * MB + micro_of)
    second = first + lookup(lengths[:, 1], group * MB + micro_of)
    meta = jnp.concatenate([(which % blocks)[:, None], starts], axis=1)
    at = which[:, None] * half_rows + jnp.arange(half_rows, dtype=jnp.int32)
    first, second = first[:, None], second[:, None]
    in_last = at >= second
    q_flag = jnp.where(in_last, 1.0, 0.0).reshape(2, rows, 1)
    k_flag = jnp.where(in_last, 0.0, MASKED).reshape(2, rows, 1)
    at = at - jnp.where(at < first, 0, jnp.where(at < second, first, second))
    position = at.reshape(2, rows)
    hit = index[:, :, None] == jnp.arange(rows, dtype=jnp.int32)[None, None, :]
    position_arrived = jnp.sum(jnp.where(hit, position[:, :, None], 0), axis=1)

    half_head = HEAD_SIZE // 2
    entry_of = np.arange(half_head)
    freq = (THETA ** (-2.0 * entry_of / HEAD_SIZE)).astype(np.float32)
    to_lanes = np.zeros((2, half_head, LANES), np.float32)
    to_lanes[:, entry_of, entry_of + LANES // 2] = 1.0
    to_lanes[0, entry_of, entry_of] = 1.0
    to_lanes[1, entry_of, entry_of] = -1.0

    def tables(pos):
        angle = freq[:, None] * pos.reshape(-1).astype(F32)[None, :]
        return [
            lax.dot_general(
                value,
                jnp.asarray(lanes),
                (((0,), (0,)), ((), ())),
                precision=lax.Precision.HIGHEST,
                preferred_element_type=F32,
            ).reshape(2, rows, LANES)
            for value, lanes in zip((jnp.cos(angle), jnp.sin(angle)), to_lanes, strict=True)
        ]

    cos_arrived, sin_arrived = tables(position_arrived)
    cos_place, sin_place = tables(position)

    q_width, kv_width = GROUP * HEAD_SIZE, HEAD_SIZE
    all_width = q_width + 2 * kv_width
    target = np.concatenate(
        [head_columns(HEAD_SIZE, h * LANES) for h in range(GROUP + 1)]
        + [(GROUP + 1) * LANES + np.arange(HEAD_SIZE)]
    )
    spread_np = np.zeros((all_width, (GROUP + 2) * LANES), np.float32)
    spread_np[np.arange(all_width), target] = 1.0
    spread = jnp.asarray(spread_np, BF)
    out_target = np.concatenate([h * LANES + np.arange(HEAD_SIZE) for h in range(GROUP)])
    out_np = np.zeros((q_width, GROUP * LANES), np.float32)
    out_np[np.arange(q_width), out_target] = 1.0
    out_spread = jnp.asarray(out_np, BF)

    def halves(value):
        size = value.shape[1] // 2
        return pick(low, value[:, size:], value[:, :size]), pick(low, value[:, :size], value[:, size:])

    def together(values):
        keeps, gives = zip(*(halves(value) for value in values), strict=True)
        return list(keeps), list(gives)

    x_send, cot_send = pick_rows(send_index, tokens, cotangent, True)
    w_out_t, w_down_t = w_out.T, w_down.T
    keeps, gives = together([w_query, key_weight, value_weight])
    keep_out, give_out = halves(w_out_t)
    gains = jnp.stack([gain_attn, gain_mlp], axis=1)
    out_at, gain_at = 4 * LANES, 4 * LANES + q_width
    gap = jnp.zeros((eighth, out_at - all_width), BF)
    end = jnp.zeros((eighth, 7 * LANES - gain_at - 2), BF)
    small_keep = jnp.concatenate([*keeps, gap, keep_out, gains, end], axis=1)
    small_give = jnp.concatenate([*gives, gap, give_out, gains, end], axis=1)
    keeps, gives = together([w_gate, w_up, w_down_t])
    small, large, x_low, cot_low = call_weights(
        small_keep,
        small_give,
        jnp.concatenate(keeps, axis=1),
        x_send,
        cot_send,
        2 * n_dp,
    )
    large_give = jnp.concatenate(gives, axis=1)
    w_qkv = small[:, :all_width]
    w_o_t = small[:, out_at:gain_at]
    gain_a = small[:, gain_at].astype(F32)
    gain_m = small[:, gain_at + 1].astype(F32)

    one_all, large = call_tokens(FIRST, 2, None, x_low, large, (0, 1, 2, 3), gain_a)
    large_got = swap(after(large_give, one_all), on_lo)

    split = GROUP * LANES
    kv_own = call_sort(
        one_all, mm(w_qkv, spread[:, split:]).astype(BF), cos_arrived, sin_arrived, index_col, k_flag, 1
    )
    block_first = (2 * group + high) * quarter
    across_first = (2 * group + 1 - high) * quarter
    large = lax.dynamic_update_slice_in_dim(large, large_got, block_first + (1 - low) * eighth, 0)
    kv_all, dy_all, large = call_tokens(PLAIN, 3, None, cot_low, large, (4,), None, kv_own)
    late_first, late_count = (1 - low) * eighth + eighth // 4, eighth - eighth // 4
    late = lax.dynamic_slice_in_dim(large, block_first + late_first, late_count, 0)
    late = swap(late, on_hi)
    q_sorted = call_sort(
        after(one_all, dy_all),
        mm(w_qkv, spread[:, :split]).astype(BF),
        cos_arrived,
        sin_arrived,
        index_col,
        q_flag,
        2,
    )
    o_all = call_forward(meta, q_sorted, kv_all, index_row, out_spread.T, scale)
    o_part = product(o_all, w_o_t, 1)
    o_part, late = lax.optimization_barrier((o_part, late))
    large = lax.dynamic_update_slice_in_dim(large, late, across_first + late_first, 0)
    two_all, dh_all, inner_all, d_both_all, y_part, y_other, mid, d_mid, gain_grad_m, unused = call_ffn(
        o_part, x_low, gain_m, cot_low, dy_all, large, (5, 6, 7)
    )
    units = inner_all.shape[2]
    inner_all = inner_all.reshape(2 * rows, units)
    d_both_all = d_both_all.reshape(2 * rows, 2 * units)

    def rows_at(value, index, size):
        return lax.dynamic_slice_in_dim(value, index * size, size, 0)

    def other_dp(total):
        return swap(rows_at(total, 1 - group, 2 * quarter), on_dp)

    def dp_sum(total, came):
        kept = rows_at(total, group, 2 * quarter).astype(F32) + came.astype(F32)
        return rows_at(kept, high, quarter), rows_at(kept, 1 - high, quarter).astype(BF)

    def quad_sum(kept, came):
        kept = kept + came.astype(F32)
        return rows_at(kept, low, eighth), rows_at(kept, 1 - low, eighth).astype(BF)

    y_came = swap(y_other, on_core)
    down_part = product(dy_all, inner_all, 2)
    y_came, down_part = lax.optimization_barrier((y_came, down_part))
    y_sum = (y_part.astype(F32) + y_came.astype(F32)).reshape(2, 2, local, width)
    y_sent, y_kept = y_sum[:, 1].astype(BF), y_sum[:, 0]
    y_came = swap(y_sent, on_y)
    down_came = other_dp(down_part)
    gate_part, up_part = product(after(two_all, y_sent), d_both_all, 2, cuts=2)
    d_o = product(after(dh_all, gate_part), w_o_t, 0, lanes=out_spread)
    d_o, down_came, y_came = lax.optimization_barrier((d_o, down_came, y_came))
    y_pair = y_kept + y_came.astype(F32)
    y_sent = y_pair[1].astype(BF)
    gate_came = other_dp(after(gate_part, down_came))
    down_keep, down_send = dp_sum(down_part, down_came)
    d_o, down_send, y_sent = lax.optimization_barrier((d_o, down_send, y_sent))
    y_came = swap(y_sent, on_lo)
    down_came = swap(down_send, on_hi)
    dq_all, dkv_own, dkv_sent = call_backward(
        meta,
        q_sorted,
        kv_all,
        d_o,
        index_col,
        index_row,
        cos_place.reshape(2 * rows, LANES),
        sin_place.reshape(2 * rows, LANES),
        scale,
    )

    dkv_got = swap(dkv_sent, on_hi)
    dh_late, dkv_own, down_came = lax.optimization_barrier((dh_all, dkv_own, down_came))
    out_part = product(dh_late, o_all, 2)
    gate_came, out_part = lax.optimization_barrier((gate_came, out_part))
    up_came = other_dp(after(up_part, gate_came))
    gate_keep, gate_send = dp_sum(gate_part, gate_came)
    gate_send, y_came, dkv_got = lax.optimization_barrier((gate_send, y_came, dkv_got))
    gate_came = swap(gate_send, on_hi)
    y_local = (mid + y_pair[0] + y_came.astype(F32)).astype(BF)
    d_all = call_unsort(
        dkv_own, dkv_got, cos_place, sin_place, index_row, dq_all, spread.T, scale
    )
    total_part = jnp.concatenate([product(one_all, d_all, 2), out_part], axis=1)
    up_keep, up_send = dp_sum(up_part, after(up_came, d_all))
    d_one_part, total_part, up_send = lax.optimization_barrier(
        (product(d_all, w_qkv, 1), total_part, up_send)
    )
    x_grad_rows, both_gains, y_rows, *grads = call_tokens(
        LAST,
        7,
        d_one_part,
        x_low,
        None,
        (),
        gain_a,
        d_mid,
        y_local,
        gain_grad_m,
        (up_send, up_keep, total_part),
    )
    x_grad_rows, down_came, gate_came = lax.optimization_barrier(
        (x_grad_rows, down_came, gate_came)
    )
    down_keep, down_give = quad_sum(down_keep, down_came)
    gate_keep, gate_give = quad_sum(gate_keep, gate_came)
    grad_down_t = by_low(down_keep, swap(down_give, on_lo).astype(F32), 1)
    grad_gate = by_low(gate_keep, swap(gate_give, on_lo).astype(F32), 1)
    grad_up = by_low(grads[0], grads[2].astype(F32), 1)
    keep, got = grads[1], grads[3].astype(F32)
    grad_out_t = by_low(keep[:, all_width:], got[:, all_width:], 1)
    qkv_parts = []
    for first, last in ((0, q_width), (q_width, q_width + kv_width), (q_width + kv_width, all_width)):
        qkv_parts.append(by_low(keep[:, first:last], got[:, first:last], 1))
    grad_query, grad_key, grad_value = qkv_parts
    own_gains = lax.dynamic_slice_in_dim(both_gains, my_index * eighth, eighth, 1)

    send_all = rows_sent(jnp.arange(share, dtype=jnp.int32))
    held = [row * 2 + core, (row ^ 1) * 2 + core, row * 2 + (core ^ 1), (row ^ 1) * 2 + (core ^ 1)]
    from_slot = jnp.concatenate(
        [
            lax.dynamic_slice_in_dim(send_all, device * part, part, 1).reshape(local)
            for device in held
        ]
    )
    output, input_grad = pick_rows(from_slot[None, :], y_rows, x_grad_rows, False)
    return (
        output,
        input_grad,
        own_gains[0],
        grad_query,
        grad_key,
        grad_value,
        grad_out_t.T,
        own_gains[1],
        grad_gate,
        grad_up,
        grad_down_t.T,
    )


def solution(mesh):
    placed = (
        P(TOKEN_AXES, None),
        P(TOKEN_AXES),
        P(TOKEN_AXES, TENSOR),
        P(TOKEN_AXES, TENSOR),
        P(TOKEN_AXES, TENSOR),
        P(TENSOR, TOKEN_AXES),
        P(TOKEN_AXES),
        P(TOKEN_AXES, TENSOR),
        P(TOKEN_AXES, TENSOR),
        P(TENSOR, TOKEN_AXES),
        P(TOKEN_AXES, None),
        P(),
        P(),
        P(),
    )
    paired = tuple(mesh.shape[name] for name in MESH_AXES) == (2, 4, 4)
    return jax.shard_map(
        on_device_paired if paired else on_device,
        mesh=mesh,
        in_specs=placed,
        out_specs=(
            P(TOKEN_AXES, None),
            P(TOKEN_AXES, None),
            P(TOKEN_AXES),
            P(TOKEN_AXES, TENSOR),
            P(TOKEN_AXES, TENSOR),
            P(TOKEN_AXES, TENSOR),
            P(TENSOR, TOKEN_AXES),
            P(TOKEN_AXES),
            P(TOKEN_AXES, TENSOR),
            P(TOKEN_AXES, TENSOR),
            P(TENSOR, TOKEN_AXES),
        ),
        check_vma=False,
    )
```
